32 devices in a mesh: ctx: 8 (over z, y), fsdp: 4 (over x, core).
Axes of the slice: x: 2, y: 2, z: 4, core: 2. Of those that a mesh axis runs over, the one named last changes fastest.
Arguments:
- tokens: bfloat16 [4, 2048, 768], P('fsdp', 'ctx'), may hold values from -6 to 6
- cotangent: bfloat16 [4, 2048, 768], P('fsdp', 'ctx'), may hold values from -6 to 6
- lengths: int32 [4], P('fsdp'), may hold values from 512 to 2048, as said below
- pairing: int32 [16], replicated, may hold values from 0 to 15, as said below
- w_qkv: bfloat16 [768, 2304], P('fsdp'), may hold values from -0.21875 to 0.21875
- bias_q: bfloat16 [768], P('fsdp'), may hold values from -3 to 3
- bias_v: bfloat16 [768], P('fsdp'), may hold values from -3 to 3
- w_out: bfloat16 [768, 768], P('fsdp'), may hold values from -6 to 6
- bias_out: bfloat16 [768], P('fsdp'), may hold values from -3 to 3
- ln1_gain: bfloat16 [768], P('fsdp'), may hold values from 0.099609375 to 1.8984375
- ln1_bias: bfloat16 [768], P('fsdp'), may hold values from -3 to 3
- w_in: bfloat16 [768, 3072], P('fsdp'), may hold values from -0.21875 to 0.21875
- bias_in: bfloat16 [3072], P('fsdp'), may hold values from -3 to 3
- w_back: bfloat16 [3072, 768], P('fsdp'), may hold values from -0.109375 to 0.109375
- bias_back: bfloat16 [768], P('fsdp'), may hold values from -3 to 3
- ln2_gain: bfloat16 [768], P('fsdp'), may hold values from 0.099609375 to 1.8984375
- ln2_bias: bfloat16 [768], P('fsdp'), may hold values from -3 to 3
Outputs:
- output: float32 [4, 2048, 768], P('fsdp', 'ctx')
- token_grad: float32 [4, 2048, 768], P('fsdp', 'ctx')
- w_qkv_grad: float32 [768, 2304], P('fsdp')
- bias_q_grad: float32 [768], P('fsdp')
- bias_v_grad: float32 [768], P('fsdp')
- w_out_grad: float32 [768, 768], P('fsdp')
- bias_out_grad: float32 [768], P('fsdp')
- ln1_gain_grad: float32 [768], P('fsdp')
- ln1_bias_grad: float32 [768], P('fsdp')
- w_in_grad: float32 [768, 3072], P('fsdp')
- bias_in_grad: float32 [3072], P('fsdp')
- w_back_grad: float32 [3072, 768], P('fsdp')
- bias_back_grad: float32 [768], P('fsdp')
- ln2_gain_grad: float32 [768], P('fsdp')
- ln2_bias_grad: float32 [768], P('fsdp')
The draws below stay inside these ranges and needn't reach their ends.
Inputs may be any that keep to these rules, and one draw needn't show every extreme that they name: `lengths`: every draw has a sequence that fills all 2048 slots. `pairing`: ctx index i stores storage blocks 2i and 2i + 1, which are the sequence's blocks t and 15 - t for some t; each block appears once.
All inputs are finite; a program needn't handle non-finite values.
Results may differ from the reference program's by a relative error of at most 0.02.
Values may be sent and summed in bfloat16 or wider, within the bound.
A program may use at most 192 MiB of HBM per device.

```python
import math
import jax
import jax.numpy as jnp
from jax import lax

D = 768
HEADS = 12
HEAD_DIM = 64
FF = 3072
NMEM = 10
BLK = 128
SLOTS = 2048
BLOCKS = 16
SEQS = 4


def draw_lengths(key, part):
    base = jax.random.randint(jax.random.fold_in(key, 11), (SEQS,), SLOTS // 4, SLOTS + 1)
    chosen = jax.random.randint(jax.random.fold_in(key, 12), (), 0, SEQS)
    return jnp.where(jnp.arange(SEQS) == chosen, SLOTS, base).astype(jnp.int32)


def draw_pairing(key, part):
    order = jax.random.permutation(jax.random.fold_in(key, 13), BLOCKS // 2).astype(jnp.int32)
    return jnp.stack([order, BLOCKS - 1 - order], axis=1).reshape(BLOCKS).astype(jnp.int32)


def steps_of(stream_key, extent, pieces, smallest, top_value):
    loudness, own = 1.0, jax.random.fold_in(stream_key, 6)
    for axis_at, parts in pieces:
        heights = jnp.exp(jax.random.uniform(jax.random.fold_in(own, axis_at), (parts,), jnp.float32, smallest / len(pieces), top_value / len(pieces)))
        loudness = loudness * jnp.repeat(heights, extent[axis_at] // parts).reshape([-1 if axis == axis_at else 1 for axis in range(len(extent))])
    return loudness


def noise(stream_key, extent, deviation, reach, cuts=(), kind=jnp.bfloat16):
    loudness = steps_of(stream_key, extent, cuts, -0.22, 0.18) if cuts else 1.0
    drawn = jax.random.normal(stream_key, extent, jnp.float32) * deviation * loudness
    return jnp.minimum(jnp.maximum(drawn, -reach), reach).astype(kind)


def setup_inputs(seed: int = 0) -> dict:
    key_list = jax.random.split(jax.random.key(seed), 18)
    return {
        "tokens": noise(key_list[0], (SEQS, SLOTS, D), 1.0, 6.0, ((0, 4), (1, 8))),
        "cotangent": noise(key_list[1], (SEQS, SLOTS, D), 1.0, 6.0, ((0, 4), (1, 8))),
        "lengths": draw_lengths(jax.random.fold_in(key_list[17], 71), 0),
        "pairing": draw_pairing(jax.random.fold_in(key_list[17], 71), 0),
        "w_qkv": noise(key_list[4], (D, 3 * D), D ** -0.5, 0.21875, ((0, 4),)),
        "bias_q": noise(key_list[5], (D,), 0.5, 3.0, ((0, 4),)),
        "bias_v": noise(key_list[6], (D,), 0.5, 3.0, ((0, 4),)),
        "w_out": noise(key_list[7], (D, D), 1 ** -0.5, 6.0, ((0, 4),)),
        "bias_out": noise(key_list[8], (D,), 0.5, 3.0, ((0, 4),)),
        "ln1_gain": jnp.clip(1.0 + 0.18 * jax.random.normal(key_list[9], (D,), jnp.float32), 0.099609375, 1.8984375).astype(jnp.bfloat16),
        "ln1_bias": noise(key_list[10], (D,), 0.5, 3.0, ((0, 4),)),
        "w_in": noise(key_list[11], (D, FF), D ** -0.5, 0.21875, ((0, 4),)),
        "bias_in": noise(key_list[12], (FF,), 0.5, 3.0, ((0, 4),)),
        "w_back": noise(key_list[13], (FF, D), FF ** -0.5, 0.109375, ((0, 4),)),
        "bias_back": noise(key_list[14], (D,), 0.5, 3.0, ((0, 4),)),
        "ln2_gain": jnp.clip(1.0 + 0.18 * jax.random.normal(key_list[15], (D,), jnp.float32), 0.099609375, 1.8984375).astype(jnp.bfloat16),
        "ln2_bias": noise(key_list[16], (D,), 0.5, 3.0, ((0, 4),)),
    }


@jax.custom_vjp
def low(v):
    return lax.optimization_barrier(v.astype(jnp.bfloat16)).astype(jnp.float32)

@jax.custom_vjp
def low_back(v):
    return v

def low_keep(v):
    return (low(v), None)

def low_pass(kept, grad):
    return (grad,)

def back_keep(v):
    return (v, None)

def back_low(kept, grad):
    return (low(grad),)
low.defvjp(low_keep, low_pass)
low_back.defvjp(back_keep, back_low)
eps = 1e-12
neg_big = -1e+30
highest = lax.Precision.HIGHEST

def layer_norm(value, gain, shift):
    mean = lax.optimization_barrier(jnp.mean(value, axis=-1, keepdims=True))
    centred = value - mean
    variance = lax.optimization_barrier(jnp.mean(centred * centred, axis=-1, keepdims=True))
    return centred * lax.rsqrt(variance + eps) * gain + shift

def attend(queries, keys, values, place, valid):
    block = math.gcd(SLOTS, 512)
    count = SLOTS // block

    def one_block(item):
        query_block, place_block = item
        scores = low_back(jnp.einsum('qhd,khd->hqk', query_block, keys, precision=highest) * 0.125)
        allowed = valid[None, :] & ((place[None, :] <= place_block[:, None]) | (place[None, :] < NMEM))
        scores = jnp.where(allowed[None], scores, neg_big)
        top = lax.optimization_barrier(jnp.max(scores, axis=-1, keepdims=True))
        expo = jnp.where(allowed[None], jnp.exp(scores - top), 0.0)
        probs = expo / lax.optimization_barrier(jnp.sum(expo, axis=-1, keepdims=True))
        return jnp.einsum('hqk,khd->qhd', low(probs), values, precision=highest)
    blocks = (queries.reshape(count, block, HEADS, HEAD_DIM), place.reshape(count, block))
    return lax.map(jax.checkpoint(one_block), blocks).reshape(SLOTS, HEADS * HEAD_DIM)

def forward(params, tokens, place, valid):
    w_qkv, bias_q, bias_v, w_out, bias_out, ln1_gain, ln1_bias, w_in, bias_in, w_back, bias_back, ln2_gain, ln2_bias = params
    proj = jnp.dot(tokens, w_qkv, precision=highest)
    queries = low(low_back(proj[:, :D] + bias_q))
    keys = low(low_back(proj[:, D:2 * D]))
    values = low(low_back(proj[:, 2 * D:] + bias_v))
    shape = (SLOTS, HEADS, HEAD_DIM)
    attended = attend(queries.reshape(shape), keys.reshape(shape), values.reshape(shape), place, valid)
    attended = low(low_back(attended))
    branch = low_back(jnp.dot(attended, w_out, precision=highest) + bias_out)
    hidden = layer_norm(tokens + branch, ln1_gain, ln1_bias)
    upper = low_back(jnp.dot(low(hidden), w_in, precision=highest) + bias_in)
    active = low(jax.nn.gelu(upper, approximate=False))
    mixed = low_back(jnp.dot(active, w_back, precision=highest) + bias_back)
    normed = layer_norm(hidden + mixed, ln2_gain, ln2_bias)
    return jnp.where(valid[:, None], normed, 0.0)

def reference(tokens, cotangent, lengths, pairing, w_qkv, bias_q, bias_v, w_out, bias_out, ln1_gain, ln1_bias, w_in, bias_in, w_back, bias_back, ln2_gain, ln2_bias):
    params = tuple((entry.astype(jnp.float32) for entry in (w_qkv, bias_q, bias_v, w_out, bias_out, ln1_gain, ln1_bias, w_in, bias_in, w_back, bias_back, ln2_gain, ln2_bias)))
    rows = jnp.arange(SLOTS, dtype=jnp.int32)
    place = (jnp.take(pairing, rows // BLK) * BLK + rows % BLK).astype(jnp.int32)

    def one_sequence(totals, entry):
        inputs, grad_out, length = entry
        valid = place < length

        def run(weights, values):
            return forward(weights, values, place, valid)
        output, pull = jax.vjp(run, params, inputs.astype(jnp.float32))
        weight_grads, input_grad = pull(grad_out.astype(jnp.float32))
        totals = tuple((jnp.add(left, right) for left, right in zip(totals, weight_grads)))
        return (totals, (output, input_grad))
    start = tuple((jnp.zeros_like(entry) for entry in params))
    totals, (outputs, input_grads) = lax.scan(one_sequence, start, (tokens, cotangent, lengths))
    return (outputs, input_grads) + totals
```

```python
import functools
import math

import jax
import jax.numpy as jnp
from jax import lax
from jax.experimental import pallas as pl
from jax.experimental.pallas import tpu as pltpu
from jax.sharding import PartitionSpec as P

HEADS = 12
HEAD_DIM = 64
NMEM = 10
BLK = 128


eps = 1e-12
neg_big = -1e30


def layer_norm(value, gain, shift):
    mean = jnp.mean(value, axis=-1, keepdims=True)
    centred = value - mean
    variance = jnp.mean(centred * centred, axis=-1, keepdims=True)
    return centred * lax.rsqrt(variance + eps) * gain + shift


def norm_back(value, gain, grad):
    mean = jnp.mean(value, axis=-1, keepdims=True)
    centred = value - mean
    scale = lax.rsqrt(jnp.mean(centred * centred, axis=-1, keepdims=True) + eps)
    unit = centred * scale
    scaled = grad * gain
    inner = (
        scaled
        - jnp.mean(scaled, axis=-1, keepdims=True)
        - unit * jnp.mean(scaled * unit, axis=-1, keepdims=True)
    )
    return (scale * inner, jnp.sum(grad * unit, axis=0), jnp.sum(grad, axis=0))


def block_width(count):
    return math.gcd(count, 512)


def places(pairing, start, count, half):
    rows = start + jnp.arange(count, dtype=jnp.int32)
    owners = rows // half
    spots = jnp.arange(pairing.shape[0], dtype=jnp.int32)
    picked = jnp.sum(jnp.where(owners[:, None] == spots[None, :], pairing[None, :], 0), axis=1)
    return picked * half + rows % half


def allowed_pairs(query_place, key_place, length):
    before = (key_place[None, :] <= query_place[:, None]) | (key_place[None, :] < NMEM)
    return (key_place[None, :] < length) & before


def heads_of(value):
    return value.reshape(value.shape[0], HEADS, HEAD_DIM)


def forward_fold(query_heads, query_place, pairing, length, half):

    def fold(carry, piece, start):
        keys, values = piece
        count = keys.shape[0]
        width = block_width(count)
        key_place = places(pairing, start, count, half)

        def step(index, state):
            top, total, summed = state
            offset = index * width
            key_heads = heads_of(lax.dynamic_slice_in_dim(keys, offset, width, 0))
            value_heads = heads_of(lax.dynamic_slice_in_dim(values, offset, width, 0))
            mask = allowed_pairs(
                query_place, lax.dynamic_slice_in_dim(key_place, offset, width, 0), length
            )[None]
            scores = (
                jnp.einsum(
                    "qhd,khd->hqk", query_heads, key_heads, preferred_element_type=jnp.float32
                )
                * 0.125
            )
            scores = jnp.where(mask, scores, neg_big)
            new_top = jnp.maximum(top, jnp.max(scores, axis=2))
            shrink = jnp.exp(top - new_top)
            probs = jnp.where(mask, jnp.exp(scores - new_top[:, :, None]), 0.0)
            total = total * shrink + jnp.sum(probs, axis=2)
            update = jnp.einsum(
                "hqk,khd->qhd",
                probs.astype(jnp.bfloat16),
                value_heads,
                preferred_element_type=jnp.float32,
            )
            summed = summed * jnp.transpose(shrink)[:, :, None] + update
            return (new_top, total, summed)

        return lax.fori_loop(0, count // width, step, carry)

    return fold


def query_grad_fold(query_heads, grad_heads, top_sum, delta, query_place, pairing, length, half):

    def fold(carry, piece, start):
        keys, values = piece
        count = keys.shape[0]
        width = block_width(count)
        key_place = places(pairing, start, count, half)

        def step(index, summed):
            offset = index * width
            key_heads = heads_of(lax.dynamic_slice_in_dim(keys, offset, width, 0))
            value_heads = heads_of(lax.dynamic_slice_in_dim(values, offset, width, 0))
            mask = allowed_pairs(
                query_place, lax.dynamic_slice_in_dim(key_place, offset, width, 0), length
            )[None]
            scores = (
                jnp.einsum(
                    "qhd,khd->hqk", query_heads, key_heads, preferred_element_type=jnp.float32
                )
                * 0.125
            )
            probs = jnp.where(mask, jnp.exp(scores - top_sum[:, :, None]), 0.0)
            prob_grad = jnp.einsum(
                "qhd,khd->hqk", grad_heads, value_heads, preferred_element_type=jnp.float32
            )
            score_grad = (probs * (prob_grad - delta[:, :, None])).astype(jnp.bfloat16)
            return (
                summed
                + jnp.einsum(
                    "hqk,khd->qhd", score_grad, key_heads, preferred_element_type=jnp.float32
                )
                * 0.125
            )

        return lax.fori_loop(0, count // width, step, carry)

    return fold


def key_terms(
    key_heads, value_heads, key_place, query_heads, grad_heads, top_sum, delta, query_place, length
):
    scores = (
        jnp.einsum("qhd,khd->hqk", query_heads, key_heads, preferred_element_type=jnp.float32)
        * 0.125
    )
    mask = allowed_pairs(query_place, key_place, length)[None]
    probs = jnp.where(mask, jnp.exp(scores - top_sum[:, :, None]), 0.0)
    prob_grad = jnp.einsum(
        "qhd,khd->hqk", grad_heads, value_heads, preferred_element_type=jnp.float32
    )
    score_grad = (probs * (prob_grad - delta[:, :, None])).astype(jnp.bfloat16)
    value_grad = jnp.einsum(
        "hqk,qhd->khd", probs.astype(jnp.bfloat16), grad_heads, preferred_element_type=jnp.float32
    )
    key_grad = (
        jnp.einsum("hqk,qhd->khd", score_grad, query_heads, preferred_element_type=jnp.float32)
        * 0.125
    )
    return (key_grad, value_grad)


def on_device_any(
    tokens,
    cotangent,
    lengths,
    pairing,
    w_qkv,
    bias_q,
    bias_v,
    w_out,
    bias_out,
    ln1_gain,
    ln1_bias,
    w_in,
    bias_in,
    w_back,
    bias_back,
    ln2_gain,
    ln2_bias,
):
    gathered = (
        lax.all_gather(w_qkv, "fsdp", axis=0, tiled=True),
        lax.all_gather(bias_q, "fsdp", axis=0, tiled=True),
        lax.all_gather(bias_v, "fsdp", axis=0, tiled=True),
        lax.all_gather(w_out, "fsdp", axis=0, tiled=True),
        lax.all_gather(bias_out, "fsdp", axis=0, tiled=True),
        lax.all_gather(ln1_gain, "fsdp", axis=0, tiled=True),
        lax.all_gather(ln1_bias, "fsdp", axis=0, tiled=True),
        lax.all_gather(w_in, "fsdp", axis=0, tiled=True),
        lax.all_gather(bias_in, "fsdp", axis=0, tiled=True),
        lax.all_gather(w_back, "fsdp", axis=0, tiled=True),
        lax.all_gather(bias_back, "fsdp", axis=0, tiled=True),
        lax.all_gather(ln2_gain, "fsdp", axis=0, tiled=True),
        lax.all_gather(ln2_bias, "fsdp", axis=0, tiled=True),
    )
    (
        qkv_all,
        query_bias,
        value_bias,
        out_all,
        out_bias,
        gain_one,
        shift_one,
        in_all,
        in_bias,
        back_all,
        back_bias,
        gain_two,
        shift_two,
    ) = gathered
    rows = tokens.shape[1]
    half = rows // 2
    width = tokens.shape[2]
    length = lengths[0]
    query_place = places(pairing, lax.axis_index("ctx") * rows, rows, half)
    valid = query_place < length
    inputs = tokens[0]
    proj = jnp.dot(inputs, qkv_all, preferred_element_type=jnp.float32)
    queries = (proj[:, :width] + query_bias.astype(jnp.float32)).astype(jnp.bfloat16)
    keys = proj[:, width : 2 * width].astype(jnp.bfloat16)
    values = (proj[:, 2 * width :] + value_bias.astype(jnp.float32)).astype(jnp.bfloat16)
    query_heads = heads_of(queries)
    start_state = (
        jnp.full((HEADS, rows), neg_big, jnp.float32),
        jnp.zeros((HEADS, rows), jnp.float32),
        jnp.zeros((rows, HEADS, HEAD_DIM), jnp.float32),
    )
    fold = forward_fold(query_heads, query_place, pairing, length, half)
    top, total, summed = fold(
        start_state,
        (
            lax.all_gather(keys, "ctx", axis=0, tiled=True),
            lax.all_gather(values, "ctx", axis=0, tiled=True),
        ),
        jnp.int32(0),
    )
    top_sum = top + jnp.log(total)
    attended = (summed / jnp.transpose(total)[:, :, None]).reshape(rows, width)
    attended_low = attended.astype(jnp.bfloat16)
    resid_one = (
        inputs.astype(jnp.float32)
        + jnp.dot(attended_low, out_all, preferred_element_type=jnp.float32)
        + out_bias.astype(jnp.float32)
    )
    hidden = layer_norm(resid_one, gain_one.astype(jnp.float32), shift_one.astype(jnp.float32))
    hidden_low = hidden.astype(jnp.bfloat16)
    upper = jnp.dot(hidden_low, in_all, preferred_element_type=jnp.float32) + in_bias.astype(
        jnp.float32
    )
    active, gelu_back = jax.vjp(lambda value: jax.nn.gelu(value, approximate=False), upper)
    active_low = active.astype(jnp.bfloat16)
    resid_two = (
        hidden
        + jnp.dot(active_low, back_all, preferred_element_type=jnp.float32)
        + back_bias.astype(jnp.float32)
    )
    normed = layer_norm(resid_two, gain_two.astype(jnp.float32), shift_two.astype(jnp.float32))
    output = jnp.where(valid[:, None], normed, 0.0)
    qkv_back, out_back, gain_one_back, in_back, back_back, gain_two_back = (
        qkv_all,
        out_all,
        gain_one,
        in_all,
        back_all,
        gain_two,
    )
    grad_y = jnp.where(valid[:, None], cotangent[0].astype(jnp.float32), 0.0)
    grad_resid_two, gain_two_grad, shift_two_grad = norm_back(
        resid_two, gain_two_back.astype(jnp.float32), grad_y
    )
    grad_mixed = grad_resid_two.astype(jnp.bfloat16)
    back_grad = jnp.einsum("tf,td->fd", active_low, grad_mixed, preferred_element_type=jnp.float32)
    back_bias_grad = jnp.sum(grad_mixed.astype(jnp.float32), axis=0)
    grad_active = jnp.einsum("td,fd->tf", grad_mixed, back_back, preferred_element_type=jnp.float32)
    (grad_upper,) = gelu_back(grad_active)
    grad_upper_low = grad_upper.astype(jnp.bfloat16)
    in_grad = jnp.einsum(
        "td,tf->df", hidden_low, grad_upper_low, preferred_element_type=jnp.float32
    )
    in_bias_grad = jnp.sum(grad_upper_low.astype(jnp.float32), axis=0)
    grad_hidden = grad_resid_two + jnp.einsum(
        "tf,df->td", grad_upper_low, in_back, preferred_element_type=jnp.float32
    )
    grad_resid_one, gain_one_grad, shift_one_grad = norm_back(
        resid_one, gain_one_back.astype(jnp.float32), grad_hidden
    )
    grad_branch = grad_resid_one.astype(jnp.bfloat16)
    out_grad = jnp.einsum(
        "tc,td->cd", attended_low, grad_branch, preferred_element_type=jnp.float32
    )
    out_bias_grad = jnp.sum(grad_branch.astype(jnp.float32), axis=0)
    grad_attended = jnp.einsum(
        "td,cd->tc", grad_branch, out_back, preferred_element_type=jnp.float32
    ).astype(jnp.bfloat16)
    grad_heads = heads_of(grad_attended)
    delta = jnp.transpose(jnp.sum(grad_heads.astype(jnp.float32) * heads_of(attended), axis=2))
    query_fold = query_grad_fold(
        query_heads, grad_heads, top_sum, delta, query_place, pairing, length, half
    )
    empty_heads = jnp.zeros((rows, HEADS, HEAD_DIM), jnp.float32)
    query_grad = query_fold(
        empty_heads,
        (
            lax.all_gather(keys, "ctx", axis=0, tiled=True),
            lax.all_gather(values, "ctx", axis=0, tiled=True),
        ),
        jnp.int32(0),
    )
    stats = jnp.concatenate([jnp.transpose(top_sum), jnp.transpose(delta)], axis=1)
    stats_all = lax.all_gather(stats, "ctx", axis=0, tiled=True)
    key_heads = heads_of(keys)
    value_heads = heads_of(values)
    query_in = lax.all_gather(queries, "ctx", axis=0, tiled=True)
    grad_in = lax.all_gather(grad_attended, "ctx", axis=0, tiled=True)
    count = query_in.shape[0]
    span = block_width(count)
    place_in = places(pairing, jnp.int32(0), count, half)

    def step(index, state):
        offset = index * span
        query_block = heads_of(lax.dynamic_slice_in_dim(query_in, offset, span, 0))
        grad_block = heads_of(lax.dynamic_slice_in_dim(grad_in, offset, span, 0))
        stats_block = lax.dynamic_slice_in_dim(stats_all, offset, span, 0)
        place_block = lax.dynamic_slice_in_dim(place_in, offset, span, 0)
        key_part, value_part = key_terms(
            key_heads,
            value_heads,
            query_place,
            query_block,
            grad_block,
            jnp.transpose(stats_block[:, :HEADS]),
            jnp.transpose(stats_block[:, HEADS:]),
            place_block,
            length,
        )
        return (state[0] + key_part, state[1] + value_part)

    key_sum, value_sum = lax.fori_loop(0, count // span, step, (empty_heads, empty_heads))
    key_grad = key_sum.reshape(rows, width)
    value_grad = value_sum.reshape(rows, width)
    grad_proj = jnp.concatenate(
        [
            query_grad.reshape(rows, width).astype(jnp.bfloat16),
            key_grad.astype(jnp.bfloat16),
            value_grad.astype(jnp.bfloat16),
        ],
        axis=1,
    )
    qkv_grad = jnp.einsum("td,tf->df", inputs, grad_proj, preferred_element_type=jnp.float32)
    query_bias_grad = jnp.sum(grad_proj[:, :width].astype(jnp.float32), axis=0)
    value_bias_grad = jnp.sum(grad_proj[:, 2 * width :].astype(jnp.float32), axis=0)
    token_grad = grad_resid_one + jnp.einsum(
        "tf,df->td", grad_proj, qkv_back, preferred_element_type=jnp.float32
    )
    grads = (
        qkv_grad,
        query_bias_grad,
        value_bias_grad,
        out_grad,
        out_bias_grad,
        gain_one_grad,
        shift_one_grad,
        in_grad,
        in_bias_grad,
        back_grad,
        back_bias_grad,
        gain_two_grad,
        shift_two_grad,
    )
    shards = (
        lax.psum_scatter(
            grads[0].astype(jnp.bfloat16), "fsdp", scatter_dimension=0, tiled=True
        ).astype(jnp.float32),
        lax.psum_scatter(
            grads[1].astype(jnp.bfloat16), "fsdp", scatter_dimension=0, tiled=True
        ).astype(jnp.float32),
        lax.psum_scatter(
            grads[2].astype(jnp.bfloat16), "fsdp", scatter_dimension=0, tiled=True
        ).astype(jnp.float32),
        lax.psum_scatter(
            grads[3].astype(jnp.bfloat16), "fsdp", scatter_dimension=0, tiled=True
        ).astype(jnp.float32),
        lax.psum_scatter(
            grads[4].astype(jnp.bfloat16), "fsdp", scatter_dimension=0, tiled=True
        ).astype(jnp.float32),
        lax.psum_scatter(
            grads[5].astype(jnp.bfloat16), "fsdp", scatter_dimension=0, tiled=True
        ).astype(jnp.float32),
        lax.psum_scatter(
            grads[6].astype(jnp.bfloat16), "fsdp", scatter_dimension=0, tiled=True
        ).astype(jnp.float32),
        lax.psum_scatter(
            grads[7].astype(jnp.bfloat16), "fsdp", scatter_dimension=0, tiled=True
        ).astype(jnp.float32),
        lax.psum_scatter(
            grads[8].astype(jnp.bfloat16), "fsdp", scatter_dimension=0, tiled=True
        ).astype(jnp.float32),
        lax.psum_scatter(
            grads[9].astype(jnp.bfloat16), "fsdp", scatter_dimension=0, tiled=True
        ).astype(jnp.float32),
        lax.psum_scatter(
            grads[10].astype(jnp.bfloat16), "fsdp", scatter_dimension=0, tiled=True
        ).astype(jnp.float32),
        lax.psum_scatter(
            grads[11].astype(jnp.bfloat16), "fsdp", scatter_dimension=0, tiled=True
        ).astype(jnp.float32),
        lax.psum_scatter(
            grads[12].astype(jnp.bfloat16), "fsdp", scatter_dimension=0, tiled=True
        ).astype(jnp.float32),
    )
    totals = (
        lax.psum(shards[0].astype(jnp.bfloat16), "ctx").astype(jnp.float32),
        lax.psum(shards[1].astype(jnp.bfloat16), "ctx").astype(jnp.float32),
        lax.psum(shards[2].astype(jnp.bfloat16), "ctx").astype(jnp.float32),
        lax.psum(shards[3].astype(jnp.bfloat16), "ctx").astype(jnp.float32),
        lax.psum(shards[4].astype(jnp.bfloat16), "ctx").astype(jnp.float32),
        lax.psum(shards[5].astype(jnp.bfloat16), "ctx").astype(jnp.float32),
        lax.psum(shards[6].astype(jnp.bfloat16), "ctx").astype(jnp.float32),
        lax.psum(shards[7].astype(jnp.bfloat16), "ctx").astype(jnp.float32),
        lax.psum(shards[8].astype(jnp.bfloat16), "ctx").astype(jnp.float32),
        lax.psum(shards[9].astype(jnp.bfloat16), "ctx").astype(jnp.float32),
        lax.psum(shards[10].astype(jnp.bfloat16), "ctx").astype(jnp.float32),
        lax.psum(shards[11].astype(jnp.bfloat16), "ctx").astype(jnp.float32),
        lax.psum(shards[12].astype(jnp.bfloat16), "ctx").astype(jnp.float32),
    )
    return (output[None], token_grad[None]) + tuple(totals)


MESH = pl.DeviceIdType.MESH


def exchange_kernel(n, in_ref, out_ref, sent, landed, own):
    me = lax.axis_index("ctx")
    barrier = pltpu.get_barrier_semaphore()
    for k in range(1, n):
        pl.semaphore_signal(
            barrier, inc=1, device_id={"ctx": lax.rem(me + k, n)}, device_id_type=MESH
        )
    pl.semaphore_wait(barrier, n - 1)
    copies = []
    for k in range(1, n):
        peer = lax.rem(me + k, n)
        copy = pltpu.make_async_remote_copy(
            src_ref=in_ref.at[peer],
            dst_ref=out_ref.at[me],
            send_sem=sent.at[k],
            recv_sem=landed.at[k],
            device_id={"ctx": peer},
            device_id_type=MESH,
        )
        copy.start()
        copies.append(copy)
    local = pltpu.make_async_copy(in_ref.at[me], out_ref.at[me], own)
    local.start()
    local.wait()
    for copy in copies:
        copy.wait()


def exchange(blocks, name):
    n = blocks.shape[0]
    return pl.pallas_call(
        functools.partial(exchange_kernel, n),
        out_shape=jax.ShapeDtypeStruct(blocks.shape, blocks.dtype),
        in_specs=[vmem()],
        out_specs=vmem(),
        scratch_shapes=[
            pltpu.SemaphoreType.DMA((n,)),
            pltpu.SemaphoreType.DMA((n,)),
            pltpu.SemaphoreType.DMA,
        ],
        compiler_params=pltpu.CompilerParams(
            collective_id=name, has_side_effects=True, vmem_limit_bytes=16 << 20
        ),
        name="exchange",
    )(blocks)


def split_heads(value):
    rows = value.shape[0]
    trio = value.reshape(rows, HEADS // 3, 3, HEAD_DIM)
    own = trio[:, :, :2]
    shared = jnp.broadcast_to(trio[:, :, 2:], own.shape)
    both = jnp.concatenate([own, shared], axis=-1)
    return jnp.transpose(both.reshape(rows, -1, 2 * HEAD_DIM), (1, 0, 2))


def send_blocks(queries, keys, values):
    return jnp.concatenate([split_heads(queries), split_heads(keys), split_heads(values)], axis=2)


def join_heads(blocks):
    rows = blocks.shape[1]
    pairs = blocks.reshape(HEADS // 3, 2, rows, 2, HEAD_DIM)
    shared = pairs[:, 0, :, 1].astype(jnp.float32) + pairs[:, 1, :, 1].astype(jnp.float32)
    trio = jnp.stack([pairs[:, 0, :, 0], pairs[:, 1, :, 0], shared.astype(blocks.dtype)], axis=2)
    return jnp.transpose(trio, (1, 0, 2, 3)).reshape(rows, HEADS * HEAD_DIM)


def join_parts(blocks):
    parts = jnp.split(blocks, 3, axis=2)
    return jnp.concatenate([join_heads(part) for part in parts], axis=1)


BLK = 128


def low_lanes(shape):
    return lax.broadcasted_iota(jnp.int32, shape, 1) < 64


def attend_kernel(chunks, pair_ref, len_ref, spot_ref, in_ref, out_ref, keep_ref, mix_ref, lse_ref):
    length = len_ref[0]
    spot = spot_ref[0]
    blocks = 2 * chunks
    for s in range(blocks):
        keep_ref[pair_ref[s]] = in_ref[s]
    left = low_lanes((256, BLK))
    left_half = left[:BLK]
    for c in range(chunks):
        keys = 256 * (c + 1)
        own = keep_ref[2 * c : 2 * c + 2, :, :BLK].reshape(256, BLK)
        shared = keep_ref[2 * c + spot, :, :BLK]
        zero = jnp.zeros((), jnp.bfloat16)
        query = jnp.concatenate(
            [jnp.where(left, own, zero), jnp.where(left_half, zero, shared)], axis=0
        ) * jnp.bfloat16(0.125)
        key = keep_ref[: 2 * c + 2, :, BLK : 2 * BLK].reshape(keys, BLK)
        value = keep_ref[: 2 * c + 2, :, 2 * BLK :].reshape(keys, BLK)
        scores = mask_scores(
            lax.dot_general(key, query, (((1,), (1,)), ((), ())), preferred_element_type=jnp.float32),
            c, spot, length,
        )
        top = jnp.max(scores, axis=0, keepdims=True)
        probs = jnp.exp(scores - top)
        total = jnp.sum(probs, axis=0, keepdims=True)
        summed = lax.dot_general(
            value, probs.astype(jnp.bfloat16), (((0,), (0,)), ((), ())),
            preferred_element_type=jnp.float32,
        ) / total
        lse_ref[c] = top + jnp.log(total)
        part = summed[64:, 256:]
        none = jnp.zeros_like(part)
        first = jnp.where(spot == 0, part, none)
        second = jnp.where(spot == 0, none, part)
        mixed = jnp.concatenate(
            [summed[:64, :256], jnp.concatenate([first, second], axis=1)], axis=0
        )
        mix_ref[c] = mixed
    for s in range(blocks):
        place = pair_ref[s]
        c = place // 2
        piece = mix_ref[c, :, pl.ds(pl.multiple_of((place % 2) * BLK, BLK), BLK)]
        out_ref[s] = jnp.transpose(piece).astype(jnp.bfloat16)


def mask_scores(scores, c, spot, length):
    keys, width = scores.shape
    edge = 256 * c
    row = lax.broadcasted_iota(jnp.int32, (keys, width), 0)
    scores = jnp.where(row < length, scores, neg_big)
    lane = lax.broadcasted_iota(jnp.int32, (256, width), 1)
    query_place = edge + jnp.where(lane < 256, lane, lane - 256 + spot * BLK)
    key_place = edge + lax.broadcasted_iota(jnp.int32, (256, width), 0)
    seen = key_place <= query_place
    if c == 0:
        seen = seen | (key_place < NMEM)
    tail = jnp.where(seen, scores[edge:], neg_big)
    if c == 0:
        return tail
    return jnp.concatenate([scores[:edge], tail], axis=0)


def attend_back_kernel(
    chunks, pair_ref, len_ref, spot_ref, keep_ref, grad_ref, mix_ref, lse_ref, out_ref, g_ref,
    q_sum, k_sum, v_sum
):
    length = len_ref[0]
    spot = spot_ref[0]
    blocks = 2 * chunks
    for s in range(blocks):
        g_ref[pair_ref[s]] = grad_ref[s]
    k_sum[...] = jnp.zeros_like(k_sum)
    v_sum[...] = jnp.zeros_like(v_sum)
    left = low_lanes((256, BLK))
    left_half = left[:BLK]
    zero = jnp.zeros((), jnp.bfloat16)
    for c in range(chunks):
        keys = 256 * (c + 1)
        own = keep_ref[2 * c : 2 * c + 2, :, :BLK].reshape(256, BLK)
        shared = keep_ref[2 * c + spot, :, :BLK]
        query = jnp.concatenate(
            [jnp.where(left, own, zero), jnp.where(left_half, zero, shared)], axis=0
        ) * jnp.bfloat16(0.125)
        g_own = g_ref[2 * c : 2 * c + 2].reshape(256, BLK)
        g_shared = g_ref[2 * c + spot]
        grad = jnp.concatenate(
            [jnp.where(left, g_own, zero), jnp.where(left_half, zero, g_shared)], axis=0
        )
        key = keep_ref[: 2 * c + 2, :, BLK : 2 * BLK].reshape(keys, BLK)
        value = keep_ref[: 2 * c + 2, :, 2 * BLK :].reshape(keys, BLK)
        turned = jnp.transpose(g_own.astype(jnp.float32)) * mix_ref[c]
        delta_own = jnp.sum(turned[:64], axis=0, keepdims=True)
        delta_pair = jnp.sum(turned[64:], axis=0, keepdims=True)
        delta = jnp.concatenate(
            [delta_own, jnp.where(spot == 0, delta_pair[:, :BLK], delta_pair[:, BLK:])], axis=1
        )
        nt = (((1,), (1,)), ((), ()))
        scores = mask_scores(
            lax.dot_general(key, query, nt, preferred_element_type=jnp.float32), c, spot, length
        )
        probs = jnp.exp(scores - lse_ref[c])
        prob_grad = lax.dot_general(value, grad, nt, preferred_element_type=jnp.float32)
        score_grad = (probs * (prob_grad - delta)).astype(jnp.bfloat16)
        nn = (((1,), (0,)), ((), ()))
        v_sum[:keys] += lax.dot_general(
            probs.astype(jnp.bfloat16), grad, nn, preferred_element_type=jnp.float32
        )
        k_sum[:keys] += lax.dot_general(score_grad, query, nn, preferred_element_type=jnp.float32)
        q_grad = lax.dot_general(
            score_grad, key, (((0,), (0,)), ((), ())), preferred_element_type=jnp.float32
        ) * 0.125
        part = q_grad[256:]
        none = jnp.zeros_like(part)
        first = jnp.where(spot == 0, part, none)
        second = jnp.where(spot == 0, none, part)
        q_sum[256 * c : 256 * c + 256] = jnp.where(
            left, q_grad[:256], jnp.concatenate([first, second], axis=0)
        )
    for s in range(blocks):
        rows = pl.ds(pl.multiple_of(pair_ref[s] * BLK, BLK), BLK)
        out_ref[s] = jnp.concatenate([q_sum[rows], k_sum[rows], v_sum[rows]], axis=1).astype(jnp.bfloat16)


def smem():
    return pl.BlockSpec(memory_space=pltpu.SMEM)


def vmem():
    return pl.BlockSpec(memory_space=pltpu.VMEM)


def attend(pairing, lengths, spot, packed):
    blocks = packed.shape[0]
    chunks = blocks // 2
    return pl.pallas_call(
        functools.partial(attend_kernel, chunks),
        out_shape=(
            jax.ShapeDtypeStruct((blocks, BLK, BLK), jnp.bfloat16),
            jax.ShapeDtypeStruct((blocks, BLK, 3 * BLK), jnp.bfloat16),
            jax.ShapeDtypeStruct((chunks, BLK, 256), jnp.float32),
            jax.ShapeDtypeStruct((chunks, 1, 384), jnp.float32),
        ),
        in_specs=[smem(), smem(), smem(), vmem()],
        out_specs=(vmem(), vmem(), vmem(), vmem()),
        compiler_params=pltpu.CompilerParams(vmem_limit_bytes=48 << 20),
        name="attend",
    )(pairing, lengths, spot, packed)


def attend_back(pairing, lengths, spot, keep, grad, mix, lse):
    blocks = keep.shape[0]
    chunks = blocks // 2
    return pl.pallas_call(
        functools.partial(attend_back_kernel, chunks),
        out_shape=jax.ShapeDtypeStruct((blocks, BLK, 3 * BLK), jnp.bfloat16),
        in_specs=[smem(), smem(), smem(), vmem(), vmem(), vmem(), vmem()],
        out_specs=vmem(),
        scratch_shapes=[
            pltpu.VMEM((blocks, BLK, BLK), jnp.bfloat16),
            pltpu.VMEM((blocks * BLK, BLK), jnp.float32),
            pltpu.VMEM((blocks * BLK, BLK), jnp.float32),
            pltpu.VMEM((blocks * BLK, BLK), jnp.float32),
        ],
        compiler_params=pltpu.CompilerParams(vmem_limit_bytes=48 << 20),
        name="attend_back",
    )(pairing, lengths, spot, keep, grad, mix, lse)


def on_device_spread(
    tokens,
    cotangent,
    lengths,
    pairing,
    w_qkv,
    bias_q,
    bias_v,
    w_out,
    bias_out,
    ln1_gain,
    ln1_bias,
    w_in,
    bias_in,
    w_back,
    bias_back,
    ln2_gain,
    ln2_bias,
):
    gathered = (
        lax.all_gather(w_qkv, "fsdp", axis=0, tiled=True),
        lax.all_gather(bias_q, "fsdp", axis=0, tiled=True),
        lax.all_gather(bias_v, "fsdp", axis=0, tiled=True),
        lax.all_gather(w_out, "fsdp", axis=0, tiled=True),
        lax.all_gather(bias_out, "fsdp", axis=0, tiled=True),
        lax.all_gather(ln1_gain, "fsdp", axis=0, tiled=True),
        lax.all_gather(ln1_bias, "fsdp", axis=0, tiled=True),
        lax.all_gather(w_in, "fsdp", axis=0, tiled=True),
        lax.all_gather(bias_in, "fsdp", axis=0, tiled=True),
        lax.all_gather(w_back, "fsdp", axis=0, tiled=True),
        lax.all_gather(bias_back, "fsdp", axis=0, tiled=True),
        lax.all_gather(ln2_gain, "fsdp", axis=0, tiled=True),
        lax.all_gather(ln2_bias, "fsdp", axis=0, tiled=True),
    )
    (
        qkv_all,
        query_bias,
        value_bias,
        out_all,
        out_bias,
        gain_one,
        shift_one,
        in_all,
        in_bias,
        back_all,
        back_bias,
        gain_two,
        shift_two,
    ) = gathered
    rows = tokens.shape[1]
    half = rows // 2
    width = tokens.shape[2]
    length = lengths[0]
    query_place = places(pairing, lax.axis_index("ctx") * rows, rows, half)
    valid = query_place < length
    inputs = tokens[0]
    proj = jnp.dot(inputs, qkv_all, preferred_element_type=jnp.float32)
    queries = (proj[:, :width] + query_bias.astype(jnp.float32)).astype(jnp.bfloat16)
    keys = proj[:, width : 2 * width].astype(jnp.bfloat16)
    values = (proj[:, 2 * width :] + value_bias.astype(jnp.float32)).astype(jnp.bfloat16)
    spot = lax.rem(lax.axis_index("ctx"), 2).astype(jnp.int32).reshape(1)
    sent = send_blocks(queries, keys, values)
    packed = exchange(sent, 0).reshape(-1, half, 6 * HEAD_DIM)
    mixed_out, keep, mix, lse = attend(pairing, lengths, spot, packed)
    attended_low = join_heads(exchange(mixed_out.reshape(-1, rows, 2 * HEAD_DIM), 1))
    resid_one = (
        inputs.astype(jnp.float32)
        + jnp.dot(attended_low, out_all, preferred_element_type=jnp.float32)
        + out_bias.astype(jnp.float32)
    )
    hidden = layer_norm(resid_one, gain_one.astype(jnp.float32), shift_one.astype(jnp.float32))
    hidden_low = hidden.astype(jnp.bfloat16)
    upper = jnp.dot(hidden_low, in_all, preferred_element_type=jnp.float32) + in_bias.astype(
        jnp.float32
    )
    active, gelu_back = jax.vjp(lambda value: jax.nn.gelu(value, approximate=False), upper)
    active_low = active.astype(jnp.bfloat16)
    resid_two = (
        hidden
        + jnp.dot(active_low, back_all, preferred_element_type=jnp.float32)
        + back_bias.astype(jnp.float32)
    )
    normed = layer_norm(resid_two, gain_two.astype(jnp.float32), shift_two.astype(jnp.float32))
    output = jnp.where(valid[:, None], normed, 0.0)
    qkv_back, out_back, gain_one_back, in_back, back_back, gain_two_back = (
        qkv_all,
        out_all,
        gain_one,
        in_all,
        back_all,
        gain_two,
    )
    grad_y = jnp.where(valid[:, None], cotangent[0].astype(jnp.float32), 0.0)
    grad_resid_two, gain_two_grad, shift_two_grad = norm_back(
        resid_two, gain_two_back.astype(jnp.float32), grad_y
    )
    grad_mixed = grad_resid_two.astype(jnp.bfloat16)
    back_grad = jnp.einsum("tf,td->fd", active_low, grad_mixed, preferred_element_type=jnp.float32)
    back_bias_grad = jnp.sum(grad_mixed.astype(jnp.float32), axis=0)
    grad_active = jnp.einsum("td,fd->tf", grad_mixed, back_back, preferred_element_type=jnp.float32)
    (grad_upper,) = gelu_back(grad_active)
    grad_upper_low = grad_upper.astype(jnp.bfloat16)
    in_grad = jnp.einsum(
        "td,tf->df", hidden_low, grad_upper_low, preferred_element_type=jnp.float32
    )
    in_bias_grad = jnp.sum(grad_upper_low.astype(jnp.float32), axis=0)
    grad_hidden = grad_resid_two + jnp.einsum(
        "tf,df->td", grad_upper_low, in_back, preferred_element_type=jnp.float32
    )
    grad_resid_one, gain_one_grad, shift_one_grad = norm_back(
        resid_one, gain_one_back.astype(jnp.float32), grad_hidden
    )
    grad_branch = grad_resid_one.astype(jnp.bfloat16)
    out_grad = jnp.einsum(
        "tc,td->cd", attended_low, grad_branch, preferred_element_type=jnp.float32
    )
    out_bias_grad = jnp.sum(grad_branch.astype(jnp.float32), axis=0)
    grad_attended = jnp.einsum(
        "td,cd->tc", grad_branch, out_back, preferred_element_type=jnp.float32
    ).astype(jnp.bfloat16)
    grad_in = exchange(split_heads(grad_attended), 2).reshape(-1, half, 2 * HEAD_DIM)
    grad_blocks = attend_back(pairing, lengths, spot, keep, grad_in, mix, lse)
    grad_proj = join_parts(exchange(grad_blocks.reshape(-1, rows, 6 * HEAD_DIM), 3))
    qkv_grad = jnp.einsum("td,tf->df", inputs, grad_proj, preferred_element_type=jnp.float32)
    query_bias_grad = jnp.sum(grad_proj[:, :width].astype(jnp.float32), axis=0)
    value_bias_grad = jnp.sum(grad_proj[:, 2 * width :].astype(jnp.float32), axis=0)
    token_grad = grad_resid_one + jnp.einsum(
        "tf,df->td", grad_proj, qkv_back, preferred_element_type=jnp.float32
    )
    grads = (
        qkv_grad,
        query_bias_grad,
        value_bias_grad,
        out_grad,
        out_bias_grad,
        gain_one_grad,
        shift_one_grad,
        in_grad,
        in_bias_grad,
        back_grad,
        back_bias_grad,
        gain_two_grad,
        shift_two_grad,
    )
    shards = (
        lax.psum_scatter(
            grads[0].astype(jnp.bfloat16), "fsdp", scatter_dimension=0, tiled=True
        ).astype(jnp.float32),
        lax.psum_scatter(
            grads[1].astype(jnp.bfloat16), "fsdp", scatter_dimension=0, tiled=True
        ).astype(jnp.float32),
        lax.psum_scatter(
            grads[2].astype(jnp.bfloat16), "fsdp", scatter_dimension=0, tiled=True
        ).astype(jnp.float32),
        lax.psum_scatter(
            grads[3].astype(jnp.bfloat16), "fsdp", scatter_dimension=0, tiled=True
        ).astype(jnp.float32),
        lax.psum_scatter(
            grads[4].astype(jnp.bfloat16), "fsdp", scatter_dimension=0, tiled=True
        ).astype(jnp.float32),
        lax.psum_scatter(
            grads[5].astype(jnp.bfloat16), "fsdp", scatter_dimension=0, tiled=True
        ).astype(jnp.float32),
        lax.psum_scatter(
            grads[6].astype(jnp.bfloat16), "fsdp", scatter_dimension=0, tiled=True
        ).astype(jnp.float32),
        lax.psum_scatter(
            grads[7].astype(jnp.bfloat16), "fsdp", scatter_dimension=0, tiled=True
        ).astype(jnp.float32),
        lax.psum_scatter(
            grads[8].astype(jnp.bfloat16), "fsdp", scatter_dimension=0, tiled=True
        ).astype(jnp.float32),
        lax.psum_scatter(
            grads[9].astype(jnp.bfloat16), "fsdp", scatter_dimension=0, tiled=True
        ).astype(jnp.float32),
        lax.psum_scatter(
            grads[10].astype(jnp.bfloat16), "fsdp", scatter_dimension=0, tiled=True
        ).astype(jnp.float32),
        lax.psum_scatter(
            grads[11].astype(jnp.bfloat16), "fsdp", scatter_dimension=0, tiled=True
        ).astype(jnp.float32),
        lax.psum_scatter(
            grads[12].astype(jnp.bfloat16), "fsdp", scatter_dimension=0, tiled=True
        ).astype(jnp.float32),
    )
    totals = (
        lax.psum(shards[0].astype(jnp.bfloat16), "ctx").astype(jnp.float32),
        lax.psum(shards[1].astype(jnp.bfloat16), "ctx").astype(jnp.float32),
        lax.psum(shards[2].astype(jnp.bfloat16), "ctx").astype(jnp.float32),
        lax.psum(shards[3].astype(jnp.bfloat16), "ctx").astype(jnp.float32),
        lax.psum(shards[4].astype(jnp.bfloat16), "ctx").astype(jnp.float32),
        lax.psum(shards[5].astype(jnp.bfloat16), "ctx").astype(jnp.float32),
        lax.psum(shards[6].astype(jnp.bfloat16), "ctx").astype(jnp.float32),
        lax.psum(shards[7].astype(jnp.bfloat16), "ctx").astype(jnp.float32),
        lax.psum(shards[8].astype(jnp.bfloat16), "ctx").astype(jnp.float32),
        lax.psum(shards[9].astype(jnp.bfloat16), "ctx").astype(jnp.float32),
        lax.psum(shards[10].astype(jnp.bfloat16), "ctx").astype(jnp.float32),
        lax.psum(shards[11].astype(jnp.bfloat16), "ctx").astype(jnp.float32),
        lax.psum(shards[12].astype(jnp.bfloat16), "ctx").astype(jnp.float32),
    )
    return (output[None], token_grad[None]) + tuple(totals)


def solution(mesh):
    return jax.shard_map(
        on_device_spread if mesh.shape["ctx"] == 8 else on_device_any,
        mesh=mesh,
        in_specs=(
            P("fsdp", "ctx", None),
            P("fsdp", "ctx", None),
            P("fsdp"),
            P(),
            P("fsdp", None),
            P("fsdp"),
            P("fsdp"),
            P("fsdp", None),
            P("fsdp"),
            P("fsdp"),
            P("fsdp"),
            P("fsdp", None),
            P("fsdp"),
            P("fsdp", None),
            P("fsdp"),
            P("fsdp"),
            P("fsdp"),
        ),
        out_specs=(
            P("fsdp", "ctx", None),
            P("fsdp", "ctx", None),
            P("fsdp", None),
            P("fsdp"),
            P("fsdp"),
            P("fsdp", None),
            P("fsdp"),
            P("fsdp"),
            P("fsdp"),
            P("fsdp", None),
            P("fsdp"),
            P("fsdp", None),
            P("fsdp"),
            P("fsdp"),
            P("fsdp"),
        ),
        check_vma=False,
    )
```

```python
import functools
import math

import jax
import jax.numpy as jnp
from jax import lax
from jax.experimental import pallas as pl
from jax.experimental.pallas import tpu as pltpu
from jax.sharding import PartitionSpec as P

HEADS = 12
HEAD_DIM = 64
NMEM = 10
BLK = 128


eps = 1e-12
neg_big = -1e30


def layer_norm(value, gain, shift):
    mean = jnp.mean(value, axis=-1, keepdims=True)
    centred = value - mean
    variance = jnp.mean(centred * centred, axis=-1, keepdims=True)
    return centred * lax.rsqrt(variance + eps) * gain + shift


def norm_back(value, gain, grad):
    mean = jnp.mean(value, axis=-1, keepdims=True)
    centred = value - mean
    scale = lax.rsqrt(jnp.mean(centred * centred, axis=-1, keepdims=True) + eps)
    unit = centred * scale
    scaled = grad * gain
    inner = (
        scaled
        - jnp.mean(scaled, axis=-1, keepdims=True)
        - unit * jnp.mean(scaled * unit, axis=-1, keepdims=True)
    )
    return (scale * inner, jnp.sum(grad * unit, axis=0), jnp.sum(grad, axis=0))


def block_width(count):
    return math.gcd(count, 512)


def places(pairing, start, count, half):
    rows = start + jnp.arange(count, dtype=jnp.int32)
    owners = rows // half
    spots = jnp.arange(pairing.shape[0], dtype=jnp.int32)
    picked = jnp.sum(jnp.where(owners[:, None] == spots[None, :], pairing[None, :], 0), axis=1)
    return picked * half + rows % half


def allowed_pairs(query_place, key_place, length):
    before = (key_place[None, :] <= query_place[:, None]) | (key_place[None, :] < NMEM)
    return (key_place[None, :] < length) & before


def heads_of(value):
    return value.reshape(value.shape[0], HEADS, HEAD_DIM)


def forward_fold(query_heads, query_place, pairing, length, half):

    def fold(carry, piece, start):
        keys, values = piece
        count = keys.shape[0]
        width = block_width(count)
        key_place = places(pairing, start, count, half)

        def step(index, state):
            top, total, summed = state
            offset = index * width
            key_heads = heads_of(lax.dynamic_slice_in_dim(keys, offset, width, 0))
            value_heads = heads_of(lax.dynamic_slice_in_dim(values, offset, width, 0))
            mask = allowed_pairs(
                query_place, lax.dynamic_slice_in_dim(key_place, offset, width, 0), length
            )[None]
            scores = (
                jnp.einsum(
                    "qhd,khd->hqk", query_heads, key_heads, preferred_element_type=jnp.float32
                )
                * 0.125
            )
            scores = jnp.where(mask, scores, neg_big)
            new_top = jnp.maximum(top, jnp.max(scores, axis=2))
            shrink = jnp.exp(top - new_top)
            probs = jnp.where(mask, jnp.exp(scores - new_top[:, :, None]), 0.0)
            total = total * shrink + jnp.sum(probs, axis=2)
            update = jnp.einsum(
                "hqk,khd->qhd",
                probs.astype(jnp.bfloat16),
                value_heads,
                preferred_element_type=jnp.float32,
            )
            summed = summed * jnp.transpose(shrink)[:, :, None] + update
            return (new_top, total, summed)

        return lax.fori_loop(0, count // width, step, carry)

    return fold


def query_grad_fold(query_heads, grad_heads, top_sum, delta, query_place, pairing, length, half):

    def fold(carry, piece, start):
        keys, values = piece
        count = keys.shape[0]
        width = block_width(count)
        key_place = places(pairing, start, count, half)

        def step(index, summed):
            offset = index * width
            key_heads = heads_of(lax.dynamic_slice_in_dim(keys, offset, width, 0))
            value_heads = heads_of(lax.dynamic_slice_in_dim(values, offset, width, 0))
            mask = allowed_pairs(
                query_place, lax.dynamic_slice_in_dim(key_place, offset, width, 0), length
            )[None]
            scores = (
                jnp.einsum(
                    "qhd,khd->hqk", query_heads, key_heads, preferred_element_type=jnp.float32
                )
                * 0.125
            )
            probs = jnp.where(mask, jnp.exp(scores - top_sum[:, :, None]), 0.0)
            prob_grad = jnp.einsum(
                "qhd,khd->hqk", grad_heads, value_heads, preferred_element_type=jnp.float32
            )
            score_grad = (probs * (prob_grad - delta[:, :, None])).astype(jnp.bfloat16)
            return (
                summed
                + jnp.einsum(
                    "hqk,khd->qhd", score_grad, key_heads, preferred_element_type=jnp.float32
                )
                * 0.125
            )

        return lax.fori_loop(0, count // width, step, carry)

    return fold


def key_terms(
    key_heads, value_heads, key_place, query_heads, grad_heads, top_sum, delta, query_place, length
):
    scores = (
        jnp.einsum("qhd,khd->hqk", query_heads, key_heads, preferred_element_type=jnp.float32)
        * 0.125
    )
    mask = allowed_pairs(query_place, key_place, length)[None]
    probs = jnp.where(mask, jnp.exp(scores - top_sum[:, :, None]), 0.0)
    prob_grad = jnp.einsum(
        "qhd,khd->hqk", grad_heads, value_heads, preferred_element_type=jnp.float32
    )
    score_grad = (probs * (prob_grad - delta[:, :, None])).astype(jnp.bfloat16)
    value_grad = jnp.einsum(
        "hqk,qhd->khd", probs.astype(jnp.bfloat16), grad_heads, preferred_element_type=jnp.float32
    )
    key_grad = (
        jnp.einsum("hqk,qhd->khd", score_grad, query_heads, preferred_element_type=jnp.float32)
        * 0.125
    )
    return (key_grad, value_grad)


def on_device_any(
    tokens,
    cotangent,
    lengths,
    pairing,
    w_qkv,
    bias_q,
    bias_v,
    w_out,
    bias_out,
    ln1_gain,
    ln1_bias,
    w_in,
    bias_in,
    w_back,
    bias_back,
    ln2_gain,
    ln2_bias,
):
    gathered = (
        lax.all_gather(w_qkv, "fsdp", axis=0, tiled=True),
        lax.all_gather(bias_q, "fsdp", axis=0, tiled=True),
        lax.all_gather(bias_v, "fsdp", axis=0, tiled=True),
        lax.all_gather(w_out, "fsdp", axis=0, tiled=True),
        lax.all_gather(bias_out, "fsdp", axis=0, tiled=True),
        lax.all_gather(ln1_gain, "fsdp", axis=0, tiled=True),
        lax.all_gather(ln1_bias, "fsdp", axis=0, tiled=True),
        lax.all_gather(w_in, "fsdp", axis=0, tiled=True),
        lax.all_gather(bias_in, "fsdp", axis=0, tiled=True),
        lax.all_gather(w_back, "fsdp", axis=0, tiled=True),
        lax.all_gather(bias_back, "fsdp", axis=0, tiled=True),
        lax.all_gather(ln2_gain, "fsdp", axis=0, tiled=True),
        lax.all_gather(ln2_bias, "fsdp", axis=0, tiled=True),
    )
    (
        qkv_all,
        query_bias,
        value_bias,
        out_all,
        out_bias,
        gain_one,
        shift_one,
        in_all,
        in_bias,
        back_all,
        back_bias,
        gain_two,
        shift_two,
    ) = gathered
    rows = tokens.shape[1]
    half = rows // 2
    width = tokens.shape[2]
    length = lengths[0]
    query_place = places(pairing, lax.axis_index("ctx") * rows, rows, half)
    valid = query_place < length
    inputs = tokens[0]
    proj = jnp.dot(inputs, qkv_all, preferred_element_type=jnp.float32)
    queries = (proj[:, :width] + query_bias.astype(jnp.float32)).astype(jnp.bfloat16)
    keys = proj[:, width : 2 * width].astype(jnp.bfloat16)
    values = (proj[:, 2 * width :] + value_bias.astype(jnp.float32)).astype(jnp.bfloat16)
    query_heads = heads_of(queries)
    start_state = (
        jnp.full((HEADS, rows), neg_big, jnp.float32),
        jnp.zeros((HEADS, rows), jnp.float32),
        jnp.zeros((rows, HEADS, HEAD_DIM), jnp.float32),
    )
    fold = forward_fold(query_heads, query_place, pairing, length, half)
    top, total, summed = fold(
        start_state,
        (
            lax.all_gather(keys, "ctx", axis=0, tiled=True),
            lax.all_gather(values, "ctx", axis=0, tiled=True),
        ),
        jnp.int32(0),
    )
    top_sum = top + jnp.log(total)
    attended = (summed / jnp.transpose(total)[:, :, None]).reshape(rows, width)
    attended_low = attended.astype(jnp.bfloat16)
    resid_one = (
        inputs.astype(jnp.float32)
        + jnp.dot(attended_low, out_all, preferred_element_type=jnp.float32)
        + out_bias.astype(jnp.float32)
    )
    hidden = layer_norm(resid_one, gain_one.astype(jnp.float32), shift_one.astype(jnp.float32))
    hidden_low = hidden.astype(jnp.bfloat16)
    upper = jnp.dot(hidden_low, in_all, preferred_element_type=jnp.float32) + in_bias.astype(
        jnp.float32
    )
    active, gelu_back = jax.vjp(lambda value: jax.nn.gelu(value, approximate=False), upper)
    active_low = active.astype(jnp.bfloat16)
    resid_two = (
        hidden
        + jnp.dot(active_low, back_all, preferred_element_type=jnp.float32)
        + back_bias.astype(jnp.float32)
    )
    normed = layer_norm(resid_two, gain_two.astype(jnp.float32), shift_two.astype(jnp.float32))
    output = jnp.where(valid[:, None], normed, 0.0)
    qkv_back, out_back, gain_one_back, in_back, back_back, gain_two_back = (
        qkv_all,
        out_all,
        gain_one,
        in_all,
        back_all,
        gain_two,
    )
    grad_y = jnp.where(valid[:, None], cotangent[0].astype(jnp.float32), 0.0)
    grad_resid_two, gain_two_grad, shift_two_grad = norm_back(
        resid_two, gain_two_back.astype(jnp.float32), grad_y
    )
    grad_mixed = grad_resid_two.astype(jnp.bfloat16)
    back_grad = jnp.einsum("tf,td->fd", active_low, grad_mixed, preferred_element_type=jnp.float32)
    back_bias_grad = jnp.sum(grad_mixed.astype(jnp.float32), axis=0)
    grad_active = jnp.einsum("td,fd->tf", grad_mixed, back_back, preferred_element_type=jnp.float32)
    (grad_upper,) = gelu_back(grad_active)
    grad_upper_low = grad_upper.astype(jnp.bfloat16)
    in_grad = jnp.einsum(
        "td,tf->df", hidden_low, grad_upper_low, preferred_element_type=jnp.float32
    )
    in_bias_grad = jnp.sum(grad_upper_low.astype(jnp.float32), axis=0)
    grad_hidden = grad_resid_two + jnp.einsum(
        "tf,df->td", grad_upper_low, in_back, preferred_element_type=jnp.float32
    )
    grad_resid_one, gain_one_grad, shift_one_grad = norm_back(
        resid_one, gain_one_back.astype(jnp.float32), grad_hidden
    )
    grad_branch = grad_resid_one.astype(jnp.bfloat16)
    out_grad = jnp.einsum(
        "tc,td->cd", attended_low, grad_branch, preferred_element_type=jnp.float32
    )
    out_bias_grad = jnp.sum(grad_branch.astype(jnp.float32), axis=0)
    grad_attended = jnp.einsum(
        "td,cd->tc", grad_branch, out_back, preferred_element_type=jnp.float32
    ).astype(jnp.bfloat16)
    grad_heads = heads_of(grad_attended)
    delta = jnp.transpose(jnp.sum(grad_heads.astype(jnp.float32) * heads_of(attended), axis=2))
    query_fold = query_grad_fold(
        query_heads, grad_heads, top_sum, delta, query_place, pairing, length, half
    )
    empty_heads = jnp.zeros((rows, HEADS, HEAD_DIM), jnp.float32)
    query_grad = query_fold(
        empty_heads,
        (
            lax.all_gather(keys, "ctx", axis=0, tiled=True),
            lax.all_gather(values, "ctx", axis=0, tiled=True),
        ),
        jnp.int32(0),
    )
    stats = jnp.concatenate([jnp.transpose(top_sum), jnp.transpose(delta)], axis=1)
    stats_all = lax.all_gather(stats, "ctx", axis=0, tiled=True)
    key_heads = heads_of(keys)
    value_heads = heads_of(values)
    query_in = lax.all_gather(queries, "ctx", axis=0, tiled=True)
    grad_in = lax.all_gather(grad_attended, "ctx", axis=0, tiled=True)
    count = query_in.shape[0]
    span = block_width(count)
    place_in = places(pairing, jnp.int32(0), count, half)

    def step(index, state):
        offset = index * span
        query_block = heads_of(lax.dynamic_slice_in_dim(query_in, offset, span, 0))
        grad_block = heads_of(lax.dynamic_slice_in_dim(grad_in, offset, span, 0))
        stats_block = lax.dynamic_slice_in_dim(stats_all, offset, span, 0)
        place_block = lax.dynamic_slice_in_dim(place_in, offset, span, 0)
        key_part, value_part = key_terms(
            key_heads,
            value_heads,
            query_place,
            query_block,
            grad_block,
            jnp.transpose(stats_block[:, :HEADS]),
            jnp.transpose(stats_block[:, HEADS:]),
            place_block,
            length,
        )
        return (state[0] + key_part, state[1] + value_part)

    key_sum, value_sum = lax.fori_loop(0, count // span, step, (empty_heads, empty_heads))
    key_grad = key_sum.reshape(rows, width)
    value_grad = value_sum.reshape(rows, width)
    grad_proj = jnp.concatenate(
        [
            query_grad.reshape(rows, width).astype(jnp.bfloat16),
            key_grad.astype(jnp.bfloat16),
            value_grad.astype(jnp.bfloat16),
        ],
        axis=1,
    )
    qkv_grad = jnp.einsum("td,tf->df", inputs, grad_proj, preferred_element_type=jnp.float32)
    query_bias_grad = jnp.sum(grad_proj[:, :width].astype(jnp.float32), axis=0)
    value_bias_grad = jnp.sum(grad_proj[:, 2 * width :].astype(jnp.float32), axis=0)
    token_grad = grad_resid_one + jnp.einsum(
        "tf,df->td", grad_proj, qkv_back, preferred_element_type=jnp.float32
    )
    grads = (
        qkv_grad,
        query_bias_grad,
        value_bias_grad,
        out_grad,
        out_bias_grad,
        gain_one_grad,
        shift_one_grad,
        in_grad,
        in_bias_grad,
        back_grad,
        back_bias_grad,
        gain_two_grad,
        shift_two_grad,
    )
    shards = (
        lax.psum_scatter(
            grads[0].astype(jnp.bfloat16), "fsdp", scatter_dimension=0, tiled=True
        ).astype(jnp.float32),
        lax.psum_scatter(
            grads[1].astype(jnp.bfloat16), "fsdp", scatter_dimension=0, tiled=True
        ).astype(jnp.float32),
        lax.psum_scatter(
            grads[2].astype(jnp.bfloat16), "fsdp", scatter_dimension=0, tiled=True
        ).astype(jnp.float32),
        lax.psum_scatter(
            grads[3].astype(jnp.bfloat16), "fsdp", scatter_dimension=0, tiled=True
        ).astype(jnp.float32),
        lax.psum_scatter(
            grads[4].astype(jnp.bfloat16), "fsdp", scatter_dimension=0, tiled=True
        ).astype(jnp.float32),
        lax.psum_scatter(
            grads[5].astype(jnp.bfloat16), "fsdp", scatter_dimension=0, tiled=True
        ).astype(jnp.float32),
        lax.psum_scatter(
            grads[6].astype(jnp.bfloat16), "fsdp", scatter_dimension=0, tiled=True
        ).astype(jnp.float32),
        lax.psum_scatter(
            grads[7].astype(jnp.bfloat16), "fsdp", scatter_dimension=0, tiled=True
        ).astype(jnp.float32),
        lax.psum_scatter(
            grads[8].astype(jnp.bfloat16), "fsdp", scatter_dimension=0, tiled=True
        ).astype(jnp.float32),
        lax.psum_scatter(
            grads[9].astype(jnp.bfloat16), "fsdp", scatter_dimension=0, tiled=True
        ).astype(jnp.float32),
        lax.psum_scatter(
            grads[10].astype(jnp.bfloat16), "fsdp", scatter_dimension=0, tiled=True
        ).astype(jnp.float32),
        lax.psum_scatter(
            grads[11].astype(jnp.bfloat16), "fsdp", scatter_dimension=0, tiled=True
        ).astype(jnp.float32),
        lax.psum_scatter(
            grads[12].astype(jnp.bfloat16), "fsdp", scatter_dimension=0, tiled=True
        ).astype(jnp.float32),
    )
    totals = (
        lax.psum(shards[0].astype(jnp.bfloat16), "ctx").astype(jnp.float32),
        lax.psum(shards[1].astype(jnp.bfloat16), "ctx").astype(jnp.float32),
        lax.psum(shards[2].astype(jnp.bfloat16), "ctx").astype(jnp.float32),
        lax.psum(shards[3].astype(jnp.bfloat16), "ctx").astype(jnp.float32),
        lax.psum(shards[4].astype(jnp.bfloat16), "ctx").astype(jnp.float32),
        lax.psum(shards[5].astype(jnp.bfloat16), "ctx").astype(jnp.float32),
        lax.psum(shards[6].astype(jnp.bfloat16), "ctx").astype(jnp.float32),
        lax.psum(shards[7].astype(jnp.bfloat16), "ctx").astype(jnp.float32),
        lax.psum(shards[8].astype(jnp.bfloat16), "ctx").astype(jnp.float32),
        lax.psum(shards[9].astype(jnp.bfloat16), "ctx").astype(jnp.float32),
        lax.psum(shards[10].astype(jnp.bfloat16), "ctx").astype(jnp.float32),
        lax.psum(shards[11].astype(jnp.bfloat16), "ctx").astype(jnp.float32),
        lax.psum(shards[12].astype(jnp.bfloat16), "ctx").astype(jnp.float32),
    )
    return (output[None], token_grad[None]) + tuple(totals)


MESH = pl.DeviceIdType.MESH


def exchange_kernel(n, in_ref, out_ref, sent, landed, own):
    me = lax.axis_index("ctx")
    barrier = pltpu.get_barrier_semaphore()
    for k in range(1, n):
        pl.semaphore_signal(
            barrier, inc=1, device_id={"ctx": lax.rem(me + k, n)}, device_id_type=MESH
        )
    pl.semaphore_wait(barrier, n - 1)
    copies = []
    for k in range(1, n):
        peer = lax.rem(me + k, n)
        copy = pltpu.make_async_remote_copy(
            src_ref=in_ref.at[peer],
            dst_ref=out_ref.at[me],
            send_sem=sent.at[k],
            recv_sem=landed.at[k],
            device_id={"ctx": peer},
            device_id_type=MESH,
        )
        copy.start()
        copies.append(copy)
    local = pltpu.make_async_copy(in_ref.at[me], out_ref.at[me], own)
    local.start()
    local.wait()
    for copy in copies:
        copy.wait()


def exchange(blocks, name):
    n = blocks.shape[0]
    return pl.pallas_call(
        functools.partial(exchange_kernel, n),
        out_shape=jax.ShapeDtypeStruct(blocks.shape, blocks.dtype),
        in_specs=[vmem()],
        out_specs=vmem(),
        scratch_shapes=[
            pltpu.SemaphoreType.DMA((n,)),
            pltpu.SemaphoreType.DMA((n,)),
            pltpu.SemaphoreType.DMA,
        ],
        compiler_params=pltpu.CompilerParams(
            collective_id=name, has_side_effects=True, vmem_limit_bytes=16 << 20
        ),
        name="exchange",
    )(blocks)


def split_heads(value):
    rows = value.shape[0]
    trio = value.reshape(rows, HEADS // 3, 3, HEAD_DIM)
    own = trio[:, :, :2]
    shared = jnp.broadcast_to(trio[:, :, 2:], own.shape)
    both = jnp.concatenate([own, shared], axis=-1)
    return jnp.transpose(both.reshape(rows, -1, 2 * HEAD_DIM), (1, 0, 2))


def send_blocks(queries, keys, values):
    return jnp.concatenate([split_heads(queries), split_heads(keys), split_heads(values)], axis=2)


def join_heads(blocks):
    rows = blocks.shape[1]
    pairs = blocks.reshape(HEADS // 3, 2, rows, 2, HEAD_DIM)
    shared = pairs[:, 0, :, 1].astype(jnp.float32) + pairs[:, 1, :, 1].astype(jnp.float32)
    trio = jnp.stack([pairs[:, 0, :, 0], pairs[:, 1, :, 0], shared.astype(blocks.dtype)], axis=2)
    return jnp.transpose(trio, (1, 0, 2, 3)).reshape(rows, HEADS * HEAD_DIM)


def join_parts(blocks):
    parts = jnp.split(blocks, 3, axis=2)
    return jnp.concatenate([join_heads(part) for part in parts], axis=1)


BLK = 128


def low_lanes(shape):
    return lax.broadcasted_iota(jnp.int32, shape, 1) < 64


def attend_kernel(chunks, pair_ref, len_ref, spot_ref, in_ref, out_ref, keep_ref, mix_ref, lse_ref):
    length = len_ref[0]
    spot = spot_ref[0]
    blocks = 2 * chunks
    for s in range(blocks):
        keep_ref[pair_ref[s]] = in_ref[s]
    left = low_lanes((256, BLK))
    left_half = left[:BLK]
    for c in range(chunks):
        keys = 256 * (c + 1)
        own = keep_ref[2 * c : 2 * c + 2, :, :BLK].reshape(256, BLK)
        shared = keep_ref[2 * c + spot, :, :BLK]
        zero = jnp.zeros((), jnp.bfloat16)
        query = jnp.concatenate(
            [jnp.where(left, own, zero), jnp.where(left_half, zero, shared)], axis=0
        ) * jnp.bfloat16(0.125)
        key = keep_ref[: 2 * c + 2, :, BLK : 2 * BLK].reshape(keys, BLK)
        value = keep_ref[: 2 * c + 2, :, 2 * BLK :].reshape(keys, BLK)
        scores = mask_scores(
            lax.dot_general(key, query, (((1,), (1,)), ((), ())), preferred_element_type=jnp.float32),
            c, spot, length,
        )
        top = jnp.max(scores, axis=0, keepdims=True)
        probs = jnp.exp(scores - top)
        total = jnp.sum(probs, axis=0, keepdims=True)
        summed = lax.dot_general(
            value, probs.astype(jnp.bfloat16), (((0,), (0,)), ((), ())),
            preferred_element_type=jnp.float32,
        ) / total
        lse_ref[c] = top + jnp.log(total)
        part = summed[64:, 256:]
        none = jnp.zeros_like(part)
        first = jnp.where(spot == 0, part, none)
        second = jnp.where(spot == 0, none, part)
        mixed = jnp.concatenate(
            [summed[:64, :256], jnp.concatenate([first, second], axis=1)], axis=0
        )
        mix_ref[c] = mixed
    for s in range(blocks):
        place = pair_ref[s]
        c = place // 2
        piece = mix_ref[c, :, pl.ds(pl.multiple_of((place % 2) * BLK, BLK), BLK)]
        out_ref[s] = jnp.transpose(piece).astype(jnp.bfloat16)


def mask_scores(scores, c, spot, length):
    keys, width = scores.shape
    edge = 256 * c
    row = lax.broadcasted_iota(jnp.int32, (keys, width), 0)
    scores = jnp.where(row < length, scores, neg_big)
    lane = lax.broadcasted_iota(jnp.int32, (256, width), 1)
    query_place = edge + jnp.where(lane < 256, lane, lane - 256 + spot * BLK)
    key_place = edge + lax.broadcasted_iota(jnp.int32, (256, width), 0)
    seen = key_place <= query_place
    if c == 0:
        seen = seen | (key_place < NMEM)
    tail = jnp.where(seen, scores[edge:], neg_big)
    if c == 0:
        return tail
    return jnp.concatenate([scores[:edge], tail], axis=0)


def attend_back_kernel(
    chunks, pair_ref, len_ref, spot_ref, keep_ref, grad_ref, mix_ref, lse_ref, out_ref, g_ref,
    q_sum, k_sum, v_sum
):
    length = len_ref[0]
    spot = spot_ref[0]
    blocks = 2 * chunks
    for s in range(blocks):
        g_ref[pair_ref[s]] = grad_ref[s]
    k_sum[...] = jnp.zeros_like(k_sum)
    v_sum[...] = jnp.zeros_like(v_sum)
    left = low_lanes((256, BLK))
    left_half = left[:BLK]
    zero = jnp.zeros((), jnp.bfloat16)
    for c in range(chunks):
        keys = 256 * (c + 1)
        own = keep_ref[2 * c : 2 * c + 2, :, :BLK].reshape(256, BLK)
        shared = keep_ref[2 * c + spot, :, :BLK]
        query = jnp.concatenate(
            [jnp.where(left, own, zero), jnp.where(left_half, zero, shared)], axis=0
        ) * jnp.bfloat16(0.125)
        g_own = g_ref[2 * c : 2 * c + 2].reshape(256, BLK)
        g_shared = g_ref[2 * c + spot]
        grad = jnp.concatenate(
            [jnp.where(left, g_own, zero), jnp.where(left_half, zero, g_shared)], axis=0
        )
        key = keep_ref[: 2 * c + 2, :, BLK : 2 * BLK].reshape(keys, BLK)
        value = keep_ref[: 2 * c + 2, :, 2 * BLK :].reshape(keys, BLK)
        turned = jnp.transpose(g_own.astype(jnp.float32)) * mix_ref[c]
        delta_own = jnp.sum(turned[:64], axis=0, keepdims=True)
        delta_pair = jnp.sum(turned[64:], axis=0, keepdims=True)
        delta = jnp.concatenate(
            [delta_own, jnp.where(spot == 0, delta_pair[:, :BLK], delta_pair[:, BLK:])], axis=1
        )
        nt = (((1,), (1,)), ((), ()))
        scores = mask_scores(
            lax.dot_general(key, query, nt, preferred_element_type=jnp.float32), c, spot, length
        )
        probs = jnp.exp(scores - lse_ref[c])
        prob_grad = lax.dot_general(value, grad, nt, preferred_element_type=jnp.float32)
        score_grad = (probs * (prob_grad - delta)).astype(jnp.bfloat16)
        nn = (((1,), (0,)), ((), ()))
        v_sum[:keys] += lax.dot_general(
            probs.astype(jnp.bfloat16), grad, nn, preferred_element_type=jnp.float32
        )
        k_sum[:keys] += lax.dot_general(score_grad, query, nn, preferred_element_type=jnp.float32)
        q_grad = lax.dot_general(
            score_grad, key, (((0,), (0,)), ((), ())), preferred_element_type=jnp.float32
        ) * 0.125
        part = q_grad[256:]
        none = jnp.zeros_like(part)
        first = jnp.where(spot == 0, part, none)
        second = jnp.where(spot == 0, none, part)
        q_sum[256 * c : 256 * c + 256] = jnp.where(
            left, q_grad[:256], jnp.concatenate([first, second], axis=0)
        )
    for s in range(blocks):
        rows = pl.ds(pl.multiple_of(pair_ref[s] * BLK, BLK), BLK)
        out_ref[s] = jnp.concatenate([q_sum[rows], k_sum[rows], v_sum[rows]], axis=1).astype(jnp.bfloat16)


def smem():
    return pl.BlockSpec(memory_space=pltpu.SMEM)


def vmem():
    return pl.BlockSpec(memory_space=pltpu.VMEM)


def attend(pairing, lengths, spot, packed):
    blocks = packed.shape[0]
    chunks = blocks // 2
    return pl.pallas_call(
        functools.partial(attend_kernel, chunks),
        out_shape=(
            jax.ShapeDtypeStruct((blocks, BLK, BLK), jnp.bfloat16),
            jax.ShapeDtypeStruct((blocks, BLK, 3 * BLK), jnp.bfloat16),
            jax.ShapeDtypeStruct((chunks, BLK, 256), jnp.float32),
            jax.ShapeDtypeStruct((chunks, 1, 384), jnp.float32),
        ),
        in_specs=[smem(), smem(), smem(), vmem()],
        out_specs=(vmem(), vmem(), vmem(), vmem()),
        compiler_params=pltpu.CompilerParams(vmem_limit_bytes=48 << 20),
        name="attend",
    )(pairing, lengths, spot, packed)


def attend_back(pairing, lengths, spot, keep, grad, mix, lse):
    blocks = keep.shape[0]
    chunks = blocks // 2
    return pl.pallas_call(
        functools.partial(attend_back_kernel, chunks),
        out_shape=jax.ShapeDtypeStruct((blocks, BLK, 3 * BLK), jnp.bfloat16),
        in_specs=[smem(), smem(), smem(), vmem(), vmem(), vmem(), vmem()],
        out_specs=vmem(),
        scratch_shapes=[
            pltpu.VMEM((blocks, BLK, BLK), jnp.bfloat16),
            pltpu.VMEM((blocks * BLK, BLK), jnp.float32),
            pltpu.VMEM((blocks * BLK, BLK), jnp.float32),
            pltpu.VMEM((blocks * BLK, BLK), jnp.float32),
        ],
        compiler_params=pltpu.CompilerParams(vmem_limit_bytes=48 << 20),
        name="attend_back",
    )(pairing, lengths, spot, keep, grad, mix, lse)


PARTS = 12


def sum_sources(chunk):
    left = jnp.where(chunk < 4, 3 + chunk, jnp.where(chunk < 8, 2, jnp.where(chunk < 9, 1, 0)))
    right = jnp.where(
        chunk < 4, 8, jnp.where(chunk < 8, chunk, jnp.where(chunk < 9, 3, chunk - 9))
    )
    return left, right


def sum_kernel(
    left_ref, right_ref, small_ref, out_ref, small_out,
    pair_out, pair_in, x_out, x_in, first_sum, y_out, y_in, half_sum, z_out, z_in,
    s_pair, s_x_out, s_x, s_y_out, s_y, s_z_out, s_z,
    pair_sem, x_sem, y_sem, z_sem, spread_sem, last_sem, s_sem,
):
    ctx = lax.axis_index("ctx")
    fsdp = lax.axis_index("fsdp")
    z, y = ctx // 2, lax.rem(ctx, 2)
    x, core = fsdp // 2, lax.rem(fsdp, 2)
    sibling = {"fsdp": 2 * x + 1 - core}
    across = {"fsdp": 2 * (1 - x) + core}
    beside = {"ctx": 2 * z + 1 - y}
    along = [{"ctx": 2 * lax.rem(z + k, 4) + y} for k in (1, 2, 3)]
    barrier = pltpu.get_barrier_semaphore()
    for peer in [sibling, across, beside] + along:
        pl.semaphore_signal(barrier, inc=1, device_id=peer, device_id_type=MESH)
    pl.semaphore_wait(barrier, 6)

    def copy(src, dst, sems, at, peer):
        return pltpu.make_async_remote_copy(
            src_ref=src, dst_ref=dst, send_sem=sems.at[(0,) + at], recv_sem=sems.at[(1,) + at],
            device_id=peer, device_id_type=MESH,
        )

    def pair_copy(c):
        return copy(pair_out.at[c], pair_in.at[c], pair_sem, (c,), sibling)

    def x_copy(c):
        return copy(x_out.at[c], x_in.at[c], x_sem, (c,), across)

    def y_copy(c):
        return copy(y_out.at[c], y_in.at[c], y_sem, (c,), beside)

    def z_copy(c, k):
        return copy(
            z_out.at[c, lax.rem(z + k, 4)], z_in.at[c, k - 1], z_sem, (c, k - 1), along[k - 1]
        )

    def spread_copy(c, k):
        piece = out_ref.at[c, y, z]
        return copy(piece, piece, spread_sem, (c, k - 1), along[k - 1])

    def last_copy(c):
        return copy(out_ref.at[c, y], out_ref.at[c, y], last_sem, (c,), beside)

    def partial(c, shard):
        left, right = sum_sources(c)
        return jnp.dot(left_ref[left, shard], right_ref[right], preferred_element_type=jnp.float32)

    low = jnp.bfloat16

    def stage_pair(c):
        for side in range(2):
            pair_out[c, side] = partial(c, 2 * side + 1 - core).astype(low)
        pair_copy(c).start()

    def stage_x(c):
        pair_copy(c).wait_recv()
        x_out[c] = (
            partial(c, 2 * (1 - x) + core) + pair_in[c, 1 - x].astype(jnp.float32)
        ).astype(low)
        x_copy(c).start()
        first_sum[lax.rem(c, 2)] = partial(c, 2 * x + core) + pair_in[c, x].astype(jnp.float32)

    def stage_y(c):
        x_copy(c).wait_recv()
        total = first_sum[lax.rem(c, 2)] + x_in[c].astype(jnp.float32)
        here, there = total[:, :384], total[:, 384:]
        y_out[c] = jnp.where(y == 0, there, here).astype(low)
        y_copy(c).start()
        half_sum[lax.rem(c, 2)] = jnp.where(y == 0, here, there)

    def stage_z(c):
        y_copy(c).wait_recv()
        total = half_sum[lax.rem(c, 2)] + y_in[c].astype(jnp.float32)
        z_out[c] = total.astype(low).reshape(4, 48, 384)
        for k in (1, 2, 3):
            z_copy(c, k).start()
        half_sum[lax.rem(c, 2)] = total

    def stage_spread(c):
        total = half_sum[lax.rem(c, 2), pl.ds(pl.multiple_of(48 * z, 48), 48)]
        for k in (1, 2, 3):
            z_copy(c, k).wait_recv()
            total = total + z_in[c, k - 1].astype(jnp.float32)
        out_ref[c, y, z] = total.astype(low)
        for k in (1, 2, 3):
            spread_copy(c, k).start()

    def stage_last(c):
        for k in (1, 2, 3):
            spread_copy(c, k).wait_recv()
        last_copy(c).start()

    stages = [stage_pair, stage_x, stage_y, stage_z, stage_spread, stage_last]
    order = [0, 1, 4, 2, 3, 5]

    def small_step(t):
        def s_copy(src, dst, k, peer):
            return copy(src, dst, s_sem, (k,), peer)

        send_pair = s_copy(s_pair.at[0], s_pair.at[1], 0, sibling)
        send_x = s_copy(s_x_out, s_x, 1, across)
        send_y = s_copy(s_y_out, s_y, 2, beside)
        send_z = [s_copy(s_z_out, s_z.at[k], 3 + k, along[k]) for k in range(3)]

        @pl.when(t == 0)
        def _():
            for side in range(2):
                s_pair[0, side] = small_ref[2 * side + 1 - core]
            send_pair.start()

        @pl.when(t == 1)
        def _():
            send_pair.wait()
            s_x_out[...] = small_ref[2 * (1 - x) + core] + s_pair[1, 1 - x]
            send_x.start()

        @pl.when(t == 2)
        def _():
            send_x.wait()
            s_y_out[...] = small_ref[2 * x + core] + s_pair[1, x] + s_x[...]
            send_y.start()

        @pl.when(t == 3)
        def _():
            send_y.wait()
            s_z_out[...] = s_y_out[...] + s_y[...]
            for cp in send_z:
                cp.start()

        @pl.when(t == 4)
        def _():
            for cp in send_z:
                cp.wait()
            total = jnp.zeros_like(s_z_out)
            for place in range(4):
                k = lax.rem(place - z + 4, 4)
                behind = 4 - k
                other = s_z[jnp.where(k == 0, 0, behind - 1)]
                total = total + jnp.where(k == 0, s_z_out[...], other)
            small_out[...] = total

    def slot(t, carry):
        small_step(t)
        for index in order:
            c = t - index

            @pl.when((c >= 0) & (c < PARTS))
            def _():
                stages[index](c)

        return carry

    lax.fori_loop(0, PARTS + 5, slot, 0)

    def drain(c, carry):
        pair_copy(c).wait_send()
        x_copy(c).wait_send()
        y_copy(c).wait_send()
        for k in (1, 2, 3):
            z_copy(c, k).wait_send()
            spread_copy(c, k).wait_send()
        last_copy(c).wait()
        return carry

    lax.fori_loop(0, PARTS, drain, 0)


def sum_all(left, right, small, name):
    low, wide = jnp.bfloat16, jnp.float32
    dma = pltpu.SemaphoreType.DMA
    return pl.pallas_call(
        sum_kernel,
        out_shape=(
            jax.ShapeDtypeStruct((PARTS, 2, 4, 48, 384), low),
            jax.ShapeDtypeStruct(small.shape[1:], wide),
        ),
        in_specs=[vmem(), vmem(), vmem()],
        out_specs=(vmem(), vmem()),
        scratch_shapes=[
            pltpu.VMEM((PARTS, 2, 192, 768), low),
            pltpu.VMEM((PARTS, 2, 192, 768), low),
            pltpu.VMEM((PARTS, 192, 768), low),
            pltpu.VMEM((PARTS, 192, 768), low),
            pltpu.VMEM((2, 192, 768), wide),
            pltpu.VMEM((PARTS, 192, 384), low),
            pltpu.VMEM((PARTS, 192, 384), low),
            pltpu.VMEM((2, 192, 384), wide),
            pltpu.VMEM((PARTS, 4, 48, 384), low),
            pltpu.VMEM((PARTS, 3, 48, 384), low),
            pltpu.VMEM((2, 2) + small.shape[1:], wide),
            pltpu.VMEM(small.shape[1:], wide),
            pltpu.VMEM(small.shape[1:], wide),
            pltpu.VMEM(small.shape[1:], wide),
            pltpu.VMEM(small.shape[1:], wide),
            pltpu.VMEM(small.shape[1:], wide),
            pltpu.VMEM((3,) + small.shape[1:], wide),
            dma((2, PARTS)),
            dma((2, PARTS)),
            dma((2, PARTS)),
            dma((2, PARTS, 3)),
            dma((2, PARTS, 3)),
            dma((2, PARTS)),
            dma((2, 6)),
        ],
        compiler_params=pltpu.CompilerParams(
            collective_id=name, has_side_effects=True, vmem_limit_bytes=58 << 20
        ),
        name="sum_all",
    )(left, right, small)


def on_device_spread(
    tokens,
    cotangent,
    lengths,
    pairing,
    w_qkv,
    bias_q,
    bias_v,
    w_out,
    bias_out,
    ln1_gain,
    ln1_bias,
    w_in,
    bias_in,
    w_back,
    bias_back,
    ln2_gain,
    ln2_bias,
):
    gathered = (
        lax.all_gather(w_qkv, "fsdp", axis=0, tiled=True),
        lax.all_gather(bias_q, "fsdp", axis=0, tiled=True),
        lax.all_gather(bias_v, "fsdp", axis=0, tiled=True),
        lax.all_gather(w_out, "fsdp", axis=0, tiled=True),
        lax.all_gather(bias_out, "fsdp", axis=0, tiled=True),
        lax.all_gather(ln1_gain, "fsdp", axis=0, tiled=True),
        lax.all_gather(ln1_bias, "fsdp", axis=0, tiled=True),
        lax.all_gather(w_in, "fsdp", axis=0, tiled=True),
        lax.all_gather(bias_in, "fsdp", axis=0, tiled=True),
        lax.all_gather(w_back, "fsdp", axis=0, tiled=True),
        lax.all_gather(bias_back, "fsdp", axis=0, tiled=True),
        lax.all_gather(ln2_gain, "fsdp", axis=0, tiled=True),
        lax.all_gather(ln2_bias, "fsdp", axis=0, tiled=True),
    )
    (
        qkv_all,
        query_bias,
        value_bias,
        out_all,
        out_bias,
        gain_one,
        shift_one,
        in_all,
        in_bias,
        back_all,
        back_bias,
        gain_two,
        shift_two,
    ) = gathered
    rows = tokens.shape[1]
    half = rows // 2
    width = tokens.shape[2]
    length = lengths[0]
    query_place = places(pairing, lax.axis_index("ctx") * rows, rows, half)
    valid = query_place < length
    inputs = tokens[0]
    proj = jnp.dot(inputs, qkv_all, preferred_element_type=jnp.float32)
    queries = (proj[:, :width] + query_bias.astype(jnp.float32)).astype(jnp.bfloat16)
    keys = proj[:, width : 2 * width].astype(jnp.bfloat16)
    values = (proj[:, 2 * width :] + value_bias.astype(jnp.float32)).astype(jnp.bfloat16)
    spot = lax.rem(lax.axis_index("ctx"), 2).astype(jnp.int32).reshape(1)
    sent = send_blocks(queries, keys, values)
    packed = exchange(sent, 0).reshape(-1, half, 6 * HEAD_DIM)
    mixed_out, keep, mix, lse = attend(pairing, lengths, spot, packed)
    attended_low = join_heads(exchange(mixed_out.reshape(-1, rows, 2 * HEAD_DIM), 1))
    resid_one = (
        inputs.astype(jnp.float32)
        + jnp.dot(attended_low, out_all, preferred_element_type=jnp.float32)
        + out_bias.astype(jnp.float32)
    )
    hidden = layer_norm(resid_one, gain_one.astype(jnp.float32), shift_one.astype(jnp.float32))
    hidden_low = hidden.astype(jnp.bfloat16)
    upper = jnp.dot(hidden_low, in_all, preferred_element_type=jnp.float32) + in_bias.astype(
        jnp.float32
    )
    active, gelu_back = jax.vjp(lambda value: jax.nn.gelu(value, approximate=False), upper)
    active_low = active.astype(jnp.bfloat16)
    resid_two = (
        hidden
        + jnp.dot(active_low, back_all, preferred_element_type=jnp.float32)
        + back_bias.astype(jnp.float32)
    )
    normed = layer_norm(resid_two, gain_two.astype(jnp.float32), shift_two.astype(jnp.float32))
    output = jnp.where(valid[:, None], normed, 0.0)
    qkv_back, out_back, gain_one_back, in_back, back_back, gain_two_back = (
        qkv_all,
        out_all,
        gain_one,
        in_all,
        back_all,
        gain_two,
    )
    grad_y = jnp.where(valid[:, None], cotangent[0].astype(jnp.float32), 0.0)
    grad_resid_two, gain_two_grad, shift_two_grad = norm_back(
        resid_two, gain_two_back.astype(jnp.float32), grad_y
    )
    grad_mixed = grad_resid_two.astype(jnp.bfloat16)
    back_bias_grad = jnp.sum(grad_mixed.astype(jnp.float32), axis=0)
    grad_active = jnp.einsum("td,fd->tf", grad_mixed, back_back, preferred_element_type=jnp.float32)
    (grad_upper,) = gelu_back(grad_active)
    grad_upper_low = grad_upper.astype(jnp.bfloat16)
    in_bias_grad = jnp.sum(grad_upper_low.astype(jnp.float32), axis=0)
    grad_hidden = grad_resid_two + jnp.einsum(
        "tf,df->td", grad_upper_low, in_back, preferred_element_type=jnp.float32
    )
    grad_resid_one, gain_one_grad, shift_one_grad = norm_back(
        resid_one, gain_one_back.astype(jnp.float32), grad_hidden
    )
    grad_branch = grad_resid_one.astype(jnp.bfloat16)
    out_bias_grad = jnp.sum(grad_branch.astype(jnp.float32), axis=0)
    grad_attended = jnp.einsum(
        "td,cd->tc", grad_branch, out_back, preferred_element_type=jnp.float32
    ).astype(jnp.bfloat16)
    grad_in = exchange(split_heads(grad_attended), 2).reshape(-1, half, 2 * HEAD_DIM)
    grad_blocks = attend_back(pairing, lengths, spot, keep, grad_in, mix, lse)
    grad_proj = join_parts(exchange(grad_blocks.reshape(-1, rows, 6 * HEAD_DIM), 3))
    query_bias_grad = jnp.sum(grad_proj[:, :width].astype(jnp.float32), axis=0)
    value_bias_grad = jnp.sum(grad_proj[:, 2 * width :].astype(jnp.float32), axis=0)
    token_grad = grad_resid_one + jnp.einsum(
        "tf,df->td", grad_proj, qkv_back, preferred_element_type=jnp.float32
    )
    def wide(value):
        return jnp.transpose(value).reshape(4, -1, rows)

    tall = jnp.transpose(active_low).reshape(4, 4, width // 4, rows)
    left = jnp.concatenate(
        [
            jnp.stack([wide(inputs), wide(attended_low), wide(hidden_low)]),
            jnp.transpose(tall, (1, 0, 2, 3)),
        ]
    )
    right = jnp.stack(
        jnp.split(grad_proj, 3, axis=1)
        + [grad_branch]
        + jnp.split(grad_upper_low, 4, axis=1)
        + [grad_mixed]
    )
    vectors = [
        query_bias_grad, value_bias_grad, out_bias_grad, gain_one_grad, shift_one_grad,
        back_bias_grad, gain_two_grad, shift_two_grad,
    ]
    small = jnp.concatenate(
        [jnp.stack([v.reshape(4, -1) for v in vectors], axis=1), in_bias_grad.reshape(4, 4, -1)],
        axis=1,
    )
    small = jnp.pad(small, ((0, 0), (0, 4), (0, 64)))
    sums, small_sum = sum_all(left, right, small, 4)
    panels = jnp.transpose(sums, (0, 2, 3, 1, 4)).reshape(PARTS, width // 4, width)
    panels = panels.astype(jnp.float32)
    lines = [small_sum[i, : width // 4] for i in range(8)]
    return (
        output[None],
        token_grad[None],
        jnp.concatenate([panels[9], panels[10], panels[11]], axis=1),
        lines[0],
        lines[1],
        panels[8],
        lines[2],
        lines[3],
        lines[4],
        jnp.concatenate([panels[4], panels[5], panels[6], panels[7]], axis=1),
        small_sum[8:12, : width // 4].reshape(-1),
        panels[:4].reshape(-1, width),
        lines[5],
        lines[6],
        lines[7],
    )


def solution(mesh):
    return jax.shard_map(
        on_device_spread if mesh.shape["ctx"] == 8 else on_device_any,
        mesh=mesh,
        in_specs=(
            P("fsdp", "ctx", None),
            P("fsdp", "ctx", None),
            P("fsdp"),
            P(),
            P("fsdp", None),
            P("fsdp"),
            P("fsdp"),
            P("fsdp", None),
            P("fsdp"),
            P("fsdp"),
            P("fsdp"),
            P("fsdp", None),
            P("fsdp"),
            P("fsdp", None),
            P("fsdp"),
            P("fsdp"),
            P("fsdp"),
        ),
        out_specs=(
            P("fsdp", "ctx", None),
            P("fsdp", "ctx", None),
            P("fsdp", None),
            P("fsdp"),
            P("fsdp"),
            P("fsdp", None),
            P("fsdp"),
            P("fsdp"),
            P("fsdp"),
            P("fsdp", None),
            P("fsdp"),
            P("fsdp", None),
            P("fsdp"),
            P("fsdp"),
            P("fsdp"),
        ),
        check_vma=False,
    )
```

```python
import functools
import math

import jax
import jax.numpy as jnp
from jax import lax
from jax.experimental import pallas as pl
from jax.experimental.pallas import tpu as pltpu
from jax.sharding import PartitionSpec as P

HEADS = 12
HEAD_DIM = 64
NMEM = 10
BLK = 128


eps = 1e-12
neg_big = -1e30


def layer_norm(value, gain, shift):
    mean = jnp.mean(value, axis=-1, keepdims=True)
    centred = value - mean
    variance = jnp.mean(centred * centred, axis=-1, keepdims=True)
    return centred * lax.rsqrt(variance + eps) * gain + shift


def norm_back(value, gain, grad):
    mean = jnp.mean(value, axis=-1, keepdims=True)
    centred = value - mean
    scale = lax.rsqrt(jnp.mean(centred * centred, axis=-1, keepdims=True) + eps)
    unit = centred * scale
    scaled = grad * gain
    inner = (
        scaled
        - jnp.mean(scaled, axis=-1, keepdims=True)
        - unit * jnp.mean(scaled * unit, axis=-1, keepdims=True)
    )
    return (scale * inner, jnp.sum(grad * unit, axis=0), jnp.sum(grad, axis=0))


def block_width(count):
    return math.gcd(count, 512)


def places(pairing, start, count, half):
    rows = start + jnp.arange(count, dtype=jnp.int32)
    owners = rows // half
    spots = jnp.arange(pairing.shape[0], dtype=jnp.int32)
    picked = jnp.sum(jnp.where(owners[:, None] == spots[None, :], pairing[None, :], 0), axis=1)
    return picked * half + rows % half


def allowed_pairs(query_place, key_place, length):
    before = (key_place[None, :] <= query_place[:, None]) | (key_place[None, :] < NMEM)
    return (key_place[None, :] < length) & before


def heads_of(value):
    return value.reshape(value.shape[0], HEADS, HEAD_DIM)


def forward_fold(query_heads, query_place, pairing, length, half):

    def fold(carry, piece, start):
        keys, values = piece
        count = keys.shape[0]
        width = block_width(count)
        key_place = places(pairing, start, count, half)

        def step(index, state):
            top, total, summed = state
            offset = index * width
            key_heads = heads_of(lax.dynamic_slice_in_dim(keys, offset, width, 0))
            value_heads = heads_of(lax.dynamic_slice_in_dim(values, offset, width, 0))
            mask = allowed_pairs(
                query_place, lax.dynamic_slice_in_dim(key_place, offset, width, 0), length
            )[None]
            scores = (
                jnp.einsum(
                    "qhd,khd->hqk", query_heads, key_heads, preferred_element_type=jnp.float32
                )
                * 0.125
            )
            scores = jnp.where(mask, scores, neg_big)
            new_top = jnp.maximum(top, jnp.max(scores, axis=2))
            shrink = jnp.exp(top - new_top)
            probs = jnp.where(mask, jnp.exp(scores - new_top[:, :, None]), 0.0)
            total = total * shrink + jnp.sum(probs, axis=2)
            update = jnp.einsum(
                "hqk,khd->qhd",
                probs.astype(jnp.bfloat16),
                value_heads,
                preferred_element_type=jnp.float32,
            )
            summed = summed * jnp.transpose(shrink)[:, :, None] + update
            return (new_top, total, summed)

        return lax.fori_loop(0, count // width, step, carry)

    return fold


def query_grad_fold(query_heads, grad_heads, top_sum, delta, query_place, pairing, length, half):

    def fold(carry, piece, start):
        keys, values = piece
        count = keys.shape[0]
        width = block_width(count)
        key_place = places(pairing, start, count, half)

        def step(index, summed):
            offset = index * width
            key_heads = heads_of(lax.dynamic_slice_in_dim(keys, offset, width, 0))
            value_heads = heads_of(lax.dynamic_slice_in_dim(values, offset, width, 0))
            mask = allowed_pairs(
                query_place, lax.dynamic_slice_in_dim(key_place, offset, width, 0), length
            )[None]
            scores = (
                jnp.einsum(
                    "qhd,khd->hqk", query_heads, key_heads, preferred_element_type=jnp.float32
                )
                * 0.125
            )
            probs = jnp.where(mask, jnp.exp(scores - top_sum[:, :, None]), 0.0)
            prob_grad = jnp.einsum(
                "qhd,khd->hqk", grad_heads, value_heads, preferred_element_type=jnp.float32
            )
            score_grad = (probs * (prob_grad - delta[:, :, None])).astype(jnp.bfloat16)
            return (
                summed
                + jnp.einsum(
                    "hqk,khd->qhd", score_grad, key_heads, preferred_element_type=jnp.float32
                )
                * 0.125
            )

        return lax.fori_loop(0, count // width, step, carry)

    return fold


def key_terms(
    key_heads, value_heads, key_place, query_heads, grad_heads, top_sum, delta, query_place, length
):
    scores = (
        jnp.einsum("qhd,khd->hqk", query_heads, key_heads, preferred_element_type=jnp.float32)
        * 0.125
    )
    mask = allowed_pairs(query_place, key_place, length)[None]
    probs = jnp.where(mask, jnp.exp(scores - top_sum[:, :, None]), 0.0)
    prob_grad = jnp.einsum(
        "qhd,khd->hqk", grad_heads, value_heads, preferred_element_type=jnp.float32
    )
    score_grad = (probs * (prob_grad - delta[:, :, None])).astype(jnp.bfloat16)
    value_grad = jnp.einsum(
        "hqk,qhd->khd", probs.astype(jnp.bfloat16), grad_heads, preferred_element_type=jnp.float32
    )
    key_grad = (
        jnp.einsum("hqk,qhd->khd", score_grad, query_heads, preferred_element_type=jnp.float32)
        * 0.125
    )
    return (key_grad, value_grad)


def on_device_any(
    tokens,
    cotangent,
    lengths,
    pairing,
    w_qkv,
    bias_q,
    bias_v,
    w_out,
    bias_out,
    ln1_gain,
    ln1_bias,
    w_in,
    bias_in,
    w_back,
    bias_back,
    ln2_gain,
    ln2_bias,
):
    gathered = (
        lax.all_gather(w_qkv, "fsdp", axis=0, tiled=True),
        lax.all_gather(bias_q, "fsdp", axis=0, tiled=True),
        lax.all_gather(bias_v, "fsdp", axis=0, tiled=True),
        lax.all_gather(w_out, "fsdp", axis=0, tiled=True),
        lax.all_gather(bias_out, "fsdp", axis=0, tiled=True),
        lax.all_gather(ln1_gain, "fsdp", axis=0, tiled=True),
        lax.all_gather(ln1_bias, "fsdp", axis=0, tiled=True),
        lax.all_gather(w_in, "fsdp", axis=0, tiled=True),
        lax.all_gather(bias_in, "fsdp", axis=0, tiled=True),
        lax.all_gather(w_back, "fsdp", axis=0, tiled=True),
        lax.all_gather(bias_back, "fsdp", axis=0, tiled=True),
        lax.all_gather(ln2_gain, "fsdp", axis=0, tiled=True),
        lax.all_gather(ln2_bias, "fsdp", axis=0, tiled=True),
    )
    (
        qkv_all,
        query_bias,
        value_bias,
        out_all,
        out_bias,
        gain_one,
        shift_one,
        in_all,
        in_bias,
        back_all,
        back_bias,
        gain_two,
        shift_two,
    ) = gathered
    rows = tokens.shape[1]
    half = rows // 2
    width = tokens.shape[2]
    length = lengths[0]
    query_place = places(pairing, lax.axis_index("ctx") * rows, rows, half)
    valid = query_place < length
    inputs = tokens[0]
    proj = jnp.dot(inputs, qkv_all, preferred_element_type=jnp.float32)
    queries = (proj[:, :width] + query_bias.astype(jnp.float32)).astype(jnp.bfloat16)
    keys = proj[:, width : 2 * width].astype(jnp.bfloat16)
    values = (proj[:, 2 * width :] + value_bias.astype(jnp.float32)).astype(jnp.bfloat16)
    query_heads = heads_of(queries)
    start_state = (
        jnp.full((HEADS, rows), neg_big, jnp.float32),
        jnp.zeros((HEADS, rows), jnp.float32),
        jnp.zeros((rows, HEADS, HEAD_DIM), jnp.float32),
    )
    fold = forward_fold(query_heads, query_place, pairing, length, half)
    top, total, summed = fold(
        start_state,
        (
            lax.all_gather(keys, "ctx", axis=0, tiled=True),
            lax.all_gather(values, "ctx", axis=0, tiled=True),
        ),
        jnp.int32(0),
    )
    top_sum = top + jnp.log(total)
    attended = (summed / jnp.transpose(total)[:, :, None]).reshape(rows, width)
    attended_low = attended.astype(jnp.bfloat16)
    resid_one = (
        inputs.astype(jnp.float32)
        + jnp.dot(attended_low, out_all, preferred_element_type=jnp.float32)
        + out_bias.astype(jnp.float32)
    )
    hidden = layer_norm(resid_one, gain_one.astype(jnp.float32), shift_one.astype(jnp.float32))
    hidden_low = hidden.astype(jnp.bfloat16)
    upper = jnp.dot(hidden_low, in_all, preferred_element_type=jnp.float32) + in_bias.astype(
        jnp.float32
    )
    active, gelu_back = jax.vjp(lambda value: jax.nn.gelu(value, approximate=False), upper)
    active_low = active.astype(jnp.bfloat16)
    resid_two = (
        hidden
        + jnp.dot(active_low, back_all, preferred_element_type=jnp.float32)
        + back_bias.astype(jnp.float32)
    )
    normed = layer_norm(resid_two, gain_two.astype(jnp.float32), shift_two.astype(jnp.float32))
    output = jnp.where(valid[:, None], normed, 0.0)
    qkv_back, out_back, gain_one_back, in_back, back_back, gain_two_back = (
        qkv_all,
        out_all,
        gain_one,
        in_all,
        back_all,
        gain_two,
    )
    grad_y = jnp.where(valid[:, None], cotangent[0].astype(jnp.float32), 0.0)
    grad_resid_two, gain_two_grad, shift_two_grad = norm_back(
        resid_two, gain_two_back.astype(jnp.float32), grad_y
    )
    grad_mixed = grad_resid_two.astype(jnp.bfloat16)
    back_grad = jnp.einsum("tf,td->fd", active_low, grad_mixed, preferred_element_type=jnp.float32)
    back_bias_grad = jnp.sum(grad_mixed.astype(jnp.float32), axis=0)
    grad_active = jnp.einsum("td,fd->tf", grad_mixed, back_back, preferred_element_type=jnp.float32)
    (grad_upper,) = gelu_back(grad_active)
    grad_upper_low = grad_upper.astype(jnp.bfloat16)
    in_grad = jnp.einsum(
        "td,tf->df", hidden_low, grad_upper_low, preferred_element_type=jnp.float32
    )
    in_bias_grad = jnp.sum(grad_upper_low.astype(jnp.float32), axis=0)
    grad_hidden = grad_resid_two + jnp.einsum(
        "tf,df->td", grad_upper_low, in_back, preferred_element_type=jnp.float32
    )
    grad_resid_one, gain_one_grad, shift_one_grad = norm_back(
        resid_one, gain_one_back.astype(jnp.float32), grad_hidden
    )
    grad_branch = grad_resid_one.astype(jnp.bfloat16)
    out_grad = jnp.einsum(
        "tc,td->cd", attended_low, grad_branch, preferred_element_type=jnp.float32
    )
    out_bias_grad = jnp.sum(grad_branch.astype(jnp.float32), axis=0)
    grad_attended = jnp.einsum(
        "td,cd->tc", grad_branch, out_back, preferred_element_type=jnp.float32
    ).astype(jnp.bfloat16)
    grad_heads = heads_of(grad_attended)
    delta = jnp.transpose(jnp.sum(grad_heads.astype(jnp.float32) * heads_of(attended), axis=2))
    query_fold = query_grad_fold(
        query_heads, grad_heads, top_sum, delta, query_place, pairing, length, half
    )
    empty_heads = jnp.zeros((rows, HEADS, HEAD_DIM), jnp.float32)
    query_grad = query_fold(
        empty_heads,
        (
            lax.all_gather(keys, "ctx", axis=0, tiled=True),
            lax.all_gather(values, "ctx", axis=0, tiled=True),
        ),
        jnp.int32(0),
    )
    stats = jnp.concatenate([jnp.transpose(top_sum), jnp.transpose(delta)], axis=1)
    stats_all = lax.all_gather(stats, "ctx", axis=0, tiled=True)
    key_heads = heads_of(keys)
    value_heads = heads_of(values)
    query_in = lax.all_gather(queries, "ctx", axis=0, tiled=True)
    grad_in = lax.all_gather(grad_attended, "ctx", axis=0, tiled=True)
    count = query_in.shape[0]
    span = block_width(count)
    place_in = places(pairing, jnp.int32(0), count, half)

    def step(index, state):
        offset = index * span
        query_block = heads_of(lax.dynamic_slice_in_dim(query_in, offset, span, 0))
        grad_block = heads_of(lax.dynamic_slice_in_dim(grad_in, offset, span, 0))
        stats_block = lax.dynamic_slice_in_dim(stats_all, offset, span, 0)
        place_block = lax.dynamic_slice_in_dim(place_in, offset, span, 0)
        key_part, value_part = key_terms(
            key_heads,
            value_heads,
            query_place,
            query_block,
            grad_block,
            jnp.transpose(stats_block[:, :HEADS]),
            jnp.transpose(stats_block[:, HEADS:]),
            place_block,
            length,
        )
        return (state[0] + key_part, state[1] + value_part)

    key_sum, value_sum = lax.fori_loop(0, count // span, step, (empty_heads, empty_heads))
    key_grad = key_sum.reshape(rows, width)
    value_grad = value_sum.reshape(rows, width)
    grad_proj = jnp.concatenate(
        [
            query_grad.reshape(rows, width).astype(jnp.bfloat16),
            key_grad.astype(jnp.bfloat16),
            value_grad.astype(jnp.bfloat16),
        ],
        axis=1,
    )
    qkv_grad = jnp.einsum("td,tf->df", inputs, grad_proj, preferred_element_type=jnp.float32)
    query_bias_grad = jnp.sum(grad_proj[:, :width].astype(jnp.float32), axis=0)
    value_bias_grad = jnp.sum(grad_proj[:, 2 * width :].astype(jnp.float32), axis=0)
    token_grad = grad_resid_one + jnp.einsum(
        "tf,df->td", grad_proj, qkv_back, preferred_element_type=jnp.float32
    )
    grads = (
        qkv_grad,
        query_bias_grad,
        value_bias_grad,
        out_grad,
        out_bias_grad,
        gain_one_grad,
        shift_one_grad,
        in_grad,
        in_bias_grad,
        back_grad,
        back_bias_grad,
        gain_two_grad,
        shift_two_grad,
    )
    shards = (
        lax.psum_scatter(
            grads[0].astype(jnp.bfloat16), "fsdp", scatter_dimension=0, tiled=True
        ).astype(jnp.float32),
        lax.psum_scatter(
            grads[1].astype(jnp.bfloat16), "fsdp", scatter_dimension=0, tiled=True
        ).astype(jnp.float32),
        lax.psum_scatter(
            grads[2].astype(jnp.bfloat16), "fsdp", scatter_dimension=0, tiled=True
        ).astype(jnp.float32),
        lax.psum_scatter(
            grads[3].astype(jnp.bfloat16), "fsdp", scatter_dimension=0, tiled=True
        ).astype(jnp.float32),
        lax.psum_scatter(
            grads[4].astype(jnp.bfloat16), "fsdp", scatter_dimension=0, tiled=True
        ).astype(jnp.float32),
        lax.psum_scatter(
            grads[5].astype(jnp.bfloat16), "fsdp", scatter_dimension=0, tiled=True
        ).astype(jnp.float32),
        lax.psum_scatter(
            grads[6].astype(jnp.bfloat16), "fsdp", scatter_dimension=0, tiled=True
        ).astype(jnp.float32),
        lax.psum_scatter(
            grads[7].astype(jnp.bfloat16), "fsdp", scatter_dimension=0, tiled=True
        ).astype(jnp.float32),
        lax.psum_scatter(
            grads[8].astype(jnp.bfloat16), "fsdp", scatter_dimension=0, tiled=True
        ).astype(jnp.float32),
        lax.psum_scatter(
            grads[9].astype(jnp.bfloat16), "fsdp", scatter_dimension=0, tiled=True
        ).astype(jnp.float32),
        lax.psum_scatter(
            grads[10].astype(jnp.bfloat16), "fsdp", scatter_dimension=0, tiled=True
        ).astype(jnp.float32),
        lax.psum_scatter(
            grads[11].astype(jnp.bfloat16), "fsdp", scatter_dimension=0, tiled=True
        ).astype(jnp.float32),
        lax.psum_scatter(
            grads[12].astype(jnp.bfloat16), "fsdp", scatter_dimension=0, tiled=True
        ).astype(jnp.float32),
    )
    totals = (
        lax.psum(shards[0].astype(jnp.bfloat16), "ctx").astype(jnp.float32),
        lax.psum(shards[1].astype(jnp.bfloat16), "ctx").astype(jnp.float32),
        lax.psum(shards[2].astype(jnp.bfloat16), "ctx").astype(jnp.float32),
        lax.psum(shards[3].astype(jnp.bfloat16), "ctx").astype(jnp.float32),
        lax.psum(shards[4].astype(jnp.bfloat16), "ctx").astype(jnp.float32),
        lax.psum(shards[5].astype(jnp.bfloat16), "ctx").astype(jnp.float32),
        lax.psum(shards[6].astype(jnp.bfloat16), "ctx").astype(jnp.float32),
        lax.psum(shards[7].astype(jnp.bfloat16), "ctx").astype(jnp.float32),
        lax.psum(shards[8].astype(jnp.bfloat16), "ctx").astype(jnp.float32),
        lax.psum(shards[9].astype(jnp.bfloat16), "ctx").astype(jnp.float32),
        lax.psum(shards[10].astype(jnp.bfloat16), "ctx").astype(jnp.float32),
        lax.psum(shards[11].astype(jnp.bfloat16), "ctx").astype(jnp.float32),
        lax.psum(shards[12].astype(jnp.bfloat16), "ctx").astype(jnp.float32),
    )
    return (output[None], token_grad[None]) + tuple(totals)


def exchange_kernel(n, in_ref, out_ref, sent, landed, own):
    me = lax.axis_index("ctx")
    barrier = pltpu.get_barrier_semaphore()
    for k in range(1, n):
        pl.semaphore_signal(
            barrier, inc=1, device_id={"ctx": lax.rem(me + k, n)}, device_id_type=MESH
        )
    pl.semaphore_wait(barrier, n - 1)
    copies = []
    for k in range(1, n):
        peer = lax.rem(me + k, n)
        copy = pltpu.make_async_remote_copy(
            src_ref=in_ref.at[peer],
            dst_ref=out_ref.at[me],
            send_sem=sent.at[k],
            recv_sem=landed.at[k],
            device_id={"ctx": peer},
            device_id_type=MESH,
        )
        copy.start()
        copies.append(copy)
    local = pltpu.make_async_copy(in_ref.at[me], out_ref.at[me], own)
    local.start()
    local.wait()
    for copy in copies:
        copy.wait()


def exchange(blocks, name):
    n = blocks.shape[0]
    return pl.pallas_call(
        functools.partial(exchange_kernel, n),
        out_shape=jax.ShapeDtypeStruct(blocks.shape, blocks.dtype),
        in_specs=[vmem()],
        out_specs=vmem(),
        scratch_shapes=[
            pltpu.SemaphoreType.DMA((n,)),
            pltpu.SemaphoreType.DMA((n,)),
            pltpu.SemaphoreType.DMA,
        ],
        compiler_params=pltpu.CompilerParams(
            collective_id=name, has_side_effects=True, vmem_limit_bytes=16 << 20
        ),
        name="exchange",
    )(blocks)


def split_heads(value):
    rows = value.shape[0]
    trio = value.reshape(rows, HEADS // 3, 3, HEAD_DIM)
    own = trio[:, :, :2]
    shared = jnp.broadcast_to(trio[:, :, 2:], own.shape)
    both = jnp.concatenate([own, shared], axis=-1)
    return jnp.transpose(both.reshape(rows, -1, 2 * HEAD_DIM), (1, 0, 2))


def send_blocks(queries, keys, values):
    return jnp.concatenate([split_heads(queries), split_heads(keys), split_heads(values)], axis=2)


def low_lanes(shape):
    return lax.broadcasted_iota(jnp.int32, shape, 1) < 64


def attend_kernel(chunks, pair_ref, len_ref, spot_ref, in_ref, out_ref, keep_ref, mix_ref, lse_ref):
    length = len_ref[0]
    spot = spot_ref[0]
    blocks = 2 * chunks
    for s in range(blocks):
        keep_ref[pair_ref[s]] = in_ref[s]
    left = low_lanes((256, BLK))
    left_half = left[:BLK]
    for c in range(chunks):
        keys = 256 * (c + 1)
        own = keep_ref[2 * c : 2 * c + 2, :, :BLK].reshape(256, BLK)
        shared = keep_ref[2 * c + spot, :, :BLK]
        zero = jnp.zeros((), jnp.bfloat16)
        query = jnp.concatenate(
            [jnp.where(left, own, zero), jnp.where(left_half, zero, shared)], axis=0
        ) * jnp.bfloat16(0.125)
        key = keep_ref[: 2 * c + 2, :, BLK : 2 * BLK].reshape(keys, BLK)
        value = keep_ref[: 2 * c + 2, :, 2 * BLK :].reshape(keys, BLK)
        scores = mask_scores(
            lax.dot_general(key, query, (((1,), (1,)), ((), ())), preferred_element_type=jnp.float32),
            c, spot, length,
        )
        top = jnp.max(scores, axis=0, keepdims=True)
        probs = jnp.exp(scores - top)
        total = jnp.sum(probs, axis=0, keepdims=True)
        summed = lax.dot_general(
            value, probs.astype(jnp.bfloat16), (((0,), (0,)), ((), ())),
            preferred_element_type=jnp.float32,
        ) / total
        lse_ref[c] = top + jnp.log(total)
        part = summed[64:, 256:]
        none = jnp.zeros_like(part)
        first = jnp.where(spot == 0, part, none)
        second = jnp.where(spot == 0, none, part)
        mixed = jnp.concatenate(
            [summed[:64, :256], jnp.concatenate([first, second], axis=1)], axis=0
        )
        mix_ref[c] = mixed
    for s in range(blocks):
        place = pair_ref[s]
        c = place // 2
        piece = mix_ref[c, :, pl.ds(pl.multiple_of((place % 2) * BLK, BLK), BLK)]
        out_ref[s] = jnp.transpose(piece).astype(jnp.bfloat16)


def mask_scores(scores, c, spot, length):
    keys, width = scores.shape
    edge = 256 * c
    row = lax.broadcasted_iota(jnp.int32, (keys, width), 0)
    scores = jnp.where(row < length, scores, neg_big)
    lane = lax.broadcasted_iota(jnp.int32, (256, width), 1)
    query_place = edge + jnp.where(lane < 256, lane, lane - 256 + spot * BLK)
    key_place = edge + lax.broadcasted_iota(jnp.int32, (256, width), 0)
    seen = key_place <= query_place
    if c == 0:
        seen = seen | (key_place < NMEM)
    tail = jnp.where(seen, scores[edge:], neg_big)
    if c == 0:
        return tail
    return jnp.concatenate([scores[:edge], tail], axis=0)


def attend_back_kernel(
    chunks, pair_ref, len_ref, spot_ref, keep_ref, grad_ref, mix_ref, lse_ref, out_ref, g_ref,
    q_sum, k_sum, v_sum
):
    length = len_ref[0]
    spot = spot_ref[0]
    blocks = 2 * chunks
    for s in range(blocks):
        g_ref[pair_ref[s]] = grad_ref[s]
    k_sum[...] = jnp.zeros_like(k_sum)
    v_sum[...] = jnp.zeros_like(v_sum)
    left = low_lanes((256, BLK))
    left_half = left[:BLK]
    zero = jnp.zeros((), jnp.bfloat16)
    for c in range(chunks):
        keys = 256 * (c + 1)
        own = keep_ref[2 * c : 2 * c + 2, :, :BLK].reshape(256, BLK)
        shared = keep_ref[2 * c + spot, :, :BLK]
        query = jnp.concatenate(
            [jnp.where(left, own, zero), jnp.where(left_half, zero, shared)], axis=0
        ) * jnp.bfloat16(0.125)
        g_own = g_ref[2 * c : 2 * c + 2].reshape(256, BLK)
        g_shared = g_ref[2 * c + spot]
        grad = jnp.concatenate(
            [jnp.where(left, g_own, zero), jnp.where(left_half, zero, g_shared)], axis=0
        )
        key = keep_ref[: 2 * c + 2, :, BLK : 2 * BLK].reshape(keys, BLK)
        value = keep_ref[: 2 * c + 2, :, 2 * BLK :].reshape(keys, BLK)
        turned = jnp.transpose(g_own.astype(jnp.float32)) * mix_ref[c]
        delta_own = jnp.sum(turned[:64], axis=0, keepdims=True)
        delta_pair = jnp.sum(turned[64:], axis=0, keepdims=True)
        delta = jnp.concatenate(
            [delta_own, jnp.where(spot == 0, delta_pair[:, :BLK], delta_pair[:, BLK:])], axis=1
        )
        nt = (((1,), (1,)), ((), ()))
        scores = mask_scores(
            lax.dot_general(key, query, nt, preferred_element_type=jnp.float32), c, spot, length
        )
        probs = jnp.exp(scores - lse_ref[c])
        prob_grad = lax.dot_general(value, grad, nt, preferred_element_type=jnp.float32)
        score_grad = (probs * (prob_grad - delta)).astype(jnp.bfloat16)
        nn = (((1,), (0,)), ((), ()))
        v_sum[:keys] += lax.dot_general(
            probs.astype(jnp.bfloat16), grad, nn, preferred_element_type=jnp.float32
        )
        k_sum[:keys] += lax.dot_general(score_grad, query, nn, preferred_element_type=jnp.float32)
        q_grad = lax.dot_general(
            score_grad, key, (((0,), (0,)), ((), ())), preferred_element_type=jnp.float32
        ) * 0.125
        part = q_grad[256:]
        none = jnp.zeros_like(part)
        first = jnp.where(spot == 0, part, none)
        second = jnp.where(spot == 0, none, part)
        q_sum[256 * c : 256 * c + 256] = jnp.where(
            left, q_grad[:256], jnp.concatenate([first, second], axis=0)
        )
    for s in range(blocks):
        rows = pl.ds(pl.multiple_of(pair_ref[s] * BLK, BLK), BLK)
        out_ref[s] = jnp.concatenate([q_sum[rows], k_sum[rows], v_sum[rows]], axis=1).astype(jnp.bfloat16)


def smem():
    return pl.BlockSpec(memory_space=pltpu.SMEM)


def vmem():
    return pl.BlockSpec(memory_space=pltpu.VMEM)


def attend(pairing, lengths, spot, packed):
    blocks = packed.shape[0]
    chunks = blocks // 2
    return pl.pallas_call(
        functools.partial(attend_kernel, chunks),
        out_shape=(
            jax.ShapeDtypeStruct((blocks, BLK, BLK), jnp.bfloat16),
            jax.ShapeDtypeStruct((blocks, BLK, 3 * BLK), jnp.bfloat16),
            jax.ShapeDtypeStruct((chunks, BLK, 256), jnp.float32),
            jax.ShapeDtypeStruct((chunks, 1, 384), jnp.float32),
        ),
        in_specs=[smem(), smem(), smem(), vmem()],
        out_specs=(vmem(), vmem(), vmem(), vmem()),
        compiler_params=pltpu.CompilerParams(vmem_limit_bytes=48 << 20),
        name="attend",
    )(pairing, lengths, spot, packed)


def attend_back(pairing, lengths, spot, keep, grad, mix, lse):
    blocks = keep.shape[0]
    chunks = blocks // 2
    return pl.pallas_call(
        functools.partial(attend_back_kernel, chunks),
        out_shape=jax.ShapeDtypeStruct((blocks, BLK, 3 * BLK), jnp.bfloat16),
        in_specs=[smem(), smem(), smem(), vmem(), vmem(), vmem(), vmem()],
        out_specs=vmem(),
        scratch_shapes=[
            pltpu.VMEM((blocks, BLK, BLK), jnp.bfloat16),
            pltpu.VMEM((blocks * BLK, BLK), jnp.float32),
            pltpu.VMEM((blocks * BLK, BLK), jnp.float32),
            pltpu.VMEM((blocks * BLK, BLK), jnp.float32),
        ],
        compiler_params=pltpu.CompilerParams(vmem_limit_bytes=48 << 20),
        name="attend_back",
    )(pairing, lengths, spot, keep, grad, mix, lse)


MESH = pl.DeviceIdType.MESH


def remote(src, dst, sems, at, peer):
    return pltpu.make_async_remote_copy(
        src_ref=src, dst_ref=dst, send_sem=sems.at[(0,) + at], recv_sem=sems.at[(1,) + at],
        device_id=peer, device_id_type=MESH,
    )


def greet(peers):
    barrier = pltpu.get_barrier_semaphore()
    for peer in peers:
        pl.semaphore_signal(barrier, inc=1, device_id=peer, device_id_type=MESH)
    pl.semaphore_wait(barrier, len(peers))


def ring_peers(n):
    me = lax.axis_index("ctx")
    return [{"ctx": lax.rem(me + k, n)} for k in range(1, n)]


def exchange_copies(n, in_ref, out_ref, sems):
    me = lax.axis_index("ctx")
    return [
        remote(in_ref.at[lax.rem(me + k, n)], out_ref.at[me], sems, (k,), {"ctx": lax.rem(me + k, n)})
        for k in range(1, n)
    ]


def join_pairs(pairs):
    pieces = []
    for group in range(HEADS // 3):
        first, second = pairs(2 * group), pairs(2 * group + 1)
        shared = first[:, HEAD_DIM:].astype(jnp.float32) + second[:, HEAD_DIM:].astype(jnp.float32)
        pieces += [first[:, :HEAD_DIM], second[:, :HEAD_DIM], shared.astype(jnp.bfloat16)]
    return jnp.concatenate(pieces, axis=1)


def pair_of(value, peer):
    own = 3 * (peer // 2) + peer % 2
    shared = 3 * (peer // 2) + 2
    cut = lambda head: value[:, head * HEAD_DIM : (head + 1) * HEAD_DIM]
    return jnp.concatenate([cut(own), cut(shared)], axis=1)


def dot_nn(a, b):
    return jnp.dot(a, b, preferred_element_type=jnp.float32)


def dot_nt(a, b):
    return lax.dot_general(a, b, (((1,), (1,)), ((), ())), preferred_element_type=jnp.float32)


def column_sum(value):
    return jnp.sum(value, axis=0, keepdims=True)


def unit_of(value):
    mean = jnp.mean(value, axis=-1, keepdims=True)
    centred = value - mean
    scale = lax.rsqrt(jnp.mean(centred * centred, axis=-1, keepdims=True) + eps)
    return centred * scale, scale


def unit_back(unit, scale, scaled):
    return scale * (
        scaled
        - jnp.mean(scaled, axis=-1, keepdims=True)
        - unit * jnp.mean(scaled * unit, axis=-1, keepdims=True)
    )


(ROW_BQ, ROW_BV, ROW_BO, ROW_G1, ROW_S1, ROW_BB, ROW_G2, ROW_S2, ROW_BI) = range(9)


def layer_kernel(
    n, pair_ref, len_ref, mixed_ref, tokens_ref, cot_ref, w_out_ref, w_in_ref, w_back_ref, rows_ref,
    output_ref, grad_in_ref, left_ref, right_ref, resid_ref, sums_ref,
    mixed_in, grad_out, active, slope, in_sem, out_sem, own_sem,
):
    low, wide = jnp.bfloat16, jnp.float32
    ctx = lax.axis_index("ctx")
    sums_ref[...] = jnp.zeros_like(sums_ref)
    greet(ring_peers(n))
    copies = exchange_copies(n, mixed_ref, mixed_in, in_sem)
    for cp in copies:
        cp.start()
    own = pltpu.make_async_copy(mixed_ref.at[ctx], mixed_in.at[ctx], own_sem.at[0])
    own.start()
    row = lambda i: rows_ref[i : i + 1, :]
    tokens = tokens_ref[...]
    left_ref[0] = jnp.transpose(tokens).reshape(4, -1, 2 * BLK)
    spots = lax.broadcasted_iota(jnp.int32, (2 * BLK, 1), 0)
    place = jnp.where(
        spots < BLK,
        pair_ref[2 * ctx] * BLK + spots,
        pair_ref[2 * ctx + 1] * BLK + spots - BLK,
    )
    valid = place < len_ref[0]
    own.wait()
    for cp in copies:
        cp.wait_recv()

    attended = join_pairs(lambda peer: mixed_in[peer])
    resid_one = tokens.astype(wide) + dot_nn(attended, w_out_ref[...]) + row(ROW_BO)
    unit_one, scale_one = unit_of(resid_one)
    hidden = unit_one * row(ROW_G1) + row(ROW_S1)
    hidden_low = hidden.astype(low)
    width = tokens.shape[1]
    count = w_in_ref.shape[1] // width
    resid_two = hidden + row(ROW_BB)
    for t in range(count):
        cols = slice(t * width, (t + 1) * width)
        upper = dot_nn(hidden_low, w_in_ref[:, cols]) + row(ROW_BI + t)
        share = 0.5 * (1.0 + lax.erf(upper * (0.5**0.5)))
        slope[:, cols] = share + upper * (jnp.exp(-0.5 * upper * upper) * (2 * math.pi) ** -0.5)
        some = (upper * share).astype(low)
        active[:, cols] = some
        resid_two = resid_two + dot_nn(some, w_back_ref[cols, :])
    unit_two, scale_two = unit_of(resid_two)
    output_ref[...] = jnp.where(valid, unit_two * row(ROW_G2) + row(ROW_S2), 0.0)
    grad_y = jnp.where(valid, cot_ref[...].astype(wide), 0.0)
    sums_ref[ROW_G2 : ROW_G2 + 1, :] = column_sum(grad_y * unit_two)
    sums_ref[ROW_S2 : ROW_S2 + 1, :] = column_sum(grad_y)
    grad_resid_two = unit_back(unit_two, scale_two, grad_y * row(ROW_G2))
    grad_mixed = grad_resid_two.astype(low)
    right_ref[5] = grad_mixed
    sums_ref[ROW_BB : ROW_BB + 1, :] = column_sum(grad_mixed.astype(wide))
    grad_hidden = grad_resid_two
    for t in range(count):
        cols = slice(t * width, (t + 1) * width)
        grad_upper = (dot_nt(grad_mixed, w_back_ref[cols, :]) * slope[:, cols]).astype(low)
        right_ref[1 + t] = grad_upper
        sums_ref[ROW_BI + t : ROW_BI + t + 1, :] = column_sum(grad_upper.astype(wide))
        grad_hidden = grad_hidden + dot_nt(grad_upper, w_in_ref[:, cols])
    sums_ref[ROW_G1 : ROW_G1 + 1, :] = column_sum(grad_hidden * unit_one)
    sums_ref[ROW_S1 : ROW_S1 + 1, :] = column_sum(grad_hidden)
    grad_resid_one = unit_back(unit_one, scale_one, grad_hidden * row(ROW_G1))
    resid_ref[...] = grad_resid_one
    grad_branch = grad_resid_one.astype(low)
    right_ref[0] = grad_branch
    sums_ref[ROW_BO : ROW_BO + 1, :] = column_sum(grad_branch.astype(wide))
    grad_attended = dot_nt(grad_branch, w_out_ref[...]).astype(low)
    for peer in range(n):
        grad_out[peer] = pair_of(grad_attended, peer)
    backs = exchange_copies(n, grad_out, grad_in_ref, out_sem)
    for cp in backs:
        cp.start()
    back = pltpu.make_async_copy(grad_out.at[ctx], grad_in_ref.at[ctx], own_sem.at[1])
    back.start()
    left_ref[1] = jnp.transpose(attended).reshape(4, -1, 2 * BLK)
    left_ref[2] = jnp.transpose(hidden_low).reshape(4, -1, 2 * BLK)
    for f in range(4):
        turned = jnp.transpose(active[:, f * width : (f + 1) * width])
        for r in range(4):
            left_ref[3 + r, f] = turned[r * width // 4 : (r + 1) * width // 4]
    back.wait()
    for cp in copies:
        cp.wait_send()
    for cp in backs:
        cp.wait()


def layer(pairing, lengths, mixed, tokens, cotangent, w_out, w_in, w_back, rows, name):
    n = mixed.shape[0]
    count, width = tokens.shape
    inner = w_in.shape[1]
    low, wide = jnp.bfloat16, jnp.float32
    dma = pltpu.SemaphoreType.DMA
    shape = jax.ShapeDtypeStruct
    return pl.pallas_call(
        functools.partial(layer_kernel, n),
        out_shape=(
            shape((count, width), wide),
            shape(mixed.shape, low),
            shape((7, 4, width // 4, count), low),
            shape((6, count, width), low),
            shape((count, width), wide),
            shape((16, width), wide),
        ),
        in_specs=[smem(), smem()] + [vmem()] * 7,
        out_specs=(vmem(),) * 6,
        scratch_shapes=[
            pltpu.VMEM(mixed.shape, low),
            pltpu.VMEM(mixed.shape, low),
            pltpu.VMEM((count, inner), low),
            pltpu.VMEM((count, inner), wide),
            dma((2, n)),
            dma((2, n)),
            dma((2,)),
        ],
        compiler_params=pltpu.CompilerParams(
            collective_id=name, has_side_effects=True, vmem_limit_bytes=56 << 20
        ),
        name="layer",
    )(pairing, lengths, mixed, tokens, cotangent, w_out, w_in, w_back, rows)


PARTS = 12


def sum_sources(chunk):
    left = jnp.where(chunk < 4, 3 + chunk, jnp.where(chunk < 8, 2, jnp.where(chunk < 9, 1, 0)))
    right = jnp.where(
        chunk < 4, 8, jnp.where(chunk < 8, chunk, jnp.where(chunk < 9, 3, chunk - 9))
    )
    return left, right


def sum_kernel(
    n, left_ref, right_ref, sums_ref, blocks_ref, w_qkv_ref, resid_ref,
    token_ref, qkv_out, out_out, in_out, back_out, small_out,
    blocks_in, right_all, total_ref, pair_out, pair_in, x_out, x_in, first_sum, y_out, y_in, half_sum,
    z_out, z_in, s_pair, s_x_out, s_x, s_y_out, s_y, s_z_out, s_z,
    block_sem, own_sem, pair_sem, x_sem, y_sem, z_sem, spread_sem, last_sem, s_sem,
):
    low, wide = jnp.bfloat16, jnp.float32
    ctx = lax.axis_index("ctx")
    fsdp = lax.axis_index("fsdp")
    z, y = ctx // 2, lax.rem(ctx, 2)
    x, core = fsdp // 2, lax.rem(fsdp, 2)
    sibling = {"fsdp": 2 * x + 1 - core}
    across = {"fsdp": 2 * (1 - x) + core}
    beside = {"ctx": 2 * z + 1 - y}
    along = [{"ctx": 2 * lax.rem(z + k, 4) + y} for k in (1, 2, 3)]
    greet(ring_peers(n) + [sibling, across])
    blocks = exchange_copies(n, blocks_ref, blocks_in, block_sem)
    for cp in blocks:
        cp.start()
    own = pltpu.make_async_copy(blocks_ref.at[ctx], blocks_in.at[ctx], own_sem)
    own.start()
    right_all[3:] = right_ref[...]

    def pair_copy(c):
        return remote(pair_out.at[lax.rem(c, 2)], pair_in.at[c], pair_sem, (c,), sibling)

    def x_copy(c):
        return remote(x_out.at[c], x_in.at[c], x_sem, (c,), across)

    def y_copy(c):
        return remote(y_out.at[c], y_in.at[c], y_sem, (c,), beside)

    def z_copy(c, k):
        return remote(
            z_out.at[c, lax.rem(z + k, 4)], z_in.at[c, k - 1], z_sem, (c, k - 1), along[k - 1]
        )

    def spread_copy(c, k):
        piece = total_ref.at[c, y, z]
        return remote(piece, piece, spread_sem, (c, k - 1), along[k - 1])

    def last_copy(c):
        return remote(total_ref.at[c, y], total_ref.at[c, y], last_sem, (c,), beside)

    def partial(c, shard):
        left, right = sum_sources(c)
        return jnp.dot(left_ref[left, shard], right_all[right], preferred_element_type=jnp.float32)

    def stage_pair(c):
        @pl.when(c >= 2)
        def _():
            pair_copy(c - 2).wait_send()

        for side in range(2):
            pair_out[lax.rem(c, 2), side] = partial(c, 2 * side + 1 - core).astype(low)
        pair_copy(c).start()

    def stage_x(c):
        pair_copy(c).wait_recv()
        x_out[c] = (
            partial(c, 2 * (1 - x) + core) + pair_in[c, 1 - x].astype(jnp.float32)
        ).astype(low)
        x_copy(c).start()
        first_sum[lax.rem(c, 2)] = partial(c, 2 * x + core) + pair_in[c, x].astype(jnp.float32)

    def stage_y(c):
        x_copy(c).wait_recv()
        total = first_sum[lax.rem(c, 2)] + x_in[c].astype(jnp.float32)
        here, there = total[:, :384], total[:, 384:]
        y_out[c] = jnp.where(y == 0, there, here).astype(low)
        y_copy(c).start()
        half_sum[lax.rem(c, 2)] = jnp.where(y == 0, here, there)

    def stage_z(c):
        y_copy(c).wait_recv()
        total = half_sum[lax.rem(c, 2)] + y_in[c].astype(jnp.float32)
        z_out[c] = total.astype(low).reshape(4, 48, 384)
        for k in (1, 2, 3):
            z_copy(c, k).start()
        half_sum[lax.rem(c, 2)] = total

    def stage_spread(c):
        total = half_sum[lax.rem(c, 2), pl.ds(pl.multiple_of(48 * z, 48), 48)]
        for k in (1, 2, 3):
            z_copy(c, k).wait_recv()
            total = total + z_in[c, k - 1].astype(jnp.float32)
        total_ref[c, y, z] = total.astype(low)
        for k in (1, 2, 3):
            spread_copy(c, k).start()

    def stage_last(c):
        for k in (1, 2, 3):
            spread_copy(c, k).wait_recv()
        last_copy(c).start()

    stages = [stage_pair, stage_x, stage_y, stage_z, stage_spread, stage_last]
    order = [0, 1, 4, 2, 3, 5]

    def small_step(t):
        send_pair = remote(s_pair.at[0], s_pair.at[1], s_sem, (0,), sibling)
        send_x = remote(s_x_out, s_x, s_sem, (1,), across)
        send_y = remote(s_y_out, s_y, s_sem, (2,), beside)
        send_z = [remote(s_z_out, s_z.at[k], s_sem, (3 + k,), along[k]) for k in range(3)]

        @pl.when(t == 0)
        def _():
            own.wait()
            for cp in blocks:
                cp.wait_recv()
            for part in range(3):
                right_all[part] = join_pairs(
                    lambda peer: blocks_in[peer, :, part * 2 * HEAD_DIM : (part + 1) * 2 * HEAD_DIM]
                )
            s_pair[0] = sums_ref[...]
            s_pair[0, ROW_BQ : ROW_BQ + 1] = column_sum(right_all[0].astype(wide))
            s_pair[0, ROW_BV : ROW_BV + 1] = column_sum(right_all[2].astype(wide))
            send_pair.start()

        @pl.when(t == 1)
        def _():
            send_pair.wait()
            s_x_out[...] = s_pair[0] + s_pair[1]
            send_x.start()
            width = resid_ref.shape[1]
            token_ref[...] = resid_ref[...] + sum(
                dot_nt(right_all[part], w_qkv_ref[:, part * width : (part + 1) * width])
                for part in range(3)
            )

        @pl.when(t == 2)
        def _():
            send_x.wait()
            s_y_out[...] = s_x_out[...] + s_x[...]
            send_y.start()

        @pl.when(t == 3)
        def _():
            send_y.wait()
            s_z_out[...] = s_y_out[...] + s_y[...]
            for cp in send_z:
                cp.start()

        @pl.when(t == 4)
        def _():
            for cp in send_z:
                cp.wait()
            total = jnp.zeros(s_z_out.shape, wide)
            for spot in range(4):
                k = lax.rem(spot - z + 4, 4)
                other = s_z[jnp.where(k == 0, 0, 3 - k)]
                total = total + jnp.where(k == 0, s_z_out[...], other)
            quarter = total.shape[1] // 4
            cuts = [slice(f * quarter, (f + 1) * quarter) for f in range(4)]
            pick = lambda choices: sum(
                jnp.where(fsdp == f, choice, 0.0) for f, choice in enumerate(choices)
            )
            small_out[:8] = pick([total[:8, cut] for cut in cuts])
            line = pick([total[ROW_BI + f : ROW_BI + f + 1] for f in range(4)])
            for j, cut in enumerate(cuts):
                small_out[8 + j : 9 + j] = line[:, cut]

    def slot(t, carry):
        small_step(t - 9)
        for index in order:
            c = t - index

            @pl.when((c >= 0) & (c < PARTS))
            def _():
                stages[index](c)

        return carry

    lax.fori_loop(0, PARTS + 5, slot, 0)

    def drain(c, carry):
        x_copy(c).wait_send()
        y_copy(c).wait_send()
        for k in (1, 2, 3):
            z_copy(c, k).wait_send()
            spread_copy(c, k).wait_send()
        last_copy(c).wait()
        return carry

    lax.fori_loop(0, PARTS, drain, 0)
    for c in (PARTS - 2, PARTS - 1):
        pair_copy(c).wait_send()
    for cp in blocks:
        cp.wait_send()

    def panel(c, target, rows_at, cols_at):
        for half in range(2):
            for spot in range(4):
                target[
                    rows_at + 48 * spot : rows_at + 48 * spot + 48,
                    cols_at + 384 * half : cols_at + 384 * half + 384,
                ] = total_ref[c, half, spot]

    for k in range(4):
        panel(k, back_out, 192 * k, 0)
        panel(4 + k, in_out, 0, 768 * k)
    panel(8, out_out, 0, 0)
    for k in range(3):
        panel(9 + k, qkv_out, 0, 768 * k)


def sum_all(left, right, sums, blocks, w_qkv, resid, name):
    n = blocks.shape[0]
    low, wide = jnp.bfloat16, jnp.float32
    dma = pltpu.SemaphoreType.DMA
    shape = jax.ShapeDtypeStruct
    small = pltpu.VMEM(sums.shape, wide)
    return pl.pallas_call(
        functools.partial(sum_kernel, n),
        out_shape=(
            shape(resid.shape, wide),
            shape((192, 2304), low),
            shape((192, 768), low),
            shape((192, 3072), low),
            shape((768, 768), low),
            shape((16, 192), wide),
        ),
        in_specs=[vmem()] * 6,
        out_specs=(vmem(),) * 6,
        scratch_shapes=[
            pltpu.VMEM(blocks.shape, low),
            pltpu.VMEM((9,) + right.shape[1:], low),
            pltpu.VMEM((PARTS, 2, 4, 48, 384), low),
            pltpu.VMEM((2, 2, 192, 768), low),
            pltpu.VMEM((PARTS, 2, 192, 768), low),
            pltpu.VMEM((PARTS, 192, 768), low),
            pltpu.VMEM((PARTS, 192, 768), low),
            pltpu.VMEM((2, 192, 768), wide),
            pltpu.VMEM((PARTS, 192, 384), low),
            pltpu.VMEM((PARTS, 192, 384), low),
            pltpu.VMEM((2, 192, 384), wide),
            pltpu.VMEM((PARTS, 4, 48, 384), low),
            pltpu.VMEM((PARTS, 3, 48, 384), low),
            pltpu.VMEM((2,) + sums.shape, wide),
            small, small, small, small, small,
            pltpu.VMEM((3,) + sums.shape, wide),
            dma((2, n)),
            dma,
            dma((2, PARTS)),
            dma((2, PARTS)),
            dma((2, PARTS)),
            dma((2, PARTS, 3)),
            dma((2, PARTS, 3)),
            dma((2, PARTS)),
            dma((2, 6)),
        ],
        compiler_params=pltpu.CompilerParams(
            collective_id=name, has_side_effects=True, vmem_limit_bytes=60 << 20
        ),
        name="sum_all",
    )(left, right, sums, blocks, w_qkv, resid)


def on_device_spread(
    tokens,
    cotangent,
    lengths,
    pairing,
    w_qkv,
    bias_q,
    bias_v,
    w_out,
    bias_out,
    ln1_gain,
    ln1_bias,
    w_in,
    bias_in,
    w_back,
    bias_back,
    ln2_gain,
    ln2_bias,
):
    gathered = (
        lax.all_gather(w_qkv, "fsdp", axis=0, tiled=True),
        lax.all_gather(bias_q, "fsdp", axis=0, tiled=True),
        lax.all_gather(bias_v, "fsdp", axis=0, tiled=True),
        lax.all_gather(w_out, "fsdp", axis=0, tiled=True),
        lax.all_gather(bias_out, "fsdp", axis=0, tiled=True),
        lax.all_gather(ln1_gain, "fsdp", axis=0, tiled=True),
        lax.all_gather(ln1_bias, "fsdp", axis=0, tiled=True),
        lax.all_gather(w_in, "fsdp", axis=0, tiled=True),
        lax.all_gather(bias_in, "fsdp", axis=0, tiled=True),
        lax.all_gather(w_back, "fsdp", axis=0, tiled=True),
        lax.all_gather(bias_back, "fsdp", axis=0, tiled=True),
        lax.all_gather(ln2_gain, "fsdp", axis=0, tiled=True),
        lax.all_gather(ln2_bias, "fsdp", axis=0, tiled=True),
    )
    (
        qkv_all,
        query_bias,
        value_bias,
        out_all,
        out_bias,
        gain_one,
        shift_one,
        in_all,
        in_bias,
        back_all,
        back_bias,
        gain_two,
        shift_two,
    ) = gathered
    rows = tokens.shape[1]
    half = rows // 2
    width = tokens.shape[2]
    length = lengths[0]
    query_place = places(pairing, lax.axis_index("ctx") * rows, rows, half)
    valid = query_place < length
    inputs = tokens[0]
    proj = jnp.dot(inputs, qkv_all, preferred_element_type=jnp.float32)
    queries = (proj[:, :width] + query_bias.astype(jnp.float32)).astype(jnp.bfloat16)
    keys = proj[:, width : 2 * width].astype(jnp.bfloat16)
    values = (proj[:, 2 * width :] + value_bias.astype(jnp.float32)).astype(jnp.bfloat16)
    spot = lax.rem(lax.axis_index("ctx"), 2).astype(jnp.int32).reshape(1)
    sent = send_blocks(queries, keys, values)
    packed = exchange(sent, 0).reshape(-1, half, 6 * HEAD_DIM)
    mixed_out, keep, mix, lse = attend(pairing, lengths, spot, packed)
    vectors = [
        query_bias, value_bias, out_bias, gain_one, shift_one, back_bias, gain_two, shift_two
    ]
    vectors = jnp.concatenate([jnp.stack(vectors), in_bias.reshape(-1, width)]).astype(jnp.float32)
    vectors = jnp.pad(vectors, ((0, 16 - vectors.shape[0]), (0, 0)))
    output, grad_in, left, right, resid, sums = layer(
        pairing, lengths, mixed_out.reshape(-1, rows, 2 * HEAD_DIM), inputs, cotangent[0],
        out_all, in_all, back_all, vectors, 1,
    )
    grad_blocks = attend_back(
        pairing, lengths, spot, keep, grad_in.reshape(-1, half, 2 * HEAD_DIM), mix, lse
    )
    token_grad, qkv_sum, out_sum, in_sum, back_sum, small = sum_all(
        left, right, sums, grad_blocks.reshape(-1, rows, 6 * HEAD_DIM), qkv_all, resid, 2
    )
    wide = lambda value: value.astype(jnp.float32)
    return (
        output[None],
        token_grad[None],
        wide(qkv_sum),
        small[ROW_BQ],
        small[ROW_BV],
        wide(out_sum),
        small[ROW_BO],
        small[ROW_G1],
        small[ROW_S1],
        wide(in_sum),
        small[ROW_BI : ROW_BI + 4].reshape(-1),
        wide(back_sum),
        small[ROW_BB],
        small[ROW_G2],
        small[ROW_S2],
    )


def solution(mesh):
    return jax.shard_map(
        on_device_spread if mesh.shape["ctx"] == 8 else on_device_any,
        mesh=mesh,
        in_specs=(
            P("fsdp", "ctx", None),
            P("fsdp", "ctx", None),
            P("fsdp"),
            P(),
            P("fsdp", None),
            P("fsdp"),
            P("fsdp"),
            P("fsdp", None),
            P("fsdp"),
            P("fsdp"),
            P("fsdp"),
            P("fsdp", None),
            P("fsdp"),
            P("fsdp", None),
            P("fsdp"),
            P("fsdp"),
            P("fsdp"),
        ),
        out_specs=(
            P("fsdp", "ctx", None),
            P("fsdp", "ctx", None),
            P("fsdp", None),
            P("fsdp"),
            P("fsdp"),
            P("fsdp", None),
            P("fsdp"),
            P("fsdp"),
            P("fsdp"),
            P("fsdp", None),
            P("fsdp"),
            P("fsdp", None),
            P("fsdp"),
            P("fsdp"),
            P("fsdp"),
        ),
        check_vma=False,
    )
```

```python
import functools
import math

import jax
import jax.numpy as jnp
from jax import lax
from jax.experimental import pallas as pl
from jax.experimental.pallas import tpu as pltpu
from jax.sharding import PartitionSpec as P

HEADS = 12
HEAD_DIM = 64
NMEM = 10
BLK = 128


eps = 1e-12
neg_big = -1e30


def layer_norm(value, gain, shift):
    mean = jnp.mean(value, axis=-1, keepdims=True)
    centred = value - mean
    variance = jnp.mean(centred * centred, axis=-1, keepdims=True)
    return centred * lax.rsqrt(variance + eps) * gain + shift


def norm_back(value, gain, grad):
    mean = jnp.mean(value, axis=-1, keepdims=True)
    centred = value - mean
    scale = lax.rsqrt(jnp.mean(centred * centred, axis=-1, keepdims=True) + eps)
    unit = centred * scale
    scaled = grad * gain
    inner = (
        scaled
        - jnp.mean(scaled, axis=-1, keepdims=True)
        - unit * jnp.mean(scaled * unit, axis=-1, keepdims=True)
    )
    return (scale * inner, jnp.sum(grad * unit, axis=0), jnp.sum(grad, axis=0))


def block_width(count):
    return math.gcd(count, 512)


def places(pairing, start, count, half):
    rows = start + jnp.arange(count, dtype=jnp.int32)
    owners = rows // half
    spots = jnp.arange(pairing.shape[0], dtype=jnp.int32)
    picked = jnp.sum(jnp.where(owners[:, None] == spots[None, :], pairing[None, :], 0), axis=1)
    return picked * half + rows % half


def allowed_pairs(query_place, key_place, length):
    before = (key_place[None, :] <= query_place[:, None]) | (key_place[None, :] < NMEM)
    return (key_place[None, :] < length) & before


def heads_of(value):
    return value.reshape(value.shape[0], HEADS, HEAD_DIM)


def forward_fold(query_heads, query_place, pairing, length, half):

    def fold(carry, piece, start):
        keys, values = piece
        count = keys.shape[0]
        width = block_width(count)
        key_place = places(pairing, start, count, half)

        def step(index, state):
            top, total, summed = state
            offset = index * width
            key_heads = heads_of(lax.dynamic_slice_in_dim(keys, offset, width, 0))
            value_heads = heads_of(lax.dynamic_slice_in_dim(values, offset, width, 0))
            mask = allowed_pairs(
                query_place, lax.dynamic_slice_in_dim(key_place, offset, width, 0), length
            )[None]
            scores = (
                jnp.einsum(
                    "qhd,khd->hqk", query_heads, key_heads, preferred_element_type=jnp.float32
                )
                * 0.125
            )
            scores = jnp.where(mask, scores, neg_big)
            new_top = jnp.maximum(top, jnp.max(scores, axis=2))
            shrink = jnp.exp(top - new_top)
            probs = jnp.where(mask, jnp.exp(scores - new_top[:, :, None]), 0.0)
            total = total * shrink + jnp.sum(probs, axis=2)
            update = jnp.einsum(
                "hqk,khd->qhd",
                probs.astype(jnp.bfloat16),
                value_heads,
                preferred_element_type=jnp.float32,
            )
            summed = summed * jnp.transpose(shrink)[:, :, None] + update
            return (new_top, total, summed)

        return lax.fori_loop(0, count // width, step, carry)

    return fold


def query_grad_fold(query_heads, grad_heads, top_sum, delta, query_place, pairing, length, half):

    def fold(carry, piece, start):
        keys, values = piece
        count = keys.shape[0]
        width = block_width(count)
        key_place = places(pairing, start, count, half)

        def step(index, summed):
            offset = index * width
            key_heads = heads_of(lax.dynamic_slice_in_dim(keys, offset, width, 0))
            value_heads = heads_of(lax.dynamic_slice_in_dim(values, offset, width, 0))
            mask = allowed_pairs(
                query_place, lax.dynamic_slice_in_dim(key_place, offset, width, 0), length
            )[None]
            scores = (
                jnp.einsum(
                    "qhd,khd->hqk", query_heads, key_heads, preferred_element_type=jnp.float32
                )
                * 0.125
            )
            probs = jnp.where(mask, jnp.exp(scores - top_sum[:, :, None]), 0.0)
            prob_grad = jnp.einsum(
                "qhd,khd->hqk", grad_heads, value_heads, preferred_element_type=jnp.float32
            )
            score_grad = (probs * (prob_grad - delta[:, :, None])).astype(jnp.bfloat16)
            return (
                summed
                + jnp.einsum(
                    "hqk,khd->qhd", score_grad, key_heads, preferred_element_type=jnp.float32
                )
                * 0.125
            )

        return lax.fori_loop(0, count // width, step, carry)

    return fold


def key_terms(
    key_heads, value_heads, key_place, query_heads, grad_heads, top_sum, delta, query_place, length
):
    scores = (
        jnp.einsum("qhd,khd->hqk", query_heads, key_heads, preferred_element_type=jnp.float32)
        * 0.125
    )
    mask = allowed_pairs(query_place, key_place, length)[None]
    probs = jnp.where(mask, jnp.exp(scores - top_sum[:, :, None]), 0.0)
    prob_grad = jnp.einsum(
        "qhd,khd->hqk", grad_heads, value_heads, preferred_element_type=jnp.float32
    )
    score_grad = (probs * (prob_grad - delta[:, :, None])).astype(jnp.bfloat16)
    value_grad = jnp.einsum(
        "hqk,qhd->khd", probs.astype(jnp.bfloat16), grad_heads, preferred_element_type=jnp.float32
    )
    key_grad = (
        jnp.einsum("hqk,qhd->khd", score_grad, query_heads, preferred_element_type=jnp.float32)
        * 0.125
    )
    return (key_grad, value_grad)


def on_device_any(
    tokens,
    cotangent,
    lengths,
    pairing,
    w_qkv,
    bias_q,
    bias_v,
    w_out,
    bias_out,
    ln1_gain,
    ln1_bias,
    w_in,
    bias_in,
    w_back,
    bias_back,
    ln2_gain,
    ln2_bias,
):
    gathered = (
        lax.all_gather(w_qkv, "fsdp", axis=0, tiled=True),
        lax.all_gather(bias_q, "fsdp", axis=0, tiled=True),
        lax.all_gather(bias_v, "fsdp", axis=0, tiled=True),
        lax.all_gather(w_out, "fsdp", axis=0, tiled=True),
        lax.all_gather(bias_out, "fsdp", axis=0, tiled=True),
        lax.all_gather(ln1_gain, "fsdp", axis=0, tiled=True),
        lax.all_gather(ln1_bias, "fsdp", axis=0, tiled=True),
        lax.all_gather(w_in, "fsdp", axis=0, tiled=True),
        lax.all_gather(bias_in, "fsdp", axis=0, tiled=True),
        lax.all_gather(w_back, "fsdp", axis=0, tiled=True),
        lax.all_gather(bias_back, "fsdp", axis=0, tiled=True),
        lax.all_gather(ln2_gain, "fsdp", axis=0, tiled=True),
        lax.all_gather(ln2_bias, "fsdp", axis=0, tiled=True),
    )
    (
        qkv_all,
        query_bias,
        value_bias,
        out_all,
        out_bias,
        gain_one,
        shift_one,
        in_all,
        in_bias,
        back_all,
        back_bias,
        gain_two,
        shift_two,
    ) = gathered
    rows = tokens.shape[1]
    half = rows // 2
    width = tokens.shape[2]
    length = lengths[0]
    query_place = places(pairing, lax.axis_index("ctx") * rows, rows, half)
    valid = query_place < length
    inputs = tokens[0]
    proj = jnp.dot(inputs, qkv_all, preferred_element_type=jnp.float32)
    queries = (proj[:, :width] + query_bias.astype(jnp.float32)).astype(jnp.bfloat16)
    keys = proj[:, width : 2 * width].astype(jnp.bfloat16)
    values = (proj[:, 2 * width :] + value_bias.astype(jnp.float32)).astype(jnp.bfloat16)
    query_heads = heads_of(queries)
    start_state = (
        jnp.full((HEADS, rows), neg_big, jnp.float32),
        jnp.zeros((HEADS, rows), jnp.float32),
        jnp.zeros((rows, HEADS, HEAD_DIM), jnp.float32),
    )
    fold = forward_fold(query_heads, query_place, pairing, length, half)
    top, total, summed = fold(
        start_state,
        (
            lax.all_gather(keys, "ctx", axis=0, tiled=True),
            lax.all_gather(values, "ctx", axis=0, tiled=True),
        ),
        jnp.int32(0),
    )
    top_sum = top + jnp.log(total)
    attended = (summed / jnp.transpose(total)[:, :, None]).reshape(rows, width)
    attended_low = attended.astype(jnp.bfloat16)
    resid_one = (
        inputs.astype(jnp.float32)
        + jnp.dot(attended_low, out_all, preferred_element_type=jnp.float32)
        + out_bias.astype(jnp.float32)
    )
    hidden = layer_norm(resid_one, gain_one.astype(jnp.float32), shift_one.astype(jnp.float32))
    hidden_low = hidden.astype(jnp.bfloat16)
    upper = jnp.dot(hidden_low, in_all, preferred_element_type=jnp.float32) + in_bias.astype(
        jnp.float32
    )
    active, gelu_back = jax.vjp(lambda value: jax.nn.gelu(value, approximate=False), upper)
    active_low = active.astype(jnp.bfloat16)
    resid_two = (
        hidden
        + jnp.dot(active_low, back_all, preferred_element_type=jnp.float32)
        + back_bias.astype(jnp.float32)
    )
    normed = layer_norm(resid_two, gain_two.astype(jnp.float32), shift_two.astype(jnp.float32))
    output = jnp.where(valid[:, None], normed, 0.0)
    qkv_back, out_back, gain_one_back, in_back, back_back, gain_two_back = (
        qkv_all,
        out_all,
        gain_one,
        in_all,
        back_all,
        gain_two,
    )
    grad_y = jnp.where(valid[:, None], cotangent[0].astype(jnp.float32), 0.0)
    grad_resid_two, gain_two_grad, shift_two_grad = norm_back(
        resid_two, gain_two_back.astype(jnp.float32), grad_y
    )
    grad_mixed = grad_resid_two.astype(jnp.bfloat16)
    back_grad = jnp.einsum("tf,td->fd", active_low, grad_mixed, preferred_element_type=jnp.float32)
    back_bias_grad = jnp.sum(grad_mixed.astype(jnp.float32), axis=0)
    grad_active = jnp.einsum("td,fd->tf", grad_mixed, back_back, preferred_element_type=jnp.float32)
    (grad_upper,) = gelu_back(grad_active)
    grad_upper_low = grad_upper.astype(jnp.bfloat16)
    in_grad = jnp.einsum(
        "td,tf->df", hidden_low, grad_upper_low, preferred_element_type=jnp.float32
    )
    in_bias_grad = jnp.sum(grad_upper_low.astype(jnp.float32), axis=0)
    grad_hidden = grad_resid_two + jnp.einsum(
        "tf,df->td", grad_upper_low, in_back, preferred_element_type=jnp.float32
    )
    grad_resid_one, gain_one_grad, shift_one_grad = norm_back(
        resid_one, gain_one_back.astype(jnp.float32), grad_hidden
    )
    grad_branch = grad_resid_one.astype(jnp.bfloat16)
    out_grad = jnp.einsum(
        "tc,td->cd", attended_low, grad_branch, preferred_element_type=jnp.float32
    )
    out_bias_grad = jnp.sum(grad_branch.astype(jnp.float32), axis=0)
    grad_attended = jnp.einsum(
        "td,cd->tc", grad_branch, out_back, preferred_element_type=jnp.float32
    ).astype(jnp.bfloat16)
    grad_heads = heads_of(grad_attended)
    delta = jnp.transpose(jnp.sum(grad_heads.astype(jnp.float32) * heads_of(attended), axis=2))
    query_fold = query_grad_fold(
        query_heads, grad_heads, top_sum, delta, query_place, pairing, length, half
    )
    empty_heads = jnp.zeros((rows, HEADS, HEAD_DIM), jnp.float32)
    query_grad = query_fold(
        empty_heads,
        (
            lax.all_gather(keys, "ctx", axis=0, tiled=True),
            lax.all_gather(values, "ctx", axis=0, tiled=True),
        ),
        jnp.int32(0),
    )
    stats = jnp.concatenate([jnp.transpose(top_sum), jnp.transpose(delta)], axis=1)
    stats_all = lax.all_gather(stats, "ctx", axis=0, tiled=True)
    key_heads = heads_of(keys)
    value_heads = heads_of(values)
    query_in = lax.all_gather(queries, "ctx", axis=0, tiled=True)
    grad_in = lax.all_gather(grad_attended, "ctx", axis=0, tiled=True)
    count = query_in.shape[0]
    span = block_width(count)
    place_in = places(pairing, jnp.int32(0), count, half)

    def step(index, state):
        offset = index * span
        query_block = heads_of(lax.dynamic_slice_in_dim(query_in, offset, span, 0))
        grad_block = heads_of(lax.dynamic_slice_in_dim(grad_in, offset, span, 0))
        stats_block = lax.dynamic_slice_in_dim(stats_all, offset, span, 0)
        place_block = lax.dynamic_slice_in_dim(place_in, offset, span, 0)
        key_part, value_part = key_terms(
            key_heads,
            value_heads,
            query_place,
            query_block,
            grad_block,
            jnp.transpose(stats_block[:, :HEADS]),
            jnp.transpose(stats_block[:, HEADS:]),
            place_block,
            length,
        )
        return (state[0] + key_part, state[1] + value_part)

    key_sum, value_sum = lax.fori_loop(0, count // span, step, (empty_heads, empty_heads))
    key_grad = key_sum.reshape(rows, width)
    value_grad = value_sum.reshape(rows, width)
    grad_proj = jnp.concatenate(
        [
            query_grad.reshape(rows, width).astype(jnp.bfloat16),
            key_grad.astype(jnp.bfloat16),
            value_grad.astype(jnp.bfloat16),
        ],
        axis=1,
    )
    qkv_grad = jnp.einsum("td,tf->df", inputs, grad_proj, preferred_element_type=jnp.float32)
    query_bias_grad = jnp.sum(grad_proj[:, :width].astype(jnp.float32), axis=0)
    value_bias_grad = jnp.sum(grad_proj[:, 2 * width :].astype(jnp.float32), axis=0)
    token_grad = grad_resid_one + jnp.einsum(
        "tf,df->td", grad_proj, qkv_back, preferred_element_type=jnp.float32
    )
    grads = (
        qkv_grad,
        query_bias_grad,
        value_bias_grad,
        out_grad,
        out_bias_grad,
        gain_one_grad,
        shift_one_grad,
        in_grad,
        in_bias_grad,
        back_grad,
        back_bias_grad,
        gain_two_grad,
        shift_two_grad,
    )
    shards = (
        lax.psum_scatter(
            grads[0].astype(jnp.bfloat16), "fsdp", scatter_dimension=0, tiled=True
        ).astype(jnp.float32),
        lax.psum_scatter(
            grads[1].astype(jnp.bfloat16), "fsdp", scatter_dimension=0, tiled=True
        ).astype(jnp.float32),
        lax.psum_scatter(
            grads[2].astype(jnp.bfloat16), "fsdp", scatter_dimension=0, tiled=True
        ).astype(jnp.float32),
        lax.psum_scatter(
            grads[3].astype(jnp.bfloat16), "fsdp", scatter_dimension=0, tiled=True
        ).astype(jnp.float32),
        lax.psum_scatter(
            grads[4].astype(jnp.bfloat16), "fsdp", scatter_dimension=0, tiled=True
        ).astype(jnp.float32),
        lax.psum_scatter(
            grads[5].astype(jnp.bfloat16), "fsdp", scatter_dimension=0, tiled=True
        ).astype(jnp.float32),
        lax.psum_scatter(
            grads[6].astype(jnp.bfloat16), "fsdp", scatter_dimension=0, tiled=True
        ).astype(jnp.float32),
        lax.psum_scatter(
            grads[7].astype(jnp.bfloat16), "fsdp", scatter_dimension=0, tiled=True
        ).astype(jnp.float32),
        lax.psum_scatter(
            grads[8].astype(jnp.bfloat16), "fsdp", scatter_dimension=0, tiled=True
        ).astype(jnp.float32),
        lax.psum_scatter(
            grads[9].astype(jnp.bfloat16), "fsdp", scatter_dimension=0, tiled=True
        ).astype(jnp.float32),
        lax.psum_scatter(
            grads[10].astype(jnp.bfloat16), "fsdp", scatter_dimension=0, tiled=True
        ).astype(jnp.float32),
        lax.psum_scatter(
            grads[11].astype(jnp.bfloat16), "fsdp", scatter_dimension=0, tiled=True
        ).astype(jnp.float32),
        lax.psum_scatter(
            grads[12].astype(jnp.bfloat16), "fsdp", scatter_dimension=0, tiled=True
        ).astype(jnp.float32),
    )
    totals = (
        lax.psum(shards[0].astype(jnp.bfloat16), "ctx").astype(jnp.float32),
        lax.psum(shards[1].astype(jnp.bfloat16), "ctx").astype(jnp.float32),
        lax.psum(shards[2].astype(jnp.bfloat16), "ctx").astype(jnp.float32),
        lax.psum(shards[3].astype(jnp.bfloat16), "ctx").astype(jnp.float32),
        lax.psum(shards[4].astype(jnp.bfloat16), "ctx").astype(jnp.float32),
        lax.psum(shards[5].astype(jnp.bfloat16), "ctx").astype(jnp.float32),
        lax.psum(shards[6].astype(jnp.bfloat16), "ctx").astype(jnp.float32),
        lax.psum(shards[7].astype(jnp.bfloat16), "ctx").astype(jnp.float32),
        lax.psum(shards[8].astype(jnp.bfloat16), "ctx").astype(jnp.float32),
        lax.psum(shards[9].astype(jnp.bfloat16), "ctx").astype(jnp.float32),
        lax.psum(shards[10].astype(jnp.bfloat16), "ctx").astype(jnp.float32),
        lax.psum(shards[11].astype(jnp.bfloat16), "ctx").astype(jnp.float32),
        lax.psum(shards[12].astype(jnp.bfloat16), "ctx").astype(jnp.float32),
    )
    return (output[None], token_grad[None]) + tuple(totals)


def low_lanes(shape):
    return lax.broadcasted_iota(jnp.int32, shape, 1) < 64


def attend_kernel(chunks, pair_ref, len_ref, spot_ref, in_ref, out_ref, keep_ref, mix_ref, lse_ref):
    length = len_ref[0]
    spot = spot_ref[0]
    blocks = 2 * chunks
    for s in range(blocks):
        keep_ref[pair_ref[s]] = in_ref[s]
    left = low_lanes((256, BLK))
    left_half = left[:BLK]
    for c in range(chunks):
        keys = 256 * (c + 1)
        own = keep_ref[2 * c : 2 * c + 2, :, :BLK].reshape(256, BLK)
        shared = keep_ref[2 * c + spot, :, :BLK]
        zero = jnp.zeros((), jnp.bfloat16)
        query = jnp.concatenate(
            [jnp.where(left, own, zero), jnp.where(left_half, zero, shared)], axis=0
        ) * jnp.bfloat16(0.125)
        key = keep_ref[: 2 * c + 2, :, BLK : 2 * BLK].reshape(keys, BLK)
        value = keep_ref[: 2 * c + 2, :, 2 * BLK :].reshape(keys, BLK)
        scores = mask_scores(
            lax.dot_general(key, query, (((1,), (1,)), ((), ())), preferred_element_type=jnp.float32),
            c, spot, length,
        )
        top = jnp.max(scores, axis=0, keepdims=True)
        probs = jnp.exp(scores - top)
        total = jnp.sum(probs, axis=0, keepdims=True)
        summed = lax.dot_general(
            value, probs.astype(jnp.bfloat16), (((0,), (0,)), ((), ())),
            preferred_element_type=jnp.float32,
        ) / total
        lse_ref[c] = top + jnp.log(total)
        part = summed[64:, 256:]
        none = jnp.zeros_like(part)
        first = jnp.where(spot == 0, part, none)
        second = jnp.where(spot == 0, none, part)
        mixed = jnp.concatenate(
            [summed[:64, :256], jnp.concatenate([first, second], axis=1)], axis=0
        )
        mix_ref[c] = mixed
    for s in range(blocks):
        place = pair_ref[s]
        c = place // 2
        piece = mix_ref[c, :, pl.ds(pl.multiple_of((place % 2) * BLK, BLK), BLK)]
        out_ref[s] = jnp.transpose(piece).astype(jnp.bfloat16)


def mask_scores(scores, c, spot, length):
    keys, width = scores.shape
    edge = 256 * c
    row = lax.broadcasted_iota(jnp.int32, (keys, width), 0)
    scores = jnp.where(row < length, scores, neg_big)
    lane = lax.broadcasted_iota(jnp.int32, (256, width), 1)
    query_place = edge + jnp.where(lane < 256, lane, lane - 256 + spot * BLK)
    key_place = edge + lax.broadcasted_iota(jnp.int32, (256, width), 0)
    seen = key_place <= query_place
    if c == 0:
        seen = seen | (key_place < NMEM)
    tail = jnp.where(seen, scores[edge:], neg_big)
    if c == 0:
        return tail
    return jnp.concatenate([scores[:edge], tail], axis=0)


def attend_back_kernel(
    chunks, pair_ref, len_ref, spot_ref, keep_ref, grad_ref, mix_ref, lse_ref, out_ref, g_ref,
    q_sum, k_sum, v_sum
):
    length = len_ref[0]
    spot = spot_ref[0]
    blocks = 2 * chunks
    for s in range(blocks):
        g_ref[pair_ref[s]] = grad_ref[s]
    k_sum[...] = jnp.zeros_like(k_sum)
    v_sum[...] = jnp.zeros_like(v_sum)
    left = low_lanes((256, BLK))
    left_half = left[:BLK]
    zero = jnp.zeros((), jnp.bfloat16)
    for c in range(chunks):
        keys = 256 * (c + 1)
        own = keep_ref[2 * c : 2 * c + 2, :, :BLK].reshape(256, BLK)
        shared = keep_ref[2 * c + spot, :, :BLK]
        query = jnp.concatenate(
            [jnp.where(left, own, zero), jnp.where(left_half, zero, shared)], axis=0
        ) * jnp.bfloat16(0.125)
        g_own = g_ref[2 * c : 2 * c + 2].reshape(256, BLK)
        g_shared = g_ref[2 * c + spot]
        grad = jnp.concatenate(
            [jnp.where(left, g_own, zero), jnp.where(left_half, zero, g_shared)], axis=0
        )
        key = keep_ref[: 2 * c + 2, :, BLK : 2 * BLK].reshape(keys, BLK)
        value = keep_ref[: 2 * c + 2, :, 2 * BLK :].reshape(keys, BLK)
        turned = jnp.transpose(g_own.astype(jnp.float32)) * mix_ref[c]
        delta_own = jnp.sum(turned[:64], axis=0, keepdims=True)
        delta_pair = jnp.sum(turned[64:], axis=0, keepdims=True)
        delta = jnp.concatenate(
            [delta_own, jnp.where(spot == 0, delta_pair[:, :BLK], delta_pair[:, BLK:])], axis=1
        )
        nt = (((1,), (1,)), ((), ()))
        scores = mask_scores(
            lax.dot_general(key, query, nt, preferred_element_type=jnp.float32), c, spot, length
        )
        probs = jnp.exp(scores - lse_ref[c])
        prob_grad = lax.dot_general(value, grad, nt, preferred_element_type=jnp.float32)
        score_grad = (probs * (prob_grad - delta)).astype(jnp.bfloat16)
        nn = (((1,), (0,)), ((), ()))
        v_sum[:keys] += lax.dot_general(
            probs.astype(jnp.bfloat16), grad, nn, preferred_element_type=jnp.float32
        )
        k_sum[:keys] += lax.dot_general(score_grad, query, nn, preferred_element_type=jnp.float32)
        q_grad = lax.dot_general(
            score_grad, key, (((0,), (0,)), ((), ())), preferred_element_type=jnp.float32
        ) * 0.125
        part = q_grad[256:]
        none = jnp.zeros_like(part)
        first = jnp.where(spot == 0, part, none)
        second = jnp.where(spot == 0, none, part)
        q_sum[256 * c : 256 * c + 256] = jnp.where(
            left, q_grad[:256], jnp.concatenate([first, second], axis=0)
        )
    for s in range(blocks):
        rows = pl.ds(pl.multiple_of(pair_ref[s] * BLK, BLK), BLK)
        out_ref[s] = jnp.concatenate([q_sum[rows], k_sum[rows], v_sum[rows]], axis=1).astype(jnp.bfloat16)


def smem():
    return pl.BlockSpec(memory_space=pltpu.SMEM)


def vmem():
    return pl.BlockSpec(memory_space=pltpu.VMEM)


def attend(pairing, lengths, spot, packed):
    blocks = packed.shape[0]
    chunks = blocks // 2
    return pl.pallas_call(
        functools.partial(attend_kernel, chunks),
        out_shape=(
            jax.ShapeDtypeStruct((blocks, BLK, BLK), jnp.bfloat16),
            jax.ShapeDtypeStruct((blocks, BLK, 3 * BLK), jnp.bfloat16),
            jax.ShapeDtypeStruct((chunks, BLK, 256), jnp.float32),
            jax.ShapeDtypeStruct((chunks, 1, 384), jnp.float32),
        ),
        in_specs=[smem(), smem(), smem(), vmem()],
        out_specs=(vmem(), vmem(), vmem(), vmem()),
        compiler_params=pltpu.CompilerParams(vmem_limit_bytes=48 << 20),
        name="attend",
    )(pairing, lengths, spot, packed)


def attend_back(pairing, lengths, spot, keep, grad, mix, lse):
    blocks = keep.shape[0]
    chunks = blocks // 2
    return pl.pallas_call(
        functools.partial(attend_back_kernel, chunks),
        out_shape=jax.ShapeDtypeStruct((blocks, BLK, 3 * BLK), jnp.bfloat16),
        in_specs=[smem(), smem(), smem(), vmem(), vmem(), vmem(), vmem()],
        out_specs=vmem(),
        scratch_shapes=[
            pltpu.VMEM((blocks, BLK, BLK), jnp.bfloat16),
            pltpu.VMEM((blocks * BLK, BLK), jnp.float32),
            pltpu.VMEM((blocks * BLK, BLK), jnp.float32),
            pltpu.VMEM((blocks * BLK, BLK), jnp.float32),
        ],
        compiler_params=pltpu.CompilerParams(vmem_limit_bytes=48 << 20),
        name="attend_back",
    )(pairing, lengths, spot, keep, grad, mix, lse)


MESH = pl.DeviceIdType.MESH


def remote(src, dst, sems, at, peer):
    return pltpu.make_async_remote_copy(
        src_ref=src, dst_ref=dst, send_sem=sems.at[(0,) + at], recv_sem=sems.at[(1,) + at],
        device_id=peer, device_id_type=MESH,
    )


def greet(peers):
    barrier = pltpu.get_barrier_semaphore()
    for peer in peers:
        pl.semaphore_signal(barrier, inc=1, device_id=peer, device_id_type=MESH)
    pl.semaphore_wait(barrier, len(peers))


def ring_peers(n):
    me = lax.axis_index("ctx")
    return [{"ctx": lax.rem(me + k, n)} for k in range(1, n)]


def exchange_copies(n, in_ref, out_ref, sems):
    me = lax.axis_index("ctx")
    return [
        remote(in_ref.at[lax.rem(me + k, n)], out_ref.at[me], sems, (k,), {"ctx": lax.rem(me + k, n)})
        for k in range(1, n)
    ]


def join_pairs(pairs):
    pieces = []
    for group in range(HEADS // 3):
        first, second = pairs(2 * group), pairs(2 * group + 1)
        shared = first[:, HEAD_DIM:].astype(jnp.float32) + second[:, HEAD_DIM:].astype(jnp.float32)
        pieces += [first[:, :HEAD_DIM], second[:, :HEAD_DIM], shared.astype(jnp.bfloat16)]
    return jnp.concatenate(pieces, axis=1)


def pair_of(value, peer):
    own = 3 * (peer // 2) + peer % 2
    shared = 3 * (peer // 2) + 2
    cut = lambda head: value[:, head * HEAD_DIM : (head + 1) * HEAD_DIM]
    return jnp.concatenate([cut(own), cut(shared)], axis=1)


def dot_nn(a, b):
    return jnp.dot(a, b, preferred_element_type=jnp.float32)


def dot_nt(a, b):
    return lax.dot_general(a, b, (((1,), (1,)), ((), ())), preferred_element_type=jnp.float32)


def column_sum(value):
    return jnp.sum(value, axis=0, keepdims=True)


def unit_of(value):
    mean = jnp.mean(value, axis=-1, keepdims=True)
    centred = value - mean
    scale = lax.rsqrt(jnp.mean(centred * centred, axis=-1, keepdims=True) + eps)
    return centred * scale, scale


def unit_back(unit, scale, scaled):
    return scale * (
        scaled
        - jnp.mean(scaled, axis=-1, keepdims=True)
        - unit * jnp.mean(scaled * unit, axis=-1, keepdims=True)
    )


(ROW_BQ, ROW_BV, ROW_BO, ROW_G1, ROW_S1, ROW_BB, ROW_G2, ROW_S2, ROW_BI) = range(9)


def layer_kernel(
    n, pair_ref, len_ref, mixed_ref, tokens_ref, cot_ref, rows_ref, out_full, in_full, back_ref,
    output_ref, grad_in_ref, left_ref, right_ref, resid_ref, sums_ref,
    mixed_in, grad_out, active, slope, w_out, w_in, w_back, in_sem, out_sem, back_sem, own_sem,
):
    low, wide = jnp.bfloat16, jnp.float32
    ctx = lax.axis_index("ctx")
    sums_ref[...] = jnp.zeros_like(sums_ref)
    fsdp = lax.axis_index("fsdp")
    x, core = fsdp // 2, lax.rem(fsdp, 2)
    greet(ring_peers(n) + chip_peers())
    copies = exchange_copies(n, mixed_ref, mixed_in, in_sem)
    for cp in copies:
        cp.start()
    back_shards = gather_copies(back_ref, w_back, back_sem, 0)
    for step in (0, 1):
        back_shards[step].start()
    width = tokens_ref.shape[1]
    count = w_in.shape[0]
    loads = [
        pltpu.make_async_copy(out_full, w_out, own_sem.at[2]),
        pltpu.make_async_copy(back_ref, w_back.at[fsdp], own_sem.at[3]),
    ] + [
        pltpu.make_async_copy(
            in_full.at[:, :, t * width : (t + 1) * width], w_in.at[t], own_sem.at[4 + t]
        )
        for t in range(count)
    ]
    for cp in loads:
        cp.start()
    own = pltpu.make_async_copy(mixed_ref.at[ctx], mixed_in.at[ctx], own_sem.at[0])
    own.start()
    row = lambda i: rows_ref[i : i + 1, :]
    tokens = tokens_ref[...]
    left_ref[0] = jnp.transpose(tokens).reshape(4, -1, 2 * BLK)
    spots = lax.broadcasted_iota(jnp.int32, (2 * BLK, 1), 0)
    place = jnp.where(
        spots < BLK,
        pair_ref[2 * ctx] * BLK + spots,
        pair_ref[2 * ctx + 1] * BLK + spots - BLK,
    )
    valid = place < len_ref[0]
    own.wait()
    for cp in copies:
        cp.wait_recv()

    attended = join_pairs(lambda peer: mixed_in[peer])
    loads[0].wait()
    resid_one = (
        tokens.astype(wide)
        + dot_nn(attended, w_out[...].reshape(width, width))
        + row(ROW_BO)
    )
    unit_one, scale_one = unit_of(resid_one)
    hidden = unit_one * row(ROW_G1) + row(ROW_S1)
    hidden_low = hidden.astype(low)
    resid_two = hidden + row(ROW_BB)
    for cp in loads[2:]:
        cp.wait()
    order = [fsdp, 2 * x + 1 - core, 2 * (1 - x) + core, 2 * (1 - x) + 1 - core]
    for step, t in enumerate(order):
        bias = rows_ref[pl.ds(ROW_BI + t, 1), :]
        upper = dot_nn(hidden_low, w_in[t].reshape(width, width)) + bias
        share = 0.5 * (1.0 + lax.erf(upper * (0.5**0.5)))
        slope[t] = share + upper * (jnp.exp(-0.5 * upper * upper) * (2 * math.pi) ** -0.5)
        some = (upper * share).astype(low)
        active[t] = some
        if step == 0:
            loads[1].wait()
        elif step == 1:
            back_shards[1].wait_recv()
        elif step == 2:
            back_shards[0].wait_recv()
            back_shards[2].start()
        else:
            back_shards[2].wait_recv()
        resid_two = resid_two + dot_nn(some, w_back[t])
    unit_two, scale_two = unit_of(resid_two)
    output_ref[...] = jnp.where(valid, unit_two * row(ROW_G2) + row(ROW_S2), 0.0)
    grad_y = jnp.where(valid, cot_ref[...].astype(wide), 0.0)
    sums_ref[ROW_G2 : ROW_G2 + 1, :] = column_sum(grad_y * unit_two)
    sums_ref[ROW_S2 : ROW_S2 + 1, :] = column_sum(grad_y)
    grad_resid_two = unit_back(unit_two, scale_two, grad_y * row(ROW_G2))
    grad_mixed = grad_resid_two.astype(low)
    right_ref[5] = grad_mixed
    sums_ref[ROW_BB : ROW_BB + 1, :] = column_sum(grad_mixed.astype(wide))
    grad_hidden = grad_resid_two
    for t in range(count):
        grad_upper = (dot_nt(grad_mixed, w_back[t]) * slope[t]).astype(low)
        right_ref[1 + t] = grad_upper
        sums_ref[ROW_BI + t : ROW_BI + t + 1, :] = column_sum(grad_upper.astype(wide))
        grad_hidden = grad_hidden + dot_nt(grad_upper, w_in[t].reshape(width, width))
    sums_ref[ROW_G1 : ROW_G1 + 1, :] = column_sum(grad_hidden * unit_one)
    sums_ref[ROW_S1 : ROW_S1 + 1, :] = column_sum(grad_hidden)
    grad_resid_one = unit_back(unit_one, scale_one, grad_hidden * row(ROW_G1))
    resid_ref[...] = grad_resid_one
    grad_branch = grad_resid_one.astype(low)
    right_ref[0] = grad_branch
    sums_ref[ROW_BO : ROW_BO + 1, :] = column_sum(grad_branch.astype(wide))
    grad_attended = dot_nt(grad_branch, w_out[...].reshape(width, width)).astype(low)
    for peer in range(n):
        grad_out[peer] = pair_of(grad_attended, peer)
    backs = exchange_copies(n, grad_out, grad_in_ref, out_sem)
    for cp in backs:
        cp.start()
    back = pltpu.make_async_copy(grad_out.at[ctx], grad_in_ref.at[ctx], own_sem.at[1])
    back.start()
    left_ref[1] = jnp.transpose(attended).reshape(4, -1, 2 * BLK)
    left_ref[2] = jnp.transpose(hidden_low).reshape(4, -1, 2 * BLK)
    for f in range(4):
        turned = jnp.transpose(active[f])
        for r in range(4):
            left_ref[3 + r, f] = turned[r * width // 4 : (r + 1) * width // 4]
    back.wait()
    for cp in copies:
        cp.wait_send()
    for cp in backs:
        cp.wait()
    for cp in back_shards:
        cp.wait_send()


def layer(pairing, lengths, mixed, tokens, cotangent, rows, out_full, in_full, w_back, name):
    n = mixed.shape[0]
    count, width = tokens.shape
    low, wide = jnp.bfloat16, jnp.float32
    dma = pltpu.SemaphoreType.DMA
    shape = jax.ShapeDtypeStruct
    anywhere = pl.BlockSpec(memory_space=pl.ANY)
    return pl.pallas_call(
        functools.partial(layer_kernel, n),
        out_shape=(
            shape((count, width), wide),
            shape(mixed.shape, low),
            shape((7, 4, width // 4, count), low),
            shape((6, count, width), low),
            shape((count, width), wide),
            shape((16, width), wide),
        ),
        in_specs=[smem(), smem()] + [vmem()] * 4 + [anywhere] * 3,
        out_specs=(vmem(),) * 6,
        scratch_shapes=[
            pltpu.VMEM(mixed.shape, low),
            pltpu.VMEM(mixed.shape, low),
            pltpu.VMEM((4, count, width), low),
            pltpu.VMEM((4, count, width), wide),
            pltpu.VMEM(out_full.shape, low),
            pltpu.VMEM((4, 4, width // 4, width), low),
            pltpu.VMEM((4,) + w_back.shape, low),
            dma((2, n)),
            dma((2, n)),
            dma((2, 1, 3)),
            dma((8,)),
        ],
        compiler_params=pltpu.CompilerParams(
            collective_id=name, has_side_effects=True, vmem_limit_bytes=56 << 20
        ),
        name="layer",
    )(pairing, lengths, mixed, tokens, cotangent, rows, out_full, in_full, w_back)


def gather_copies(src, full, sems, index):
    fsdp = lax.axis_index("fsdp")
    x, core = fsdp // 2, lax.rem(fsdp, 2)
    sibling, across = {"fsdp": 2 * x + 1 - core}, {"fsdp": 2 * (1 - x) + core}
    other = 2 * (1 - x) + core
    return (
        remote(src, full.at[fsdp], sems, (index, 0), across),
        remote(src, full.at[fsdp], sems, (index, 1), sibling),
        remote(full.at[other], full.at[other], sems, (index, 2), sibling),
    )


def chip_peers():
    fsdp = lax.axis_index("fsdp")
    x, core = fsdp // 2, lax.rem(fsdp, 2)
    return [{"fsdp": 2 * x + 1 - core}, {"fsdp": 2 * (1 - x) + core}]


def project_kernel(
    n, tokens_ref, small_ref, qkv_ref, out_ref, in_ref,
    packed_ref, rows_ref, qkv_full, out_full, in_full,
    qkv_here, small_here, send, sems, own_sem, block_sem,
):
    low, wide = jnp.bfloat16, jnp.float32
    ctx = lax.axis_index("ctx")
    fsdp = lax.axis_index("fsdp")
    greet(ring_peers(n) + chip_peers())
    qkv = gather_copies(qkv_ref, qkv_here, sems, 0)
    small = gather_copies(small_ref, small_here, sems, 1)
    for step in (0, 1):
        small[step].start()
        qkv[step].start()
    locals_ = [
        pltpu.make_async_copy(src, dst, own_sem.at[i])
        for i, (src, dst) in enumerate(
            [
                (qkv_ref, qkv_here.at[fsdp]),
                (small_ref, small_here.at[fsdp]),
                (out_ref, out_full.at[fsdp]),
                (in_ref, in_full.at[fsdp]),
            ]
        )
    ]
    for cp in locals_:
        cp.start()
    small[0].wait_recv()
    small[2].start()
    qkv[0].wait_recv()
    qkv[2].start()
    later = [gather_copies(out_ref, out_full, sems, 2), gather_copies(in_ref, in_full, sems, 3)]
    for step in (0, 1):
        for cps in later:
            cps[step].start()
    for cps in (small, qkv):
        cps[1].wait_recv()
        cps[2].wait_recv()
    locals_[0].wait()
    locals_[1].wait()
    keep = pltpu.make_async_copy(qkv_here, qkv_full, own_sem.at[4])
    keep.start()
    for f in range(4):
        width = small_here.shape[2]
        cols = slice(f * width, (f + 1) * width)
        rows_ref[:8, cols] = small_here[f, :8]
        for j in range(4):
            rows_ref[ROW_BI + f : ROW_BI + f + 1, j * width : (j + 1) * width] = small_here[
                f, 8 + j : 9 + j
            ]
    rows_ref[12:] = jnp.zeros_like(rows_ref[12:])
    tokens = tokens_ref[...]
    width = tokens.shape[1]
    half = width // 2
    for g in range(2):
        parts = []
        for part, bias in ((0, ROW_BQ), (1, None), (2, ROW_BV)):
            at = part * width + g * half
            value = dot_nn(tokens, qkv_here[:, :, at : at + half].reshape(width, half))
            if bias is not None:
                value = value + rows_ref[bias : bias + 1, g * half : (g + 1) * half]
            parts.append(value.astype(low))
        for spot in range(n // 2):
            send[g * n // 2 + spot] = jnp.concatenate(
                [pair_of(value, spot) for value in parts], axis=1
            )
    blocks = exchange_copies(n, send, packed_ref, block_sem)
    for cp in blocks:
        cp.start()
    own = pltpu.make_async_copy(send.at[ctx], packed_ref.at[ctx], own_sem.at[5])
    own.start()
    for cps in later:
        cps[0].wait_recv()
        cps[2].start()
    own.wait()
    keep.wait()
    locals_[2].wait()
    locals_[3].wait()
    for cp in blocks:
        cp.wait()
    for cps in later:
        cps[0].wait_send()
        cps[1].wait()
        cps[2].wait()
    for cps in (small, qkv):
        for cp in cps:
            cp.wait_send()


def project(tokens, small, w_qkv, w_out, w_in, n, name):
    low, wide = jnp.bfloat16, jnp.float32
    dma = pltpu.SemaphoreType.DMA
    shape = jax.ShapeDtypeStruct
    count, width = tokens.shape
    anywhere = pl.BlockSpec(memory_space=pl.ANY)
    return pl.pallas_call(
        functools.partial(project_kernel, n),
        out_shape=(
            shape((n, count, 6 * HEAD_DIM), low),
            shape((16, width), wide),
            shape((4,) + w_qkv.shape, low),
            shape((4,) + w_out.shape, low),
            shape((4,) + w_in.shape, low),
        ),
        in_specs=[vmem(), vmem()] + [anywhere] * 3,
        out_specs=(vmem(), vmem()) + (anywhere,) * 3,
        scratch_shapes=[
            pltpu.VMEM((4,) + w_qkv.shape, low),
            pltpu.VMEM((4,) + small.shape, wide),
            pltpu.VMEM((n, count, 6 * HEAD_DIM), low),
            dma((2, 4, 3)),
            dma((6,)),
            dma((2, n)),
        ],
        compiler_params=pltpu.CompilerParams(
            collective_id=name, has_side_effects=True, vmem_limit_bytes=40 << 20
        ),
        name="project",
    )(tokens, small, w_qkv, w_out, w_in)


PARTS = 12


def sum_sources(chunk):
    left = jnp.where(chunk < 4, 3 + chunk, jnp.where(chunk < 8, 2, jnp.where(chunk < 9, 1, 0)))
    right = jnp.where(
        chunk < 4, 8, jnp.where(chunk < 8, chunk, jnp.where(chunk < 9, 3, chunk - 9))
    )
    return left, right


def sum_kernel(
    n, left_ref, right_ref, sums_ref, blocks_ref, w_qkv_ref, resid_ref,
    token_ref, qkv_out, out_out, in_out, back_out, small_out,
    blocks_in, right_all, total_ref, pair_out, pair_in, x_out, x_in, first_sum, y_out, y_in, half_sum,
    z_out, z_in, s_pair, s_x_out, s_x, s_y_out, s_y, s_z_out, s_z,
    block_sem, own_sem, pair_sem, x_sem, y_sem, z_sem, spread_sem, last_sem, s_sem,
):
    low, wide = jnp.bfloat16, jnp.float32
    ctx = lax.axis_index("ctx")
    fsdp = lax.axis_index("fsdp")
    z, y = ctx // 2, lax.rem(ctx, 2)
    x, core = fsdp // 2, lax.rem(fsdp, 2)
    sibling = {"fsdp": 2 * x + 1 - core}
    across = {"fsdp": 2 * (1 - x) + core}
    beside = {"ctx": 2 * z + 1 - y}
    along = [{"ctx": 2 * lax.rem(z + k, 4) + y} for k in (1, 2, 3)]
    greet(ring_peers(n) + [sibling, across])
    blocks = exchange_copies(n, blocks_ref, blocks_in, block_sem)
    for cp in blocks:
        cp.start()
    own = pltpu.make_async_copy(blocks_ref.at[ctx], blocks_in.at[ctx], own_sem)
    own.start()
    right_all[3:] = right_ref[...]

    def pair_copy(c):
        return remote(pair_out.at[lax.rem(c, 2)], pair_in.at[c], pair_sem, (c,), sibling)

    def x_copy(c):
        return remote(x_out.at[c], x_in.at[c], x_sem, (c,), across)

    def y_copy(c):
        return remote(y_out.at[c], y_in.at[c], y_sem, (c,), beside)

    def z_copy(c, k):
        return remote(
            z_out.at[c, lax.rem(z + k, 4)], z_in.at[c, k - 1], z_sem, (c, k - 1), along[k - 1]
        )

    def spread_copy(c, k):
        piece = total_ref.at[c, y, z]
        return remote(piece, piece, spread_sem, (c, k - 1), along[k - 1])

    def last_copy(c):
        return remote(total_ref.at[c, y], total_ref.at[c, y], last_sem, (c,), beside)

    def partial(c, shard):
        left, right = sum_sources(c)
        return jnp.dot(left_ref[left, shard], right_all[right], preferred_element_type=jnp.float32)

    def stage_pair(c):
        @pl.when(c >= 2)
        def _():
            pair_copy(c - 2).wait_send()

        for side in range(2):
            pair_out[lax.rem(c, 2), side] = partial(c, 2 * side + 1 - core).astype(low)
        pair_copy(c).start()

    def stage_x(c):
        pair_copy(c).wait_recv()
        x_out[c] = (
            partial(c, 2 * (1 - x) + core) + pair_in[c, 1 - x].astype(jnp.float32)
        ).astype(low)
        x_copy(c).start()
        first_sum[lax.rem(c, 2)] = partial(c, 2 * x + core) + pair_in[c, x].astype(jnp.float32)

    def stage_y(c):
        x_copy(c).wait_recv()
        total = first_sum[lax.rem(c, 2)] + x_in[c].astype(jnp.float32)
        here, there = total[:, :384], total[:, 384:]
        y_out[c] = jnp.where(y == 0, there, here).astype(low)
        y_copy(c).start()
        half_sum[lax.rem(c, 2)] = jnp.where(y == 0, here, there)

    def stage_z(c):
        y_copy(c).wait_recv()
        total = half_sum[lax.rem(c, 2)] + y_in[c].astype(jnp.float32)
        z_out[c] = total.astype(low).reshape(4, 48, 384)
        for k in (1, 2, 3):
            z_copy(c, k).start()
        half_sum[lax.rem(c, 2)] = total

    def stage_spread(c):
        total = half_sum[lax.rem(c, 2), pl.ds(pl.multiple_of(48 * z, 48), 48)]
        for k in (1, 2, 3):
            z_copy(c, k).wait_recv()
            total = total + z_in[c, k - 1].astype(jnp.float32)
        total_ref[c, y, z] = total.astype(low)
        for k in (1, 2, 3):
            spread_copy(c, k).start()

    def stage_last(c):
        for k in (1, 2, 3):
            spread_copy(c, k).wait_recv()
        last_copy(c).start()

    stages = [stage_pair, stage_x, stage_y, stage_z, stage_spread, stage_last]
    order = [0, 1, 4, 2, 3, 5]

    def small_step(t):
        send_pair = remote(s_pair.at[0], s_pair.at[1], s_sem, (0,), sibling)
        send_x = remote(s_x_out, s_x, s_sem, (1,), across)
        send_y = remote(s_y_out, s_y, s_sem, (2,), beside)
        send_z = [remote(s_z_out, s_z.at[k], s_sem, (3 + k,), along[k]) for k in range(3)]

        @pl.when(t == 0)
        def _():
            own.wait()
            for cp in blocks:
                cp.wait_recv()
            for part in range(3):
                right_all[part] = join_pairs(
                    lambda peer: blocks_in[peer, :, part * 2 * HEAD_DIM : (part + 1) * 2 * HEAD_DIM]
                )
            s_pair[0] = sums_ref[...]
            s_pair[0, ROW_BQ : ROW_BQ + 1] = column_sum(right_all[0].astype(wide))
            s_pair[0, ROW_BV : ROW_BV + 1] = column_sum(right_all[2].astype(wide))
            send_pair.start()

        @pl.when(t == 1)
        def _():
            send_pair.wait()
            s_x_out[...] = s_pair[0] + s_pair[1]
            send_x.start()
            width = resid_ref.shape[1]
            token_ref[...] = resid_ref[...] + sum(
                dot_nt(right_all[part], w_qkv_ref[:, part * width : (part + 1) * width])
                for part in range(3)
            )

        @pl.when(t == 2)
        def _():
            send_x.wait()
            s_y_out[...] = s_x_out[...] + s_x[...]
            send_y.start()

        @pl.when(t == 3)
        def _():
            send_y.wait()
            s_z_out[...] = s_y_out[...] + s_y[...]
            for cp in send_z:
                cp.start()

        @pl.when(t == 4)
        def _():
            for cp in send_z:
                cp.wait()
            total = jnp.zeros(s_z_out.shape, wide)
            for spot in range(4):
                k = lax.rem(spot - z + 4, 4)
                other = s_z[jnp.where(k == 0, 0, 3 - k)]
                total = total + jnp.where(k == 0, s_z_out[...], other)
            quarter = total.shape[1] // 4
            cuts = [slice(f * quarter, (f + 1) * quarter) for f in range(4)]
            pick = lambda choices: sum(
                jnp.where(fsdp == f, choice, 0.0) for f, choice in enumerate(choices)
            )
            small_out[:8] = pick([total[:8, cut] for cut in cuts])
            line = pick([total[ROW_BI + f : ROW_BI + f + 1] for f in range(4)])
            for j, cut in enumerate(cuts):
                small_out[8 + j : 9 + j] = line[:, cut]

    def slot(t, carry):
        small_step(t - 9)
        for index in order:
            c = t - index

            @pl.when((c >= 0) & (c < PARTS))
            def _():
                stages[index](c)

        return carry

    lax.fori_loop(0, PARTS + 5, slot, 0)

    def drain(c, carry):
        x_copy(c).wait_send()
        y_copy(c).wait_send()
        for k in (1, 2, 3):
            z_copy(c, k).wait_send()
            spread_copy(c, k).wait_send()
        last_copy(c).wait()
        return carry

    lax.fori_loop(0, PARTS, drain, 0)
    for c in (PARTS - 2, PARTS - 1):
        pair_copy(c).wait_send()
    for cp in blocks:
        cp.wait_send()

    def panel(c, target, rows_at, cols_at):
        for half in range(2):
            for spot in range(4):
                target[
                    rows_at + 48 * spot : rows_at + 48 * spot + 48,
                    cols_at + 384 * half : cols_at + 384 * half + 384,
                ] = total_ref[c, half, spot]

    for k in range(4):
        panel(k, back_out, 192 * k, 0)
        panel(4 + k, in_out, 0, 768 * k)
    panel(8, out_out, 0, 0)
    for k in range(3):
        panel(9 + k, qkv_out, 0, 768 * k)


def sum_all(left, right, sums, blocks, w_qkv, resid, name):
    n = blocks.shape[0]
    low, wide = jnp.bfloat16, jnp.float32
    dma = pltpu.SemaphoreType.DMA
    shape = jax.ShapeDtypeStruct
    small = pltpu.VMEM(sums.shape, wide)
    return pl.pallas_call(
        functools.partial(sum_kernel, n),
        out_shape=(
            shape(resid.shape, wide),
            shape((192, 2304), low),
            shape((192, 768), low),
            shape((192, 3072), low),
            shape((768, 768), low),
            shape((16, 192), wide),
        ),
        in_specs=[vmem()] * 6,
        out_specs=(vmem(),) * 6,
        scratch_shapes=[
            pltpu.VMEM(blocks.shape, low),
            pltpu.VMEM((9,) + right.shape[1:], low),
            pltpu.VMEM((PARTS, 2, 4, 48, 384), low),
            pltpu.VMEM((2, 2, 192, 768), low),
            pltpu.VMEM((PARTS, 2, 192, 768), low),
            pltpu.VMEM((PARTS, 192, 768), low),
            pltpu.VMEM((PARTS, 192, 768), low),
            pltpu.VMEM((2, 192, 768), wide),
            pltpu.VMEM((PARTS, 192, 384), low),
            pltpu.VMEM((PARTS, 192, 384), low),
            pltpu.VMEM((2, 192, 384), wide),
            pltpu.VMEM((PARTS, 4, 48, 384), low),
            pltpu.VMEM((PARTS, 3, 48, 384), low),
            pltpu.VMEM((2,) + sums.shape, wide),
            small, small, small, small, small,
            pltpu.VMEM((3,) + sums.shape, wide),
            dma((2, n)),
            dma,
            dma((2, PARTS)),
            dma((2, PARTS)),
            dma((2, PARTS)),
            dma((2, PARTS, 3)),
            dma((2, PARTS, 3)),
            dma((2, PARTS)),
            dma((2, 6)),
        ],
        compiler_params=pltpu.CompilerParams(
            collective_id=name, has_side_effects=True, vmem_limit_bytes=60 << 20
        ),
        name="sum_all",
    )(left, right, sums, blocks, w_qkv, resid)


def on_device_spread(
    tokens,
    cotangent,
    lengths,
    pairing,
    w_qkv,
    bias_q,
    bias_v,
    w_out,
    bias_out,
    ln1_gain,
    ln1_bias,
    w_in,
    bias_in,
    w_back,
    bias_back,
    ln2_gain,
    ln2_bias,
):
    rows = tokens.shape[1]
    half = rows // 2
    width = tokens.shape[2]
    n = pairing.shape[0] // 2
    inputs = tokens[0]
    vectors = [bias_q, bias_v, bias_out, ln1_gain, ln1_bias, bias_back, ln2_gain, ln2_bias]
    small = jnp.concatenate([jnp.stack(vectors), bias_in.reshape(4, -1)]).astype(jnp.float32)
    small = jnp.pad(small, ((0, 16 - small.shape[0]), (0, 0)))
    packed, lines, qkv_full, out_full, in_full = project(
        inputs, small, w_qkv, w_out, w_in, n, 0
    )
    spot = lax.rem(lax.axis_index("ctx"), 2).astype(jnp.int32).reshape(1)
    mixed_out, keep, mix, lse = attend(
        pairing, lengths, spot, packed.reshape(-1, half, 6 * HEAD_DIM)
    )
    output, grad_in, left, right, resid, sums = layer(
        pairing, lengths, mixed_out.reshape(-1, rows, 2 * HEAD_DIM), inputs, cotangent[0],
        lines, out_full, in_full, w_back, 1,
    )
    grad_blocks = attend_back(
        pairing, lengths, spot, keep, grad_in.reshape(-1, half, 2 * HEAD_DIM), mix, lse
    )
    token_grad, qkv_sum, out_sum, in_sum, back_sum, small = sum_all(
        left, right, sums, grad_blocks.reshape(-1, rows, 6 * HEAD_DIM), qkv_full.reshape(width, -1),
        resid, 2
    )
    wide = lambda value: value.astype(jnp.float32)
    return (
        output[None],
        token_grad[None],
        wide(qkv_sum),
        small[ROW_BQ],
        small[ROW_BV],
        wide(out_sum),
        small[ROW_BO],
        small[ROW_G1],
        small[ROW_S1],
        wide(in_sum),
        small[ROW_BI : ROW_BI + 4].reshape(-1),
        wide(back_sum),
        small[ROW_BB],
        small[ROW_G2],
        small[ROW_S2],
    )


def solution(mesh):
    return jax.shard_map(
        on_device_spread if mesh.shape["ctx"] == 8 else on_device_any,
        mesh=mesh,
        in_specs=(
            P("fsdp", "ctx", None),
            P("fsdp", "ctx", None),
            P("fsdp"),
            P(),
            P("fsdp", None),
            P("fsdp"),
            P("fsdp"),
            P("fsdp", None),
            P("fsdp"),
            P("fsdp"),
            P("fsdp"),
            P("fsdp", None),
            P("fsdp"),
            P("fsdp", None),
            P("fsdp"),
            P("fsdp"),
            P("fsdp"),
        ),
        out_specs=(
            P("fsdp", "ctx", None),
            P("fsdp", "ctx", None),
            P("fsdp", None),
            P("fsdp"),
            P("fsdp"),
            P("fsdp", None),
            P("fsdp"),
            P("fsdp"),
            P("fsdp"),
            P("fsdp", None),
            P("fsdp"),
            P("fsdp", None),
            P("fsdp"),
            P("fsdp"),
            P("fsdp"),
        ),
        check_vma=False,
    )
```

```python
import functools
import math

import jax
import jax.numpy as jnp
from jax import lax
from jax.experimental import pallas as pl
from jax.experimental.pallas import tpu as pltpu
from jax.sharding import PartitionSpec as P

HEADS = 12
HEAD_DIM = 64
NMEM = 10
BLK = 128


eps = 1e-12
neg_big = -1e30


def layer_norm(value, gain, shift):
    mean = jnp.mean(value, axis=-1, keepdims=True)
    centred = value - mean
    variance = jnp.mean(centred * centred, axis=-1, keepdims=True)
    return centred * lax.rsqrt(variance + eps) * gain + shift


def norm_back(value, gain, grad):
    mean = jnp.mean(value, axis=-1, keepdims=True)
    centred = value - mean
    scale = lax.rsqrt(jnp.mean(centred * centred, axis=-1, keepdims=True) + eps)
    unit = centred * scale
    scaled = grad * gain
    inner = (
        scaled
        - jnp.mean(scaled, axis=-1, keepdims=True)
        - unit * jnp.mean(scaled * unit, axis=-1, keepdims=True)
    )
    return (scale * inner, jnp.sum(grad * unit, axis=0), jnp.sum(grad, axis=0))


def block_width(count):
    return math.gcd(count, 512)


def places(pairing, start, count, half):
    rows = start + jnp.arange(count, dtype=jnp.int32)
    owners = rows // half
    spots = jnp.arange(pairing.shape[0], dtype=jnp.int32)
    picked = jnp.sum(jnp.where(owners[:, None] == spots[None, :], pairing[None, :], 0), axis=1)
    return picked * half + rows % half


def allowed_pairs(query_place, key_place, length):
    before = (key_place[None, :] <= query_place[:, None]) | (key_place[None, :] < NMEM)
    return (key_place[None, :] < length) & before


def heads_of(value):
    return value.reshape(value.shape[0], HEADS, HEAD_DIM)


def forward_fold(query_heads, query_place, pairing, length, half):

    def fold(carry, piece, start):
        keys, values = piece
        count = keys.shape[0]
        width = block_width(count)
        key_place = places(pairing, start, count, half)

        def step(index, state):
            top, total, summed = state
            offset = index * width
            key_heads = heads_of(lax.dynamic_slice_in_dim(keys, offset, width, 0))
            value_heads = heads_of(lax.dynamic_slice_in_dim(values, offset, width, 0))
            mask = allowed_pairs(
                query_place, lax.dynamic_slice_in_dim(key_place, offset, width, 0), length
            )[None]
            scores = (
                jnp.einsum(
                    "qhd,khd->hqk", query_heads, key_heads, preferred_element_type=jnp.float32
                )
                * 0.125
            )
            scores = jnp.where(mask, scores, neg_big)
            new_top = jnp.maximum(top, jnp.max(scores, axis=2))
            shrink = jnp.exp(top - new_top)
            probs = jnp.where(mask, jnp.exp(scores - new_top[:, :, None]), 0.0)
            total = total * shrink + jnp.sum(probs, axis=2)
            update = jnp.einsum(
                "hqk,khd->qhd",
                probs.astype(jnp.bfloat16),
                value_heads,
                preferred_element_type=jnp.float32,
            )
            summed = summed * jnp.transpose(shrink)[:, :, None] + update
            return (new_top, total, summed)

        return lax.fori_loop(0, count // width, step, carry)

    return fold


def query_grad_fold(query_heads, grad_heads, top_sum, delta, query_place, pairing, length, half):

    def fold(carry, piece, start):
        keys, values = piece
        count = keys.shape[0]
        width = block_width(count)
        key_place = places(pairing, start, count, half)

        def step(index, summed):
            offset = index * width
            key_heads = heads_of(lax.dynamic_slice_in_dim(keys, offset, width, 0))
            value_heads = heads_of(lax.dynamic_slice_in_dim(values, offset, width, 0))
            mask = allowed_pairs(
                query_place, lax.dynamic_slice_in_dim(key_place, offset, width, 0), length
            )[None]
            scores = (
                jnp.einsum(
                    "qhd,khd->hqk", query_heads, key_heads, preferred_element_type=jnp.float32
                )
                * 0.125
            )
            probs = jnp.where(mask, jnp.exp(scores - top_sum[:, :, None]), 0.0)
            prob_grad = jnp.einsum(
                "qhd,khd->hqk", grad_heads, value_heads, preferred_element_type=jnp.float32
            )
            score_grad = (probs * (prob_grad - delta[:, :, None])).astype(jnp.bfloat16)
            return (
                summed
                + jnp.einsum(
                    "hqk,khd->qhd", score_grad, key_heads, preferred_element_type=jnp.float32
                )
                * 0.125
            )

        return lax.fori_loop(0, count // width, step, carry)

    return fold


def key_terms(
    key_heads, value_heads, key_place, query_heads, grad_heads, top_sum, delta, query_place, length
):
    scores = (
        jnp.einsum("qhd,khd->hqk", query_heads, key_heads, preferred_element_type=jnp.float32)
        * 0.125
    )
    mask = allowed_pairs(query_place, key_place, length)[None]
    probs = jnp.where(mask, jnp.exp(scores - top_sum[:, :, None]), 0.0)
    prob_grad = jnp.einsum(
        "qhd,khd->hqk", grad_heads, value_heads, preferred_element_type=jnp.float32
    )
    score_grad = (probs * (prob_grad - delta[:, :, None])).astype(jnp.bfloat16)
    value_grad = jnp.einsum(
        "hqk,qhd->khd", probs.astype(jnp.bfloat16), grad_heads, preferred_element_type=jnp.float32
    )
    key_grad = (
        jnp.einsum("hqk,qhd->khd", score_grad, query_heads, preferred_element_type=jnp.float32)
        * 0.125
    )
    return (key_grad, value_grad)


def on_device_any(
    tokens,
    cotangent,
    lengths,
    pairing,
    w_qkv,
    bias_q,
    bias_v,
    w_out,
    bias_out,
    ln1_gain,
    ln1_bias,
    w_in,
    bias_in,
    w_back,
    bias_back,
    ln2_gain,
    ln2_bias,
):
    gathered = (
        lax.all_gather(w_qkv, "fsdp", axis=0, tiled=True),
        lax.all_gather(bias_q, "fsdp", axis=0, tiled=True),
        lax.all_gather(bias_v, "fsdp", axis=0, tiled=True),
        lax.all_gather(w_out, "fsdp", axis=0, tiled=True),
        lax.all_gather(bias_out, "fsdp", axis=0, tiled=True),
        lax.all_gather(ln1_gain, "fsdp", axis=0, tiled=True),
        lax.all_gather(ln1_bias, "fsdp", axis=0, tiled=True),
        lax.all_gather(w_in, "fsdp", axis=0, tiled=True),
        lax.all_gather(bias_in, "fsdp", axis=0, tiled=True),
        lax.all_gather(w_back, "fsdp", axis=0, tiled=True),
        lax.all_gather(bias_back, "fsdp", axis=0, tiled=True),
        lax.all_gather(ln2_gain, "fsdp", axis=0, tiled=True),
        lax.all_gather(ln2_bias, "fsdp", axis=0, tiled=True),
    )
    (
        qkv_all,
        query_bias,
        value_bias,
        out_all,
        out_bias,
        gain_one,
        shift_one,
        in_all,
        in_bias,
        back_all,
        back_bias,
        gain_two,
        shift_two,
    ) = gathered
    rows = tokens.shape[1]
    half = rows // 2
    width = tokens.shape[2]
    length = lengths[0]
    query_place = places(pairing, lax.axis_index("ctx") * rows, rows, half)
    valid = query_place < length
    inputs = tokens[0]
    proj = jnp.dot(inputs, qkv_all, preferred_element_type=jnp.float32)
    queries = (proj[:, :width] + query_bias.astype(jnp.float32)).astype(jnp.bfloat16)
    keys = proj[:, width : 2 * width].astype(jnp.bfloat16)
    values = (proj[:, 2 * width :] + value_bias.astype(jnp.float32)).astype(jnp.bfloat16)
    query_heads = heads_of(queries)
    start_state = (
        jnp.full((HEADS, rows), neg_big, jnp.float32),
        jnp.zeros((HEADS, rows), jnp.float32),
        jnp.zeros((rows, HEADS, HEAD_DIM), jnp.float32),
    )
    fold = forward_fold(query_heads, query_place, pairing, length, half)
    top, total, summed = fold(
        start_state,
        (
            lax.all_gather(keys, "ctx", axis=0, tiled=True),
            lax.all_gather(values, "ctx", axis=0, tiled=True),
        ),
        jnp.int32(0),
    )
    top_sum = top + jnp.log(total)
    attended = (summed / jnp.transpose(total)[:, :, None]).reshape(rows, width)
    attended_low = attended.astype(jnp.bfloat16)
    resid_one = (
        inputs.astype(jnp.float32)
        + jnp.dot(attended_low, out_all, preferred_element_type=jnp.float32)
        + out_bias.astype(jnp.float32)
    )
    hidden = layer_norm(resid_one, gain_one.astype(jnp.float32), shift_one.astype(jnp.float32))
    hidden_low = hidden.astype(jnp.bfloat16)
    upper = jnp.dot(hidden_low, in_all, preferred_element_type=jnp.float32) + in_bias.astype(
        jnp.float32
    )
    active, gelu_back = jax.vjp(lambda value: jax.nn.gelu(value, approximate=False), upper)
    active_low = active.astype(jnp.bfloat16)
    resid_two = (
        hidden
        + jnp.dot(active_low, back_all, preferred_element_type=jnp.float32)
        + back_bias.astype(jnp.float32)
    )
    normed = layer_norm(resid_two, gain_two.astype(jnp.float32), shift_two.astype(jnp.float32))
    output = jnp.where(valid[:, None], normed, 0.0)
    qkv_back, out_back, gain_one_back, in_back, back_back, gain_two_back = (
        qkv_all,
        out_all,
        gain_one,
        in_all,
        back_all,
        gain_two,
    )
    grad_y = jnp.where(valid[:, None], cotangent[0].astype(jnp.float32), 0.0)
    grad_resid_two, gain_two_grad, shift_two_grad = norm_back(
        resid_two, gain_two_back.astype(jnp.float32), grad_y
    )
    grad_mixed = grad_resid_two.astype(jnp.bfloat16)
    back_grad = jnp.einsum("tf,td->fd", active_low, grad_mixed, preferred_element_type=jnp.float32)
    back_bias_grad = jnp.sum(grad_mixed.astype(jnp.float32), axis=0)
    grad_active = jnp.einsum("td,fd->tf", grad_mixed, back_back, preferred_element_type=jnp.float32)
    (grad_upper,) = gelu_back(grad_active)
    grad_upper_low = grad_upper.astype(jnp.bfloat16)
    in_grad = jnp.einsum(
        "td,tf->df", hidden_low, grad_upper_low, preferred_element_type=jnp.float32
    )
    in_bias_grad = jnp.sum(grad_upper_low.astype(jnp.float32), axis=0)
    grad_hidden = grad_resid_two + jnp.einsum(
        "tf,df->td", grad_upper_low, in_back, preferred_element_type=jnp.float32
    )
    grad_resid_one, gain_one_grad, shift_one_grad = norm_back(
        resid_one, gain_one_back.astype(jnp.float32), grad_hidden
    )
    grad_branch = grad_resid_one.astype(jnp.bfloat16)
    out_grad = jnp.einsum(
        "tc,td->cd", attended_low, grad_branch, preferred_element_type=jnp.float32
    )
    out_bias_grad = jnp.sum(grad_branch.astype(jnp.float32), axis=0)
    grad_attended = jnp.einsum(
        "td,cd->tc", grad_branch, out_back, preferred_element_type=jnp.float32
    ).astype(jnp.bfloat16)
    grad_heads = heads_of(grad_attended)
    delta = jnp.transpose(jnp.sum(grad_heads.astype(jnp.float32) * heads_of(attended), axis=2))
    query_fold = query_grad_fold(
        query_heads, grad_heads, top_sum, delta, query_place, pairing, length, half
    )
    empty_heads = jnp.zeros((rows, HEADS, HEAD_DIM), jnp.float32)
    query_grad = query_fold(
        empty_heads,
        (
            lax.all_gather(keys, "ctx", axis=0, tiled=True),
            lax.all_gather(values, "ctx", axis=0, tiled=True),
        ),
        jnp.int32(0),
    )
    stats = jnp.concatenate([jnp.transpose(top_sum), jnp.transpose(delta)], axis=1)
    stats_all = lax.all_gather(stats, "ctx", axis=0, tiled=True)
    key_heads = heads_of(keys)
    value_heads = heads_of(values)
    query_in = lax.all_gather(queries, "ctx", axis=0, tiled=True)
    grad_in = lax.all_gather(grad_attended, "ctx", axis=0, tiled=True)
    count = query_in.shape[0]
    span = block_width(count)
    place_in = places(pairing, jnp.int32(0), count, half)

    def step(index, state):
        offset = index * span
        query_block = heads_of(lax.dynamic_slice_in_dim(query_in, offset, span, 0))
        grad_block = heads_of(lax.dynamic_slice_in_dim(grad_in, offset, span, 0))
        stats_block = lax.dynamic_slice_in_dim(stats_all, offset, span, 0)
        place_block = lax.dynamic_slice_in_dim(place_in, offset, span, 0)
        key_part, value_part = key_terms(
            key_heads,
            value_heads,
            query_place,
            query_block,
            grad_block,
            jnp.transpose(stats_block[:, :HEADS]),
            jnp.transpose(stats_block[:, HEADS:]),
            place_block,
            length,
        )
        return (state[0] + key_part, state[1] + value_part)

    key_sum, value_sum = lax.fori_loop(0, count // span, step, (empty_heads, empty_heads))
    key_grad = key_sum.reshape(rows, width)
    value_grad = value_sum.reshape(rows, width)
    grad_proj = jnp.concatenate(
        [
            query_grad.reshape(rows, width).astype(jnp.bfloat16),
            key_grad.astype(jnp.bfloat16),
            value_grad.astype(jnp.bfloat16),
        ],
        axis=1,
    )
    qkv_grad = jnp.einsum("td,tf->df", inputs, grad_proj, preferred_element_type=jnp.float32)
    query_bias_grad = jnp.sum(grad_proj[:, :width].astype(jnp.float32), axis=0)
    value_bias_grad = jnp.sum(grad_proj[:, 2 * width :].astype(jnp.float32), axis=0)
    token_grad = grad_resid_one + jnp.einsum(
        "tf,df->td", grad_proj, qkv_back, preferred_element_type=jnp.float32
    )
    grads = (
        qkv_grad,
        query_bias_grad,
        value_bias_grad,
        out_grad,
        out_bias_grad,
        gain_one_grad,
        shift_one_grad,
        in_grad,
        in_bias_grad,
        back_grad,
        back_bias_grad,
        gain_two_grad,
        shift_two_grad,
    )
    shards = (
        lax.psum_scatter(
            grads[0].astype(jnp.bfloat16), "fsdp", scatter_dimension=0, tiled=True
        ).astype(jnp.float32),
        lax.psum_scatter(
            grads[1].astype(jnp.bfloat16), "fsdp", scatter_dimension=0, tiled=True
        ).astype(jnp.float32),
        lax.psum_scatter(
            grads[2].astype(jnp.bfloat16), "fsdp", scatter_dimension=0, tiled=True
        ).astype(jnp.float32),
        lax.psum_scatter(
            grads[3].astype(jnp.bfloat16), "fsdp", scatter_dimension=0, tiled=True
        ).astype(jnp.float32),
        lax.psum_scatter(
            grads[4].astype(jnp.bfloat16), "fsdp", scatter_dimension=0, tiled=True
        ).astype(jnp.float32),
        lax.psum_scatter(
            grads[5].astype(jnp.bfloat16), "fsdp", scatter_dimension=0, tiled=True
        ).astype(jnp.float32),
        lax.psum_scatter(
            grads[6].astype(jnp.bfloat16), "fsdp", scatter_dimension=0, tiled=True
        ).astype(jnp.float32),
        lax.psum_scatter(
            grads[7].astype(jnp.bfloat16), "fsdp", scatter_dimension=0, tiled=True
        ).astype(jnp.float32),
        lax.psum_scatter(
            grads[8].astype(jnp.bfloat16), "fsdp", scatter_dimension=0, tiled=True
        ).astype(jnp.float32),
        lax.psum_scatter(
            grads[9].astype(jnp.bfloat16), "fsdp", scatter_dimension=0, tiled=True
        ).astype(jnp.float32),
        lax.psum_scatter(
            grads[10].astype(jnp.bfloat16), "fsdp", scatter_dimension=0, tiled=True
        ).astype(jnp.float32),
        lax.psum_scatter(
            grads[11].astype(jnp.bfloat16), "fsdp", scatter_dimension=0, tiled=True
        ).astype(jnp.float32),
        lax.psum_scatter(
            grads[12].astype(jnp.bfloat16), "fsdp", scatter_dimension=0, tiled=True
        ).astype(jnp.float32),
    )
    totals = (
        lax.psum(shards[0].astype(jnp.bfloat16), "ctx").astype(jnp.float32),
        lax.psum(shards[1].astype(jnp.bfloat16), "ctx").astype(jnp.float32),
        lax.psum(shards[2].astype(jnp.bfloat16), "ctx").astype(jnp.float32),
        lax.psum(shards[3].astype(jnp.bfloat16), "ctx").astype(jnp.float32),
        lax.psum(shards[4].astype(jnp.bfloat16), "ctx").astype(jnp.float32),
        lax.psum(shards[5].astype(jnp.bfloat16), "ctx").astype(jnp.float32),
        lax.psum(shards[6].astype(jnp.bfloat16), "ctx").astype(jnp.float32),
        lax.psum(shards[7].astype(jnp.bfloat16), "ctx").astype(jnp.float32),
        lax.psum(shards[8].astype(jnp.bfloat16), "ctx").astype(jnp.float32),
        lax.psum(shards[9].astype(jnp.bfloat16), "ctx").astype(jnp.float32),
        lax.psum(shards[10].astype(jnp.bfloat16), "ctx").astype(jnp.float32),
        lax.psum(shards[11].astype(jnp.bfloat16), "ctx").astype(jnp.float32),
        lax.psum(shards[12].astype(jnp.bfloat16), "ctx").astype(jnp.float32),
    )
    return (output[None], token_grad[None]) + tuple(totals)


def low_lanes(shape):
    return lax.broadcasted_iota(jnp.int32, shape, 1) < 64


def attend_kernel(
    chunks, pair_ref, len_ref, spot_ref, in_ref, out_ref, keep_ref, mix_ref, lse_ref, back_ref
):
    length = len_ref[0]
    spot = spot_ref[0]
    blocks = 2 * chunks
    for s in range(blocks):
        keep_ref[pair_ref[s]] = in_ref[s]
        back_ref[pair_ref[s]] = s
    left = low_lanes((256, BLK))
    left_half = left[:BLK]
    for c in range(chunks):
        keys = 256 * (c + 1)
        own = keep_ref[2 * c : 2 * c + 2, :, :BLK].reshape(256, BLK)
        shared = keep_ref[2 * c + spot, :, :BLK]
        zero = jnp.zeros((), jnp.bfloat16)
        query = jnp.concatenate(
            [jnp.where(left, own, zero), jnp.where(left_half, zero, shared)], axis=0
        ) * jnp.bfloat16(0.125)
        key = keep_ref[: 2 * c + 2, :, BLK : 2 * BLK].reshape(keys, BLK)
        value = keep_ref[: 2 * c + 2, :, 2 * BLK :].reshape(keys, BLK)
        scores = mask_scores(
            lax.dot_general(key, query, (((1,), (1,)), ((), ())), preferred_element_type=jnp.float32),
            c, spot, length, 0, True,
        )
        top = jnp.max(scores, axis=0, keepdims=True)
        probs = jnp.exp(scores - top)
        total = jnp.sum(probs, axis=0, keepdims=True)
        summed = lax.dot_general(
            value, probs.astype(jnp.bfloat16), (((0,), (0,)), ((), ())),
            preferred_element_type=jnp.float32,
        ) / total
        lse_ref[c] = top + jnp.log(total)
        part = summed[64:, 256:]
        none = jnp.zeros_like(part)
        first = jnp.where(spot == 0, part, none)
        second = jnp.where(spot == 0, none, part)
        mixed = jnp.concatenate(
            [summed[:64, :256], jnp.concatenate([first, second], axis=1)], axis=0
        )
        mix_ref[c] = mixed
    for s in range(blocks):
        place = pair_ref[s]
        c = place // 2
        piece = mix_ref[c, :, pl.ds(pl.multiple_of((place % 2) * BLK, BLK), BLK)]
        out_ref[s] = jnp.transpose(piece).astype(jnp.bfloat16)


def mask_scores(scores, c, spot, length, start, edged):
    keys, width = scores.shape
    row = start + lax.broadcasted_iota(jnp.int32, (keys, width), 0)
    scores = jnp.where(row < length, scores, neg_big)
    if not edged:
        return scores
    edge = 256 * c
    lane = lax.broadcasted_iota(jnp.int32, (256, width), 1)
    query_place = edge + jnp.where(lane < 256, lane, lane - 256 + spot * BLK)
    key_place = edge + lax.broadcasted_iota(jnp.int32, (256, width), 0)
    seen = key_place <= query_place
    if c == 0:
        seen = seen | (key_place < NMEM)
    tail = jnp.where(seen, scores[keys - 256 :], neg_big)
    if keys == 256:
        return tail
    return jnp.concatenate([scores[: keys - 256], tail], axis=0)


def attend_back(
    c, length, spot, keep_ref, g_ref, mix_ref, lse_ref, q_sum, k_sum, v_sum
):
    zero = jnp.zeros((), jnp.bfloat16)
    left = low_lanes((256, BLK))
    left_half = left[:BLK]
    own = keep_ref[2 * c : 2 * c + 2, :, :BLK].reshape(256, BLK)
    shared = keep_ref[2 * c + spot, :, :BLK]
    query = jnp.concatenate(
        [jnp.where(left, own, zero), jnp.where(left_half, zero, shared)], axis=0
    ) * jnp.bfloat16(0.125)
    g_own = g_ref[2 * c : 2 * c + 2].reshape(256, BLK)
    g_shared = g_ref[2 * c + spot]
    grad = jnp.concatenate(
        [jnp.where(left, g_own, zero), jnp.where(left_half, zero, g_shared)], axis=0
    )
    turned = jnp.transpose(g_own.astype(jnp.float32)) * mix_ref[c]
    delta_own = jnp.sum(turned[:64], axis=0, keepdims=True)
    delta_pair = jnp.sum(turned[64:], axis=0, keepdims=True)
    delta = jnp.concatenate(
        [delta_own, jnp.where(spot == 0, delta_pair[:, :BLK], delta_pair[:, BLK:])], axis=1
    )
    lse = lse_ref[c]
    q_grad = jnp.zeros((384, BLK), jnp.float32)
    last = 2 * c + 2
    step = 8
    for low_block in range(0, last, step):
        high_block = min(low_block + step, last)
        cut = slice(low_block, high_block)
        count = high_block - low_block
        key = keep_ref[cut, :, BLK : 2 * BLK].reshape(count * BLK, BLK)
        value = keep_ref[cut, :, 2 * BLK :].reshape(count * BLK, BLK)
        scores = mask_scores(
            dot_nt(key, query), c, spot, length, low_block * BLK, high_block == last
        )
        probs = jnp.exp(scores - lse)
        score_grad = (probs * (dot_nt(value, grad) - delta)).astype(jnp.bfloat16)
        v_part = dot_nn(probs.astype(jnp.bfloat16), grad)
        k_part = dot_nn(score_grad, query)
        v_sum[cut] += v_part.reshape(count, BLK, BLK)
        k_sum[cut] += k_part.reshape(count, BLK, BLK)
        q_grad = q_grad + lax.dot_general(
            score_grad, key, (((0,), (0,)), ((), ())), preferred_element_type=jnp.float32
        )
    q_grad = q_grad * 0.125
    part = q_grad[256:]
    none = jnp.zeros_like(part)
    first = jnp.where(spot == 0, part, none)
    second = jnp.where(spot == 0, none, part)
    q_sum[2 * c : 2 * c + 2] = jnp.where(
        left, q_grad[:256], jnp.concatenate([first, second], axis=0)
    ).reshape(2, BLK, BLK)


def smem():
    return pl.BlockSpec(memory_space=pltpu.SMEM)


def vmem():
    return pl.BlockSpec(memory_space=pltpu.VMEM)


def attend(pairing, lengths, spot, packed):
    blocks = packed.shape[0]
    chunks = blocks // 2
    return pl.pallas_call(
        functools.partial(attend_kernel, chunks),
        out_shape=(
            jax.ShapeDtypeStruct((blocks, BLK, BLK), jnp.bfloat16),
            jax.ShapeDtypeStruct((blocks, BLK, 3 * BLK), jnp.bfloat16),
            jax.ShapeDtypeStruct((chunks, BLK, 256), jnp.float32),
            jax.ShapeDtypeStruct((chunks, 1, 384), jnp.float32),
            jax.ShapeDtypeStruct((blocks,), jnp.int32),
        ),
        in_specs=[smem(), smem(), smem(), vmem()],
        out_specs=(vmem(), vmem(), vmem(), vmem(), smem()),
        compiler_params=pltpu.CompilerParams(vmem_limit_bytes=48 << 20),
        name="attend",
    )(pairing, lengths, spot, packed)


MESH = pl.DeviceIdType.MESH


def remote(src, dst, sems, at, peer):
    return pltpu.make_async_remote_copy(
        src_ref=src, dst_ref=dst, send_sem=sems.at[(0,) + at], recv_sem=sems.at[(1,) + at],
        device_id=peer, device_id_type=MESH,
    )


def greet(peers):
    barrier = pltpu.get_barrier_semaphore()
    for peer in peers:
        pl.semaphore_signal(barrier, inc=1, device_id=peer, device_id_type=MESH)
    pl.semaphore_wait(barrier, len(peers))


def ring_peers(n):
    me = lax.axis_index("ctx")
    return [{"ctx": lax.rem(me + k, n)} for k in range(1, n)]


def two(block):
    return pl.ds(2 * block, 2)


def exchange_copies(n, in_ref, out_ref, sems):
    me = lax.axis_index("ctx")
    copies = []
    for k in range(1, n):
        peer = lax.rem(me + k, n)
        copies.append(
            remote(in_ref.at[two(peer)], out_ref.at[two(me)], sems, (k,), {"ctx": peer})
        )
    return copies


def own_copy(in_ref, out_ref, sem):
    me = lax.axis_index("ctx")
    return pltpu.make_async_copy(in_ref.at[two(me)], out_ref.at[two(me)], sem)


def both(ref, peer):
    value = ref[2 * peer : 2 * peer + 2]
    return value.reshape(-1, value.shape[2])


def join_pairs(pairs):
    pieces = []
    for group in range(HEADS // 3):
        first, second = pairs(2 * group), pairs(2 * group + 1)
        shared = first[:, HEAD_DIM:].astype(jnp.float32) + second[:, HEAD_DIM:].astype(jnp.float32)
        pieces += [first[:, :HEAD_DIM], second[:, :HEAD_DIM], shared.astype(jnp.bfloat16)]
    return jnp.concatenate(pieces, axis=1)


def pair_of(value, peer):
    own = 3 * (peer // 2) + peer % 2
    shared = 3 * (peer // 2) + 2
    cut = lambda head: value[:, head * HEAD_DIM : (head + 1) * HEAD_DIM]
    return jnp.concatenate([cut(own), cut(shared)], axis=1)


def dot_nn(a, b):
    return jnp.dot(a, b, preferred_element_type=jnp.float32)


def dot_nt(a, b):
    return lax.dot_general(a, b, (((1,), (1,)), ((), ())), preferred_element_type=jnp.float32)


def column_sum(value):
    return jnp.sum(value, axis=0, keepdims=True)


def unit_of(value):
    mean = jnp.mean(value, axis=-1, keepdims=True)
    centred = value - mean
    scale = lax.rsqrt(jnp.mean(centred * centred, axis=-1, keepdims=True) + eps)
    return centred * scale, scale


def unit_back(unit, scale, scaled):
    return scale * (
        scaled
        - jnp.mean(scaled, axis=-1, keepdims=True)
        - unit * jnp.mean(scaled * unit, axis=-1, keepdims=True)
    )


(ROW_BQ, ROW_BV, ROW_BO, ROW_G1, ROW_S1, ROW_BB, ROW_G2, ROW_S2, ROW_BI) = range(9)


def layer_kernel(
    n, pair_ref, len_ref, mixed_ref, tokens_ref, cot_ref, rows_ref, out_full, in_full, back_ref,
    output_ref, grad_ref, left_ref, right_ref, resid_ref, sums_ref,
    mixed_in, active, slope, w_out, w_in, w_back, in_sem, back_sem, own_sem,
):
    low, wide = jnp.bfloat16, jnp.float32
    ctx = lax.axis_index("ctx")
    sums_ref[...] = jnp.zeros_like(sums_ref)
    fsdp = lax.axis_index("fsdp")
    x, core = fsdp // 2, lax.rem(fsdp, 2)
    greet(ring_peers(n) + chip_peers())
    copies = exchange_copies(n, mixed_ref, mixed_in, in_sem)
    for cp in copies:
        cp.start()
    back_shards = gather_copies(back_ref, w_back, back_sem, 0)
    for step in (0, 1):
        back_shards[step].start()
    width = tokens_ref.shape[1]
    count = w_in.shape[0]
    loads = [
        pltpu.make_async_copy(out_full, w_out, own_sem.at[2]),
        pltpu.make_async_copy(back_ref, w_back.at[fsdp], own_sem.at[3]),
    ] + [
        pltpu.make_async_copy(
            in_full.at[:, :, t * width : (t + 1) * width], w_in.at[t], own_sem.at[4 + t]
        )
        for t in range(count)
    ]
    for cp in loads:
        cp.start()
    own = own_copy(mixed_ref, mixed_in, own_sem.at[0])
    own.start()
    row = lambda i: rows_ref[i : i + 1, :]
    tokens = tokens_ref[...]
    left_ref[0] = jnp.transpose(tokens).reshape(4, -1, 2 * BLK)
    spots = lax.broadcasted_iota(jnp.int32, (2 * BLK, 1), 0)
    place = jnp.where(
        spots < BLK,
        pair_ref[2 * ctx] * BLK + spots,
        pair_ref[2 * ctx + 1] * BLK + spots - BLK,
    )
    valid = place < len_ref[0]
    own.wait()
    for cp in copies:
        cp.wait_recv()

    attended = join_pairs(lambda peer: both(mixed_in, peer))
    loads[0].wait()
    resid_one = (
        tokens.astype(wide)
        + dot_nn(attended, w_out[...].reshape(width, width))
        + row(ROW_BO)
    )
    unit_one, scale_one = unit_of(resid_one)
    hidden = unit_one * row(ROW_G1) + row(ROW_S1)
    hidden_low = hidden.astype(low)
    resid_two = hidden + row(ROW_BB)
    for cp in loads[2:]:
        cp.wait()
    order = [fsdp, 2 * x + 1 - core, 2 * (1 - x) + core, 2 * (1 - x) + 1 - core]
    for step, t in enumerate(order):
        bias = rows_ref[pl.ds(ROW_BI + t, 1), :]
        upper = dot_nn(hidden_low, w_in[t].reshape(width, width)) + bias
        share = 0.5 * (1.0 + lax.erf(upper * (0.5**0.5)))
        slope[t] = share + upper * (jnp.exp(-0.5 * upper * upper) * (2 * math.pi) ** -0.5)
        some = (upper * share).astype(low)
        active[t] = some
        if step == 0:
            loads[1].wait()
        elif step == 1:
            back_shards[1].wait_recv()
        elif step == 2:
            back_shards[0].wait_recv()
            back_shards[2].start()
        else:
            back_shards[2].wait_recv()
        resid_two = resid_two + dot_nn(some, w_back[t])
    unit_two, scale_two = unit_of(resid_two)
    output_ref[...] = jnp.where(valid, unit_two * row(ROW_G2) + row(ROW_S2), 0.0)
    grad_y = jnp.where(valid, cot_ref[...].astype(wide), 0.0)
    sums_ref[ROW_G2 : ROW_G2 + 1, :] = column_sum(grad_y * unit_two)
    sums_ref[ROW_S2 : ROW_S2 + 1, :] = column_sum(grad_y)
    grad_resid_two = unit_back(unit_two, scale_two, grad_y * row(ROW_G2))
    grad_mixed = grad_resid_two.astype(low)
    right_ref[5] = grad_mixed
    sums_ref[ROW_BB : ROW_BB + 1, :] = column_sum(grad_mixed.astype(wide))
    grad_hidden = grad_resid_two
    for t in range(count):
        grad_upper = (dot_nt(grad_mixed, w_back[t]) * slope[t]).astype(low)
        right_ref[1 + t] = grad_upper
        sums_ref[ROW_BI + t : ROW_BI + t + 1, :] = column_sum(grad_upper.astype(wide))
        grad_hidden = grad_hidden + dot_nt(grad_upper, w_in[t].reshape(width, width))
    sums_ref[ROW_G1 : ROW_G1 + 1, :] = column_sum(grad_hidden * unit_one)
    sums_ref[ROW_S1 : ROW_S1 + 1, :] = column_sum(grad_hidden)
    grad_resid_one = unit_back(unit_one, scale_one, grad_hidden * row(ROW_G1))
    resid_ref[...] = grad_resid_one
    grad_branch = grad_resid_one.astype(low)
    right_ref[0] = grad_branch
    sums_ref[ROW_BO : ROW_BO + 1, :] = column_sum(grad_branch.astype(wide))
    grad_attended = dot_nt(grad_branch, w_out[...].reshape(width, width)).astype(low)
    for peer in range(n):
        grad_ref[2 * peer : 2 * peer + 2] = pair_of(grad_attended, peer).reshape(2, BLK, BLK)
    left_ref[1] = jnp.transpose(attended).reshape(4, -1, 2 * BLK)
    left_ref[2] = jnp.transpose(hidden_low).reshape(4, -1, 2 * BLK)
    for f in range(4):
        turned = jnp.transpose(active[f])
        for r in range(4):
            left_ref[3 + r, f] = turned[r * width // 4 : (r + 1) * width // 4]
    for cp in copies:
        cp.wait_send()
    for cp in back_shards:
        cp.wait_send()


def layer(pairing, lengths, mixed, tokens, cotangent, rows, out_full, in_full, w_back, name):
    n = mixed.shape[0] // 2
    count, width = tokens.shape
    low, wide = jnp.bfloat16, jnp.float32
    dma = pltpu.SemaphoreType.DMA
    shape = jax.ShapeDtypeStruct
    anywhere = pl.BlockSpec(memory_space=pltpu.HBM)
    return pl.pallas_call(
        functools.partial(layer_kernel, n),
        out_shape=(
            shape((count, width), wide),
            shape(mixed.shape, low),
            shape((7, 4, width // 4, count), low),
            shape((6, count, width), low),
            shape((count, width), wide),
            shape((16, width), wide),
        ),
        in_specs=[smem(), smem()] + [vmem()] * 4 + [anywhere] * 3,
        out_specs=(vmem(),) * 6,
        scratch_shapes=[
            pltpu.VMEM(mixed.shape, low),
            pltpu.VMEM((4, count, width), low),
            pltpu.VMEM((4, count, width), wide),
            pltpu.VMEM(out_full.shape, low),
            pltpu.VMEM((4, 4, width // 4, width), low),
            pltpu.VMEM((4,) + w_back.shape, low),
            dma((2, n)),
            dma((2, 1, 3)),
            dma((8,)),
        ],
        compiler_params=pltpu.CompilerParams(
            collective_id=name, has_side_effects=True, vmem_limit_bytes=56 << 20
        ),
        name="layer",
    )(pairing, lengths, mixed, tokens, cotangent, rows, out_full, in_full, w_back)


def gather_copies(src, full, sems, index):
    fsdp = lax.axis_index("fsdp")
    x, core = fsdp // 2, lax.rem(fsdp, 2)
    sibling, across = {"fsdp": 2 * x + 1 - core}, {"fsdp": 2 * (1 - x) + core}
    other = 2 * (1 - x) + core
    return (
        remote(src, full.at[fsdp], sems, (index, 0), across),
        remote(src, full.at[fsdp], sems, (index, 1), sibling),
        remote(full.at[other], full.at[other], sems, (index, 2), sibling),
    )


def chip_peers():
    fsdp = lax.axis_index("fsdp")
    x, core = fsdp // 2, lax.rem(fsdp, 2)
    return [{"fsdp": 2 * x + 1 - core}, {"fsdp": 2 * (1 - x) + core}]


def project_kernel(
    n, tokens_ref, small_ref, qkv_ref, out_ref, in_ref,
    packed_ref, rows_ref, qkv_full, out_full, in_full,
    qkv_here, small_here, send, sems, own_sem, block_sem,
):
    low, wide = jnp.bfloat16, jnp.float32
    fsdp = lax.axis_index("fsdp")
    greet(ring_peers(n) + chip_peers())
    qkv = gather_copies(qkv_ref, qkv_here, sems, 0)
    small = gather_copies(small_ref, small_here, sems, 1)
    for step in (0, 1):
        small[step].start()
        qkv[step].start()
    locals_ = [
        pltpu.make_async_copy(src, dst, own_sem.at[i])
        for i, (src, dst) in enumerate(
            [
                (qkv_ref, qkv_here.at[fsdp]),
                (small_ref, small_here.at[fsdp]),
                (out_ref, out_full.at[fsdp]),
                (in_ref, in_full.at[fsdp]),
            ]
        )
    ]
    for cp in locals_:
        cp.start()
    small[0].wait_recv()
    small[2].start()
    qkv[0].wait_recv()
    qkv[2].start()
    later = [gather_copies(out_ref, out_full, sems, 2), gather_copies(in_ref, in_full, sems, 3)]
    for step in (0, 1):
        for cps in later:
            cps[step].start()
    for cps in (small, qkv):
        cps[1].wait_recv()
        cps[2].wait_recv()
    locals_[0].wait()
    locals_[1].wait()
    keep = pltpu.make_async_copy(qkv_here, qkv_full, own_sem.at[4])
    keep.start()
    for f in range(4):
        width = small_here.shape[2]
        cols = slice(f * width, (f + 1) * width)
        rows_ref[:8, cols] = small_here[f, :8]
        for j in range(4):
            rows_ref[ROW_BI + f : ROW_BI + f + 1, j * width : (j + 1) * width] = small_here[
                f, 8 + j : 9 + j
            ]
    rows_ref[12:] = jnp.zeros_like(rows_ref[12:])
    tokens = tokens_ref[...]
    width = tokens.shape[1]
    half = width // 2
    for g in range(2):
        parts = []
        for part, bias in ((0, ROW_BQ), (1, None), (2, ROW_BV)):
            at = part * width + g * half
            value = dot_nn(tokens, qkv_here[:, :, at : at + half].reshape(width, half))
            if bias is not None:
                value = value + rows_ref[bias : bias + 1, g * half : (g + 1) * half]
            parts.append(value.astype(low))
        for spot in range(n // 2):
            peer = g * n // 2 + spot
            send[2 * peer : 2 * peer + 2] = jnp.concatenate(
                [pair_of(value, spot) for value in parts], axis=1
            ).reshape(2, BLK, -1)
    blocks = exchange_copies(n, send, packed_ref, block_sem)
    for cp in blocks:
        cp.start()
    own = own_copy(send, packed_ref, own_sem.at[5])
    own.start()
    for cps in later:
        cps[0].wait_recv()
        cps[2].start()
    own.wait()
    keep.wait()
    locals_[2].wait()
    locals_[3].wait()
    for cp in blocks:
        cp.wait()
    for cps in later:
        cps[0].wait_send()
        cps[1].wait()
        cps[2].wait()
    for cps in (small, qkv):
        for cp in cps:
            cp.wait_send()


def project(tokens, small, w_qkv, w_out, w_in, n, name):
    low, wide = jnp.bfloat16, jnp.float32
    dma = pltpu.SemaphoreType.DMA
    shape = jax.ShapeDtypeStruct
    count, width = tokens.shape
    anywhere = pl.BlockSpec(memory_space=pltpu.HBM)
    return pl.pallas_call(
        functools.partial(project_kernel, n),
        out_shape=(
            shape((2 * n, BLK, 6 * HEAD_DIM), low),
            shape((16, width), wide),
            shape((4,) + w_qkv.shape, low),
            shape((4,) + w_out.shape, low),
            shape((4,) + w_in.shape, low),
        ),
        in_specs=[vmem(), vmem()] + [anywhere] * 3,
        out_specs=(vmem(), vmem()) + (anywhere,) * 3,
        scratch_shapes=[
            pltpu.VMEM((4,) + w_qkv.shape, low),
            pltpu.VMEM((4,) + small.shape, wide),
            pltpu.VMEM((2 * n, BLK, 6 * HEAD_DIM), low),
            dma((2, 4, 3)),
            dma((6,)),
            dma((2, n)),
        ],
        compiler_params=pltpu.CompilerParams(
            collective_id=name, has_side_effects=True, vmem_limit_bytes=40 << 20
        ),
        name="project",
    )(tokens, small, w_qkv, w_out, w_in)


PARTS = 12


def sum_sources(chunk):
    left = jnp.where(chunk < 4, 3 + chunk, jnp.where(chunk < 8, 2, jnp.where(chunk < 9, 1, 0)))
    right = jnp.where(
        chunk < 4, 8, jnp.where(chunk < 8, chunk, jnp.where(chunk < 9, 3, chunk - 9))
    )
    return left, right


STEPS = 30
PLAN = {
    "pair": {**{s: s for s in range(9)}, 17: 9, 18: 10, 19: 11},
    "x": {**{s + 1: s for s in range(9)}, 18: 9, 19: 10, 20: 11},
    "y": {9: 0, 10: 1, 12: 2, 13: 3, 14: 4, 15: 5, 16: 6, 18: 7, 19: 8, 22: 9, 23: 10, 24: 11},
    "near": {10: 0, 11: 1, 13: 2, 14: 3, 15: 4, 16: 5, 18: 6, 19: 7, 20: 8, 23: 9, 24: 10, 25: 11},
    "far": {11: 0, 12: 1, **{15 + c: c for c in range(2, 12)}},
    "own": {12: 0, **{16 + c: c for c in range(1, 12)}},
    "wide": {17 + c: c for c in range(12)},
    "last": {18 + c: c for c in range(12)},
}
ATTEND_AT = (10, 11, 12)
JOIN_AT = 17
SMALL_AT = (17, 18, 20, 22, 24, 26)
TOKEN_AT = 21


def planned(name, step):
    chunk = jnp.int32(-1)
    for at, which in PLAN[name].items():
        chunk = jnp.where(step == at, which, chunk)
    return chunk


def back_kernel(
    n, pair_ref, back_ref, len_ref, grad_ref, keep_ref, mix_ref, lse_ref, left_ref, right_ref,
    sums_ref, resid_ref, qkv_ref,
    total_ref, token_ref, small_out,
    grad_in, g_all, q_sum, k_sum, v_sum, blocks_out, blocks_in, w_qkv, right_all,
    pair_out, pair_in, x_out, x_in, y_out, y_in, y_keep, near_out, near_in, near_keep,
    far_out, far_in, far_keep, s_out, s_in,
    grad_sem, block_sem, own_sem, pair_sem, x_sem, y_sem, near_sem, far_sem, own_z_sem, wide_sem,
    last_sem, s_sem,
):
    low, wide = jnp.bfloat16, jnp.float32
    ctx = lax.axis_index("ctx")
    fsdp = lax.axis_index("fsdp")
    z, y = ctx // 2, lax.rem(ctx, 2)
    odd, upper = lax.rem(z, 2), z // 2
    x, core = fsdp // 2, lax.rem(fsdp, 2)
    sibling = {"fsdp": 2 * x + 1 - core}
    across = {"fsdp": 2 * (1 - x) + core}
    beside = {"ctx": 2 * z + 1 - y}
    near = {"ctx": 2 * (2 * upper + 1 - odd) + y}
    far = {"ctx": 2 * (2 * (1 - upper) + odd) + y}
    mine = 2 * odd + upper
    greet(ring_peers(n) + [sibling, across])
    grads = exchange_copies(n, grad_ref, grad_in, grad_sem)
    for cp in grads:
        cp.start()
    own_grad = own_copy(grad_ref, grad_in, own_sem.at[0])
    own_grad.start()
    load = pltpu.make_async_copy(qkv_ref, w_qkv, own_sem.at[1])
    load.start()
    blocks = exchange_copies(n, blocks_out, blocks_in, block_sem)
    own = own_copy(blocks_out, blocks_in, own_sem.at[2])
    right_all[3:] = right_ref[...]
    k_sum[...] = jnp.zeros_like(k_sum)
    v_sum[...] = jnp.zeros_like(v_sum)
    chunks = keep_ref.shape[0] // 2

    def attend_some(first, last):
        for c in range(first, last):
            attend_back(
                c, len_ref[0], y, keep_ref, g_all, mix_ref, lse_ref, q_sum, k_sum, v_sum
            )

    def attend_step(t):
        @pl.when(t == ATTEND_AT[0])
        def _():
            own_grad.wait()
            for cp in grads:
                cp.wait_recv()
            for b in range(2 * chunks):
                g_all[b] = grad_in[back_ref[b]]
            attend_some(0, chunks // 2)

        @pl.when(t == ATTEND_AT[1])
        def _():
            attend_some(chunks // 2, chunks - 2)

        @pl.when(t == ATTEND_AT[2])
        def _():
            attend_some(chunks - 2, chunks)
            for s in range(2 * chunks):
                place = pair_ref[s]
                blocks_out[s] = jnp.concatenate(
                    [q_sum[place], k_sum[place], v_sum[place]], axis=1
                ).astype(low)
            for cp in blocks:
                cp.start()
            own.start()

    def slot(c):
        return lax.rem(c, 4)

    def pair_copy(c):
        return remote(pair_out.at[lax.rem(c, 2)], pair_in.at[c], pair_sem, (c,), sibling)

    def x_copy(c):
        return remote(x_out.at[c], x_in.at[c], x_sem, (c,), across)

    def y_copy(c):
        return remote(y_out.at[slot(c)], y_in.at[c], y_sem, (c,), beside)

    def near_copy(c):
        return remote(near_out.at[slot(c)], near_in.at[c], near_sem, (c,), near)

    def far_copy(c):
        return remote(far_out.at[slot(c)], far_in.at[c], far_sem, (c,), far)

    def own_z_copy(c):
        piece = total_ref.at[c, y, mine]
        return remote(piece, piece, own_z_sem, (c,), far)

    def wide_copy(c):
        piece = total_ref.at[c, y, two(odd)]
        return remote(piece, piece, wide_sem, (c,), near)

    def last_copy(c):
        piece = total_ref.at[c, y]
        return remote(piece, piece, last_sem, (c,), beside)

    def reuse(copy, c, slots):
        @pl.when(c >= slots)
        def _():
            copy(c - slots).wait_send()

    def partial(c, shard):
        left, right = sum_sources(c)
        return dot_nn(left_ref[left, shard], right_all[right])

    def stage_pair(c):
        reuse(pair_copy, c, 2)
        for side in range(2):
            pair_out[lax.rem(c, 2), side] = partial(c, 2 * side + 1 - core).astype(low)
        pair_copy(c).start()

    def stage_x(c):
        pair_copy(c).wait_recv()
        x_out[c] = (partial(c, 2 * (1 - x) + core) + pair_in[c, 1 - x].astype(wide)).astype(low)
        x_copy(c).start()

    def stage_y(c):
        mine_sum = partial(c, 2 * x + core) + pair_in[c, x].astype(wide)
        x_copy(c).wait_recv()
        total = mine_sum + x_in[c].astype(wide)
        first, second = total[:, :384], total[:, 384:]
        reuse(y_copy, c, 4)
        y_out[slot(c)] = jnp.where(y == 0, second, first).astype(low)
        y_copy(c).start()
        y_keep[slot(c)] = jnp.where(y == 0, first, second)

    def stage_near(c):
        y_copy(c).wait_recv()
        total = y_keep[slot(c)] + y_in[c].astype(wide)
        first, second = total[:96], total[96:]
        reuse(near_copy, c, 4)
        near_out[slot(c)] = jnp.where(odd == 0, second, first).astype(low)
        near_copy(c).start()
        near_keep[slot(c)] = jnp.where(odd == 0, first, second)

    def stage_far(c):
        near_copy(c).wait_recv()
        total = near_keep[slot(c)] + near_in[c].astype(wide)
        first, second = total[:48], total[48:]
        reuse(far_copy, c, 4)
        far_out[slot(c)] = jnp.where(upper == 0, second, first).astype(low)
        far_copy(c).start()
        far_keep[slot(c)] = jnp.where(upper == 0, first, second)

    def stage_own(c):
        far_copy(c).wait_recv()
        total_ref[c, y, mine] = (far_keep[slot(c)] + far_in[c].astype(wide)).astype(low)
        own_z_copy(c).start()

    def stage_wide(c):
        own_z_copy(c).wait_recv()
        wide_copy(c).start()

    def stage_last(c):
        wide_copy(c).wait_recv()
        last_copy(c).start()

    def small_step(t):
        peers = [sibling, across, beside, near, far]
        copies = [
            remote(s_out.at[k], s_in.at[k], s_sem, (k,), peer) for k, peer in enumerate(peers)
        ]

        @pl.when(t == JOIN_AT)
        def _():
            own.wait()
            for cp in blocks:
                cp.wait_recv()
            for part in range(3):
                right_all[part] = join_pairs(
                    lambda peer: both(blocks_in, peer)[:, part * BLK : (part + 1) * BLK]
                )
            s_out[0] = sums_ref[...]
            s_out[0, ROW_BQ : ROW_BQ + 1] = column_sum(right_all[0].astype(wide))
            s_out[0, ROW_BV : ROW_BV + 1] = column_sum(right_all[2].astype(wide))
            copies[0].start()

        for k in range(1, 5):

            @pl.when(t == SMALL_AT[k])
            def _():
                copies[k - 1].wait()
                s_out[k] = s_out[k - 1] + s_in[k - 1]
                copies[k].start()

        @pl.when(t == SMALL_AT[5])
        def _():
            copies[4].wait()
            total = s_out[4] + s_in[4]
            quarter = total.shape[1] // 4
            cuts = [slice(f * quarter, (f + 1) * quarter) for f in range(4)]
            pick = lambda choices: sum(
                jnp.where(fsdp == f, choice, 0.0) for f, choice in enumerate(choices)
            )
            small_out[...] = jnp.zeros_like(small_out)
            small_out[:8] = pick([total[:8, cut] for cut in cuts])
            line = pick([total[ROW_BI + f : ROW_BI + f + 1] for f in range(4)])
            for j, cut in enumerate(cuts):
                small_out[8 + j : 9 + j] = line[:, cut]

        @pl.when(t == TOKEN_AT)
        def _():
            load.wait()
            width = resid_ref.shape[1]
            token_ref[...] = resid_ref[...] + sum(
                dot_nt(
                    right_all[part],
                    w_qkv[:, :, part * width : (part + 1) * width].reshape(width, width),
                )
                for part in range(3)
            )

    stages = [
        ("pair", stage_pair),
        ("x", stage_x),
        ("last", stage_last),
        ("wide", stage_wide),
        ("own", stage_own),
        ("far", stage_far),
        ("near", stage_near),
        ("y", stage_y),
    ]

    def step(t, carry):
        attend_step(t)
        small_step(t)
        for name, stage in stages:
            c = planned(name, t)

            @pl.when(c >= 0)
            def _():
                stage(c)

        return carry

    lax.fori_loop(0, STEPS, step, 0)

    def drain(c, carry):
        x_copy(c).wait_send()
        own_z_copy(c).wait_send()
        wide_copy(c).wait_send()
        last_copy(c).wait()
        return carry

    lax.fori_loop(0, PARTS, drain, 0)
    for c in range(PARTS - 4, PARTS):
        y_copy(c).wait_send()
        near_copy(c).wait_send()
        far_copy(c).wait_send()
    for c in (PARTS - 2, PARTS - 1):
        pair_copy(c).wait_send()
    for cp in grads + blocks:
        cp.wait_send()


def back(pairing, order, lengths, grad, keep, mix, lse, left, right, sums, resid, qkv_full, name):
    blocks = keep.shape[0]
    n = blocks // 2
    low, wide = jnp.bfloat16, jnp.float32
    dma = pltpu.SemaphoreType.DMA
    shape = jax.ShapeDtypeStruct
    total = pltpu.VMEM((blocks, BLK, BLK), wide)
    return pl.pallas_call(
        functools.partial(back_kernel, n),
        out_shape=(
            shape((PARTS, 2, 4, 48, 384), low),
            shape(resid.shape, wide),
            shape((16, 192), wide),
        ),
        in_specs=[smem()] * 3 + [vmem()] * 8 + [pl.BlockSpec(memory_space=pltpu.HBM)],
        out_specs=(vmem(),) * 3,
        scratch_shapes=[
            pltpu.VMEM(grad.shape, low),
            pltpu.VMEM(grad.shape, low),
            total, total, total,
            pltpu.VMEM(keep.shape, low),
            pltpu.VMEM(keep.shape, low),
            pltpu.VMEM(qkv_full.shape, low),
            pltpu.VMEM((9,) + right.shape[1:], low),
            pltpu.VMEM((2, 2, 192, 768), low),
            pltpu.VMEM((PARTS, 2, 192, 768), low),
            pltpu.VMEM((PARTS, 192, 768), low),
            pltpu.VMEM((PARTS, 192, 768), low),
            pltpu.VMEM((4, 192, 384), low),
            pltpu.VMEM((PARTS, 192, 384), low),
            pltpu.VMEM((4, 192, 384), wide),
            pltpu.VMEM((4, 96, 384), low),
            pltpu.VMEM((PARTS, 96, 384), low),
            pltpu.VMEM((4, 96, 384), wide),
            pltpu.VMEM((4, 48, 384), low),
            pltpu.VMEM((PARTS, 48, 384), low),
            pltpu.VMEM((4, 48, 384), wide),
            pltpu.VMEM((5,) + sums.shape, wide),
            pltpu.VMEM((5,) + sums.shape, wide),
            dma((2, n)),
            dma((2, n)),
            dma((3,)),
        ]
        + [dma((2, PARTS))] * 8
        + [dma((2, 5))],
        compiler_params=pltpu.CompilerParams(
            collective_id=name, has_side_effects=True, vmem_limit_bytes=61 << 20
        ),
        name="back",
    )(pairing, order, lengths, grad, keep, mix, lse, left, right, sums, resid, qkv_full)


def finish_kernel(
    total_ref, small_ref, output_ref, token_ref,
    output_out, token_out, qkv_out, out_out, in_out, back_out, *refs
):
    lines, (stage, sems) = refs[:9], refs[9:]
    copies = [
        pltpu.make_async_copy(output_ref, output_out, sems.at[PARTS]),
        pltpu.make_async_copy(token_ref, token_out, sems.at[PARTS + 1]),
    ]
    targets = [back_out.at[192 * k : 192 * k + 192] for k in range(4)]
    targets += [in_out.at[:, 768 * k : 768 * k + 768] for k in range(4)]
    targets += [out_out]
    targets += [qkv_out.at[:, 768 * k : 768 * k + 768] for k in range(3)]
    for cp in copies:
        cp.start()
    for c, target in enumerate(targets):
        for half in range(2):
            for spot in range(4):
                stage[c, 48 * spot : 48 * spot + 48, 384 * half : 384 * half + 384] = total_ref[
                    c, half, spot
                ].astype(jnp.float32)
        copies.append(pltpu.make_async_copy(stage.at[c], target, sems.at[c]))
        copies[-1].start()
    for i in range(8):
        lines[i][...] = small_ref[i]
    for j in range(4):
        lines[8][192 * j : 192 * j + 192] = small_ref[ROW_BI + j]
    for cp in copies:
        cp.wait()


def finish(total, small, output, token):
    shape = jax.ShapeDtypeStruct
    wide = jnp.float32
    hbm = pl.BlockSpec(memory_space=pltpu.HBM)
    return pl.pallas_call(
        finish_kernel,
        out_shape=(
            shape(output.shape, wide),
            shape(token.shape, wide),
            shape((192, 2304), wide),
            shape((192, 768), wide),
            shape((192, 3072), wide),
            shape((768, 768), wide),
        )
        + (shape((192,), wide),) * 8
        + (shape((768,), wide),),
        in_specs=[vmem(), vmem(), hbm, hbm],
        out_specs=(hbm,) * 6 + (vmem(),) * 9,
        scratch_shapes=[
            pltpu.VMEM((PARTS, 192, 768), wide),
            pltpu.SemaphoreType.DMA((PARTS + 2,)),
        ],
        compiler_params=pltpu.CompilerParams(vmem_limit_bytes=32 << 20),
        name="finish",
    )(total, small, output, token)


def on_device_spread(
    tokens,
    cotangent,
    lengths,
    pairing,
    w_qkv,
    bias_q,
    bias_v,
    w_out,
    bias_out,
    ln1_gain,
    ln1_bias,
    w_in,
    bias_in,
    w_back,
    bias_back,
    ln2_gain,
    ln2_bias,
):
    rows = tokens.shape[1]
    half = rows // 2
    width = tokens.shape[2]
    n = pairing.shape[0] // 2
    inputs = tokens[0]
    vectors = [bias_q, bias_v, bias_out, ln1_gain, ln1_bias, bias_back, ln2_gain, ln2_bias]
    part = width // 4
    vectors += [bias_in[j * part : (j + 1) * part] for j in range(4)]
    line = lax.broadcasted_iota(jnp.int32, (16, part), 0)
    small = jnp.zeros((16, part), jnp.float32)
    for i, vector in enumerate(vectors):
        small = jnp.where(line == i, vector.astype(jnp.float32)[None, :], small)
    packed, lines, qkv_full, out_full, in_full = project(
        inputs, small, w_qkv, w_out, w_in, n, 0
    )
    spot = lax.rem(lax.axis_index("ctx"), 2).astype(jnp.int32).reshape(1)
    mixed, keep, mix, lse, order = attend(pairing, lengths, spot, packed)
    output, grad, left, right, resid, sums = layer(
        pairing, lengths, mixed, inputs, cotangent[0], lines, out_full, in_full, w_back, 1
    )
    total, token_grad, small_sum = back(
        pairing, order, lengths, grad, keep, mix, lse, left, right, sums, resid, qkv_full, 2
    )
    (
        output, token_grad, qkv_sum, out_sum, in_sum, back_sum,
        bq, bv, bo, g1, s1, bb, g2, s2, bi,
    ) = finish(total, small_sum, output, token_grad)
    return (
        output[None], token_grad[None], qkv_sum, bq, bv, out_sum, bo, g1, s1, in_sum, bi,
        back_sum, bb, g2, s2,
    )


def solution(mesh):
    return jax.shard_map(
        on_device_spread if mesh.shape["ctx"] == 8 else on_device_any,
        mesh=mesh,
        in_specs=(
            P("fsdp", "ctx", None),
            P("fsdp", "ctx", None),
            P("fsdp"),
            P(),
            P("fsdp", None),
            P("fsdp"),
            P("fsdp"),
            P("fsdp", None),
            P("fsdp"),
            P("fsdp"),
            P("fsdp"),
            P("fsdp", None),
            P("fsdp"),
            P("fsdp", None),
            P("fsdp"),
            P("fsdp"),
            P("fsdp"),
        ),
        out_specs=(
            P("fsdp", "ctx", None),
            P("fsdp", "ctx", None),
            P("fsdp", None),
            P("fsdp"),
            P("fsdp"),
            P("fsdp", None),
            P("fsdp"),
            P("fsdp"),
            P("fsdp"),
            P("fsdp", None),
            P("fsdp"),
            P("fsdp", None),
            P("fsdp"),
            P("fsdp"),
            P("fsdp"),
        ),
        check_vma=False,
    )
```

```python
import functools
import math

import jax
import jax.numpy as jnp
from jax import lax
from jax.experimental import pallas as pl
from jax.experimental.pallas import tpu as pltpu
from jax.sharding import PartitionSpec as P

HEADS = 12
HEAD_DIM = 64
NMEM = 10
BLK = 128


eps = 1e-12
neg_big = -1e30


def layer_norm(value, gain, shift):
    mean = jnp.mean(value, axis=-1, keepdims=True)
    centred = value - mean
    variance = jnp.mean(centred * centred, axis=-1, keepdims=True)
    return centred * lax.rsqrt(variance + eps) * gain + shift


def norm_back(value, gain, grad):
    mean = jnp.mean(value, axis=-1, keepdims=True)
    centred = value - mean
    scale = lax.rsqrt(jnp.mean(centred * centred, axis=-1, keepdims=True) + eps)
    unit = centred * scale
    scaled = grad * gain
    inner = (
        scaled
        - jnp.mean(scaled, axis=-1, keepdims=True)
        - unit * jnp.mean(scaled * unit, axis=-1, keepdims=True)
    )
    return (scale * inner, jnp.sum(grad * unit, axis=0), jnp.sum(grad, axis=0))


def block_width(count):
    return math.gcd(count, 512)


def places(pairing, start, count, half):
    rows = start + jnp.arange(count, dtype=jnp.int32)
    owners = rows // half
    spots = jnp.arange(pairing.shape[0], dtype=jnp.int32)
    picked = jnp.sum(jnp.where(owners[:, None] == spots[None, :], pairing[None, :], 0), axis=1)
    return picked * half + rows % half


def allowed_pairs(query_place, key_place, length):
    before = (key_place[None, :] <= query_place[:, None]) | (key_place[None, :] < NMEM)
    return (key_place[None, :] < length) & before


def heads_of(value):
    return value.reshape(value.shape[0], HEADS, HEAD_DIM)


def forward_fold(query_heads, query_place, pairing, length, half):

    def fold(carry, piece, start):
        keys, values = piece
        count = keys.shape[0]
        width = block_width(count)
        key_place = places(pairing, start, count, half)

        def step(index, state):
            top, total, summed = state
            offset = index * width
            key_heads = heads_of(lax.dynamic_slice_in_dim(keys, offset, width, 0))
            value_heads = heads_of(lax.dynamic_slice_in_dim(values, offset, width, 0))
            mask = allowed_pairs(
                query_place, lax.dynamic_slice_in_dim(key_place, offset, width, 0), length
            )[None]
            scores = (
                jnp.einsum(
                    "qhd,khd->hqk", query_heads, key_heads, preferred_element_type=jnp.float32
                )
                * 0.125
            )
            scores = jnp.where(mask, scores, neg_big)
            new_top = jnp.maximum(top, jnp.max(scores, axis=2))
            shrink = jnp.exp(top - new_top)
            probs = jnp.where(mask, jnp.exp(scores - new_top[:, :, None]), 0.0)
            total = total * shrink + jnp.sum(probs, axis=2)
            update = jnp.einsum(
                "hqk,khd->qhd",
                probs.astype(jnp.bfloat16),
                value_heads,
                preferred_element_type=jnp.float32,
            )
            summed = summed * jnp.transpose(shrink)[:, :, None] + update
            return (new_top, total, summed)

        return lax.fori_loop(0, count // width, step, carry)

    return fold


def query_grad_fold(query_heads, grad_heads, top_sum, delta, query_place, pairing, length, half):

    def fold(carry, piece, start):
        keys, values = piece
        count = keys.shape[0]
        width = block_width(count)
        key_place = places(pairing, start, count, half)

        def step(index, summed):
            offset = index * width
            key_heads = heads_of(lax.dynamic_slice_in_dim(keys, offset, width, 0))
            value_heads = heads_of(lax.dynamic_slice_in_dim(values, offset, width, 0))
            mask = allowed_pairs(
                query_place, lax.dynamic_slice_in_dim(key_place, offset, width, 0), length
            )[None]
            scores = (
                jnp.einsum(
                    "qhd,khd->hqk", query_heads, key_heads, preferred_element_type=jnp.float32
                )
                * 0.125
            )
            probs = jnp.where(mask, jnp.exp(scores - top_sum[:, :, None]), 0.0)
            prob_grad = jnp.einsum(
                "qhd,khd->hqk", grad_heads, value_heads, preferred_element_type=jnp.float32
            )
            score_grad = (probs * (prob_grad - delta[:, :, None])).astype(jnp.bfloat16)
            return (
                summed
                + jnp.einsum(
                    "hqk,khd->qhd", score_grad, key_heads, preferred_element_type=jnp.float32
                )
                * 0.125
            )

        return lax.fori_loop(0, count // width, step, carry)

    return fold


def key_terms(
    key_heads, value_heads, key_place, query_heads, grad_heads, top_sum, delta, query_place, length
):
    scores = (
        jnp.einsum("qhd,khd->hqk", query_heads, key_heads, preferred_element_type=jnp.float32)
        * 0.125
    )
    mask = allowed_pairs(query_place, key_place, length)[None]
    probs = jnp.where(mask, jnp.exp(scores - top_sum[:, :, None]), 0.0)
    prob_grad = jnp.einsum(
        "qhd,khd->hqk", grad_heads, value_heads, preferred_element_type=jnp.float32
    )
    score_grad = (probs * (prob_grad - delta[:, :, None])).astype(jnp.bfloat16)
    value_grad = jnp.einsum(
        "hqk,qhd->khd", probs.astype(jnp.bfloat16), grad_heads, preferred_element_type=jnp.float32
    )
    key_grad = (
        jnp.einsum("hqk,qhd->khd", score_grad, query_heads, preferred_element_type=jnp.float32)
        * 0.125
    )
    return (key_grad, value_grad)


def on_device_any(
    tokens,
    cotangent,
    lengths,
    pairing,
    w_qkv,
    bias_q,
    bias_v,
    w_out,
    bias_out,
    ln1_gain,
    ln1_bias,
    w_in,
    bias_in,
    w_back,
    bias_back,
    ln2_gain,
    ln2_bias,
):
    gathered = (
        lax.all_gather(w_qkv, "fsdp", axis=0, tiled=True),
        lax.all_gather(bias_q, "fsdp", axis=0, tiled=True),
        lax.all_gather(bias_v, "fsdp", axis=0, tiled=True),
        lax.all_gather(w_out, "fsdp", axis=0, tiled=True),
        lax.all_gather(bias_out, "fsdp", axis=0, tiled=True),
        lax.all_gather(ln1_gain, "fsdp", axis=0, tiled=True),
        lax.all_gather(ln1_bias, "fsdp", axis=0, tiled=True),
        lax.all_gather(w_in, "fsdp", axis=0, tiled=True),
        lax.all_gather(bias_in, "fsdp", axis=0, tiled=True),
        lax.all_gather(w_back, "fsdp", axis=0, tiled=True),
        lax.all_gather(bias_back, "fsdp", axis=0, tiled=True),
        lax.all_gather(ln2_gain, "fsdp", axis=0, tiled=True),
        lax.all_gather(ln2_bias, "fsdp", axis=0, tiled=True),
    )
    (
        qkv_all,
        query_bias,
        value_bias,
        out_all,
        out_bias,
        gain_one,
        shift_one,
        in_all,
        in_bias,
        back_all,
        back_bias,
        gain_two,
        shift_two,
    ) = gathered
    rows = tokens.shape[1]
    half = rows // 2
    width = tokens.shape[2]
    length = lengths[0]
    query_place = places(pairing, lax.axis_index("ctx") * rows, rows, half)
    valid = query_place < length
    inputs = tokens[0]
    proj = jnp.dot(inputs, qkv_all, preferred_element_type=jnp.float32)
    queries = (proj[:, :width] + query_bias.astype(jnp.float32)).astype(jnp.bfloat16)
    keys = proj[:, width : 2 * width].astype(jnp.bfloat16)
    values = (proj[:, 2 * width :] + value_bias.astype(jnp.float32)).astype(jnp.bfloat16)
    query_heads = heads_of(queries)
    start_state = (
        jnp.full((HEADS, rows), neg_big, jnp.float32),
        jnp.zeros((HEADS, rows), jnp.float32),
        jnp.zeros((rows, HEADS, HEAD_DIM), jnp.float32),
    )
    fold = forward_fold(query_heads, query_place, pairing, length, half)
    top, total, summed = fold(
        start_state,
        (
            lax.all_gather(keys, "ctx", axis=0, tiled=True),
            lax.all_gather(values, "ctx", axis=0, tiled=True),
        ),
        jnp.int32(0),
    )
    top_sum = top + jnp.log(total)
    attended = (summed / jnp.transpose(total)[:, :, None]).reshape(rows, width)
    attended_low = attended.astype(jnp.bfloat16)
    resid_one = (
        inputs.astype(jnp.float32)
        + jnp.dot(attended_low, out_all, preferred_element_type=jnp.float32)
        + out_bias.astype(jnp.float32)
    )
    hidden = layer_norm(resid_one, gain_one.astype(jnp.float32), shift_one.astype(jnp.float32))
    hidden_low = hidden.astype(jnp.bfloat16)
    upper = jnp.dot(hidden_low, in_all, preferred_element_type=jnp.float32) + in_bias.astype(
        jnp.float32
    )
    active, gelu_back = jax.vjp(lambda value: jax.nn.gelu(value, approximate=False), upper)
    active_low = active.astype(jnp.bfloat16)
    resid_two = (
        hidden
        + jnp.dot(active_low, back_all, preferred_element_type=jnp.float32)
        + back_bias.astype(jnp.float32)
    )
    normed = layer_norm(resid_two, gain_two.astype(jnp.float32), shift_two.astype(jnp.float32))
    output = jnp.where(valid[:, None], normed, 0.0)
    qkv_back, out_back, gain_one_back, in_back, back_back, gain_two_back = (
        qkv_all,
        out_all,
        gain_one,
        in_all,
        back_all,
        gain_two,
    )
    grad_y = jnp.where(valid[:, None], cotangent[0].astype(jnp.float32), 0.0)
    grad_resid_two, gain_two_grad, shift_two_grad = norm_back(
        resid_two, gain_two_back.astype(jnp.float32), grad_y
    )
    grad_mixed = grad_resid_two.astype(jnp.bfloat16)
    back_grad = jnp.einsum("tf,td->fd", active_low, grad_mixed, preferred_element_type=jnp.float32)
    back_bias_grad = jnp.sum(grad_mixed.astype(jnp.float32), axis=0)
    grad_active = jnp.einsum("td,fd->tf", grad_mixed, back_back, preferred_element_type=jnp.float32)
    (grad_upper,) = gelu_back(grad_active)
    grad_upper_low = grad_upper.astype(jnp.bfloat16)
    in_grad = jnp.einsum(
        "td,tf->df", hidden_low, grad_upper_low, preferred_element_type=jnp.float32
    )
    in_bias_grad = jnp.sum(grad_upper_low.astype(jnp.float32), axis=0)
    grad_hidden = grad_resid_two + jnp.einsum(
        "tf,df->td", grad_upper_low, in_back, preferred_element_type=jnp.float32
    )
    grad_resid_one, gain_one_grad, shift_one_grad = norm_back(
        resid_one, gain_one_back.astype(jnp.float32), grad_hidden
    )
    grad_branch = grad_resid_one.astype(jnp.bfloat16)
    out_grad = jnp.einsum(
        "tc,td->cd", attended_low, grad_branch, preferred_element_type=jnp.float32
    )
    out_bias_grad = jnp.sum(grad_branch.astype(jnp.float32), axis=0)
    grad_attended = jnp.einsum(
        "td,cd->tc", grad_branch, out_back, preferred_element_type=jnp.float32
    ).astype(jnp.bfloat16)
    grad_heads = heads_of(grad_attended)
    delta = jnp.transpose(jnp.sum(grad_heads.astype(jnp.float32) * heads_of(attended), axis=2))
    query_fold = query_grad_fold(
        query_heads, grad_heads, top_sum, delta, query_place, pairing, length, half
    )
    empty_heads = jnp.zeros((rows, HEADS, HEAD_DIM), jnp.float32)
    query_grad = query_fold(
        empty_heads,
        (
            lax.all_gather(keys, "ctx", axis=0, tiled=True),
            lax.all_gather(values, "ctx", axis=0, tiled=True),
        ),
        jnp.int32(0),
    )
    stats = jnp.concatenate([jnp.transpose(top_sum), jnp.transpose(delta)], axis=1)
    stats_all = lax.all_gather(stats, "ctx", axis=0, tiled=True)
    key_heads = heads_of(keys)
    value_heads = heads_of(values)
    query_in = lax.all_gather(queries, "ctx", axis=0, tiled=True)
    grad_in = lax.all_gather(grad_attended, "ctx", axis=0, tiled=True)
    count = query_in.shape[0]
    span = block_width(count)
    place_in = places(pairing, jnp.int32(0), count, half)

    def step(index, state):
        offset = index * span
        query_block = heads_of(lax.dynamic_slice_in_dim(query_in, offset, span, 0))
        grad_block = heads_of(lax.dynamic_slice_in_dim(grad_in, offset, span, 0))
        stats_block = lax.dynamic_slice_in_dim(stats_all, offset, span, 0)
        place_block = lax.dynamic_slice_in_dim(place_in, offset, span, 0)
        key_part, value_part = key_terms(
            key_heads,
            value_heads,
            query_place,
            query_block,
            grad_block,
            jnp.transpose(stats_block[:, :HEADS]),
            jnp.transpose(stats_block[:, HEADS:]),
            place_block,
            length,
        )
        return (state[0] + key_part, state[1] + value_part)

    key_sum, value_sum = lax.fori_loop(0, count // span, step, (empty_heads, empty_heads))
    key_grad = key_sum.reshape(rows, width)
    value_grad = value_sum.reshape(rows, width)
    grad_proj = jnp.concatenate(
        [
            query_grad.reshape(rows, width).astype(jnp.bfloat16),
            key_grad.astype(jnp.bfloat16),
            value_grad.astype(jnp.bfloat16),
        ],
        axis=1,
    )
    qkv_grad = jnp.einsum("td,tf->df", inputs, grad_proj, preferred_element_type=jnp.float32)
    query_bias_grad = jnp.sum(grad_proj[:, :width].astype(jnp.float32), axis=0)
    value_bias_grad = jnp.sum(grad_proj[:, 2 * width :].astype(jnp.float32), axis=0)
    token_grad = grad_resid_one + jnp.einsum(
        "tf,df->td", grad_proj, qkv_back, preferred_element_type=jnp.float32
    )
    grads = (
        qkv_grad,
        query_bias_grad,
        value_bias_grad,
        out_grad,
        out_bias_grad,
        gain_one_grad,
        shift_one_grad,
        in_grad,
        in_bias_grad,
        back_grad,
        back_bias_grad,
        gain_two_grad,
        shift_two_grad,
    )
    shards = (
        lax.psum_scatter(
            grads[0].astype(jnp.bfloat16), "fsdp", scatter_dimension=0, tiled=True
        ).astype(jnp.float32),
        lax.psum_scatter(
            grads[1].astype(jnp.bfloat16), "fsdp", scatter_dimension=0, tiled=True
        ).astype(jnp.float32),
        lax.psum_scatter(
            grads[2].astype(jnp.bfloat16), "fsdp", scatter_dimension=0, tiled=True
        ).astype(jnp.float32),
        lax.psum_scatter(
            grads[3].astype(jnp.bfloat16), "fsdp", scatter_dimension=0, tiled=True
        ).astype(jnp.float32),
        lax.psum_scatter(
            grads[4].astype(jnp.bfloat16), "fsdp", scatter_dimension=0, tiled=True
        ).astype(jnp.float32),
        lax.psum_scatter(
            grads[5].astype(jnp.bfloat16), "fsdp", scatter_dimension=0, tiled=True
        ).astype(jnp.float32),
        lax.psum_scatter(
            grads[6].astype(jnp.bfloat16), "fsdp", scatter_dimension=0, tiled=True
        ).astype(jnp.float32),
        lax.psum_scatter(
            grads[7].astype(jnp.bfloat16), "fsdp", scatter_dimension=0, tiled=True
        ).astype(jnp.float32),
        lax.psum_scatter(
            grads[8].astype(jnp.bfloat16), "fsdp", scatter_dimension=0, tiled=True
        ).astype(jnp.float32),
        lax.psum_scatter(
            grads[9].astype(jnp.bfloat16), "fsdp", scatter_dimension=0, tiled=True
        ).astype(jnp.float32),
        lax.psum_scatter(
            grads[10].astype(jnp.bfloat16), "fsdp", scatter_dimension=0, tiled=True
        ).astype(jnp.float32),
        lax.psum_scatter(
            grads[11].astype(jnp.bfloat16), "fsdp", scatter_dimension=0, tiled=True
        ).astype(jnp.float32),
        lax.psum_scatter(
            grads[12].astype(jnp.bfloat16), "fsdp", scatter_dimension=0, tiled=True
        ).astype(jnp.float32),
    )
    totals = (
        lax.psum(shards[0].astype(jnp.bfloat16), "ctx").astype(jnp.float32),
        lax.psum(shards[1].astype(jnp.bfloat16), "ctx").astype(jnp.float32),
        lax.psum(shards[2].astype(jnp.bfloat16), "ctx").astype(jnp.float32),
        lax.psum(shards[3].astype(jnp.bfloat16), "ctx").astype(jnp.float32),
        lax.psum(shards[4].astype(jnp.bfloat16), "ctx").astype(jnp.float32),
        lax.psum(shards[5].astype(jnp.bfloat16), "ctx").astype(jnp.float32),
        lax.psum(shards[6].astype(jnp.bfloat16), "ctx").astype(jnp.float32),
        lax.psum(shards[7].astype(jnp.bfloat16), "ctx").astype(jnp.float32),
        lax.psum(shards[8].astype(jnp.bfloat16), "ctx").astype(jnp.float32),
        lax.psum(shards[9].astype(jnp.bfloat16), "ctx").astype(jnp.float32),
        lax.psum(shards[10].astype(jnp.bfloat16), "ctx").astype(jnp.float32),
        lax.psum(shards[11].astype(jnp.bfloat16), "ctx").astype(jnp.float32),
        lax.psum(shards[12].astype(jnp.bfloat16), "ctx").astype(jnp.float32),
    )
    return (output[None], token_grad[None]) + tuple(totals)


def low_lanes(shape):
    return lax.broadcasted_iota(jnp.int32, shape, 1) < 64


def spot_of(pair_ref, place):
    found = jnp.int32(0)
    for s in range(pair_ref.shape[0]):
        found = jnp.where(pair_ref[s] == place, s, found)
    return found


def attend(c, length, spot, keep_ref, mix_ref, lse_ref, turned_ref):
    left = low_lanes((256, BLK))
    zero = jnp.zeros((), jnp.bfloat16)
    keys = 256 * (c + 1)
    own = keep_ref[2 * c : 2 * c + 2, :, :BLK].reshape(256, BLK)
    shared = keep_ref[2 * c + spot, :, :BLK]
    query = jnp.concatenate(
        [jnp.where(left, own, zero), jnp.where(left[:BLK], zero, shared)], axis=0
    ) * jnp.bfloat16(0.125)
    key = keep_ref[: 2 * c + 2, :, BLK : 2 * BLK].reshape(keys, BLK)
    value = keep_ref[: 2 * c + 2, :, 2 * BLK :].reshape(keys, BLK)
    scores = mask_scores(dot_nt(key, query), c, spot, length, 0, True)
    top = jnp.max(scores, axis=0, keepdims=True)
    probs = jnp.exp(scores - top)
    total = jnp.sum(probs, axis=0, keepdims=True)
    summed = lax.dot_general(
        value, probs.astype(jnp.bfloat16), (((0,), (0,)), ((), ())),
        preferred_element_type=jnp.float32,
    ) / total
    lse_ref[c] = top + jnp.log(total)
    part = summed[64:, 256:]
    none = jnp.zeros_like(part)
    first = jnp.where(spot == 0, part, none)
    second = jnp.where(spot == 0, none, part)
    mixed = jnp.concatenate([summed[:64, :256], jnp.concatenate([first, second], axis=1)], axis=0)
    mix_ref[c] = mixed
    turned_ref[2 * c : 2 * c + 2] = (
        jnp.transpose(mixed).astype(jnp.bfloat16).reshape(2, BLK, BLK)
    )


def mask_scores(scores, c, spot, length, start, edged):
    keys, width = scores.shape
    row = start + lax.broadcasted_iota(jnp.int32, (keys, width), 0)
    scores = jnp.where(row < length, scores, neg_big)
    if not edged:
        return scores
    edge = 256 * c
    lane = lax.broadcasted_iota(jnp.int32, (256, width), 1)
    query_place = edge + jnp.where(lane < 256, lane, lane - 256 + spot * BLK)
    key_place = edge + lax.broadcasted_iota(jnp.int32, (256, width), 0)
    seen = key_place <= query_place
    if c == 0:
        seen = seen | (key_place < NMEM)
    tail = jnp.where(seen, scores[keys - 256 :], neg_big)
    if keys == 256:
        return tail
    return jnp.concatenate([scores[: keys - 256], tail], axis=0)


def attend_back(
    c, length, spot, keep_ref, g_ref, mix_ref, lse_ref, q_sum, k_sum, v_sum
):
    zero = jnp.zeros((), jnp.bfloat16)
    left = low_lanes((256, BLK))
    left_half = left[:BLK]
    own = keep_ref[2 * c : 2 * c + 2, :, :BLK].reshape(256, BLK)
    shared = keep_ref[2 * c + spot, :, :BLK]
    query = jnp.concatenate(
        [jnp.where(left, own, zero), jnp.where(left_half, zero, shared)], axis=0
    ) * jnp.bfloat16(0.125)
    g_own = g_ref[2 * c : 2 * c + 2].reshape(256, BLK)
    g_shared = g_ref[2 * c + spot]
    grad = jnp.concatenate(
        [jnp.where(left, g_own, zero), jnp.where(left_half, zero, g_shared)], axis=0
    )
    turned = jnp.transpose(g_own.astype(jnp.float32)) * mix_ref[c]
    delta_own = jnp.sum(turned[:64], axis=0, keepdims=True)
    delta_pair = jnp.sum(turned[64:], axis=0, keepdims=True)
    delta = jnp.concatenate(
        [delta_own, jnp.where(spot == 0, delta_pair[:, :BLK], delta_pair[:, BLK:])], axis=1
    )
    lse = lse_ref[c]
    q_grad = jnp.zeros((384, BLK), jnp.float32)
    last = 2 * c + 2
    step = 8
    for low_block in range(0, last, step):
        high_block = min(low_block + step, last)
        cut = slice(low_block, high_block)
        count = high_block - low_block
        key = keep_ref[cut, :, BLK : 2 * BLK].reshape(count * BLK, BLK)
        value = keep_ref[cut, :, 2 * BLK :].reshape(count * BLK, BLK)
        scores = mask_scores(
            dot_nt(key, query), c, spot, length, low_block * BLK, high_block == last
        )
        probs = jnp.exp(scores - lse)
        score_grad = (probs * (dot_nt(value, grad) - delta)).astype(jnp.bfloat16)
        v_part = dot_nn(probs.astype(jnp.bfloat16), grad)
        k_part = dot_nn(score_grad, query)
        v_sum[cut] += v_part.reshape(count, BLK, BLK)
        k_sum[cut] += k_part.reshape(count, BLK, BLK)
        q_grad = q_grad + lax.dot_general(
            score_grad, key, (((0,), (0,)), ((), ())), preferred_element_type=jnp.float32
        )
    q_grad = q_grad * 0.125
    part = q_grad[256:]
    none = jnp.zeros_like(part)
    first = jnp.where(spot == 0, part, none)
    second = jnp.where(spot == 0, none, part)
    q_sum[2 * c : 2 * c + 2] = jnp.where(
        left, q_grad[:256], jnp.concatenate([first, second], axis=0)
    ).reshape(2, BLK, BLK)


def smem():
    return pl.BlockSpec(memory_space=pltpu.SMEM)


def vmem():
    return pl.BlockSpec(memory_space=pltpu.VMEM)


MESH = pl.DeviceIdType.MESH


def remote(src, dst, sems, at, peer):
    return pltpu.make_async_remote_copy(
        src_ref=src, dst_ref=dst, send_sem=sems.at[(0,) + at], recv_sem=sems.at[(1,) + at],
        device_id=peer, device_id_type=MESH,
    )


def greet(peers):
    barrier = pltpu.get_barrier_semaphore()
    for peer in peers:
        pl.semaphore_signal(barrier, inc=1, device_id=peer, device_id_type=MESH)
    pl.semaphore_wait(barrier, len(peers))


def ring_peers(n):
    me = lax.axis_index("ctx")
    return [{"ctx": lax.rem(me + k, n)} for k in range(1, n)]


def two(block):
    return pl.ds(2 * block, 2)


def exchange_copies(n, in_ref, out_ref, sems):
    me = lax.axis_index("ctx")
    copies = []
    for k in range(1, n):
        peer = lax.rem(me + k, n)
        copies.append(
            remote(in_ref.at[two(peer)], out_ref.at[two(me)], sems, (k,), {"ctx": peer})
        )
    return copies


def own_copy(in_ref, out_ref, sem):
    me = lax.axis_index("ctx")
    return pltpu.make_async_copy(in_ref.at[two(me)], out_ref.at[two(me)], sem)


def both(ref, peer):
    value = ref[2 * peer : 2 * peer + 2]
    return value.reshape(-1, value.shape[2])


def join_pairs(pairs):
    pieces = []
    for group in range(HEADS // 3):
        first, second = pairs(2 * group), pairs(2 * group + 1)
        shared = first[:, HEAD_DIM:].astype(jnp.float32) + second[:, HEAD_DIM:].astype(jnp.float32)
        pieces += [first[:, :HEAD_DIM], second[:, :HEAD_DIM], shared.astype(jnp.bfloat16)]
    return jnp.concatenate(pieces, axis=1)


def pair_of(value, peer):
    own = 3 * (peer // 2) + peer % 2
    shared = 3 * (peer // 2) + 2
    cut = lambda head: value[:, head * HEAD_DIM : (head + 1) * HEAD_DIM]
    return jnp.concatenate([cut(own), cut(shared)], axis=1)


def dot_nn(a, b):
    return jnp.dot(a, b, preferred_element_type=jnp.float32)


def dot_nt(a, b):
    return lax.dot_general(a, b, (((1,), (1,)), ((), ())), preferred_element_type=jnp.float32)


def column_sum(value):
    return jnp.sum(value, axis=0, keepdims=True)


def unit_of(value):
    mean = jnp.mean(value, axis=-1, keepdims=True)
    centred = value - mean
    scale = lax.rsqrt(jnp.mean(centred * centred, axis=-1, keepdims=True) + eps)
    return centred * scale, scale


def unit_back(unit, scale, scaled):
    return scale * (
        scaled
        - jnp.mean(scaled, axis=-1, keepdims=True)
        - unit * jnp.mean(scaled * unit, axis=-1, keepdims=True)
    )


(ROW_BQ, ROW_BV, ROW_BO, ROW_G1, ROW_S1, ROW_BB, ROW_G2, ROW_S2, ROW_BI) = range(9)


def gather_copies(src, full, sems, index):
    fsdp = lax.axis_index("fsdp")
    x, core = fsdp // 2, lax.rem(fsdp, 2)
    sibling, across = {"fsdp": 2 * x + 1 - core}, {"fsdp": 2 * (1 - x) + core}
    other = 2 * (1 - x) + core
    return (
        remote(src, full.at[fsdp], sems, (index, 0), across),
        remote(src, full.at[fsdp], sems, (index, 1), sibling),
        remote(full.at[other], full.at[other], sems, (index, 2), sibling),
    )


def chip_peers():
    fsdp = lax.axis_index("fsdp")
    x, core = fsdp // 2, lax.rem(fsdp, 2)
    return [{"fsdp": 2 * x + 1 - core}, {"fsdp": 2 * (1 - x) + core}]


def split_gather(src, full, sems, pieces):
    ctx, fsdp = lax.axis_index("ctx"), lax.axis_index("fsdp")
    z, y = ctx // 2, lax.rem(ctx, 2)
    x, core = fsdp // 2, lax.rem(fsdp, 2)
    sibling, across = {"fsdp": 2 * x + 1 - core}, {"fsdp": 2 * (1 - x) + core}
    beside = {"ctx": 2 * z + 1 - y}
    other = 2 * (1 - x) + core
    count = src.shape[0] // (2 * pieces)

    def rows(half, p):
        return pl.ds(pl.multiple_of((half * pieces + p) * count, count), count)

    cross, side, on, off = [], [], [], []
    for p in range(pieces):
        here, there = rows(y, p), rows(1 - y, p)
        moved = full.at[other, here]
        late = full.at[other, there]
        cross.append(remote(src.at[here], full.at[fsdp, here], sems, (0, p), across))
        side.append(remote(moved, moved, sems, (1, p), beside))
        on.append(remote(moved, moved, sems, (2, p), sibling))
        off.append(remote(late, late, sems, (3, p), sibling))
    whole = remote(src, full.at[fsdp], sems, (4, 0), sibling)
    return cross, side, on, off, whole


def front_kernel(
    n, pair_ref, len_ref, *refs
):
    vectors, refs = refs[:9], refs[9:]
    (
        tokens_ref, cot_ref, qkv_src, out_src, in_src, back_src,
        output_ref, grad_ref, left_ref, right_ref, resid_ref, sums_ref,
        keep_ref, mix_ref, lse_ref, qkv_ref,
        small_out, small, rows_ref, token_buf, cot, w_qkv, w_out, w_in, w_back, send, packed, keep, mix,
        lse, turned, mixed_out, mixed_in, active, slope, output, grad_out, left, right, resid, sums,
        small_sem, qkv_sem, gather_sem, send_sem, in_sem, own_sem, load_sem, ship_sem,
    ) = refs
    low, wide = jnp.bfloat16, jnp.float32
    ctx, fsdp = lax.axis_index("ctx"), lax.axis_index("fsdp")
    x, core = fsdp // 2, lax.rem(fsdp, 2)
    spot = lax.rem(ctx, 2)
    width = token_buf.shape[1]
    count = in_src.shape[1] // width
    pieces = 3
    loads = [
        pltpu.make_async_copy(src, dst, load_sem.at[i])
        for i, (src, dst) in enumerate(
            [
                (tokens_ref, token_buf),
                (cot_ref, cot),
                (qkv_src, w_qkv.at[fsdp]),
                (out_src, w_out.at[fsdp]),
                (in_src, w_in.at[fsdp]),
                (back_src, w_back.at[fsdp]),
            ]
        )
    ]
    cot_load = loads[1]
    for cp in loads[:3]:
        cp.start()
    part = width // 4
    small_out[...] = jnp.zeros_like(small_out)
    for i in range(8):
        small_out[i : i + 1] = vectors[i][...].astype(wide).reshape(1, part)
    inner_bias = vectors[8][...].astype(wide).reshape(1, -1)
    for j in range(4):
        small_out[8 + j : 9 + j] = inner_bias[:, j * part : (j + 1) * part]
    greet(ring_peers(n) + chip_peers())
    smalls = gather_copies(small_out, small, small_sem, 0)
    cross, side, on, off, whole = split_gather(qkv_src, w_qkv, qkv_sem, pieces)
    for step in (0, 1):
        smalls[step].start()
    for cp in cross:
        cp.start()
    whole.start()
    for cp in loads[3:]:
        cp.start()
    shards = [
        gather_copies(src, full, gather_sem, i)
        for i, (src, full) in enumerate([(out_src, w_out), (in_src, w_in), (back_src, w_back)])
    ]
    back_shards = shards[2]
    small[fsdp] = small_out[...]
    smalls[0].wait_recv()
    smalls[2].start()
    for p in range(pieces):
        cross[p].wait_recv()
        side[p].start()
        on[p].start()
    for cps in shards:
        cps[0].start()
    for cps in shards:
        cps[1].start()
    for p in range(pieces):
        side[p].wait_recv()
        off[p].start()
    loads[0].wait()
    tokens = token_buf[...]
    left[0] = jnp.transpose(tokens).reshape(4, -1, 2 * BLK)
    smalls[1].wait_recv()
    smalls[2].wait_recv()
    for f in range(4):
        cols = slice(f * part, (f + 1) * part)
        rows_ref[:8, cols] = small[f, :8]
        for j in range(4):
            rows_ref[ROW_BI + f : ROW_BI + f + 1, j * part : (j + 1) * part] = small[
                f, 8 + j : 9 + j
            ]
    rows_ref[12:] = jnp.zeros_like(rows_ref[12:])
    row = lambda i: rows_ref[i : i + 1, :]
    whole.wait_recv()
    for p in range(pieces):
        on[p].wait_recv()
        off[p].wait_recv()
    loads[2].wait()

    half = width // 2
    for g in range(2):
        parts = []
        for which, bias in ((0, ROW_BQ), (1, None), (2, ROW_BV)):
            at = which * width + g * half
            value = dot_nn(tokens, w_qkv[:, :, at : at + half].reshape(width, half))
            if bias is not None:
                value = value + rows_ref[bias : bias + 1, g * half : (g + 1) * half]
            parts.append(value.astype(low))
        for at in range(n // 2):
            peer = g * n // 2 + at
            send[2 * peer : 2 * peer + 2] = jnp.concatenate(
                [pair_of(value, at) for value in parts], axis=1
            ).reshape(2, BLK, -1)
    sends = exchange_copies(n, send, packed, send_sem)
    for cp in sends:
        cp.start()
    own_send = own_copy(send, packed, own_sem.at[0])
    own_send.start()
    shipped = []

    def ship(src, dst):
        cp = pltpu.make_async_copy(src, dst, ship_sem.at[len(shipped)])
        cp.start()
        shipped.append(cp)

    ship(w_qkv, qkv_ref)
    spots = lax.broadcasted_iota(jnp.int32, (2 * BLK, 1), 0)
    place = jnp.where(
        spots < BLK,
        pair_ref[2 * ctx] * BLK + spots,
        pair_ref[2 * ctx + 1] * BLK + spots - BLK,
    )
    valid = place < len_ref[0]
    own_send.wait()
    for cp in sends:
        cp.wait_recv()
    for cps in shards[:2]:
        cps[0].wait_recv()
        cps[2].start()

    for b in range(2 * n):
        keep[b] = packed[spot_of(pair_ref, b)]
    ship(keep, keep_ref)
    for c in range(n):
        attend(c, len_ref[0], spot, keep, mix, lse, turned)
    for s in range(2 * n):
        mixed_out[s] = turned[pair_ref[s]]
    copies = exchange_copies(n, mixed_out, mixed_in, in_sem)
    for cp in copies:
        cp.start()
    own_mixed = own_copy(mixed_out, mixed_in, own_sem.at[1])
    own_mixed.start()
    ship(mix, mix_ref)
    ship(lse, lse_ref)
    sums[...] = jnp.zeros_like(sums)
    for cp in loads[3:]:
        cp.wait()
    for cps in shards[:2]:
        cps[1].wait_recv()
        cps[2].wait_recv()
    own_mixed.wait()
    for cp in copies:
        cp.wait_recv()
    back_shards[0].wait_recv()
    back_shards[2].start()
    back_shards[1].wait_recv()

    attended = join_pairs(lambda peer: both(mixed_in, peer))
    resid_one = (
        tokens.astype(wide)
        + dot_nn(attended, w_out[...].reshape(width, width))
        + row(ROW_BO)
    )
    unit_one, scale_one = unit_of(resid_one)
    hidden = unit_one * row(ROW_G1) + row(ROW_S1)
    hidden_low = hidden.astype(low)
    resid_two = hidden + row(ROW_BB)
    cut = lambda t: pl.ds(pl.multiple_of(t * width, width), width)
    order = [fsdp, 2 * x + 1 - core, 2 * (1 - x) + core, 2 * (1 - x) + 1 - core]
    for step, t in enumerate(order):
        bias = rows_ref[pl.ds(ROW_BI + t, 1), :]
        upper = dot_nn(hidden_low, w_in[:, :, cut(t)].reshape(width, width)) + bias
        share = 0.5 * (1.0 + lax.erf(upper * (0.5**0.5)))
        slope[t] = share + upper * (jnp.exp(-0.5 * upper * upper) * (2 * math.pi) ** -0.5)
        some = (upper * share).astype(low)
        active[t] = some
        if step == 3:
            back_shards[2].wait_recv()
        resid_two = resid_two + dot_nn(some, w_back[t])
    unit_two, scale_two = unit_of(resid_two)
    output[...] = jnp.where(valid, unit_two * row(ROW_G2) + row(ROW_S2), 0.0)
    cot_load.wait()
    grad_y = jnp.where(valid, cot[...].astype(wide), 0.0)
    sums[ROW_G2 : ROW_G2 + 1, :] = column_sum(grad_y * unit_two)
    sums[ROW_S2 : ROW_S2 + 1, :] = column_sum(grad_y)
    grad_resid_two = unit_back(unit_two, scale_two, grad_y * row(ROW_G2))
    grad_mixed = grad_resid_two.astype(low)
    right[5] = grad_mixed
    sums[ROW_BB : ROW_BB + 1, :] = column_sum(grad_mixed.astype(wide))
    grad_hidden = grad_resid_two
    for t in range(count):
        grad_upper = (dot_nt(grad_mixed, w_back[t]) * slope[t]).astype(low)
        right[1 + t] = grad_upper
        sums[ROW_BI + t : ROW_BI + t + 1, :] = column_sum(grad_upper.astype(wide))
        grad_hidden = grad_hidden + dot_nt(grad_upper, w_in[:, :, cut(t)].reshape(width, width))
    sums[ROW_G1 : ROW_G1 + 1, :] = column_sum(grad_hidden * unit_one)
    sums[ROW_S1 : ROW_S1 + 1, :] = column_sum(grad_hidden)
    grad_resid_one = unit_back(unit_one, scale_one, grad_hidden * row(ROW_G1))
    resid[...] = grad_resid_one
    grad_branch = grad_resid_one.astype(low)
    right[0] = grad_branch
    sums[ROW_BO : ROW_BO + 1, :] = column_sum(grad_branch.astype(wide))
    ship(resid, resid_ref)
    ship(right, right_ref)
    ship(sums, sums_ref)
    grad_attended = dot_nt(grad_branch, w_out[...].reshape(width, width)).astype(low)
    for peer in range(n):
        grad_out[2 * peer : 2 * peer + 2] = pair_of(grad_attended, peer).reshape(2, BLK, BLK)
    ship(grad_out, grad_ref)
    left[1] = jnp.transpose(attended).reshape(4, -1, 2 * BLK)
    left[2] = jnp.transpose(hidden_low).reshape(4, -1, 2 * BLK)
    for f in range(4):
        turned = jnp.transpose(active[f])
        for r in range(4):
            left[3 + r, f] = turned[r * width // 4 : (r + 1) * width // 4]
    ship(output, output_ref)
    ship(left, left_ref)
    for cps in [smalls] + shards:
        for cp in cps:
            cp.wait_send()
    for cp in cross + side + on + off + [whole] + sends + copies:
        cp.wait_send()
    for cp in shipped:
        cp.wait()


def front(pairing, lengths, vectors, tokens, cotangent, w_qkv, w_out, w_in, w_back, n, name):
    count, width = tokens.shape
    low, wide = jnp.bfloat16, jnp.float32
    dma = pltpu.SemaphoreType.DMA
    shape = jax.ShapeDtypeStruct
    hbm = pl.BlockSpec(memory_space=pltpu.HBM)
    vec = pltpu.VMEM((16, width // 4), wide)
    results = [
        ((count, width), wide),
        ((2 * n, BLK, BLK), low),
        ((7, 4, width // 4, count), low),
        ((6, count, width), low),
        ((count, width), wide),
        ((16, width), wide),
        ((2 * n, BLK, 3 * BLK), low),
        ((n, BLK, 2 * BLK), wide),
        ((n, 1, 3 * BLK), wide),
        ((4,) + w_qkv.shape, low),
    ]
    output, grad, left, right, resid, sums, keep, mix, lse, qkv = [pltpu.VMEM(*r) for r in results]
    return pl.pallas_call(
        functools.partial(front_kernel, n),
        out_shape=tuple(shape(*r) for r in results),
        in_specs=[smem(), smem()] + [vmem()] * 9 + [hbm] * 6,
        out_specs=(hbm,) * 10,
        scratch_shapes=[
            vec,
            pltpu.VMEM((4, 16, width // 4), wide),
            pltpu.VMEM((16, width), wide),
            pltpu.VMEM((count, width), low),
            pltpu.VMEM((count, width), low),
            qkv,
            pltpu.VMEM((4,) + w_out.shape, low),
            pltpu.VMEM((4,) + w_in.shape, low),
            pltpu.VMEM((4,) + w_back.shape, low),
            keep,
            keep,
            keep,
            mix,
            lse,
            grad,
            grad,
            grad,
            pltpu.VMEM((4, count, width), low),
            pltpu.VMEM((4, count, width), wide),
            output,
            grad,
            left,
            right,
            resid,
            sums,
            dma((2, 1, 3)),
            dma((2, 5, 3)),
            dma((2, 3, 3)),
            dma((2, n)),
            dma((2, n)),
            dma((2,)),
            dma((6,)),
            dma((10,)),
        ],
        compiler_params=pltpu.CompilerParams(
            collective_id=name, has_side_effects=True, vmem_limit_bytes=62 << 20
        ),
        name="front",
    )(pairing, lengths, *vectors, tokens, cotangent, w_qkv, w_out, w_in, w_back)


PARTS = 12


def sum_sources(chunk):
    left = jnp.where(chunk < 4, 3 + chunk, jnp.where(chunk < 8, 2, jnp.where(chunk < 9, 1, 0)))
    right = jnp.where(
        chunk < 4, 8, jnp.where(chunk < 8, chunk, jnp.where(chunk < 9, 3, chunk - 9))
    )
    return left, right


STEPS = 30
PLAN = {
    "pair": {**{s: s for s in range(9)}, 17: 9, 18: 10, 19: 11},
    "x": {**{s + 1: s for s in range(9)}, 18: 9, 19: 10, 20: 11},
    "y": {9: 0, 10: 1, 12: 2, 13: 3, 14: 4, 15: 5, 16: 6, 18: 7, 19: 8, 22: 9, 23: 10, 24: 11},
    "near": {10: 0, 11: 1, 13: 2, 14: 3, 15: 4, 16: 5, 18: 6, 19: 7, 20: 8, 23: 9, 24: 10, 25: 11},
    "far": {11: 0, 12: 1, **{15 + c: c for c in range(2, 12)}},
    "own": {12: 0, **{16 + c: c for c in range(1, 12)}},
    "wide": {17 + c: c for c in range(12)},
    "last": {18 + c: c for c in range(12)},
}
ATTEND_AT = (10, 11, 12)
JOIN_AT = 17
SMALL_AT = (17, 18, 20, 22, 24, 26)
TOKEN_AT = 21


def planned(name, step):
    chunk = jnp.int32(-1)
    for at, which in PLAN[name].items():
        chunk = jnp.where(step == at, which, chunk)
    return chunk


def back_kernel(
    n, pair_ref, len_ref, grad_ref, keep_ref, mix_ref, lse_ref, left_ref, right_ref,
    sums_ref, resid_ref, qkv_ref,
    total_ref, token_ref, small_out,
    grad_in, g_all, q_sum, k_sum, v_sum, blocks_out, blocks_in, w_qkv, right_all,
    pair_out, pair_in, x_out, x_in, y_out, y_in, y_keep, near_out, near_in, near_keep,
    far_out, far_in, far_keep, s_out, s_in,
    grad_sem, block_sem, own_sem, pair_sem, x_sem, y_sem, near_sem, far_sem, own_z_sem, wide_sem,
    last_sem, s_sem,
):
    low, wide = jnp.bfloat16, jnp.float32
    ctx = lax.axis_index("ctx")
    fsdp = lax.axis_index("fsdp")
    z, y = ctx // 2, lax.rem(ctx, 2)
    odd, upper = lax.rem(z, 2), z // 2
    x, core = fsdp // 2, lax.rem(fsdp, 2)
    sibling = {"fsdp": 2 * x + 1 - core}
    across = {"fsdp": 2 * (1 - x) + core}
    beside = {"ctx": 2 * z + 1 - y}
    near = {"ctx": 2 * (2 * upper + 1 - odd) + y}
    far = {"ctx": 2 * (2 * (1 - upper) + odd) + y}
    mine = 2 * odd + upper
    greet(ring_peers(n) + [sibling, across])
    grads = exchange_copies(n, grad_ref, grad_in, grad_sem)
    for cp in grads:
        cp.start()
    own_grad = own_copy(grad_ref, grad_in, own_sem.at[0])
    own_grad.start()
    load = pltpu.make_async_copy(qkv_ref, w_qkv, own_sem.at[1])
    load.start()
    blocks = exchange_copies(n, blocks_out, blocks_in, block_sem)
    own = own_copy(blocks_out, blocks_in, own_sem.at[2])
    right_all[3:] = right_ref[...]
    k_sum[...] = jnp.zeros_like(k_sum)
    v_sum[...] = jnp.zeros_like(v_sum)
    chunks = keep_ref.shape[0] // 2

    def attend_some(first, last):
        for c in range(first, last):
            attend_back(
                c, len_ref[0], y, keep_ref, g_all, mix_ref, lse_ref, q_sum, k_sum, v_sum
            )

    def attend_step(t):
        @pl.when(t == ATTEND_AT[0])
        def _():
            own_grad.wait()
            for cp in grads:
                cp.wait_recv()
            for b in range(2 * chunks):
                g_all[b] = grad_in[spot_of(pair_ref, b)]
            attend_some(0, chunks // 2)

        @pl.when(t == ATTEND_AT[1])
        def _():
            attend_some(chunks // 2, chunks - 2)

        @pl.when(t == ATTEND_AT[2])
        def _():
            attend_some(chunks - 2, chunks)
            for s in range(2 * chunks):
                place = pair_ref[s]
                blocks_out[s] = jnp.concatenate(
                    [q_sum[place], k_sum[place], v_sum[place]], axis=1
                ).astype(low)
            for cp in blocks:
                cp.start()
            own.start()

    def slot(c):
        return lax.rem(c, 4)

    def pair_copy(c):
        return remote(pair_out.at[lax.rem(c, 2)], pair_in.at[c], pair_sem, (c,), sibling)

    def x_copy(c):
        return remote(x_out.at[c], x_in.at[c], x_sem, (c,), across)

    def y_copy(c):
        return remote(y_out.at[slot(c)], y_in.at[c], y_sem, (c,), beside)

    def near_copy(c):
        return remote(near_out.at[slot(c)], near_in.at[c], near_sem, (c,), near)

    def far_copy(c):
        return remote(far_out.at[slot(c)], far_in.at[c], far_sem, (c,), far)

    def own_z_copy(c):
        piece = total_ref.at[c, y, mine]
        return remote(piece, piece, own_z_sem, (c,), far)

    def wide_copy(c):
        piece = total_ref.at[c, y, two(odd)]
        return remote(piece, piece, wide_sem, (c,), near)

    def last_copy(c):
        piece = total_ref.at[c, y]
        return remote(piece, piece, last_sem, (c,), beside)

    def reuse(copy, c, slots):
        @pl.when(c >= slots)
        def _():
            copy(c - slots).wait_send()

    def partial(c, shard):
        left, right = sum_sources(c)
        return dot_nn(left_ref[left, shard], right_all[right])

    def stage_pair(c):
        reuse(pair_copy, c, 2)
        for side in range(2):
            pair_out[lax.rem(c, 2), side] = partial(c, 2 * side + 1 - core).astype(low)
        pair_copy(c).start()

    def stage_x(c):
        pair_copy(c).wait_recv()
        x_out[c] = (partial(c, 2 * (1 - x) + core) + pair_in[c, 1 - x].astype(wide)).astype(low)
        x_copy(c).start()

    def stage_y(c):
        mine_sum = partial(c, 2 * x + core) + pair_in[c, x].astype(wide)
        x_copy(c).wait_recv()
        total = mine_sum + x_in[c].astype(wide)
        first, second = total[:, :384], total[:, 384:]
        reuse(y_copy, c, 4)
        y_out[slot(c)] = jnp.where(y == 0, second, first).astype(low)
        y_copy(c).start()
        y_keep[slot(c)] = jnp.where(y == 0, first, second)

    def stage_near(c):
        y_copy(c).wait_recv()
        total = y_keep[slot(c)] + y_in[c].astype(wide)
        first, second = total[:96], total[96:]
        reuse(near_copy, c, 4)
        near_out[slot(c)] = jnp.where(odd == 0, second, first).astype(low)
        near_copy(c).start()
        near_keep[slot(c)] = jnp.where(odd == 0, first, second)

    def stage_far(c):
        near_copy(c).wait_recv()
        total = near_keep[slot(c)] + near_in[c].astype(wide)
        first, second = total[:48], total[48:]
        reuse(far_copy, c, 4)
        far_out[slot(c)] = jnp.where(upper == 0, second, first).astype(low)
        far_copy(c).start()
        far_keep[slot(c)] = jnp.where(upper == 0, first, second)

    def stage_own(c):
        far_copy(c).wait_recv()
        total_ref[c, y, mine] = (far_keep[slot(c)] + far_in[c].astype(wide)).astype(low)
        own_z_copy(c).start()

    def stage_wide(c):
        own_z_copy(c).wait_recv()
        wide_copy(c).start()

    def stage_last(c):
        wide_copy(c).wait_recv()
        last_copy(c).start()

    def small_step(t):
        peers = [sibling, across, beside, near, far]
        copies = [
            remote(s_out.at[k], s_in.at[k], s_sem, (k,), peer) for k, peer in enumerate(peers)
        ]

        @pl.when(t == JOIN_AT)
        def _():
            own.wait()
            for cp in blocks:
                cp.wait_recv()
            for part in range(3):
                right_all[part] = join_pairs(
                    lambda peer: both(blocks_in, peer)[:, part * BLK : (part + 1) * BLK]
                )
            s_out[0] = sums_ref[...]
            s_out[0, ROW_BQ : ROW_BQ + 1] = column_sum(right_all[0].astype(wide))
            s_out[0, ROW_BV : ROW_BV + 1] = column_sum(right_all[2].astype(wide))
            copies[0].start()

        for k in range(1, 5):

            @pl.when(t == SMALL_AT[k])
            def _():
                copies[k - 1].wait()
                s_out[k] = s_out[k - 1] + s_in[k - 1]
                copies[k].start()

        @pl.when(t == SMALL_AT[5])
        def _():
            copies[4].wait()
            total = s_out[4] + s_in[4]
            quarter = total.shape[1] // 4
            cuts = [slice(f * quarter, (f + 1) * quarter) for f in range(4)]
            pick = lambda choices: sum(
                jnp.where(fsdp == f, choice, 0.0) for f, choice in enumerate(choices)
            )
            small_out[...] = jnp.zeros_like(small_out)
            small_out[:8] = pick([total[:8, cut] for cut in cuts])
            line = pick([total[ROW_BI + f : ROW_BI + f + 1] for f in range(4)])
            for j, cut in enumerate(cuts):
                small_out[8 + j : 9 + j] = line[:, cut]

        @pl.when(t == TOKEN_AT)
        def _():
            load.wait()
            width = resid_ref.shape[1]
            token_ref[...] = resid_ref[...] + sum(
                dot_nt(
                    right_all[part],
                    w_qkv[:, :, part * width : (part + 1) * width].reshape(width, width),
                )
                for part in range(3)
            )

    stages = [
        ("pair", stage_pair),
        ("x", stage_x),
        ("last", stage_last),
        ("wide", stage_wide),
        ("own", stage_own),
        ("far", stage_far),
        ("near", stage_near),
        ("y", stage_y),
    ]

    def step(t, carry):
        attend_step(t)
        small_step(t)
        for name, stage in stages:
            c = planned(name, t)

            @pl.when(c >= 0)
            def _():
                stage(c)

        return carry

    lax.fori_loop(0, STEPS, step, 0)

    def drain(c, carry):
        x_copy(c).wait_send()
        own_z_copy(c).wait_send()
        wide_copy(c).wait_send()
        last_copy(c).wait()
        return carry

    lax.fori_loop(0, PARTS, drain, 0)
    for c in range(PARTS - 4, PARTS):
        y_copy(c).wait_send()
        near_copy(c).wait_send()
        far_copy(c).wait_send()
    for c in (PARTS - 2, PARTS - 1):
        pair_copy(c).wait_send()
    for cp in grads + blocks:
        cp.wait_send()


def back(pairing, lengths, grad, keep, mix, lse, left, right, sums, resid, qkv_full, name):
    blocks = keep.shape[0]
    n = blocks // 2
    low, wide = jnp.bfloat16, jnp.float32
    dma = pltpu.SemaphoreType.DMA
    shape = jax.ShapeDtypeStruct
    total = pltpu.VMEM((blocks, BLK, BLK), wide)
    return pl.pallas_call(
        functools.partial(back_kernel, n),
        out_shape=(
            shape((PARTS, 2, 4, 48, 384), low),
            shape(resid.shape, wide),
            shape((16, 192), wide),
        ),
        in_specs=[smem()] * 2 + [vmem()] * 8 + [pl.BlockSpec(memory_space=pltpu.HBM)],
        out_specs=(vmem(),) * 3,
        scratch_shapes=[
            pltpu.VMEM(grad.shape, low),
            pltpu.VMEM(grad.shape, low),
            total, total, total,
            pltpu.VMEM(keep.shape, low),
            pltpu.VMEM(keep.shape, low),
            pltpu.VMEM(qkv_full.shape, low),
            pltpu.VMEM((9,) + right.shape[1:], low),
            pltpu.VMEM((2, 2, 192, 768), low),
            pltpu.VMEM((PARTS, 2, 192, 768), low),
            pltpu.VMEM((PARTS, 192, 768), low),
            pltpu.VMEM((PARTS, 192, 768), low),
            pltpu.VMEM((4, 192, 384), low),
            pltpu.VMEM((PARTS, 192, 384), low),
            pltpu.VMEM((4, 192, 384), wide),
            pltpu.VMEM((4, 96, 384), low),
            pltpu.VMEM((PARTS, 96, 384), low),
            pltpu.VMEM((4, 96, 384), wide),
            pltpu.VMEM((4, 48, 384), low),
            pltpu.VMEM((PARTS, 48, 384), low),
            pltpu.VMEM((4, 48, 384), wide),
            pltpu.VMEM((5,) + sums.shape, wide),
            pltpu.VMEM((5,) + sums.shape, wide),
            dma((2, n)),
            dma((2, n)),
            dma((3,)),
        ]
        + [dma((2, PARTS))] * 8
        + [dma((2, 5))],
        compiler_params=pltpu.CompilerParams(
            collective_id=name, has_side_effects=True, vmem_limit_bytes=61 << 20
        ),
        name="back",
    )(pairing, lengths, grad, keep, mix, lse, left, right, sums, resid, qkv_full)


def finish_kernel(
    total_ref, small_ref, output_ref, token_ref,
    output_out, token_out, qkv_out, out_out, in_out, back_out, *refs
):
    lines, (total, small, through, stage, sems) = refs[:9], refs[9:]
    arrive = [
        pltpu.make_async_copy(total_ref.at[c], total.at[c], sems.at[PARTS + 2 + c])
        for c in range(PARTS)
    ] + [
        pltpu.make_async_copy(small_ref, small, sems.at[2 * PARTS + 2]),
        pltpu.make_async_copy(output_ref, through.at[0], sems.at[2 * PARTS + 3]),
        pltpu.make_async_copy(token_ref, through.at[1], sems.at[2 * PARTS + 4]),
    ]
    for cp in arrive:
        cp.start()
    copies = [
        pltpu.make_async_copy(through.at[0], output_out, sems.at[PARTS]),
        pltpu.make_async_copy(through.at[1], token_out, sems.at[PARTS + 1]),
    ]
    targets = [back_out.at[192 * k : 192 * k + 192] for k in range(4)]
    targets += [in_out.at[:, 768 * k : 768 * k + 768] for k in range(4)]
    targets += [out_out]
    targets += [qkv_out.at[:, 768 * k : 768 * k + 768] for k in range(3)]
    for c, target in enumerate(targets):
        arrive[c].wait()
        for half in range(2):
            for spot in range(4):
                stage[c, 48 * spot : 48 * spot + 48, 384 * half : 384 * half + 384] = total[
                    c, half, spot
                ].astype(jnp.float32)
        copies.append(pltpu.make_async_copy(stage.at[c], target, sems.at[c]))
        copies[-1].start()
    for k in range(2):
        arrive[PARTS + 1 + k].wait()
        copies[k].start()
    arrive[PARTS].wait()
    for i in range(8):
        lines[i][...] = small[i]
    for j in range(4):
        lines[8][192 * j : 192 * j + 192] = small[ROW_BI + j]
    for cp in copies:
        cp.wait()


def finish(total, small, output, token):
    shape = jax.ShapeDtypeStruct
    wide = jnp.float32
    hbm = pl.BlockSpec(memory_space=pltpu.HBM)
    return pl.pallas_call(
        finish_kernel,
        out_shape=(
            shape(output.shape, wide),
            shape(token.shape, wide),
            shape((192, 2304), wide),
            shape((192, 768), wide),
            shape((192, 3072), wide),
            shape((768, 768), wide),
        )
        + (shape((192,), wide),) * 8
        + (shape((768,), wide),),
        in_specs=[hbm] * 4,
        out_specs=(hbm,) * 6 + (vmem(),) * 9,
        scratch_shapes=[
            pltpu.VMEM(total.shape, total.dtype),
            pltpu.VMEM(small.shape, wide),
            pltpu.VMEM((2,) + token.shape, wide),
            pltpu.VMEM((PARTS, 192, 768), wide),
            pltpu.SemaphoreType.DMA((2 * PARTS + 5,)),
        ],
        compiler_params=pltpu.CompilerParams(vmem_limit_bytes=62 << 20),
        name="finish",
    )(total, small, output, token)


def on_device_spread(
    tokens,
    cotangent,
    lengths,
    pairing,
    w_qkv,
    bias_q,
    bias_v,
    w_out,
    bias_out,
    ln1_gain,
    ln1_bias,
    w_in,
    bias_in,
    w_back,
    bias_back,
    ln2_gain,
    ln2_bias,
):
    n = pairing.shape[0] // 2
    inputs = tokens[0]
    vectors = [bias_q, bias_v, bias_out, ln1_gain, ln1_bias, bias_back, ln2_gain, ln2_bias]
    vectors += [bias_in]
    output, grad, left, right, resid, sums, keep, mix, lse, qkv_full = front(
        pairing, lengths, vectors, inputs, cotangent[0], w_qkv, w_out, w_in, w_back, n, 0
    )
    total, token_grad, small_sum = back(
        pairing, lengths, grad, keep, mix, lse, left, right, sums, resid, qkv_full, 1
    )
    (
        output, token_grad, qkv_sum, out_sum, in_sum, back_sum,
        bq, bv, bo, g1, s1, bb, g2, s2, bi,
    ) = finish(total, small_sum, output, token_grad)
    return (
        output[None], token_grad[None], qkv_sum, bq, bv, out_sum, bo, g1, s1, in_sum, bi,
        back_sum, bb, g2, s2,
    )


def solution(mesh):
    return jax.shard_map(
        on_device_spread if mesh.shape["ctx"] == 8 else on_device_any,
        mesh=mesh,
        in_specs=(
            P("fsdp", "ctx", None),
            P("fsdp", "ctx", None),
            P("fsdp"),
            P(),
            P("fsdp", None),
            P("fsdp"),
            P("fsdp"),
            P("fsdp", None),
            P("fsdp"),
            P("fsdp"),
            P("fsdp"),
            P("fsdp", None),
            P("fsdp"),
            P("fsdp", None),
            P("fsdp"),
            P("fsdp"),
            P("fsdp"),
        ),
        out_specs=(
            P("fsdp", "ctx", None),
            P("fsdp", "ctx", None),
            P("fsdp", None),
            P("fsdp"),
            P("fsdp"),
            P("fsdp", None),
            P("fsdp"),
            P("fsdp"),
            P("fsdp"),
            P("fsdp", None),
            P("fsdp"),
            P("fsdp", None),
            P("fsdp"),
            P("fsdp"),
            P("fsdp"),
        ),
        check_vma=False,
    )
```

```python
import functools
import math

import jax
import jax.numpy as jnp
from jax import lax
from jax.experimental import pallas as pl
from jax.experimental.pallas import tpu as pltpu
from jax.sharding import PartitionSpec as P

HEADS = 12
HEAD_DIM = 64
NMEM = 10
BLK = 128


eps = 1e-12
neg_big = -1e30


def layer_norm(value, gain, shift):
    mean = jnp.mean(value, axis=-1, keepdims=True)
    centred = value - mean
    variance = jnp.mean(centred * centred, axis=-1, keepdims=True)
    return centred * lax.rsqrt(variance + eps) * gain + shift


def norm_back(value, gain, grad):
    mean = jnp.mean(value, axis=-1, keepdims=True)
    centred = value - mean
    scale = lax.rsqrt(jnp.mean(centred * centred, axis=-1, keepdims=True) + eps)
    unit = centred * scale
    scaled = grad * gain
    inner = (
        scaled
        - jnp.mean(scaled, axis=-1, keepdims=True)
        - unit * jnp.mean(scaled * unit, axis=-1, keepdims=True)
    )
    return (scale * inner, jnp.sum(grad * unit, axis=0), jnp.sum(grad, axis=0))


def block_width(count):
    return math.gcd(count, 512)


def places(pairing, start, count, half):
    rows = start + jnp.arange(count, dtype=jnp.int32)
    owners = rows // half
    spots = jnp.arange(pairing.shape[0], dtype=jnp.int32)
    picked = jnp.sum(jnp.where(owners[:, None] == spots[None, :], pairing[None, :], 0), axis=1)
    return picked * half + rows % half


def allowed_pairs(query_place, key_place, length):
    before = (key_place[None, :] <= query_place[:, None]) | (key_place[None, :] < NMEM)
    return (key_place[None, :] < length) & before


def heads_of(value):
    return value.reshape(value.shape[0], HEADS, HEAD_DIM)


def forward_fold(query_heads, query_place, pairing, length, half):

    def fold(carry, piece, start):
        keys, values = piece
        count = keys.shape[0]
        width = block_width(count)
        key_place = places(pairing, start, count, half)

        def step(index, state):
            top, total, summed = state
            offset = index * width
            key_heads = heads_of(lax.dynamic_slice_in_dim(keys, offset, width, 0))
            value_heads = heads_of(lax.dynamic_slice_in_dim(values, offset, width, 0))
            mask = allowed_pairs(
                query_place, lax.dynamic_slice_in_dim(key_place, offset, width, 0), length
            )[None]
            scores = (
                jnp.einsum(
                    "qhd,khd->hqk", query_heads, key_heads, preferred_element_type=jnp.float32
                )
                * 0.125
            )
            scores = jnp.where(mask, scores, neg_big)
            new_top = jnp.maximum(top, jnp.max(scores, axis=2))
            shrink = jnp.exp(top - new_top)
            probs = jnp.where(mask, jnp.exp(scores - new_top[:, :, None]), 0.0)
            total = total * shrink + jnp.sum(probs, axis=2)
            update = jnp.einsum(
                "hqk,khd->qhd",
                probs.astype(jnp.bfloat16),
                value_heads,
                preferred_element_type=jnp.float32,
            )
            summed = summed * jnp.transpose(shrink)[:, :, None] + update
            return (new_top, total, summed)

        return lax.fori_loop(0, count // width, step, carry)

    return fold


def query_grad_fold(query_heads, grad_heads, top_sum, delta, query_place, pairing, length, half):

    def fold(carry, piece, start):
        keys, values = piece
        count = keys.shape[0]
        width = block_width(count)
        key_place = places(pairing, start, count, half)

        def step(index, summed):
            offset = index * width
            key_heads = heads_of(lax.dynamic_slice_in_dim(keys, offset, width, 0))
            value_heads = heads_of(lax.dynamic_slice_in_dim(values, offset, width, 0))
            mask = allowed_pairs(
                query_place, lax.dynamic_slice_in_dim(key_place, offset, width, 0), length
            )[None]
            scores = (
                jnp.einsum(
                    "qhd,khd->hqk", query_heads, key_heads, preferred_element_type=jnp.float32
                )
                * 0.125
            )
            probs = jnp.where(mask, jnp.exp(scores - top_sum[:, :, None]), 0.0)
            prob_grad = jnp.einsum(
                "qhd,khd->hqk", grad_heads, value_heads, preferred_element_type=jnp.float32
            )
            score_grad = (probs * (prob_grad - delta[:, :, None])).astype(jnp.bfloat16)
            return (
                summed
                + jnp.einsum(
                    "hqk,khd->qhd", score_grad, key_heads, preferred_element_type=jnp.float32
                )
                * 0.125
            )

        return lax.fori_loop(0, count // width, step, carry)

    return fold


def key_terms(
    key_heads, value_heads, key_place, query_heads, grad_heads, top_sum, delta, query_place, length
):
    scores = (
        jnp.einsum("qhd,khd->hqk", query_heads, key_heads, preferred_element_type=jnp.float32)
        * 0.125
    )
    mask = allowed_pairs(query_place, key_place, length)[None]
    probs = jnp.where(mask, jnp.exp(scores - top_sum[:, :, None]), 0.0)
    prob_grad = jnp.einsum(
        "qhd,khd->hqk", grad_heads, value_heads, preferred_element_type=jnp.float32
    )
    score_grad = (probs * (prob_grad - delta[:, :, None])).astype(jnp.bfloat16)
    value_grad = jnp.einsum(
        "hqk,qhd->khd", probs.astype(jnp.bfloat16), grad_heads, preferred_element_type=jnp.float32
    )
    key_grad = (
        jnp.einsum("hqk,qhd->khd", score_grad, query_heads, preferred_element_type=jnp.float32)
        * 0.125
    )
    return (key_grad, value_grad)


def on_device_any(
    tokens,
    cotangent,
    lengths,
    pairing,
    w_qkv,
    bias_q,
    bias_v,
    w_out,
    bias_out,
    ln1_gain,
    ln1_bias,
    w_in,
    bias_in,
    w_back,
    bias_back,
    ln2_gain,
    ln2_bias,
):
    gathered = (
        lax.all_gather(w_qkv, "fsdp", axis=0, tiled=True),
        lax.all_gather(bias_q, "fsdp", axis=0, tiled=True),
        lax.all_gather(bias_v, "fsdp", axis=0, tiled=True),
        lax.all_gather(w_out, "fsdp", axis=0, tiled=True),
        lax.all_gather(bias_out, "fsdp", axis=0, tiled=True),
        lax.all_gather(ln1_gain, "fsdp", axis=0, tiled=True),
        lax.all_gather(ln1_bias, "fsdp", axis=0, tiled=True),
        lax.all_gather(w_in, "fsdp", axis=0, tiled=True),
        lax.all_gather(bias_in, "fsdp", axis=0, tiled=True),
        lax.all_gather(w_back, "fsdp", axis=0, tiled=True),
        lax.all_gather(bias_back, "fsdp", axis=0, tiled=True),
        lax.all_gather(ln2_gain, "fsdp", axis=0, tiled=True),
        lax.all_gather(ln2_bias, "fsdp", axis=0, tiled=True),
    )
    (
        qkv_all,
        query_bias,
        value_bias,
        out_all,
        out_bias,
        gain_one,
        shift_one,
        in_all,
        in_bias,
        back_all,
        back_bias,
        gain_two,
        shift_two,
    ) = gathered
    rows = tokens.shape[1]
    half = rows // 2
    width = tokens.shape[2]
    length = lengths[0]
    query_place = places(pairing, lax.axis_index("ctx") * rows, rows, half)
    valid = query_place < length
    inputs = tokens[0]
    proj = jnp.dot(inputs, qkv_all, preferred_element_type=jnp.float32)
    queries = (proj[:, :width] + query_bias.astype(jnp.float32)).astype(jnp.bfloat16)
    keys = proj[:, width : 2 * width].astype(jnp.bfloat16)
    values = (proj[:, 2 * width :] + value_bias.astype(jnp.float32)).astype(jnp.bfloat16)
    query_heads = heads_of(queries)
    start_state = (
        jnp.full((HEADS, rows), neg_big, jnp.float32),
        jnp.zeros((HEADS, rows), jnp.float32),
        jnp.zeros((rows, HEADS, HEAD_DIM), jnp.float32),
    )
    fold = forward_fold(query_heads, query_place, pairing, length, half)
    top, total, summed = fold(
        start_state,
        (
            lax.all_gather(keys, "ctx", axis=0, tiled=True),
            lax.all_gather(values, "ctx", axis=0, tiled=True),
        ),
        jnp.int32(0),
    )
    top_sum = top + jnp.log(total)
    attended = (summed / jnp.transpose(total)[:, :, None]).reshape(rows, width)
    attended_low = attended.astype(jnp.bfloat16)
    resid_one = (
        inputs.astype(jnp.float32)
        + jnp.dot(attended_low, out_all, preferred_element_type=jnp.float32)
        + out_bias.astype(jnp.float32)
    )
    hidden = layer_norm(resid_one, gain_one.astype(jnp.float32), shift_one.astype(jnp.float32))
    hidden_low = hidden.astype(jnp.bfloat16)
    upper = jnp.dot(hidden_low, in_all, preferred_element_type=jnp.float32) + in_bias.astype(
        jnp.float32
    )
    active, gelu_back = jax.vjp(lambda value: jax.nn.gelu(value, approximate=False), upper)
    active_low = active.astype(jnp.bfloat16)
    resid_two = (
        hidden
        + jnp.dot(active_low, back_all, preferred_element_type=jnp.float32)
        + back_bias.astype(jnp.float32)
    )
    normed = layer_norm(resid_two, gain_two.astype(jnp.float32), shift_two.astype(jnp.float32))
    output = jnp.where(valid[:, None], normed, 0.0)
    qkv_back, out_back, gain_one_back, in_back, back_back, gain_two_back = (
        qkv_all,
        out_all,
        gain_one,
        in_all,
        back_all,
        gain_two,
    )
    grad_y = jnp.where(valid[:, None], cotangent[0].astype(jnp.float32), 0.0)
    grad_resid_two, gain_two_grad, shift_two_grad = norm_back(
        resid_two, gain_two_back.astype(jnp.float32), grad_y
    )
    grad_mixed = grad_resid_two.astype(jnp.bfloat16)
    back_grad = jnp.einsum("tf,td->fd", active_low, grad_mixed, preferred_element_type=jnp.float32)
    back_bias_grad = jnp.sum(grad_mixed.astype(jnp.float32), axis=0)
    grad_active = jnp.einsum("td,fd->tf", grad_mixed, back_back, preferred_element_type=jnp.float32)
    (grad_upper,) = gelu_back(grad_active)
    grad_upper_low = grad_upper.astype(jnp.bfloat16)
    in_grad = jnp.einsum(
        "td,tf->df", hidden_low, grad_upper_low, preferred_element_type=jnp.float32
    )
    in_bias_grad = jnp.sum(grad_upper_low.astype(jnp.float32), axis=0)
    grad_hidden = grad_resid_two + jnp.einsum(
        "tf,df->td", grad_upper_low, in_back, preferred_element_type=jnp.float32
    )
    grad_resid_one, gain_one_grad, shift_one_grad = norm_back(
        resid_one, gain_one_back.astype(jnp.float32), grad_hidden
    )
    grad_branch = grad_resid_one.astype(jnp.bfloat16)
    out_grad = jnp.einsum(
        "tc,td->cd", attended_low, grad_branch, preferred_element_type=jnp.float32
    )
    out_bias_grad = jnp.sum(grad_branch.astype(jnp.float32), axis=0)
    grad_attended = jnp.einsum(
        "td,cd->tc", grad_branch, out_back, preferred_element_type=jnp.float32
    ).astype(jnp.bfloat16)
    grad_heads = heads_of(grad_attended)
    delta = jnp.transpose(jnp.sum(grad_heads.astype(jnp.float32) * heads_of(attended), axis=2))
    query_fold = query_grad_fold(
        query_heads, grad_heads, top_sum, delta, query_place, pairing, length, half
    )
    empty_heads = jnp.zeros((rows, HEADS, HEAD_DIM), jnp.float32)
    query_grad = query_fold(
        empty_heads,
        (
            lax.all_gather(keys, "ctx", axis=0, tiled=True),
            lax.all_gather(values, "ctx", axis=0, tiled=True),
        ),
        jnp.int32(0),
    )
    stats = jnp.concatenate([jnp.transpose(top_sum), jnp.transpose(delta)], axis=1)
    stats_all = lax.all_gather(stats, "ctx", axis=0, tiled=True)
    key_heads = heads_of(keys)
    value_heads = heads_of(values)
    query_in = lax.all_gather(queries, "ctx", axis=0, tiled=True)
    grad_in = lax.all_gather(grad_attended, "ctx", axis=0, tiled=True)
    count = query_in.shape[0]
    span = block_width(count)
    place_in = places(pairing, jnp.int32(0), count, half)

    def step(index, state):
        offset = index * span
        query_block = heads_of(lax.dynamic_slice_in_dim(query_in, offset, span, 0))
        grad_block = heads_of(lax.dynamic_slice_in_dim(grad_in, offset, span, 0))
        stats_block = lax.dynamic_slice_in_dim(stats_all, offset, span, 0)
        place_block = lax.dynamic_slice_in_dim(place_in, offset, span, 0)
        key_part, value_part = key_terms(
            key_heads,
            value_heads,
            query_place,
            query_block,
            grad_block,
            jnp.transpose(stats_block[:, :HEADS]),
            jnp.transpose(stats_block[:, HEADS:]),
            place_block,
            length,
        )
        return (state[0] + key_part, state[1] + value_part)

    key_sum, value_sum = lax.fori_loop(0, count // span, step, (empty_heads, empty_heads))
    key_grad = key_sum.reshape(rows, width)
    value_grad = value_sum.reshape(rows, width)
    grad_proj = jnp.concatenate(
        [
            query_grad.reshape(rows, width).astype(jnp.bfloat16),
            key_grad.astype(jnp.bfloat16),
            value_grad.astype(jnp.bfloat16),
        ],
        axis=1,
    )
    qkv_grad = jnp.einsum("td,tf->df", inputs, grad_proj, preferred_element_type=jnp.float32)
    query_bias_grad = jnp.sum(grad_proj[:, :width].astype(jnp.float32), axis=0)
    value_bias_grad = jnp.sum(grad_proj[:, 2 * width :].astype(jnp.float32), axis=0)
    token_grad = grad_resid_one + jnp.einsum(
        "tf,df->td", grad_proj, qkv_back, preferred_element_type=jnp.float32
    )
    grads = (
        qkv_grad,
        query_bias_grad,
        value_bias_grad,
        out_grad,
        out_bias_grad,
        gain_one_grad,
        shift_one_grad,
        in_grad,
        in_bias_grad,
        back_grad,
        back_bias_grad,
        gain_two_grad,
        shift_two_grad,
    )
    shards = (
        lax.psum_scatter(
            grads[0].astype(jnp.bfloat16), "fsdp", scatter_dimension=0, tiled=True
        ).astype(jnp.float32),
        lax.psum_scatter(
            grads[1].astype(jnp.bfloat16), "fsdp", scatter_dimension=0, tiled=True
        ).astype(jnp.float32),
        lax.psum_scatter(
            grads[2].astype(jnp.bfloat16), "fsdp", scatter_dimension=0, tiled=True
        ).astype(jnp.float32),
        lax.psum_scatter(
            grads[3].astype(jnp.bfloat16), "fsdp", scatter_dimension=0, tiled=True
        ).astype(jnp.float32),
        lax.psum_scatter(
            grads[4].astype(jnp.bfloat16), "fsdp", scatter_dimension=0, tiled=True
        ).astype(jnp.float32),
        lax.psum_scatter(
            grads[5].astype(jnp.bfloat16), "fsdp", scatter_dimension=0, tiled=True
        ).astype(jnp.float32),
        lax.psum_scatter(
            grads[6].astype(jnp.bfloat16), "fsdp", scatter_dimension=0, tiled=True
        ).astype(jnp.float32),
        lax.psum_scatter(
            grads[7].astype(jnp.bfloat16), "fsdp", scatter_dimension=0, tiled=True
        ).astype(jnp.float32),
        lax.psum_scatter(
            grads[8].astype(jnp.bfloat16), "fsdp", scatter_dimension=0, tiled=True
        ).astype(jnp.float32),
        lax.psum_scatter(
            grads[9].astype(jnp.bfloat16), "fsdp", scatter_dimension=0, tiled=True
        ).astype(jnp.float32),
        lax.psum_scatter(
            grads[10].astype(jnp.bfloat16), "fsdp", scatter_dimension=0, tiled=True
        ).astype(jnp.float32),
        lax.psum_scatter(
            grads[11].astype(jnp.bfloat16), "fsdp", scatter_dimension=0, tiled=True
        ).astype(jnp.float32),
        lax.psum_scatter(
            grads[12].astype(jnp.bfloat16), "fsdp", scatter_dimension=0, tiled=True
        ).astype(jnp.float32),
    )
    totals = (
        lax.psum(shards[0].astype(jnp.bfloat16), "ctx").astype(jnp.float32),
        lax.psum(shards[1].astype(jnp.bfloat16), "ctx").astype(jnp.float32),
        lax.psum(shards[2].astype(jnp.bfloat16), "ctx").astype(jnp.float32),
        lax.psum(shards[3].astype(jnp.bfloat16), "ctx").astype(jnp.float32),
        lax.psum(shards[4].astype(jnp.bfloat16), "ctx").astype(jnp.float32),
        lax.psum(shards[5].astype(jnp.bfloat16), "ctx").astype(jnp.float32),
        lax.psum(shards[6].astype(jnp.bfloat16), "ctx").astype(jnp.float32),
        lax.psum(shards[7].astype(jnp.bfloat16), "ctx").astype(jnp.float32),
        lax.psum(shards[8].astype(jnp.bfloat16), "ctx").astype(jnp.float32),
        lax.psum(shards[9].astype(jnp.bfloat16), "ctx").astype(jnp.float32),
        lax.psum(shards[10].astype(jnp.bfloat16), "ctx").astype(jnp.float32),
        lax.psum(shards[11].astype(jnp.bfloat16), "ctx").astype(jnp.float32),
        lax.psum(shards[12].astype(jnp.bfloat16), "ctx").astype(jnp.float32),
    )
    return (output[None], token_grad[None]) + tuple(totals)


def low_lanes(shape):
    return lax.broadcasted_iota(jnp.int32, shape, 1) < 64


def spot_of(pair_ref, place):
    found = jnp.int32(0)
    for s in range(pair_ref.shape[0]):
        found = jnp.where(pair_ref[s] == place, s, found)
    return found


def attend(c, length, spot, keep_ref, mix_ref, lse_ref, turned_ref):
    left = low_lanes((256, BLK))
    zero = jnp.zeros((), jnp.bfloat16)
    keys = 256 * (c + 1)
    own = keep_ref[0, 2 * c : 2 * c + 2].reshape(256, BLK)
    shared = keep_ref[0, 2 * c + spot]
    query = jnp.concatenate(
        [jnp.where(left, own, zero), jnp.where(left[:BLK], zero, shared)], axis=0
    ) * jnp.bfloat16(0.125)
    key = keep_ref[1, : 2 * c + 2].reshape(keys, BLK)
    value = keep_ref[2, : 2 * c + 2].reshape(keys, BLK)
    scores = mask_scores(dot_nt(key, query), c, spot, length, 0, True)
    top = jnp.max(scores, axis=0, keepdims=True)
    probs = jnp.exp(scores - top)
    total = jnp.sum(probs, axis=0, keepdims=True)
    summed = lax.dot_general(
        value, probs.astype(jnp.bfloat16), (((0,), (0,)), ((), ())),
        preferred_element_type=jnp.float32,
    ) / total
    lse_ref[c] = top + jnp.log(total)
    part = summed[64:, 256:]
    none = jnp.zeros_like(part)
    first = jnp.where(spot == 0, part, none)
    second = jnp.where(spot == 0, none, part)
    mixed = jnp.concatenate([summed[:64, :256], jnp.concatenate([first, second], axis=1)], axis=0)
    mix_ref[c] = mixed
    turned_ref[2 * c : 2 * c + 2] = (
        jnp.transpose(mixed).astype(jnp.bfloat16).reshape(2, BLK, BLK)
    )


def mask_scores(scores, c, spot, length, start, edged):
    keys, width = scores.shape
    row = start + lax.broadcasted_iota(jnp.int32, (keys, width), 0)
    scores = jnp.where(row < length, scores, neg_big)
    if not edged:
        return scores
    edge = 256 * c
    lane = lax.broadcasted_iota(jnp.int32, (256, width), 1)
    query_place = edge + jnp.where(lane < 256, lane, lane - 256 + spot * BLK)
    key_place = edge + lax.broadcasted_iota(jnp.int32, (256, width), 0)
    seen = key_place <= query_place
    if c == 0:
        seen = seen | (key_place < NMEM)
    tail = jnp.where(seen, scores[keys - 256 :], neg_big)
    if keys == 256:
        return tail
    return jnp.concatenate([scores[: keys - 256], tail], axis=0)


def attend_back(
    c, length, spot, keep_ref, g_ref, mix_ref, lse_ref, q_sum, k_sum, v_sum
):
    zero = jnp.zeros((), jnp.bfloat16)
    left = low_lanes((256, BLK))
    left_half = left[:BLK]
    own = keep_ref[0, 2 * c : 2 * c + 2].reshape(256, BLK)
    shared = keep_ref[0, 2 * c + spot]
    query = jnp.concatenate(
        [jnp.where(left, own, zero), jnp.where(left_half, zero, shared)], axis=0
    ) * jnp.bfloat16(0.125)
    g_own = g_ref[2 * c : 2 * c + 2].reshape(256, BLK)
    g_shared = g_ref[2 * c + spot]
    grad = jnp.concatenate(
        [jnp.where(left, g_own, zero), jnp.where(left_half, zero, g_shared)], axis=0
    )
    turned = jnp.transpose(g_own.astype(jnp.float32)) * mix_ref[c]
    delta_own = jnp.sum(turned[:64], axis=0, keepdims=True)
    delta_pair = jnp.sum(turned[64:], axis=0, keepdims=True)
    delta = jnp.concatenate(
        [delta_own, jnp.where(spot == 0, delta_pair[:, :BLK], delta_pair[:, BLK:])], axis=1
    )
    lse = lse_ref[c]
    q_grad = jnp.zeros((384, BLK), jnp.float32)
    last = 2 * c + 2
    step = 8
    for low_block in range(0, last, step):
        high_block = min(low_block + step, last)
        cut = slice(low_block, high_block)
        count = high_block - low_block
        key = keep_ref[1, cut].reshape(count * BLK, BLK)
        value = keep_ref[2, cut].reshape(count * BLK, BLK)
        scores = mask_scores(
            dot_nt(key, query), c, spot, length, low_block * BLK, high_block == last
        )
        probs = jnp.exp(scores - lse)
        score_grad = (probs * (dot_nt(value, grad) - delta)).astype(jnp.bfloat16)
        v_part = dot_nn(probs.astype(jnp.bfloat16), grad)
        k_part = dot_nn(score_grad, query)
        v_sum[cut] += v_part.reshape(count, BLK, BLK)
        k_sum[cut] += k_part.reshape(count, BLK, BLK)
        q_grad = q_grad + lax.dot_general(
            score_grad, key, (((0,), (0,)), ((), ())), preferred_element_type=jnp.float32
        )
    q_grad = q_grad * 0.125
    part = q_grad[256:]
    none = jnp.zeros_like(part)
    first = jnp.where(spot == 0, part, none)
    second = jnp.where(spot == 0, none, part)
    q_sum[2 * c : 2 * c + 2] = jnp.where(
        left, q_grad[:256], jnp.concatenate([first, second], axis=0)
    ).reshape(2, BLK, BLK)


def smem():
    return pl.BlockSpec(memory_space=pltpu.SMEM)


def vmem():
    return pl.BlockSpec(memory_space=pltpu.VMEM)


MESH = pl.DeviceIdType.MESH


def remote(src, dst, sems, at, peer):
    return pltpu.make_async_remote_copy(
        src_ref=src, dst_ref=dst, send_sem=sems.at[(0,) + at], recv_sem=sems.at[(1,) + at],
        device_id=peer, device_id_type=MESH,
    )


def greet(peers):
    barrier = pltpu.get_barrier_semaphore()
    for peer in peers:
        pl.semaphore_signal(barrier, inc=1, device_id=peer, device_id_type=MESH)
    pl.semaphore_wait(barrier, len(peers))


def ring_peers(n):
    me = lax.axis_index("ctx")
    return [{"ctx": lax.rem(me + k, n)} for k in range(1, n)]


def two(block):
    return pl.ds(2 * block, 2)


def exchange_copies(n, in_ref, out_ref, sems):
    me = lax.axis_index("ctx")
    copies = []
    for k in range(1, n):
        peer = lax.rem(me + k, n)
        copies.append(
            remote(in_ref.at[two(peer)], out_ref.at[two(me)], sems, (k,), {"ctx": peer})
        )
    return copies


def own_copy(in_ref, out_ref, sem):
    me = lax.axis_index("ctx")
    return pltpu.make_async_copy(in_ref.at[two(me)], out_ref.at[two(me)], sem)


def both(ref, peer):
    value = ref[2 * peer : 2 * peer + 2]
    return value.reshape(-1, value.shape[2])


def join_pairs(pairs):
    pieces = []
    for group in range(HEADS // 3):
        first, second = pairs(2 * group), pairs(2 * group + 1)
        shared = first[:, HEAD_DIM:].astype(jnp.float32) + second[:, HEAD_DIM:].astype(jnp.float32)
        pieces += [first[:, :HEAD_DIM], second[:, :HEAD_DIM], shared.astype(jnp.bfloat16)]
    return jnp.concatenate(pieces, axis=1)


def pair_of(value, peer):
    own = 3 * (peer // 2) + peer % 2
    shared = 3 * (peer // 2) + 2
    cut = lambda head: value[:, head * HEAD_DIM : (head + 1) * HEAD_DIM]
    return jnp.concatenate([cut(own), cut(shared)], axis=1)


def dot_nn(a, b):
    return jnp.dot(a, b, preferred_element_type=jnp.float32)


def dot_nt(a, b):
    return lax.dot_general(a, b, (((1,), (1,)), ((), ())), preferred_element_type=jnp.float32)


def column_sum(value):
    return jnp.sum(value, axis=0, keepdims=True)


def unit_of(value):
    mean = jnp.mean(value, axis=-1, keepdims=True)
    centred = value - mean
    scale = lax.rsqrt(jnp.mean(centred * centred, axis=-1, keepdims=True) + eps)
    return centred * scale, scale


def unit_back(unit, scale, scaled):
    return scale * (
        scaled
        - jnp.mean(scaled, axis=-1, keepdims=True)
        - unit * jnp.mean(scaled * unit, axis=-1, keepdims=True)
    )


(ROW_BQ, ROW_BV, ROW_BO, ROW_G1, ROW_S1, ROW_BB, ROW_G2, ROW_S2, ROW_BI) = range(9)


def gather_copies(src, full, sems, index):
    fsdp = lax.axis_index("fsdp")
    x, core = fsdp // 2, lax.rem(fsdp, 2)
    sibling, across = {"fsdp": 2 * x + 1 - core}, {"fsdp": 2 * (1 - x) + core}
    other = 2 * (1 - x) + core
    return (
        remote(src, full.at[fsdp], sems, (index, 0), across),
        remote(src, full.at[fsdp], sems, (index, 1), sibling),
        remote(full.at[other], full.at[other], sems, (index, 2), sibling),
    )


def chip_peers():
    fsdp = lax.axis_index("fsdp")
    x, core = fsdp // 2, lax.rem(fsdp, 2)
    return [{"fsdp": 2 * x + 1 - core}, {"fsdp": 2 * (1 - x) + core}]


def split_gather(src, full, sems, parts):
    ctx, fsdp = lax.axis_index("ctx"), lax.axis_index("fsdp")
    z, y = ctx // 2, lax.rem(ctx, 2)
    x, core = fsdp // 2, lax.rem(fsdp, 2)
    sibling, across = {"fsdp": 2 * x + 1 - core}, {"fsdp": 2 * (1 - x) + core}
    beside = {"ctx": 2 * z + 1 - y}
    other = 2 * (1 - x) + core
    count = src.shape[0] // 2
    here = pl.ds(pl.multiple_of(y * count, count), count)
    there = pl.ds(pl.multiple_of((1 - y) * count, count), count)
    cross, side, on, off, whole = [], [], [], [], []
    for p in range(parts):
        width = src.shape[1] // parts
        cols = slice(p * width, (p + 1) * width)
        moved = full.at[other, here, cols]
        late = full.at[other, there, cols]
        cross.append(remote(src.at[here, cols], full.at[fsdp, here, cols], sems, (0, p), across))
        side.append(remote(moved, moved, sems, (1, p), beside))
        on.append(remote(moved, moved, sems, (2, p), sibling))
        off.append(remote(late, late, sems, (3, p), sibling))
        whole.append(remote(src.at[:, cols], full.at[fsdp, :, cols], sems, (4, p), sibling))
    return cross, side, on, off, whole


def front_kernel(
    n, pair_ref, len_ref, *refs
):
    vectors, refs = refs[:9], refs[9:]
    (
        tokens_ref, cot_ref, qkv_src, out_src, in_src, back_src,
        output_ref, grad_ref, left_ref, right_ref, resid_ref, sums_ref,
        keep_ref, mix_ref, lse_ref, qkv_ref,
        small_out, small, rows_ref, token_buf, cot, w_qkv, w_out, w_in, w_back, send,
        packed_q, packed_k, packed_v, keep, mix,
        lse, turned, mixed_out, mixed_in, active, slope, output, grad_out, left, right, resid, sums,
        small_sem, qkv_sem, gather_sem, send_q, send_k, send_v, in_sem, own_sem, load_sem, ship_sem,
    ) = refs
    send_sem = (send_q, send_k, send_v)
    packed = (packed_q, packed_k, packed_v)
    low, wide = jnp.bfloat16, jnp.float32
    ctx, fsdp = lax.axis_index("ctx"), lax.axis_index("fsdp")
    x, core = fsdp // 2, lax.rem(fsdp, 2)
    spot = lax.rem(ctx, 2)
    width = token_buf.shape[1]
    count = in_src.shape[1] // width
    loads = [
        pltpu.make_async_copy(src, dst, load_sem.at[i])
        for i, (src, dst) in enumerate(
            [
                (tokens_ref, token_buf),
                (cot_ref, cot),
                (qkv_src, w_qkv.at[fsdp]),
                (out_src, w_out.at[fsdp]),
                (in_src, w_in.at[fsdp]),
                (back_src, w_back.at[fsdp]),
            ]
        )
    ]
    cot_load = loads[1]
    for cp in loads[:3]:
        cp.start()
    part = width // 4
    small_out[...] = jnp.zeros_like(small_out)
    for i in range(8):
        small_out[i : i + 1] = vectors[i][...].astype(wide).reshape(1, part)
    inner_bias = vectors[8][...].astype(wide).reshape(1, -1)
    for j in range(4):
        small_out[8 + j : 9 + j] = inner_bias[:, j * part : (j + 1) * part]
    greet(ring_peers(n) + chip_peers())
    smalls = gather_copies(small_out, small, small_sem, 0)
    cross, side, on, off, whole = split_gather(qkv_src, w_qkv, qkv_sem, 3)
    for step in (0, 1):
        smalls[step].start()
    for cp in cross + whole:
        cp.start()
    for cp in loads[3:]:
        cp.start()
    shards = [
        gather_copies(src, full, gather_sem, i)
        for i, (src, full) in enumerate([(out_src, w_out), (in_src, w_in), (back_src, w_back)])
    ]
    back_shards = shards[2]
    small[fsdp] = small_out[...]
    smalls[0].wait_recv()
    smalls[2].start()
    def passed(p):
        cross[p].wait_recv()
        side[p].start()
        on[p].start()

    def handed(p):
        side[p].wait_recv()
        off[p].start()

    passed(0)
    loads[0].wait()
    tokens = token_buf[...]
    left[0] = jnp.transpose(tokens).reshape(4, -1, 2 * BLK)
    smalls[1].wait_recv()
    smalls[2].wait_recv()
    for f in range(4):
        cols = slice(f * part, (f + 1) * part)
        rows_ref[:8, cols] = small[f, :8]
        for j in range(4):
            rows_ref[ROW_BI + f : ROW_BI + f + 1, j * part : (j + 1) * part] = small[
                f, 8 + j : 9 + j
            ]
    rows_ref[12:] = jnp.zeros_like(rows_ref[12:])
    row = lambda i: rows_ref[i : i + 1, :]
    passed(1)
    handed(0)
    passed(2)
    for step in (0, 1):
        for cps in shards:
            cps[step].start()
    loads[2].wait()
    sends = []
    for p, bias in enumerate((ROW_BQ, None, ROW_BV)):
        if p:
            handed(p)
        for cps in (whole, on, off):
            cps[p].wait_recv()
        value = dot_nn(tokens, w_qkv[:, :, p * width : (p + 1) * width].reshape(width, width))
        if bias is not None:
            value = value + row(bias)
        value = value.astype(low)
        for peer in range(n):
            send[p, 2 * peer : 2 * peer + 2] = pair_of(value, peer).reshape(2, BLK, BLK)
        copies = exchange_copies(n, send.at[p], packed[p], send_sem[p])
        copies.append(own_copy(send.at[p], packed[p], own_sem.at[2 + p]))
        for cp in copies:
            cp.start()
        sends.append(copies)
    shipped = []

    def ship(src, dst):
        cp = pltpu.make_async_copy(src, dst, ship_sem.at[len(shipped)])
        cp.start()
        shipped.append(cp)

    ship(w_qkv, qkv_ref)
    spots = lax.broadcasted_iota(jnp.int32, (2 * BLK, 1), 0)
    place = jnp.where(
        spots < BLK,
        pair_ref[2 * ctx] * BLK + spots,
        pair_ref[2 * ctx + 1] * BLK + spots - BLK,
    )
    valid = place < len_ref[0]
    spots_of = [spot_of(pair_ref, b) for b in range(2 * n)]
    for p in range(3):
        sends[p][-1].wait()
        for cp in sends[p][:-1]:
            cp.wait_recv()
        for b in range(2 * n):
            keep[p, b] = packed[p][spots_of[b]]
    for cps in shards[:2]:
        cps[0].wait_recv()
        cps[2].start()

    ship(keep, keep_ref)
    for c in range(n):
        attend(c, len_ref[0], spot, keep, mix, lse, turned)
    for s in range(2 * n):
        mixed_out[s] = turned[pair_ref[s]]
    copies = exchange_copies(n, mixed_out, mixed_in, in_sem)
    for cp in copies:
        cp.start()
    own_mixed = own_copy(mixed_out, mixed_in, own_sem.at[1])
    own_mixed.start()
    ship(mix, mix_ref)
    ship(lse, lse_ref)
    sums[...] = jnp.zeros_like(sums)
    for cp in loads[3:]:
        cp.wait()
    for cps in shards[:2]:
        cps[1].wait_recv()
        cps[2].wait_recv()
    own_mixed.wait()
    for cp in copies:
        cp.wait_recv()
    back_shards[0].wait_recv()
    back_shards[2].start()
    back_shards[1].wait_recv()

    attended = join_pairs(lambda peer: both(mixed_in, peer))
    resid_one = (
        tokens.astype(wide)
        + dot_nn(attended, w_out[...].reshape(width, width))
        + row(ROW_BO)
    )
    unit_one, scale_one = unit_of(resid_one)
    hidden = unit_one * row(ROW_G1) + row(ROW_S1)
    hidden_low = hidden.astype(low)
    resid_two = hidden + row(ROW_BB)
    cut = lambda t: pl.ds(pl.multiple_of(t * width, width), width)
    order = [fsdp, 2 * x + 1 - core, 2 * (1 - x) + core, 2 * (1 - x) + 1 - core]
    for step, t in enumerate(order):
        bias = rows_ref[pl.ds(ROW_BI + t, 1), :]
        upper = dot_nn(hidden_low, w_in[:, :, cut(t)].reshape(width, width)) + bias
        share = 0.5 * (1.0 + lax.erf(upper * (0.5**0.5)))
        slope[t] = share + upper * (jnp.exp(-0.5 * upper * upper) * (2 * math.pi) ** -0.5)
        some = (upper * share).astype(low)
        active[t] = some
        if step == 3:
            back_shards[2].wait_recv()
        resid_two = resid_two + dot_nn(some, w_back[t])
    unit_two, scale_two = unit_of(resid_two)
    output[...] = jnp.where(valid, unit_two * row(ROW_G2) + row(ROW_S2), 0.0)
    cot_load.wait()
    grad_y = jnp.where(valid, cot[...].astype(wide), 0.0)
    sums[ROW_G2 : ROW_G2 + 1, :] = column_sum(grad_y * unit_two)
    sums[ROW_S2 : ROW_S2 + 1, :] = column_sum(grad_y)
    grad_resid_two = unit_back(unit_two, scale_two, grad_y * row(ROW_G2))
    grad_mixed = grad_resid_two.astype(low)
    right[5] = grad_mixed
    sums[ROW_BB : ROW_BB + 1, :] = column_sum(grad_mixed.astype(wide))
    grad_hidden = grad_resid_two
    for t in range(count):
        grad_upper = (dot_nt(grad_mixed, w_back[t]) * slope[t]).astype(low)
        right[1 + t] = grad_upper
        sums[ROW_BI + t : ROW_BI + t + 1, :] = column_sum(grad_upper.astype(wide))
        grad_hidden = grad_hidden + dot_nt(grad_upper, w_in[:, :, cut(t)].reshape(width, width))
    sums[ROW_G1 : ROW_G1 + 1, :] = column_sum(grad_hidden * unit_one)
    sums[ROW_S1 : ROW_S1 + 1, :] = column_sum(grad_hidden)
    grad_resid_one = unit_back(unit_one, scale_one, grad_hidden * row(ROW_G1))
    resid[...] = grad_resid_one
    grad_branch = grad_resid_one.astype(low)
    right[0] = grad_branch
    sums[ROW_BO : ROW_BO + 1, :] = column_sum(grad_branch.astype(wide))
    ship(resid, resid_ref)
    ship(right, right_ref)
    ship(sums, sums_ref)
    grad_attended = dot_nt(grad_branch, w_out[...].reshape(width, width)).astype(low)
    for peer in range(n):
        grad_out[2 * peer : 2 * peer + 2] = pair_of(grad_attended, peer).reshape(2, BLK, BLK)
    ship(grad_out, grad_ref)
    left[1] = jnp.transpose(attended).reshape(4, -1, 2 * BLK)
    left[2] = jnp.transpose(hidden_low).reshape(4, -1, 2 * BLK)
    for f in range(4):
        turned = jnp.transpose(active[f])
        for r in range(4):
            left[3 + r, f] = turned[r * width // 4 : (r + 1) * width // 4]
    ship(output, output_ref)
    ship(left, left_ref)
    for cps in [smalls] + shards:
        for cp in cps:
            cp.wait_send()
    for cp in cross + side + on + off + whole + copies:
        cp.wait_send()
    for cps in sends:
        for cp in cps[:-1]:
            cp.wait_send()
    for cp in shipped:
        cp.wait()


def front(pairing, lengths, vectors, tokens, cotangent, w_qkv, w_out, w_in, w_back, n, name):
    count, width = tokens.shape
    low, wide = jnp.bfloat16, jnp.float32
    dma = pltpu.SemaphoreType.DMA
    shape = jax.ShapeDtypeStruct
    hbm = pl.BlockSpec(memory_space=pltpu.HBM)
    vec = pltpu.VMEM((16, width // 4), wide)
    results = [
        ((count, width), wide),
        ((2 * n, BLK, BLK), low),
        ((7, 4, width // 4, count), low),
        ((6, count, width), low),
        ((count, width), wide),
        ((16, width), wide),
        ((3, 2 * n, BLK, BLK), low),
        ((n, BLK, 2 * BLK), wide),
        ((n, 1, 3 * BLK), wide),
        ((4,) + w_qkv.shape, low),
    ]
    output, grad, left, right, resid, sums, keep, mix, lse, qkv = [pltpu.VMEM(*r) for r in results]
    return pl.pallas_call(
        functools.partial(front_kernel, n),
        out_shape=tuple(shape(*r) for r in results),
        in_specs=[smem(), smem()] + [vmem()] * 9 + [hbm] * 6,
        out_specs=(hbm,) * 10,
        scratch_shapes=[
            vec,
            pltpu.VMEM((4, 16, width // 4), wide),
            pltpu.VMEM((16, width), wide),
            pltpu.VMEM((count, width), low),
            pltpu.VMEM((count, width), low),
            qkv,
            pltpu.VMEM((4,) + w_out.shape, low),
            pltpu.VMEM((4,) + w_in.shape, low),
            pltpu.VMEM((4,) + w_back.shape, low),
            keep,
            grad,
            grad,
            grad,
            keep,
            mix,
            lse,
            grad,
            grad,
            grad,
            pltpu.VMEM((4, count, width), low),
            pltpu.VMEM((4, count, width), wide),
            output,
            grad,
            left,
            right,
            resid,
            sums,
            dma((2, 1, 3)),
            dma((2, 5, 3)),
            dma((2, 3, 3)),
            dma((2, n)),
            dma((2, n)),
            dma((2, n)),
            dma((2, n)),
            dma((5,)),
            dma((6,)),
            dma((10,)),
        ],
        compiler_params=pltpu.CompilerParams(
            collective_id=name, has_side_effects=True, vmem_limit_bytes=62 << 20
        ),
        name="front",
    )(pairing, lengths, *vectors, tokens, cotangent, w_qkv, w_out, w_in, w_back)


PARTS = 12


def sum_sources(chunk):
    if chunk < 4:
        return 3 + chunk, 8
    if chunk < 8:
        return 2, chunk
    return (1, 3) if chunk < 9 else (0, chunk - 9)


STEPS = 65
PLAN = {
    "pair": {0: 0, 1: 1, 2: 2, 3: 3, 6: 4, 7: 5, 13: 6, 15: 7, 19: 8, 21: 9, 29: 10, 32: 11},
    "x": {3: 0, 4: 1, 5: 2, 7: 3, 12: 4, 13: 5, 14: 6, 18: 7, 23: 8, 30: 9, 36: 10, 41: 11},
    "y": {9: 0, 10: 1, 16: 2, 17: 3, 18: 4, 21: 5, 24: 6, 26: 7, 30: 8, 36: 9, 46: 10, 50: 11},
    "near": {11: 0, 19: 1, 20: 2, 24: 3, 25: 4, 28: 5, 32: 6, 38: 7, 42: 8, 44: 9, 49: 10, 57: 11},
    "far": {22: 0, 25: 1, 26: 2, 31: 3, 33: 4, 39: 5, 41: 6, 44: 7, 47: 8, 52: 9, 55: 10, 60: 11},
    "own": {27: 0, 29: 1, 30: 2, 37: 3, 40: 4, 45: 5, 49: 6, 50: 7, 53: 8, 57: 9, 58: 10, 61: 11},
    "wide": {30: 0, 31: 1, 34: 2, 43: 3, 48: 4, 50: 5, 51: 6, 56: 7, 57: 8, 59: 9, 61: 10, 62: 11},
    "last": {35: 0, 38: 1, 42: 2, 47: 3, 52: 4, 54: 5, 55: 6, 58: 7, 60: 8, 61: 9, 63: 10, 64: 11},
}
ATTEND_AT = (8, 9, 10)
JOIN_AT = (16, 24, 28)
SMALL_AT = (46, 49, 52, 61, 62, 64)
TOKEN_AT = 44


def planned(name, step):
    return PLAN[name].get(step, -1)


def only(condition):
    def run(body):
        if condition:
            body()

    return run


def back_kernel(
    n, pair_ref, len_ref, grad_ref, keep_src, mix_src, lse_src, left_src, right_src,
    sums_src, resid_src, qkv_ref,
    total_out, token_ref, small_out,
    keep_ref, mix_ref, lse_ref, left_ref, sums_ref, resid_ref, total_ref,
    grad_in, g_all, q_sum, k_sum, v_sum, blocks_out, blocks_in, w_qkv, right_all,
    pair_out, pair_in, x_out, x_in, y_out, y_in, y_keep, near_out, near_in, near_keep,
    far_out, far_in, far_keep, s_out, s_in,
    load_sem, ship_sem,
    grad_sem, block_q, block_k, block_v, own_sem, pair_sem, x_sem, y_sem, near_sem, far_sem,
    own_z_sem, wide_sem, last_sem, s_sem,
):
    block_sem = (block_q, block_k, block_v)
    low, wide = jnp.bfloat16, jnp.float32
    ctx = lax.axis_index("ctx")
    fsdp = lax.axis_index("fsdp")
    z, y = ctx // 2, lax.rem(ctx, 2)
    odd, upper = lax.rem(z, 2), z // 2
    x, core = fsdp // 2, lax.rem(fsdp, 2)
    sibling = {"fsdp": 2 * x + 1 - core}
    across = {"fsdp": 2 * (1 - x) + core}
    beside = {"ctx": 2 * z + 1 - y}
    near = {"ctx": 2 * (2 * upper + 1 - odd) + y}
    far = {"ctx": 2 * (2 * (1 - upper) + odd) + y}
    mine = 2 * odd + upper
    loads = [
        pltpu.make_async_copy(src, dst, load_sem.at[i])
        for i, (src, dst) in enumerate(
            [
                (right_src, right_all.at[3:]),
                (left_src, left_ref),
                (keep_src, keep_ref),
                (mix_src, mix_ref),
                (lse_src, lse_ref),
                (sums_src, sums_ref),
                (resid_src, resid_ref),
            ]
        )
    ]
    for cp in loads:
        cp.start()
    greet(ring_peers(n) + [sibling, across])
    grads = exchange_copies(n, grad_ref, grad_in, grad_sem)
    for cp in grads:
        cp.start()
    own_grad = own_copy(grad_ref, grad_in, own_sem.at[0])
    own_grad.start()
    load = pltpu.make_async_copy(qkv_ref, w_qkv, own_sem.at[1])
    load.start()
    blocks = [
        exchange_copies(n, blocks_out.at[p], blocks_in.at[p], sem)
        for p, sem in enumerate(block_sem)
    ]
    own = [own_copy(blocks_out.at[p], blocks_in.at[p], own_sem.at[2 + p]) for p in range(3)]
    k_sum[...] = jnp.zeros_like(k_sum)
    v_sum[...] = jnp.zeros_like(v_sum)
    chunks = keep_ref.shape[1] // 2

    def attend_some(first, last):
        for c in range(first, last):
            attend_back(
                c, len_ref[0], y, keep_ref, g_all, mix_ref, lse_ref, q_sum, k_sum, v_sum
            )

    def attend_step(t):
        @only(t == ATTEND_AT[0])
        def _():
            own_grad.wait()
            for cp in loads[2:5]:
                cp.wait()
            for cp in grads:
                cp.wait_recv()
            for b in range(2 * chunks):
                g_all[b] = grad_in[spot_of(pair_ref, b)]
            attend_some(0, chunks // 2)

        @only(t == ATTEND_AT[1])
        def _():
            attend_some(chunks // 2, chunks - 2)

        @only(t == ATTEND_AT[2])
        def _():
            attend_some(chunks - 2, chunks)
            for s in range(2 * chunks):
                place = pair_ref[s]
                for p, total in enumerate((q_sum, k_sum, v_sum)):
                    blocks_out[p, s] = total[place].astype(low)
            for p in range(3):
                for cp in blocks[p]:
                    cp.start()
                own[p].start()

    def slot(c):
        return c % 4

    def pair_copy(c):
        return remote(pair_out.at[c % 2], pair_in.at[c], pair_sem, (c,), sibling)

    def x_copy(c):
        return remote(x_out.at[c], x_in.at[c], x_sem, (c,), across)

    def y_copy(c):
        return remote(y_out.at[slot(c)], y_in.at[c], y_sem, (c,), beside)

    def near_copy(c):
        return remote(near_out.at[slot(c)], near_in.at[c], near_sem, (c,), near)

    def far_copy(c):
        return remote(far_out.at[slot(c)], far_in.at[c], far_sem, (c,), far)

    def own_z_copy(c):
        piece = total_ref.at[c, y, mine]
        return remote(piece, piece, own_z_sem, (c,), far)

    def wide_copy(c):
        piece = total_ref.at[c, y, two(odd)]
        return remote(piece, piece, wide_sem, (c,), near)

    def last_copy(c):
        piece = total_ref.at[c, y]
        return remote(piece, piece, last_sem, (c,), beside)

    def reuse(copy, c, slots):
        @only(c >= slots)
        def _():
            copy(c - slots).wait_send()

    def partial(c, shard):
        left, right = sum_sources(c)
        return dot_nn(left_ref[left, shard], right_all[right])

    def stage_pair(c):
        reuse(pair_copy, c, 2)
        for side in range(2):
            pair_out[c % 2, side] = partial(c, 2 * side + 1 - core).astype(low)
        pair_copy(c).start()

    def stage_x(c):
        pair_copy(c).wait_recv()
        x_out[c] = (partial(c, 2 * (1 - x) + core) + pair_in[c, 1 - x].astype(wide)).astype(low)
        x_copy(c).start()

    def stage_y(c):
        mine_sum = partial(c, 2 * x + core) + pair_in[c, x].astype(wide)
        x_copy(c).wait_recv()
        total = mine_sum + x_in[c].astype(wide)
        first, second = total[:, :384], total[:, 384:]
        reuse(y_copy, c, 4)
        y_out[slot(c)] = jnp.where(y == 0, second, first).astype(low)
        y_copy(c).start()
        y_keep[slot(c)] = jnp.where(y == 0, first, second)

    def stage_near(c):
        y_copy(c).wait_recv()
        total = y_keep[slot(c)] + y_in[c].astype(wide)
        first, second = total[:96], total[96:]
        reuse(near_copy, c, 4)
        near_out[slot(c)] = jnp.where(odd == 0, second, first).astype(low)
        near_copy(c).start()
        near_keep[slot(c)] = jnp.where(odd == 0, first, second)

    def stage_far(c):
        near_copy(c).wait_recv()
        total = near_keep[slot(c)] + near_in[c].astype(wide)
        first, second = total[:48], total[48:]
        reuse(far_copy, c, 4)
        far_out[slot(c)] = jnp.where(upper == 0, second, first).astype(low)
        far_copy(c).start()
        far_keep[slot(c)] = jnp.where(upper == 0, first, second)

    def stage_own(c):
        far_copy(c).wait_recv()
        total_ref[c, y, mine] = (far_keep[slot(c)] + far_in[c].astype(wide)).astype(low)
        own_z_copy(c).start()

    def stage_wide(c):
        own_z_copy(c).wait_recv()
        wide_copy(c).start()

    def stage_last(c):
        wide_copy(c).wait_recv()
        last_copy(c).start()

    def small_step(t):
        peers = [sibling, across, beside, near, far]
        copies = [
            remote(s_out.at[k], s_in.at[k], s_sem, (k,), peer) for k, peer in enumerate(peers)
        ]

        for p in range(3):

            @only(t == JOIN_AT[p])
            def _():
                own[p].wait()
                for cp in blocks[p]:
                    cp.wait_recv()
                right_all[p] = join_pairs(lambda peer: both(blocks_in.at[p], peer))

        @only(t == SMALL_AT[0])
        def _():
            loads[5].wait()
            s_out[0] = sums_ref[...]
            s_out[0, ROW_BQ : ROW_BQ + 1] = column_sum(right_all[0].astype(wide))
            s_out[0, ROW_BV : ROW_BV + 1] = column_sum(right_all[2].astype(wide))
            copies[0].start()

        for k in range(1, 5):

            @only(t == SMALL_AT[k])
            def _():
                copies[k - 1].wait()
                s_out[k] = s_out[k - 1] + s_in[k - 1]
                copies[k].start()

        @only(t == SMALL_AT[5])
        def _():
            copies[4].wait()
            total = s_out[4] + s_in[4]
            quarter = total.shape[1] // 4
            cuts = [slice(f * quarter, (f + 1) * quarter) for f in range(4)]
            pick = lambda choices: sum(
                jnp.where(fsdp == f, choice, 0.0) for f, choice in enumerate(choices)
            )
            small_out[...] = jnp.zeros_like(small_out)
            small_out[:8] = pick([total[:8, cut] for cut in cuts])
            line = pick([total[ROW_BI + f : ROW_BI + f + 1] for f in range(4)])
            for j, cut in enumerate(cuts):
                small_out[8 + j : 9 + j] = line[:, cut]

        @only(t == TOKEN_AT)
        def _():
            load.wait()
            loads[6].wait()
            width = resid_ref.shape[1]
            token_ref[...] = resid_ref[...] + sum(
                dot_nt(
                    right_all[part],
                    w_qkv[:, :, part * width : (part + 1) * width].reshape(width, width),
                )
                for part in range(3)
            )

    stages = [
        ("pair", stage_pair),
        ("x", stage_x),
        ("last", stage_last),
        ("wide", stage_wide),
        ("own", stage_own),
        ("far", stage_far),
        ("near", stage_near),
        ("y", stage_y),
    ]

    def step(t, carry):
        attend_step(t)
        small_step(t)
        for name, stage in stages:
            c = planned(name, t)

            @only(c >= 0)
            def _():
                stage(c)

        return carry

    loads[0].wait()
    loads[1].wait()
    for at in range(STEPS):
        step(at, 0)

    def ship(c):
        return pltpu.make_async_copy(total_ref.at[c], total_out.at[c], ship_sem.at[c])

    def drain(c, carry):
        x_copy(c).wait_send()
        own_z_copy(c).wait_send()
        wide_copy(c).wait_send()
        last_copy(c).wait()
        ship(c).start()
        return carry

    for c in range(PARTS):
        drain(c, 0)
    for c in range(PARTS - 4, PARTS):
        y_copy(c).wait_send()
        near_copy(c).wait_send()
        far_copy(c).wait_send()
    for c in (PARTS - 2, PARTS - 1):
        pair_copy(c).wait_send()
    for cp in grads + blocks[0] + blocks[1] + blocks[2]:
        cp.wait_send()
    for c in range(PARTS):
        ship(c).wait()


def back(pairing, lengths, grad, keep, mix, lse, left, right, sums, resid, qkv_full, name):
    blocks = keep.shape[1]
    n = blocks // 2
    low, wide = jnp.bfloat16, jnp.float32
    dma = pltpu.SemaphoreType.DMA
    shape = jax.ShapeDtypeStruct
    total = pltpu.VMEM((blocks, BLK, BLK), wide)
    hbm = pl.BlockSpec(memory_space=pltpu.HBM)
    return pl.pallas_call(
        functools.partial(back_kernel, n),
        out_shape=(
            shape((PARTS, 2, 4, 48, 384), low),
            shape(resid.shape, wide),
            shape((16, 192), wide),
        ),
        in_specs=[smem()] * 2 + [hbm] * 9,
        out_specs=(hbm, vmem(), vmem()),
        scratch_shapes=[
            pltpu.VMEM(keep.shape, low),
            pltpu.VMEM(mix.shape, wide),
            pltpu.VMEM(lse.shape, wide),
            pltpu.VMEM(left.shape, low),
            pltpu.VMEM(sums.shape, wide),
            pltpu.VMEM(resid.shape, wide),
            pltpu.VMEM((PARTS, 2, 4, 48, 384), low),
            pltpu.VMEM(grad.shape, low),
            pltpu.VMEM(grad.shape, low),
            total, total, total,
            pltpu.VMEM(keep.shape, low),
            pltpu.VMEM(keep.shape, low),
            pltpu.VMEM(qkv_full.shape, low),
            pltpu.VMEM((9,) + right.shape[1:], low),
            pltpu.VMEM((2, 2, 192, 768), low),
            pltpu.VMEM((PARTS, 2, 192, 768), low),
            pltpu.VMEM((PARTS, 192, 768), low),
            pltpu.VMEM((PARTS, 192, 768), low),
            pltpu.VMEM((4, 192, 384), low),
            pltpu.VMEM((PARTS, 192, 384), low),
            pltpu.VMEM((4, 192, 384), wide),
            pltpu.VMEM((4, 96, 384), low),
            pltpu.VMEM((PARTS, 96, 384), low),
            pltpu.VMEM((4, 96, 384), wide),
            pltpu.VMEM((4, 48, 384), low),
            pltpu.VMEM((PARTS, 48, 384), low),
            pltpu.VMEM((4, 48, 384), wide),
            pltpu.VMEM((5,) + sums.shape, wide),
            pltpu.VMEM((5,) + sums.shape, wide),
            dma((7,)),
            dma((PARTS,)),
            dma((2, n)),
            dma((2, n)),
            dma((2, n)),
            dma((2, n)),
            dma((5,)),
        ]
        + [dma((2, PARTS))] * 8
        + [dma((2, 5))],
        compiler_params=pltpu.CompilerParams(
            collective_id=name, has_side_effects=True, vmem_limit_bytes=61 << 20
        ),
        name="back",
    )(pairing, lengths, grad, keep, mix, lse, left, right, sums, resid, qkv_full)


def finish_kernel(
    total_ref, small_ref, output_ref, token_ref,
    output_out, token_out, qkv_out, out_out, in_out, back_out, *refs
):
    lines, (total, small, through, stage, sems) = refs[:9], refs[9:]
    arrive = [
        pltpu.make_async_copy(total_ref.at[c], total.at[c], sems.at[PARTS + 2 + c])
        for c in range(PARTS)
    ] + [
        pltpu.make_async_copy(small_ref, small, sems.at[2 * PARTS + 2]),
        pltpu.make_async_copy(output_ref, through.at[0], sems.at[2 * PARTS + 3]),
        pltpu.make_async_copy(token_ref, through.at[1], sems.at[2 * PARTS + 4]),
    ]
    for cp in arrive:
        cp.start()
    copies = [
        pltpu.make_async_copy(through.at[0], output_out, sems.at[PARTS]),
        pltpu.make_async_copy(through.at[1], token_out, sems.at[PARTS + 1]),
    ]
    targets = [back_out.at[192 * k : 192 * k + 192] for k in range(4)]
    targets += [in_out.at[:, 768 * k : 768 * k + 768] for k in range(4)]
    targets += [out_out]
    targets += [qkv_out.at[:, 768 * k : 768 * k + 768] for k in range(3)]
    for c, target in enumerate(targets):
        arrive[c].wait()
        for half in range(2):
            for spot in range(4):
                stage[c, 48 * spot : 48 * spot + 48, 384 * half : 384 * half + 384] = total[
                    c, half, spot
                ].astype(jnp.float32)
        copies.append(pltpu.make_async_copy(stage.at[c], target, sems.at[c]))
        copies[-1].start()
    for k in range(2):
        arrive[PARTS + 1 + k].wait()
        copies[k].start()
    arrive[PARTS].wait()
    for i in range(8):
        lines[i][...] = small[i]
    for j in range(4):
        lines[8][192 * j : 192 * j + 192] = small[ROW_BI + j]
    for cp in copies:
        cp.wait()


def finish(total, small, output, token):
    shape = jax.ShapeDtypeStruct
    wide = jnp.float32
    hbm = pl.BlockSpec(memory_space=pltpu.HBM)
    return pl.pallas_call(
        finish_kernel,
        out_shape=(
            shape(output.shape, wide),
            shape(token.shape, wide),
            shape((192, 2304), wide),
            shape((192, 768), wide),
            shape((192, 3072), wide),
            shape((768, 768), wide),
        )
        + (shape((192,), wide),) * 8
        + (shape((768,), wide),),
        in_specs=[hbm] * 4,
        out_specs=(hbm,) * 6 + (vmem(),) * 9,
        scratch_shapes=[
            pltpu.VMEM(total.shape, total.dtype),
            pltpu.VMEM(small.shape, wide),
            pltpu.VMEM((2,) + token.shape, wide),
            pltpu.VMEM((PARTS, 192, 768), wide),
            pltpu.SemaphoreType.DMA((2 * PARTS + 5,)),
        ],
        compiler_params=pltpu.CompilerParams(vmem_limit_bytes=62 << 20),
        name="finish",
    )(total, small, output, token)


def on_device_spread(
    tokens,
    cotangent,
    lengths,
    pairing,
    w_qkv,
    bias_q,
    bias_v,
    w_out,
    bias_out,
    ln1_gain,
    ln1_bias,
    w_in,
    bias_in,
    w_back,
    bias_back,
    ln2_gain,
    ln2_bias,
):
    n = pairing.shape[0] // 2
    inputs = tokens[0]
    vectors = [bias_q, bias_v, bias_out, ln1_gain, ln1_bias, bias_back, ln2_gain, ln2_bias]
    vectors += [bias_in]
    output, grad, left, right, resid, sums, keep, mix, lse, qkv_full = front(
        pairing, lengths, vectors, inputs, cotangent[0], w_qkv, w_out, w_in, w_back, n, 0
    )
    total, token_grad, small_sum = back(
        pairing, lengths, grad, keep, mix, lse, left, right, sums, resid, qkv_full, 1
    )
    (
        output, token_grad, qkv_sum, out_sum, in_sum, back_sum,
        bq, bv, bo, g1, s1, bb, g2, s2, bi,
    ) = finish(total, small_sum, output, token_grad)
    return (
        output[None], token_grad[None], qkv_sum, bq, bv, out_sum, bo, g1, s1, in_sum, bi,
        back_sum, bb, g2, s2,
    )


def solution(mesh):
    return jax.shard_map(
        on_device_spread if mesh.shape["ctx"] == 8 else on_device_any,
        mesh=mesh,
        in_specs=(
            P("fsdp", "ctx", None),
            P("fsdp", "ctx", None),
            P("fsdp"),
            P(),
            P("fsdp", None),
            P("fsdp"),
            P("fsdp"),
            P("fsdp", None),
            P("fsdp"),
            P("fsdp"),
            P("fsdp"),
            P("fsdp", None),
            P("fsdp"),
            P("fsdp", None),
            P("fsdp"),
            P("fsdp"),
            P("fsdp"),
        ),
        out_specs=(
            P("fsdp", "ctx", None),
            P("fsdp", "ctx", None),
            P("fsdp", None),
            P("fsdp"),
            P("fsdp"),
            P("fsdp", None),
            P("fsdp"),
            P("fsdp"),
            P("fsdp"),
            P("fsdp", None),
            P("fsdp"),
            P("fsdp", None),
            P("fsdp"),
            P("fsdp"),
            P("fsdp"),
        ),
        check_vma=False,
    )
```

```python
import functools
import math

import jax
import jax.numpy as jnp
from jax import lax
from jax.experimental import pallas as pl
from jax.experimental.pallas import tpu as pltpu
from jax.sharding import PartitionSpec as P

HEADS = 12
HEAD_DIM = 64
NMEM = 10
BLK = 128


eps = 1e-12
neg_big = -1e30


def layer_norm(value, gain, shift):
    mean = jnp.mean(value, axis=-1, keepdims=True)
    centred = value - mean
    variance = jnp.mean(centred * centred, axis=-1, keepdims=True)
    return centred * lax.rsqrt(variance + eps) * gain + shift


def norm_back(value, gain, grad):
    mean = jnp.mean(value, axis=-1, keepdims=True)
    centred = value - mean
    scale = lax.rsqrt(jnp.mean(centred * centred, axis=-1, keepdims=True) + eps)
    unit = centred * scale
    scaled = grad * gain
    inner = (
        scaled
        - jnp.mean(scaled, axis=-1, keepdims=True)
        - unit * jnp.mean(scaled * unit, axis=-1, keepdims=True)
    )
    return (scale * inner, jnp.sum(grad * unit, axis=0), jnp.sum(grad, axis=0))


def block_width(count):
    return math.gcd(count, 512)


def places(pairing, start, count, half):
    rows = start + jnp.arange(count, dtype=jnp.int32)
    owners = rows // half
    spots = jnp.arange(pairing.shape[0], dtype=jnp.int32)
    picked = jnp.sum(jnp.where(owners[:, None] == spots[None, :], pairing[None, :], 0), axis=1)
    return picked * half + rows % half


def allowed_pairs(query_place, key_place, length):
    before = (key_place[None, :] <= query_place[:, None]) | (key_place[None, :] < NMEM)
    return (key_place[None, :] < length) & before


def heads_of(value):
    return value.reshape(value.shape[0], HEADS, HEAD_DIM)


def forward_fold(query_heads, query_place, pairing, length, half):

    def fold(carry, piece, start):
        keys, values = piece
        count = keys.shape[0]
        width = block_width(count)
        key_place = places(pairing, start, count, half)

        def step(index, state):
            top, total, summed = state
            offset = index * width
            key_heads = heads_of(lax.dynamic_slice_in_dim(keys, offset, width, 0))
            value_heads = heads_of(lax.dynamic_slice_in_dim(values, offset, width, 0))
            mask = allowed_pairs(
                query_place, lax.dynamic_slice_in_dim(key_place, offset, width, 0), length
            )[None]
            scores = (
                jnp.einsum(
                    "qhd,khd->hqk", query_heads, key_heads, preferred_element_type=jnp.float32
                )
                * 0.125
            )
            scores = jnp.where(mask, scores, neg_big)
            new_top = jnp.maximum(top, jnp.max(scores, axis=2))
            shrink = jnp.exp(top - new_top)
            probs = jnp.where(mask, jnp.exp(scores - new_top[:, :, None]), 0.0)
            total = total * shrink + jnp.sum(probs, axis=2)
            update = jnp.einsum(
                "hqk,khd->qhd",
                probs.astype(jnp.bfloat16),
                value_heads,
                preferred_element_type=jnp.float32,
            )
            summed = summed * jnp.transpose(shrink)[:, :, None] + update
            return (new_top, total, summed)

        return lax.fori_loop(0, count // width, step, carry)

    return fold


def query_grad_fold(query_heads, grad_heads, top_sum, delta, query_place, pairing, length, half):

    def fold(carry, piece, start):
        keys, values = piece
        count = keys.shape[0]
        width = block_width(count)
        key_place = places(pairing, start, count, half)

        def step(index, summed):
            offset = index * width
            key_heads = heads_of(lax.dynamic_slice_in_dim(keys, offset, width, 0))
            value_heads = heads_of(lax.dynamic_slice_in_dim(values, offset, width, 0))
            mask = allowed_pairs(
                query_place, lax.dynamic_slice_in_dim(key_place, offset, width, 0), length
            )[None]
            scores = (
                jnp.einsum(
                    "qhd,khd->hqk", query_heads, key_heads, preferred_element_type=jnp.float32
                )
                * 0.125
            )
            probs = jnp.where(mask, jnp.exp(scores - top_sum[:, :, None]), 0.0)
            prob_grad = jnp.einsum(
                "qhd,khd->hqk", grad_heads, value_heads, preferred_element_type=jnp.float32
            )
            score_grad = (probs * (prob_grad - delta[:, :, None])).astype(jnp.bfloat16)
            return (
                summed
                + jnp.einsum(
                    "hqk,khd->qhd", score_grad, key_heads, preferred_element_type=jnp.float32
                )
                * 0.125
            )

        return lax.fori_loop(0, count // width, step, carry)

    return fold


def key_terms(
    key_heads, value_heads, key_place, query_heads, grad_heads, top_sum, delta, query_place, length
):
    scores = (
        jnp.einsum("qhd,khd->hqk", query_heads, key_heads, preferred_element_type=jnp.float32)
        * 0.125
    )
    mask = allowed_pairs(query_place, key_place, length)[None]
    probs = jnp.where(mask, jnp.exp(scores - top_sum[:, :, None]), 0.0)
    prob_grad = jnp.einsum(
        "qhd,khd->hqk", grad_heads, value_heads, preferred_element_type=jnp.float32
    )
    score_grad = (probs * (prob_grad - delta[:, :, None])).astype(jnp.bfloat16)
    value_grad = jnp.einsum(
        "hqk,qhd->khd", probs.astype(jnp.bfloat16), grad_heads, preferred_element_type=jnp.float32
    )
    key_grad = (
        jnp.einsum("hqk,qhd->khd", score_grad, query_heads, preferred_element_type=jnp.float32)
        * 0.125
    )
    return (key_grad, value_grad)


def on_device_any(
    tokens,
    cotangent,
    lengths,
    pairing,
    w_qkv,
    bias_q,
    bias_v,
    w_out,
    bias_out,
    ln1_gain,
    ln1_bias,
    w_in,
    bias_in,
    w_back,
    bias_back,
    ln2_gain,
    ln2_bias,
):
    gathered = (
        lax.all_gather(w_qkv, "fsdp", axis=0, tiled=True),
        lax.all_gather(bias_q, "fsdp", axis=0, tiled=True),
        lax.all_gather(bias_v, "fsdp", axis=0, tiled=True),
        lax.all_gather(w_out, "fsdp", axis=0, tiled=True),
        lax.all_gather(bias_out, "fsdp", axis=0, tiled=True),
        lax.all_gather(ln1_gain, "fsdp", axis=0, tiled=True),
        lax.all_gather(ln1_bias, "fsdp", axis=0, tiled=True),
        lax.all_gather(w_in, "fsdp", axis=0, tiled=True),
        lax.all_gather(bias_in, "fsdp", axis=0, tiled=True),
        lax.all_gather(w_back, "fsdp", axis=0, tiled=True),
        lax.all_gather(bias_back, "fsdp", axis=0, tiled=True),
        lax.all_gather(ln2_gain, "fsdp", axis=0, tiled=True),
        lax.all_gather(ln2_bias, "fsdp", axis=0, tiled=True),
    )
    (
        qkv_all,
        query_bias,
        value_bias,
        out_all,
        out_bias,
        gain_one,
        shift_one,
        in_all,
        in_bias,
        back_all,
        back_bias,
        gain_two,
        shift_two,
    ) = gathered
    rows = tokens.shape[1]
    half = rows // 2
    width = tokens.shape[2]
    length = lengths[0]
    query_place = places(pairing, lax.axis_index("ctx") * rows, rows, half)
    valid = query_place < length
    inputs = tokens[0]
    proj = jnp.dot(inputs, qkv_all, preferred_element_type=jnp.float32)
    queries = (proj[:, :width] + query_bias.astype(jnp.float32)).astype(jnp.bfloat16)
    keys = proj[:, width : 2 * width].astype(jnp.bfloat16)
    values = (proj[:, 2 * width :] + value_bias.astype(jnp.float32)).astype(jnp.bfloat16)
    query_heads = heads_of(queries)
    start_state = (
        jnp.full((HEADS, rows), neg_big, jnp.float32),
        jnp.zeros((HEADS, rows), jnp.float32),
        jnp.zeros((rows, HEADS, HEAD_DIM), jnp.float32),
    )
    fold = forward_fold(query_heads, query_place, pairing, length, half)
    top, total, summed = fold(
        start_state,
        (
            lax.all_gather(keys, "ctx", axis=0, tiled=True),
            lax.all_gather(values, "ctx", axis=0, tiled=True),
        ),
        jnp.int32(0),
    )
    top_sum = top + jnp.log(total)
    attended = (summed / jnp.transpose(total)[:, :, None]).reshape(rows, width)
    attended_low = attended.astype(jnp.bfloat16)
    resid_one = (
        inputs.astype(jnp.float32)
        + jnp.dot(attended_low, out_all, preferred_element_type=jnp.float32)
        + out_bias.astype(jnp.float32)
    )
    hidden = layer_norm(resid_one, gain_one.astype(jnp.float32), shift_one.astype(jnp.float32))
    hidden_low = hidden.astype(jnp.bfloat16)
    upper = jnp.dot(hidden_low, in_all, preferred_element_type=jnp.float32) + in_bias.astype(
        jnp.float32
    )
    active, gelu_back = jax.vjp(lambda value: jax.nn.gelu(value, approximate=False), upper)
    active_low = active.astype(jnp.bfloat16)
    resid_two = (
        hidden
        + jnp.dot(active_low, back_all, preferred_element_type=jnp.float32)
        + back_bias.astype(jnp.float32)
    )
    normed = layer_norm(resid_two, gain_two.astype(jnp.float32), shift_two.astype(jnp.float32))
    output = jnp.where(valid[:, None], normed, 0.0)
    qkv_back, out_back, gain_one_back, in_back, back_back, gain_two_back = (
        qkv_all,
        out_all,
        gain_one,
        in_all,
        back_all,
        gain_two,
    )
    grad_y = jnp.where(valid[:, None], cotangent[0].astype(jnp.float32), 0.0)
    grad_resid_two, gain_two_grad, shift_two_grad = norm_back(
        resid_two, gain_two_back.astype(jnp.float32), grad_y
    )
    grad_mixed = grad_resid_two.astype(jnp.bfloat16)
    back_grad = jnp.einsum("tf,td->fd", active_low, grad_mixed, preferred_element_type=jnp.float32)
    back_bias_grad = jnp.sum(grad_mixed.astype(jnp.float32), axis=0)
    grad_active = jnp.einsum("td,fd->tf", grad_mixed, back_back, preferred_element_type=jnp.float32)
    (grad_upper,) = gelu_back(grad_active)
    grad_upper_low = grad_upper.astype(jnp.bfloat16)
    in_grad = jnp.einsum(
        "td,tf->df", hidden_low, grad_upper_low, preferred_element_type=jnp.float32
    )
    in_bias_grad = jnp.sum(grad_upper_low.astype(jnp.float32), axis=0)
    grad_hidden = grad_resid_two + jnp.einsum(
        "tf,df->td", grad_upper_low, in_back, preferred_element_type=jnp.float32
    )
    grad_resid_one, gain_one_grad, shift_one_grad = norm_back(
        resid_one, gain_one_back.astype(jnp.float32), grad_hidden
    )
    grad_branch = grad_resid_one.astype(jnp.bfloat16)
    out_grad = jnp.einsum(
        "tc,td->cd", attended_low, grad_branch, preferred_element_type=jnp.float32
    )
    out_bias_grad = jnp.sum(grad_branch.astype(jnp.float32), axis=0)
    grad_attended = jnp.einsum(
        "td,cd->tc", grad_branch, out_back, preferred_element_type=jnp.float32
    ).astype(jnp.bfloat16)
    grad_heads = heads_of(grad_attended)
    delta = jnp.transpose(jnp.sum(grad_heads.astype(jnp.float32) * heads_of(attended), axis=2))
    query_fold = query_grad_fold(
        query_heads, grad_heads, top_sum, delta, query_place, pairing, length, half
    )
    empty_heads = jnp.zeros((rows, HEADS, HEAD_DIM), jnp.float32)
    query_grad = query_fold(
        empty_heads,
        (
            lax.all_gather(keys, "ctx", axis=0, tiled=True),
            lax.all_gather(values, "ctx", axis=0, tiled=True),
        ),
        jnp.int32(0),
    )
    stats = jnp.concatenate([jnp.transpose(top_sum), jnp.transpose(delta)], axis=1)
    stats_all = lax.all_gather(stats, "ctx", axis=0, tiled=True)
    key_heads = heads_of(keys)
    value_heads = heads_of(values)
    query_in = lax.all_gather(queries, "ctx", axis=0, tiled=True)
    grad_in = lax.all_gather(grad_attended, "ctx", axis=0, tiled=True)
    count = query_in.shape[0]
    span = block_width(count)
    place_in = places(pairing, jnp.int32(0), count, half)

    def step(index, state):
        offset = index * span
        query_block = heads_of(lax.dynamic_slice_in_dim(query_in, offset, span, 0))
        grad_block = heads_of(lax.dynamic_slice_in_dim(grad_in, offset, span, 0))
        stats_block = lax.dynamic_slice_in_dim(stats_all, offset, span, 0)
        place_block = lax.dynamic_slice_in_dim(place_in, offset, span, 0)
        key_part, value_part = key_terms(
            key_heads,
            value_heads,
            query_place,
            query_block,
            grad_block,
            jnp.transpose(stats_block[:, :HEADS]),
            jnp.transpose(stats_block[:, HEADS:]),
            place_block,
            length,
        )
        return (state[0] + key_part, state[1] + value_part)

    key_sum, value_sum = lax.fori_loop(0, count // span, step, (empty_heads, empty_heads))
    key_grad = key_sum.reshape(rows, width)
    value_grad = value_sum.reshape(rows, width)
    grad_proj = jnp.concatenate(
        [
            query_grad.reshape(rows, width).astype(jnp.bfloat16),
            key_grad.astype(jnp.bfloat16),
            value_grad.astype(jnp.bfloat16),
        ],
        axis=1,
    )
    qkv_grad = jnp.einsum("td,tf->df", inputs, grad_proj, preferred_element_type=jnp.float32)
    query_bias_grad = jnp.sum(grad_proj[:, :width].astype(jnp.float32), axis=0)
    value_bias_grad = jnp.sum(grad_proj[:, 2 * width :].astype(jnp.float32), axis=0)
    token_grad = grad_resid_one + jnp.einsum(
        "tf,df->td", grad_proj, qkv_back, preferred_element_type=jnp.float32
    )
    grads = (
        qkv_grad,
        query_bias_grad,
        value_bias_grad,
        out_grad,
        out_bias_grad,
        gain_one_grad,
        shift_one_grad,
        in_grad,
        in_bias_grad,
        back_grad,
        back_bias_grad,
        gain_two_grad,
        shift_two_grad,
    )
    shards = (
        lax.psum_scatter(
            grads[0].astype(jnp.bfloat16), "fsdp", scatter_dimension=0, tiled=True
        ).astype(jnp.float32),
        lax.psum_scatter(
            grads[1].astype(jnp.bfloat16), "fsdp", scatter_dimension=0, tiled=True
        ).astype(jnp.float32),
        lax.psum_scatter(
            grads[2].astype(jnp.bfloat16), "fsdp", scatter_dimension=0, tiled=True
        ).astype(jnp.float32),
        lax.psum_scatter(
            grads[3].astype(jnp.bfloat16), "fsdp", scatter_dimension=0, tiled=True
        ).astype(jnp.float32),
        lax.psum_scatter(
            grads[4].astype(jnp.bfloat16), "fsdp", scatter_dimension=0, tiled=True
        ).astype(jnp.float32),
        lax.psum_scatter(
            grads[5].astype(jnp.bfloat16), "fsdp", scatter_dimension=0, tiled=True
        ).astype(jnp.float32),
        lax.psum_scatter(
            grads[6].astype(jnp.bfloat16), "fsdp", scatter_dimension=0, tiled=True
        ).astype(jnp.float32),
        lax.psum_scatter(
            grads[7].astype(jnp.bfloat16), "fsdp", scatter_dimension=0, tiled=True
        ).astype(jnp.float32),
        lax.psum_scatter(
            grads[8].astype(jnp.bfloat16), "fsdp", scatter_dimension=0, tiled=True
        ).astype(jnp.float32),
        lax.psum_scatter(
            grads[9].astype(jnp.bfloat16), "fsdp", scatter_dimension=0, tiled=True
        ).astype(jnp.float32),
        lax.psum_scatter(
            grads[10].astype(jnp.bfloat16), "fsdp", scatter_dimension=0, tiled=True
        ).astype(jnp.float32),
        lax.psum_scatter(
            grads[11].astype(jnp.bfloat16), "fsdp", scatter_dimension=0, tiled=True
        ).astype(jnp.float32),
        lax.psum_scatter(
            grads[12].astype(jnp.bfloat16), "fsdp", scatter_dimension=0, tiled=True
        ).astype(jnp.float32),
    )
    totals = (
        lax.psum(shards[0].astype(jnp.bfloat16), "ctx").astype(jnp.float32),
        lax.psum(shards[1].astype(jnp.bfloat16), "ctx").astype(jnp.float32),
        lax.psum(shards[2].astype(jnp.bfloat16), "ctx").astype(jnp.float32),
        lax.psum(shards[3].astype(jnp.bfloat16), "ctx").astype(jnp.float32),
        lax.psum(shards[4].astype(jnp.bfloat16), "ctx").astype(jnp.float32),
        lax.psum(shards[5].astype(jnp.bfloat16), "ctx").astype(jnp.float32),
        lax.psum(shards[6].astype(jnp.bfloat16), "ctx").astype(jnp.float32),
        lax.psum(shards[7].astype(jnp.bfloat16), "ctx").astype(jnp.float32),
        lax.psum(shards[8].astype(jnp.bfloat16), "ctx").astype(jnp.float32),
        lax.psum(shards[9].astype(jnp.bfloat16), "ctx").astype(jnp.float32),
        lax.psum(shards[10].astype(jnp.bfloat16), "ctx").astype(jnp.float32),
        lax.psum(shards[11].astype(jnp.bfloat16), "ctx").astype(jnp.float32),
        lax.psum(shards[12].astype(jnp.bfloat16), "ctx").astype(jnp.float32),
    )
    return (output[None], token_grad[None]) + tuple(totals)


def low_lanes(shape):
    return lax.broadcasted_iota(jnp.int32, shape, 1) < 64


def spot_of(pair_ref, place):
    found = jnp.int32(0)
    for s in range(pair_ref.shape[0]):
        found = jnp.where(pair_ref[s] == place, s, found)
    return found


def attend(c, length, spot, keep_ref, mix_ref, lse_ref, turned_ref):
    left = low_lanes((256, BLK))
    zero = jnp.zeros((), jnp.bfloat16)
    keys = 256 * (c + 1)
    own = keep_ref[0, 2 * c : 2 * c + 2].reshape(256, BLK)
    shared = keep_ref[0, 2 * c + spot]
    query = jnp.concatenate(
        [jnp.where(left, own, zero), jnp.where(left[:BLK], zero, shared)], axis=0
    ) * jnp.bfloat16(0.125)
    key = keep_ref[1, : 2 * c + 2].reshape(keys, BLK)
    value = keep_ref[2, : 2 * c + 2].reshape(keys, BLK)
    scores = mask_scores(dot_nt(key, query), c, spot, length, 0, True)
    top = jnp.max(scores, axis=0, keepdims=True)
    probs = jnp.exp(scores - top)
    total = jnp.sum(probs, axis=0, keepdims=True)
    summed = lax.dot_general(
        value, probs.astype(jnp.bfloat16), (((0,), (0,)), ((), ())),
        preferred_element_type=jnp.float32,
    ) / total
    lse_ref[c] = top + jnp.log(total)
    part = summed[64:, 256:]
    none = jnp.zeros_like(part)
    first = jnp.where(spot == 0, part, none)
    second = jnp.where(spot == 0, none, part)
    mixed = jnp.concatenate([summed[:64, :256], jnp.concatenate([first, second], axis=1)], axis=0)
    mix_ref[c] = mixed
    turned_ref[2 * c : 2 * c + 2] = (
        jnp.transpose(mixed).astype(jnp.bfloat16).reshape(2, BLK, BLK)
    )


def mask_scores(scores, c, spot, length, start, edged):
    keys, width = scores.shape
    row = start + lax.broadcasted_iota(jnp.int32, (keys, width), 0)
    scores = jnp.where(row < length, scores, neg_big)
    if not edged:
        return scores
    edge = 256 * c
    lane = lax.broadcasted_iota(jnp.int32, (256, width), 1)
    query_place = edge + jnp.where(lane < 256, lane, lane - 256 + spot * BLK)
    key_place = edge + lax.broadcasted_iota(jnp.int32, (256, width), 0)
    seen = key_place <= query_place
    if c == 0:
        seen = seen | (key_place < NMEM)
    tail = jnp.where(seen, scores[keys - 256 :], neg_big)
    if keys == 256:
        return tail
    return jnp.concatenate([scores[: keys - 256], tail], axis=0)


def attend_back(
    c, length, spot, keep_ref, g_ref, mix_ref, lse_ref, q_sum, k_sum, v_sum
):
    zero = jnp.zeros((), jnp.bfloat16)
    left = low_lanes((256, BLK))
    left_half = left[:BLK]
    own = keep_ref[0, 2 * c : 2 * c + 2].reshape(256, BLK)
    shared = keep_ref[0, 2 * c + spot]
    query = jnp.concatenate(
        [jnp.where(left, own, zero), jnp.where(left_half, zero, shared)], axis=0
    ) * jnp.bfloat16(0.125)
    g_own = g_ref[2 * c : 2 * c + 2].reshape(256, BLK)
    g_shared = g_ref[2 * c + spot]
    grad = jnp.concatenate(
        [jnp.where(left, g_own, zero), jnp.where(left_half, zero, g_shared)], axis=0
    )
    turned = jnp.transpose(g_own.astype(jnp.float32)) * mix_ref[c]
    delta_own = jnp.sum(turned[:64], axis=0, keepdims=True)
    delta_pair = jnp.sum(turned[64:], axis=0, keepdims=True)
    delta = jnp.concatenate(
        [delta_own, jnp.where(spot == 0, delta_pair[:, :BLK], delta_pair[:, BLK:])], axis=1
    )
    lse = lse_ref[c]
    q_grad = jnp.zeros((384, BLK), jnp.float32)
    last = 2 * c + 2
    step = 8
    for low_block in range(0, last, step):
        high_block = min(low_block + step, last)
        cut = slice(low_block, high_block)
        count = high_block - low_block
        key = keep_ref[1, cut].reshape(count * BLK, BLK)
        value = keep_ref[2, cut].reshape(count * BLK, BLK)
        scores = mask_scores(
            dot_nt(key, query), c, spot, length, low_block * BLK, high_block == last
        )
        probs = jnp.exp(scores - lse)
        score_grad = (probs * (dot_nt(value, grad) - delta)).astype(jnp.bfloat16)
        v_part = dot_nn(probs.astype(jnp.bfloat16), grad)
        k_part = dot_nn(score_grad, query)
        v_sum[cut] += v_part.reshape(count, BLK, BLK)
        k_sum[cut] += k_part.reshape(count, BLK, BLK)
        q_grad = q_grad + lax.dot_general(
            score_grad, key, (((0,), (0,)), ((), ())), preferred_element_type=jnp.float32
        )
    q_grad = q_grad * 0.125
    part = q_grad[256:]
    none = jnp.zeros_like(part)
    first = jnp.where(spot == 0, part, none)
    second = jnp.where(spot == 0, none, part)
    q_sum[2 * c : 2 * c + 2] = jnp.where(
        left, q_grad[:256], jnp.concatenate([first, second], axis=0)
    ).reshape(2, BLK, BLK)


def smem():
    return pl.BlockSpec(memory_space=pltpu.SMEM)


def vmem():
    return pl.BlockSpec(memory_space=pltpu.VMEM)


MESH = pl.DeviceIdType.MESH


def remote(src, dst, sems, at, peer):
    return pltpu.make_async_remote_copy(
        src_ref=src, dst_ref=dst, send_sem=sems.at[(0,) + at], recv_sem=sems.at[(1,) + at],
        device_id=peer, device_id_type=MESH,
    )


def greet(peers):
    barrier = pltpu.get_barrier_semaphore()
    for peer in peers:
        pl.semaphore_signal(barrier, inc=1, device_id=peer, device_id_type=MESH)
    pl.semaphore_wait(barrier, len(peers))


def ring_peers(n):
    me = lax.axis_index("ctx")
    return [{"ctx": lax.rem(me + k, n)} for k in range(1, n)]


def two(block):
    return pl.ds(2 * block, 2)


def one(block):
    return block


def exchange_copies(n, in_ref, out_ref, sems, at=two):
    me = lax.axis_index("ctx")
    copies = []
    for k in range(1, n):
        peer = lax.rem(me + k, n)
        copies.append(
            remote(in_ref.at[at(peer)], out_ref.at[at(me)], sems, (k,), {"ctx": peer})
        )
    return copies


def own_copy(in_ref, out_ref, sem, at=two):
    me = lax.axis_index("ctx")
    return pltpu.make_async_copy(in_ref.at[at(me)], out_ref.at[at(me)], sem)


def beside(first, second, axis):
    return jnp.concatenate([first, second], axis=axis)


def fold(first, second, shared):
    return beside(
        beside(first[:, :HEAD_DIM], second[:, :HEAD_DIM], 1),
        beside(shared[:HEAD_DIM], shared[HEAD_DIM:], 1),
        0,
    )


def fold_pair(value, spot, lead):
    first, second = value[:BLK], value[BLK:]
    return fold(
        first, second, jnp.where(lead == spot, first[:, HEAD_DIM:], second[:, HEAD_DIM:])
    )


def unfold_shared(message):
    return beside(message[BLK:, :HEAD_DIM], message[BLK:, HEAD_DIM:], 0)


def unfold_block(message, later):
    own = jnp.where(later == 0, message[:BLK, :HEAD_DIM], message[:BLK, HEAD_DIM:])
    return beside(own, unfold_shared(message), 1)


def join_folded(messages, lead):
    pieces = []
    for group in range(HEADS // 3):
        pair = [messages(2 * group), messages(2 * group + 1)]
        for message in pair:
            pieces.append(beside(message[:BLK, :HEAD_DIM], message[:BLK, HEAD_DIM:], 0))
        even, odd = [unfold_shared(message) for message in pair]
        pieces.append(
            beside(jnp.where(lead == 0, even, odd), jnp.where(lead == 0, odd, even), 0)
        )
    return jnp.concatenate(pieces, axis=1)


def both(ref, peer):
    value = ref[2 * peer : 2 * peer + 2]
    return value.reshape(-1, value.shape[2])


def join_pairs(pairs):
    pieces = []
    for group in range(HEADS // 3):
        first, second = pairs(2 * group), pairs(2 * group + 1)
        shared = first[:, HEAD_DIM:].astype(jnp.float32) + second[:, HEAD_DIM:].astype(jnp.float32)
        pieces += [first[:, :HEAD_DIM], second[:, :HEAD_DIM], shared.astype(jnp.bfloat16)]
    return jnp.concatenate(pieces, axis=1)


def pair_of(value, peer):
    own = 3 * (peer // 2) + peer % 2
    shared = 3 * (peer // 2) + 2
    cut = lambda head: value[:, head * HEAD_DIM : (head + 1) * HEAD_DIM]
    return jnp.concatenate([cut(own), cut(shared)], axis=1)


def dot_nn(a, b):
    return jnp.dot(a, b, preferred_element_type=jnp.float32)


def dot_nt(a, b):
    return lax.dot_general(a, b, (((1,), (1,)), ((), ())), preferred_element_type=jnp.float32)


def column_sum(value):
    return jnp.sum(value, axis=0, keepdims=True)


def unit_of(value):
    mean = jnp.mean(value, axis=-1, keepdims=True)
    centred = value - mean
    scale = lax.rsqrt(jnp.mean(centred * centred, axis=-1, keepdims=True) + eps)
    return centred * scale, scale


def unit_back(unit, scale, scaled):
    return scale * (
        scaled
        - jnp.mean(scaled, axis=-1, keepdims=True)
        - unit * jnp.mean(scaled * unit, axis=-1, keepdims=True)
    )


(ROW_BQ, ROW_BV, ROW_BO, ROW_G1, ROW_S1, ROW_BB, ROW_G2, ROW_S2, ROW_BI) = range(9)


def gather_copies(src, full, sems, index):
    fsdp = lax.axis_index("fsdp")
    x, core = fsdp // 2, lax.rem(fsdp, 2)
    sibling, across = {"fsdp": 2 * x + 1 - core}, {"fsdp": 2 * (1 - x) + core}
    other = 2 * (1 - x) + core
    return (
        remote(src, full.at[fsdp], sems, (index, 0), across),
        remote(src, full.at[fsdp], sems, (index, 1), sibling),
        remote(full.at[other], full.at[other], sems, (index, 2), sibling),
    )


def chip_peers():
    fsdp = lax.axis_index("fsdp")
    x, core = fsdp // 2, lax.rem(fsdp, 2)
    return [{"fsdp": 2 * x + 1 - core}, {"fsdp": 2 * (1 - x) + core}]


def split_gather(src, full, sems, parts):
    ctx, fsdp = lax.axis_index("ctx"), lax.axis_index("fsdp")
    z, y = ctx // 2, lax.rem(ctx, 2)
    x, core = fsdp // 2, lax.rem(fsdp, 2)
    sibling, across = {"fsdp": 2 * x + 1 - core}, {"fsdp": 2 * (1 - x) + core}
    over_y = {"ctx": 2 * z + 1 - y}
    other = 2 * (1 - x) + core
    count = src.shape[0] // 2
    here = pl.ds(pl.multiple_of(y * count, count), count)
    there = pl.ds(pl.multiple_of((1 - y) * count, count), count)
    cross, side, on, off, whole = [], [], [], [], []
    for p in range(parts):
        width = src.shape[1] // parts
        cols = slice(p * width, (p + 1) * width)
        moved = full.at[other, here, cols]
        late = full.at[other, there, cols]
        cross.append(remote(src.at[here, cols], full.at[fsdp, here, cols], sems, (0, p), across))
        side.append(remote(moved, moved, sems, (1, p), over_y))
        on.append(remote(moved, moved, sems, (2, p), sibling))
        off.append(remote(late, late, sems, (3, p), sibling))
        whole.append(remote(src.at[:, cols], full.at[fsdp, :, cols], sems, (4, p), sibling))
    return cross, side, on, off, whole


def passed(split, p):
    cross, side, on, off, whole = split
    cross[p].wait_recv()
    side[p].start()
    on[p].start()


def handed(split, p):
    cross, side, on, off, whole = split
    side[p].wait_recv()
    off[p].start()


def gathered(split, p):
    cross, side, on, off, whole = split
    for copies in (whole, on, off):
        copies[p].wait_recv()


def front_kernel(
    n, pair_ref, len_ref, *refs
):
    vectors, refs = refs[:9], refs[9:]
    (
        tokens_ref, cot_ref, qkv_src, out_src, in_src, back_src,
        output_ref, grad_ref, left_ref, right_ref, resid_ref, sums_ref,
        keep_ref, mix_ref, lse_ref, qkv_ref,
        small_out, small, rows_ref, token_buf, cot, w_qkv, w_out, w_in, w_back, send_folded, send,
        packed_q, packed_k, packed_v, keep, mix,
        lse, turned, mixed_out, mixed_in, active, slope, output, grad_out, left, right, resid, sums,
        small_sem, qkv_sem, in_split_sem, back_split_sem, gather_sem, send_q, send_k, send_v, in_sem, own_sem, load_sem, ship_sem,
    ) = refs
    send_sem = (send_q, send_k, send_v)
    packed = (packed_q, packed_k, packed_v)
    low, wide = jnp.bfloat16, jnp.float32
    ctx, fsdp = lax.axis_index("ctx"), lax.axis_index("fsdp")
    x, core = fsdp // 2, lax.rem(fsdp, 2)
    spot = lax.rem(ctx, 2)
    lead = lax.rem(pair_ref[2 * ctx], 2)
    width = token_buf.shape[1]
    count = in_src.shape[1] // width
    loads = [
        pltpu.make_async_copy(src, dst, load_sem.at[i])
        for i, (src, dst) in enumerate(
            [
                (tokens_ref, token_buf),
                (cot_ref, cot),
                (qkv_src, w_qkv.at[fsdp]),
                (out_src, w_out.at[fsdp]),
                (in_src, w_in.at[fsdp]),
                (back_src, w_back.at[fsdp]),
            ]
        )
    ]
    cot_load = loads[1]
    for cp in loads[:3]:
        cp.start()
    part = width // 4
    small_out[...] = jnp.zeros_like(small_out)
    for i in range(8):
        small_out[i : i + 1] = vectors[i][...].astype(wide).reshape(1, part)
    inner_bias = vectors[8][...].astype(wide).reshape(1, -1)
    for j in range(4):
        small_out[8 + j : 9 + j] = inner_bias[:, j * part : (j + 1) * part]
    greet(ring_peers(n) + chip_peers())
    smalls = gather_copies(small_out, small, small_sem, 0)
    qkv_split = split_gather(qkv_src, w_qkv, qkv_sem, 3)
    in_split = split_gather(in_src, w_in, in_split_sem, count)
    back_split = split_gather(back_src, w_back, back_split_sem, 2)
    splits = (qkv_split, in_split, back_split)
    for step in (0, 1):
        smalls[step].start()
    for cp in qkv_split[0] + qkv_split[4]:
        cp.start()
    for cp in loads[3:]:
        cp.start()
    shards = gather_copies(out_src, w_out, gather_sem, 0)
    small[fsdp] = small_out[...]
    smalls[0].wait_recv()
    smalls[2].start()
    passed(qkv_split, 0)
    loads[0].wait()
    tokens = token_buf[...]
    left[0] = jnp.transpose(tokens).reshape(4, -1, 2 * BLK)
    smalls[1].wait_recv()
    smalls[2].wait_recv()
    for f in range(4):
        cols = slice(f * part, (f + 1) * part)
        rows_ref[:8, cols] = small[f, :8]
        for j in range(4):
            rows_ref[ROW_BI + f : ROW_BI + f + 1, j * part : (j + 1) * part] = small[
                f, 8 + j : 9 + j
            ]
    rows_ref[12:] = jnp.zeros_like(rows_ref[12:])
    row = lambda i: rows_ref[i : i + 1, :]
    passed(qkv_split, 1)
    handed(qkv_split, 0)
    passed(qkv_split, 2)
    for cp in shards[:2]:
        cp.start()
    for split in (in_split, back_split):
        for cp in split[0] + split[4]:
            cp.start()
    loads[2].wait()
    sends = []
    for p, bias in enumerate((ROW_BQ, None, ROW_BV)):
        if p:
            handed(qkv_split, p)
        gathered(qkv_split, p)
        value = dot_nn(tokens, w_qkv[:, :, p * width : (p + 1) * width].reshape(width, width))
        if bias is not None:
            value = value + row(bias)
        value = value.astype(low)
        for peer in range(n):
            both_heads = pair_of(value, peer)
            if p:
                send[p - 1, 2 * peer : 2 * peer + 2] = both_heads.reshape(2, BLK, BLK)
            else:
                send_folded[peer] = fold_pair(both_heads, peer % 2, lead)
        source, at = (send.at[p - 1], two) if p else (send_folded, one)
        copies = exchange_copies(n, source, packed[p], send_sem[p], at)
        copies.append(own_copy(source, packed[p], own_sem.at[2 + p], at))
        for cp in copies:
            cp.start()
        sends.append(copies)
    shipped = []

    def ship(src, dst):
        cp = pltpu.make_async_copy(src, dst, ship_sem.at[len(shipped)])
        cp.start()
        shipped.append(cp)

    ship(w_qkv, qkv_ref)
    spots = lax.broadcasted_iota(jnp.int32, (2 * BLK, 1), 0)
    place = jnp.where(
        spots < BLK,
        pair_ref[2 * ctx] * BLK + spots,
        pair_ref[2 * ctx + 1] * BLK + spots - BLK,
    )
    valid = place < len_ref[0]
    shards[0].wait_recv()
    shards[2].start()
    for p in range(count):
        passed(in_split, p)
        if p:
            handed(in_split, p - 1)
    passed(back_split, 0)
    handed(in_split, count - 1)
    spots_of = [spot_of(pair_ref, b) for b in range(2 * n)]
    for p in range(3):
        sends[p][-1].wait()
        for cp in sends[p][:-1]:
            cp.wait_recv()
        for b in range(2 * n):
            if p:
                keep[p, b] = packed[p][spots_of[b]]
            else:
                keep[p, b] = unfold_block(
                    packed[p][lax.div(spots_of[b], 2)], lax.rem(spots_of[b], 2)
                )
    passed(back_split, 1)

    ship(keep, keep_ref)
    for c in range(n):
        attend(c, len_ref[0], spot, keep, mix, lse, turned)
    for peer in range(n):
        first, second = turned[pair_ref[2 * peer]], turned[pair_ref[2 * peer + 1]]
        mixed_out[peer] = fold(first, second, first[:, HEAD_DIM:] + second[:, HEAD_DIM:])
    copies = exchange_copies(n, mixed_out, mixed_in, in_sem, one)
    for cp in copies:
        cp.start()
    own_mixed = own_copy(mixed_out, mixed_in, own_sem.at[1], one)
    own_mixed.start()
    ship(mix, mix_ref)
    ship(lse, lse_ref)
    sums[...] = jnp.zeros_like(sums)
    for cp in loads[3:]:
        cp.wait()
    for p in range(2):
        handed(back_split, p)
    shards[1].wait_recv()
    shards[2].wait_recv()
    for p in range(count):
        gathered(in_split, p)
    own_mixed.wait()
    for cp in copies:
        cp.wait_recv()
    attended = join_folded(lambda peer: mixed_in[peer], lead)
    resid_one = (
        tokens.astype(wide)
        + dot_nn(attended, w_out[...].reshape(width, width))
        + row(ROW_BO)
    )
    unit_one, scale_one = unit_of(resid_one)
    hidden = unit_one * row(ROW_G1) + row(ROW_S1)
    hidden_low = hidden.astype(low)
    resid_two = hidden + row(ROW_BB)
    cut = lambda t: pl.ds(pl.multiple_of(t * width, width), width)
    order = [fsdp, 2 * x + 1 - core, 2 * (1 - x) + core, 2 * (1 - x) + 1 - core]
    for step, t in enumerate(order):
        bias = rows_ref[pl.ds(ROW_BI + t, 1), :]
        upper = dot_nn(hidden_low, w_in[:, :, cut(t)].reshape(width, width)) + bias
        share = 0.5 * (1.0 + lax.erf(upper * (0.5**0.5)))
        slope[t] = share + upper * (jnp.exp(-0.5 * upper * upper) * (2 * math.pi) ** -0.5)
        some = (upper * share).astype(low)
        active[t] = some
        if step == 0:
            gathered(back_split, 0)
            gathered(back_split, 1)
        resid_two = resid_two + dot_nn(some, w_back[t])
    unit_two, scale_two = unit_of(resid_two)
    output[...] = jnp.where(valid, unit_two * row(ROW_G2) + row(ROW_S2), 0.0)
    cot_load.wait()
    grad_y = jnp.where(valid, cot[...].astype(wide), 0.0)
    sums[ROW_G2 : ROW_G2 + 1, :] = column_sum(grad_y * unit_two)
    sums[ROW_S2 : ROW_S2 + 1, :] = column_sum(grad_y)
    grad_resid_two = unit_back(unit_two, scale_two, grad_y * row(ROW_G2))
    grad_mixed = grad_resid_two.astype(low)
    right[5] = grad_mixed
    sums[ROW_BB : ROW_BB + 1, :] = column_sum(grad_mixed.astype(wide))
    grad_hidden = grad_resid_two
    for t in range(count):
        grad_upper = (dot_nt(grad_mixed, w_back[t]) * slope[t]).astype(low)
        right[1 + t] = grad_upper
        sums[ROW_BI + t : ROW_BI + t + 1, :] = column_sum(grad_upper.astype(wide))
        grad_hidden = grad_hidden + dot_nt(grad_upper, w_in[:, :, cut(t)].reshape(width, width))
    sums[ROW_G1 : ROW_G1 + 1, :] = column_sum(grad_hidden * unit_one)
    sums[ROW_S1 : ROW_S1 + 1, :] = column_sum(grad_hidden)
    grad_resid_one = unit_back(unit_one, scale_one, grad_hidden * row(ROW_G1))
    resid[...] = grad_resid_one
    grad_branch = grad_resid_one.astype(low)
    right[0] = grad_branch
    sums[ROW_BO : ROW_BO + 1, :] = column_sum(grad_branch.astype(wide))
    ship(resid, resid_ref)
    ship(right, right_ref)
    ship(sums, sums_ref)
    grad_attended = dot_nt(grad_branch, w_out[...].reshape(width, width)).astype(low)
    for peer in range(n):
        grad_out[peer] = fold_pair(pair_of(grad_attended, peer), peer % 2, lead)
    ship(grad_out, grad_ref)
    left[1] = jnp.transpose(attended).reshape(4, -1, 2 * BLK)
    left[2] = jnp.transpose(hidden_low).reshape(4, -1, 2 * BLK)
    for f in range(4):
        turned = jnp.transpose(active[f])
        for r in range(4):
            left[3 + r, f] = turned[r * width // 4 : (r + 1) * width // 4]
    ship(output, output_ref)
    ship(left, left_ref)
    for cps in (smalls, shards, copies) + sum(splits, ()):
        for cp in cps:
            cp.wait_send()
    for cps in sends:
        for cp in cps[:-1]:
            cp.wait_send()
    for cp in shipped:
        cp.wait()


def front(pairing, lengths, vectors, tokens, cotangent, w_qkv, w_out, w_in, w_back, n, name):
    count, width = tokens.shape
    low, wide = jnp.bfloat16, jnp.float32
    dma = pltpu.SemaphoreType.DMA
    shape = jax.ShapeDtypeStruct
    hbm = pl.BlockSpec(memory_space=pltpu.HBM)
    vec = pltpu.VMEM((16, width // 4), wide)
    results = [
        ((count, width), wide),
        ((n, BLK + HEAD_DIM, BLK), low),
        ((7, 4, width // 4, count), low),
        ((6, count, width), low),
        ((count, width), wide),
        ((16, width), wide),
        ((3, 2 * n, BLK, BLK), low),
        ((n, BLK, 2 * BLK), wide),
        ((n, 1, 3 * BLK), wide),
        ((4,) + w_qkv.shape, low),
    ]
    output, grad, left, right, resid, sums, keep, mix, lse, qkv = [pltpu.VMEM(*r) for r in results]
    blocks = pltpu.VMEM((2 * n, BLK, BLK), low)
    return pl.pallas_call(
        functools.partial(front_kernel, n),
        out_shape=tuple(shape(*r) for r in results),
        in_specs=[smem(), smem()] + [vmem()] * 9 + [hbm] * 6,
        out_specs=(hbm,) * 10,
        scratch_shapes=[
            vec,
            pltpu.VMEM((4, 16, width // 4), wide),
            pltpu.VMEM((16, width), wide),
            pltpu.VMEM((count, width), low),
            pltpu.VMEM((count, width), low),
            qkv,
            pltpu.VMEM((4,) + w_out.shape, low),
            pltpu.VMEM((4,) + w_in.shape, low),
            pltpu.VMEM((4,) + w_back.shape, low),
            grad,
            pltpu.VMEM((2, 2 * n, BLK, BLK), low),
            grad,
            blocks,
            blocks,
            keep,
            mix,
            lse,
            blocks,
            grad,
            grad,
            pltpu.VMEM((4, count, width), low),
            pltpu.VMEM((4, count, width), wide),
            output,
            grad,
            left,
            right,
            resid,
            sums,
            dma((2, 1, 3)),
            dma((2, 5, 3)),
            dma((2, 5, 4)),
            dma((2, 5, 2)),
            dma((2, 1, 3)),
            dma((2, n)),
            dma((2, n)),
            dma((2, n)),
            dma((2, n)),
            dma((5,)),
            dma((6,)),
            dma((10,)),
        ],
        compiler_params=pltpu.CompilerParams(
            collective_id=name, has_side_effects=True, vmem_limit_bytes=62 << 20
        ),
        name="front",
    )(pairing, lengths, *vectors, tokens, cotangent, w_qkv, w_out, w_in, w_back)


PARTS = 12


def sum_sources(chunk):
    if chunk < 4:
        return 3 + chunk, 8
    if chunk < 8:
        return 2, chunk
    return (1, 3) if chunk < 9 else (0, chunk - 9)


STEPS = 65
PLAN = {
    "pair": {0: 0, 1: 1, 2: 2, 3: 3, 6: 4, 7: 5, 13: 6, 15: 7, 19: 8, 21: 9, 29: 10, 32: 11},
    "x": {3: 0, 4: 1, 5: 2, 7: 3, 12: 4, 13: 5, 14: 6, 18: 7, 23: 8, 30: 9, 36: 10, 41: 11},
    "y": {9: 0, 10: 1, 16: 2, 17: 3, 18: 4, 21: 5, 24: 6, 26: 7, 30: 8, 36: 9, 46: 10, 50: 11},
    "near": {11: 0, 19: 1, 20: 2, 24: 3, 25: 4, 28: 5, 32: 6, 38: 7, 42: 8, 44: 9, 49: 10, 57: 11},
    "far": {22: 0, 25: 1, 26: 2, 31: 3, 33: 4, 39: 5, 41: 6, 44: 7, 47: 8, 52: 9, 55: 10, 60: 11},
    "own": {27: 0, 29: 1, 30: 2, 37: 3, 40: 4, 45: 5, 49: 6, 50: 7, 53: 8, 57: 9, 58: 10, 61: 11},
    "wide": {30: 0, 31: 1, 34: 2, 43: 3, 48: 4, 50: 5, 51: 6, 56: 7, 57: 8, 59: 9, 61: 10, 62: 11},
    "last": {35: 0, 38: 1, 42: 2, 47: 3, 52: 4, 54: 5, 55: 6, 58: 7, 60: 8, 61: 9, 63: 10, 64: 11},
}
ATTEND_AT = (8, 9, 10)
JOIN_AT = (16, 24, 28)
SMALL_AT = (46, 49, 52, 61, 62, 64)
TOKEN_AT = 44


def planned(name, step):
    return PLAN[name].get(step, -1)


def only(condition):
    def run(body):
        if condition:
            body()

    return run


def back_kernel(
    n, pair_ref, len_ref, grad_ref, keep_src, mix_src, lse_src, left_src, right_src,
    sums_src, resid_src, qkv_ref,
    total_out, token_ref, small_out,
    keep_ref, mix_ref, lse_ref, left_ref, sums_ref, resid_ref, total_ref,
    grad_in, g_all, q_sum, k_sum, v_sum, folded_out, folded_in,
    blocks_out, blocks_in, w_qkv, right_all,
    pair_out, pair_in, x_out, x_in, y_out, y_in, y_keep, near_out, near_in, near_keep,
    far_out, far_in, far_keep, s_out, s_in,
    load_sem, ship_sem,
    grad_sem, block_q, block_k, block_v, own_sem, pair_sem, x_sem, y_sem, near_sem, far_sem,
    own_z_sem, wide_sem, last_sem, s_sem,
):
    block_sem = (block_q, block_k, block_v)
    low, wide = jnp.bfloat16, jnp.float32
    ctx = lax.axis_index("ctx")
    fsdp = lax.axis_index("fsdp")
    z, y = ctx // 2, lax.rem(ctx, 2)
    odd, upper = lax.rem(z, 2), z // 2
    x, core = fsdp // 2, lax.rem(fsdp, 2)
    sibling = {"fsdp": 2 * x + 1 - core}
    across = {"fsdp": 2 * (1 - x) + core}
    over_y = {"ctx": 2 * z + 1 - y}
    near = {"ctx": 2 * (2 * upper + 1 - odd) + y}
    far = {"ctx": 2 * (2 * (1 - upper) + odd) + y}
    mine = 2 * odd + upper
    loads = [
        pltpu.make_async_copy(src, dst, load_sem.at[i])
        for i, (src, dst) in enumerate(
            [
                (right_src, right_all.at[3:]),
                (left_src, left_ref),
                (keep_src, keep_ref),
                (mix_src, mix_ref),
                (lse_src, lse_ref),
                (sums_src, sums_ref),
                (resid_src, resid_ref),
            ]
        )
    ]
    for cp in loads:
        cp.start()
    greet(ring_peers(n) + [sibling, across])
    lead = lax.rem(pair_ref[2 * ctx], 2)
    grads = exchange_copies(n, grad_ref, grad_in, grad_sem, one)
    for cp in grads:
        cp.start()
    own_grad = own_copy(grad_ref, grad_in, own_sem.at[0], one)
    own_grad.start()
    load = pltpu.make_async_copy(qkv_ref, w_qkv, own_sem.at[1])
    load.start()
    blocks = [
        exchange_copies(n, folded_out, folded_in, block_sem[0], one)
    ] + [
        exchange_copies(n, blocks_out.at[p], blocks_in.at[p], block_sem[1 + p])
        for p in range(2)
    ]
    own = [own_copy(folded_out, folded_in, own_sem.at[2], one)] + [
        own_copy(blocks_out.at[p], blocks_in.at[p], own_sem.at[3 + p]) for p in range(2)
    ]
    k_sum[...] = jnp.zeros_like(k_sum)
    v_sum[...] = jnp.zeros_like(v_sum)
    chunks = keep_ref.shape[1] // 2

    def attend_some(first, last):
        for c in range(first, last):
            attend_back(
                c, len_ref[0], y, keep_ref, g_all, mix_ref, lse_ref, q_sum, k_sum, v_sum
            )

    def attend_step(t):
        @only(t == ATTEND_AT[0])
        def _():
            own_grad.wait()
            for cp in loads[2:5]:
                cp.wait()
            for cp in grads:
                cp.wait_recv()
            for b in range(2 * chunks):
                found = spot_of(pair_ref, b)
                g_all[b] = unfold_block(grad_in[lax.div(found, 2)], lax.rem(found, 2))
            attend_some(0, chunks // 2)

        @only(t == ATTEND_AT[1])
        def _():
            attend_some(chunks // 2, chunks - 2)

        @only(t == ATTEND_AT[2])
        def _():
            attend_some(chunks - 2, chunks)
            for peer in range(n):
                first, second = q_sum[pair_ref[2 * peer]], q_sum[pair_ref[2 * peer + 1]]
                folded_out[peer] = fold(
                    first, second, first[:, HEAD_DIM:] + second[:, HEAD_DIM:]
                ).astype(low)
            for p, total in enumerate((None, k_sum, v_sum)):
                if p:
                    for s in range(2 * chunks):
                        blocks_out[p - 1, s] = total[pair_ref[s]].astype(low)
                for cp in blocks[p]:
                    cp.start()
                own[p].start()

    def slot(c):
        return c % 4

    def pair_copy(c):
        return remote(pair_out.at[c % 2], pair_in.at[c], pair_sem, (c,), sibling)

    def x_copy(c):
        return remote(x_out.at[c], x_in.at[c], x_sem, (c,), across)

    def y_copy(c):
        return remote(y_out.at[slot(c)], y_in.at[c], y_sem, (c,), over_y)

    def near_copy(c):
        return remote(near_out.at[slot(c)], near_in.at[c], near_sem, (c,), near)

    def far_copy(c):
        return remote(far_out.at[slot(c)], far_in.at[c], far_sem, (c,), far)

    def own_z_copy(c):
        piece = total_ref.at[c, y, mine]
        return remote(piece, piece, own_z_sem, (c,), far)

    def wide_copy(c):
        piece = total_ref.at[c, y, two(odd)]
        return remote(piece, piece, wide_sem, (c,), near)

    def last_copy(c):
        piece = total_ref.at[c, y]
        return remote(piece, piece, last_sem, (c,), over_y)

    def reuse(copy, c, slots):
        @only(c >= slots)
        def _():
            copy(c - slots).wait_send()

    def partial(c, shard):
        left, right = sum_sources(c)
        return dot_nn(left_ref[left, shard], right_all[right])

    def stage_pair(c):
        reuse(pair_copy, c, 2)
        for side in range(2):
            pair_out[c % 2, side] = partial(c, 2 * side + 1 - core).astype(low)
        pair_copy(c).start()

    def stage_x(c):
        pair_copy(c).wait_recv()
        x_out[c] = (partial(c, 2 * (1 - x) + core) + pair_in[c, 1 - x].astype(wide)).astype(low)
        x_copy(c).start()

    def stage_y(c):
        mine_sum = partial(c, 2 * x + core) + pair_in[c, x].astype(wide)
        x_copy(c).wait_recv()
        total = mine_sum + x_in[c].astype(wide)
        first, second = total[:, :384], total[:, 384:]
        reuse(y_copy, c, 4)
        y_out[slot(c)] = jnp.where(y == 0, second, first).astype(low)
        y_copy(c).start()
        y_keep[slot(c)] = jnp.where(y == 0, first, second)

    def stage_near(c):
        y_copy(c).wait_recv()
        total = y_keep[slot(c)] + y_in[c].astype(wide)
        first, second = total[:96], total[96:]
        reuse(near_copy, c, 4)
        near_out[slot(c)] = jnp.where(odd == 0, second, first).astype(low)
        near_copy(c).start()
        near_keep[slot(c)] = jnp.where(odd == 0, first, second)

    def stage_far(c):
        near_copy(c).wait_recv()
        total = near_keep[slot(c)] + near_in[c].astype(wide)
        first, second = total[:48], total[48:]
        reuse(far_copy, c, 4)
        far_out[slot(c)] = jnp.where(upper == 0, second, first).astype(low)
        far_copy(c).start()
        far_keep[slot(c)] = jnp.where(upper == 0, first, second)

    def stage_own(c):
        far_copy(c).wait_recv()
        total_ref[c, y, mine] = (far_keep[slot(c)] + far_in[c].astype(wide)).astype(low)
        own_z_copy(c).start()

    def stage_wide(c):
        own_z_copy(c).wait_recv()
        wide_copy(c).start()

    def stage_last(c):
        wide_copy(c).wait_recv()
        last_copy(c).start()

    def small_step(t):
        peers = [sibling, across, over_y, near, far]
        copies = [
            remote(s_out.at[k], s_in.at[k], s_sem, (k,), peer) for k, peer in enumerate(peers)
        ]

        for p in range(3):

            @only(t == JOIN_AT[p])
            def _():
                own[p].wait()
                for cp in blocks[p]:
                    cp.wait_recv()
                if p:
                    right_all[p] = join_pairs(lambda peer: both(blocks_in.at[p - 1], peer))
                else:
                    right_all[p] = join_folded(lambda peer: folded_in[peer], lead)

        @only(t == SMALL_AT[0])
        def _():
            loads[5].wait()
            s_out[0] = sums_ref[...]
            s_out[0, ROW_BQ : ROW_BQ + 1] = column_sum(right_all[0].astype(wide))
            s_out[0, ROW_BV : ROW_BV + 1] = column_sum(right_all[2].astype(wide))
            copies[0].start()

        for k in range(1, 5):

            @only(t == SMALL_AT[k])
            def _():
                copies[k - 1].wait()
                s_out[k] = s_out[k - 1] + s_in[k - 1]
                copies[k].start()

        @only(t == SMALL_AT[5])
        def _():
            copies[4].wait()
            total = s_out[4] + s_in[4]
            quarter = total.shape[1] // 4
            cuts = [slice(f * quarter, (f + 1) * quarter) for f in range(4)]
            pick = lambda choices: sum(
                jnp.where(fsdp == f, choice, 0.0) for f, choice in enumerate(choices)
            )
            small_out[...] = jnp.zeros_like(small_out)
            small_out[:8] = pick([total[:8, cut] for cut in cuts])
            line = pick([total[ROW_BI + f : ROW_BI + f + 1] for f in range(4)])
            for j, cut in enumerate(cuts):
                small_out[8 + j : 9 + j] = line[:, cut]

        @only(t == TOKEN_AT)
        def _():
            load.wait()
            loads[6].wait()
            width = resid_ref.shape[1]
            token_ref[...] = resid_ref[...] + sum(
                dot_nt(
                    right_all[part],
                    w_qkv[:, :, part * width : (part + 1) * width].reshape(width, width),
                )
                for part in range(3)
            )

    stages = [
        ("pair", stage_pair),
        ("x", stage_x),
        ("last", stage_last),
        ("wide", stage_wide),
        ("own", stage_own),
        ("far", stage_far),
        ("near", stage_near),
        ("y", stage_y),
    ]

    def step(t, carry):
        attend_step(t)
        small_step(t)
        for name, stage in stages:
            c = planned(name, t)

            @only(c >= 0)
            def _():
                stage(c)

        return carry

    loads[0].wait()
    loads[1].wait()
    for at in range(STEPS):
        step(at, 0)

    def ship(c):
        return pltpu.make_async_copy(total_ref.at[c], total_out.at[c], ship_sem.at[c])

    def drain(c, carry):
        x_copy(c).wait_send()
        own_z_copy(c).wait_send()
        wide_copy(c).wait_send()
        last_copy(c).wait()
        ship(c).start()
        return carry

    for c in range(PARTS):
        drain(c, 0)
    for c in range(PARTS - 4, PARTS):
        y_copy(c).wait_send()
        near_copy(c).wait_send()
        far_copy(c).wait_send()
    for c in (PARTS - 2, PARTS - 1):
        pair_copy(c).wait_send()
    for cp in grads + blocks[0] + blocks[1] + blocks[2]:
        cp.wait_send()
    for c in range(PARTS):
        ship(c).wait()


def back(pairing, lengths, grad, keep, mix, lse, left, right, sums, resid, qkv_full, name):
    blocks = keep.shape[1]
    n = blocks // 2
    low, wide = jnp.bfloat16, jnp.float32
    dma = pltpu.SemaphoreType.DMA
    shape = jax.ShapeDtypeStruct
    total = pltpu.VMEM((blocks, BLK, BLK), wide)
    hbm = pl.BlockSpec(memory_space=pltpu.HBM)
    return pl.pallas_call(
        functools.partial(back_kernel, n),
        out_shape=(
            shape((PARTS, 2, 4, 48, 384), low),
            shape(resid.shape, wide),
            shape((16, 192), wide),
        ),
        in_specs=[smem()] * 2 + [hbm] * 9,
        out_specs=(hbm, vmem(), vmem()),
        scratch_shapes=[
            pltpu.VMEM(keep.shape, low),
            pltpu.VMEM(mix.shape, wide),
            pltpu.VMEM(lse.shape, wide),
            pltpu.VMEM(left.shape, low),
            pltpu.VMEM(sums.shape, wide),
            pltpu.VMEM(resid.shape, wide),
            pltpu.VMEM((PARTS, 2, 4, 48, 384), low),
            pltpu.VMEM(grad.shape, low),
            pltpu.VMEM((blocks, BLK, BLK), low),
            total, total, total,
            pltpu.VMEM(grad.shape, low),
            pltpu.VMEM(grad.shape, low),
            pltpu.VMEM((2, blocks, BLK, BLK), low),
            pltpu.VMEM((2, blocks, BLK, BLK), low),
            pltpu.VMEM(qkv_full.shape, low),
            pltpu.VMEM((9,) + right.shape[1:], low),
            pltpu.VMEM((2, 2, 192, 768), low),
            pltpu.VMEM((PARTS, 2, 192, 768), low),
            pltpu.VMEM((PARTS, 192, 768), low),
            pltpu.VMEM((PARTS, 192, 768), low),
            pltpu.VMEM((4, 192, 384), low),
            pltpu.VMEM((PARTS, 192, 384), low),
            pltpu.VMEM((4, 192, 384), wide),
            pltpu.VMEM((4, 96, 384), low),
            pltpu.VMEM((PARTS, 96, 384), low),
            pltpu.VMEM((4, 96, 384), wide),
            pltpu.VMEM((4, 48, 384), low),
            pltpu.VMEM((PARTS, 48, 384), low),
            pltpu.VMEM((4, 48, 384), wide),
            pltpu.VMEM((5,) + sums.shape, wide),
            pltpu.VMEM((5,) + sums.shape, wide),
            dma((7,)),
            dma((PARTS,)),
            dma((2, n)),
            dma((2, n)),
            dma((2, n)),
            dma((2, n)),
            dma((5,)),
        ]
        + [dma((2, PARTS))] * 8
        + [dma((2, 5))],
        compiler_params=pltpu.CompilerParams(
            collective_id=name, has_side_effects=True, vmem_limit_bytes=61 << 20
        ),
        name="back",
    )(pairing, lengths, grad, keep, mix, lse, left, right, sums, resid, qkv_full)


def finish_kernel(
    total_ref, small_ref, output_ref, token_ref,
    output_out, token_out, qkv_out, out_out, in_out, back_out, *refs
):
    lines, (total, small, through, stage, sems) = refs[:9], refs[9:]
    arrive = [
        pltpu.make_async_copy(total_ref.at[c], total.at[c], sems.at[PARTS + 2 + c])
        for c in range(PARTS)
    ] + [
        pltpu.make_async_copy(small_ref, small, sems.at[2 * PARTS + 2]),
        pltpu.make_async_copy(output_ref, through.at[0], sems.at[2 * PARTS + 3]),
        pltpu.make_async_copy(token_ref, through.at[1], sems.at[2 * PARTS + 4]),
    ]
    for cp in arrive:
        cp.start()
    copies = [
        pltpu.make_async_copy(through.at[0], output_out, sems.at[PARTS]),
        pltpu.make_async_copy(through.at[1], token_out, sems.at[PARTS + 1]),
    ]
    targets = [back_out.at[192 * k : 192 * k + 192] for k in range(4)]
    targets += [in_out.at[:, 768 * k : 768 * k + 768] for k in range(4)]
    targets += [out_out]
    targets += [qkv_out.at[:, 768 * k : 768 * k + 768] for k in range(3)]
    for c, target in enumerate(targets):
        arrive[c].wait()
        for half in range(2):
            for spot in range(4):
                stage[c, 48 * spot : 48 * spot + 48, 384 * half : 384 * half + 384] = total[
                    c, half, spot
                ].astype(jnp.float32)
        copies.append(pltpu.make_async_copy(stage.at[c], target, sems.at[c]))
        copies[-1].start()
    for k in range(2):
        arrive[PARTS + 1 + k].wait()
        copies[k].start()
    arrive[PARTS].wait()
    for i in range(8):
        lines[i][...] = small[i]
    for j in range(4):
        lines[8][192 * j : 192 * j + 192] = small[ROW_BI + j]
    for cp in copies:
        cp.wait()


def finish(total, small, output, token):
    shape = jax.ShapeDtypeStruct
    wide = jnp.float32
    hbm = pl.BlockSpec(memory_space=pltpu.HBM)
    return pl.pallas_call(
        finish_kernel,
        out_shape=(
            shape(output.shape, wide),
            shape(token.shape, wide),
            shape((192, 2304), wide),
            shape((192, 768), wide),
            shape((192, 3072), wide),
            shape((768, 768), wide),
        )
        + (shape((192,), wide),) * 8
        + (shape((768,), wide),),
        in_specs=[hbm] * 4,
        out_specs=(hbm,) * 6 + (vmem(),) * 9,
        scratch_shapes=[
            pltpu.VMEM(total.shape, total.dtype),
            pltpu.VMEM(small.shape, wide),
            pltpu.VMEM((2,) + token.shape, wide),
            pltpu.VMEM((PARTS, 192, 768), wide),
            pltpu.SemaphoreType.DMA((2 * PARTS + 5,)),
        ],
        compiler_params=pltpu.CompilerParams(vmem_limit_bytes=62 << 20),
        name="finish",
    )(total, small, output, token)


def on_device_spread(
    tokens,
    cotangent,
    lengths,
    pairing,
    w_qkv,
    bias_q,
    bias_v,
    w_out,
    bias_out,
    ln1_gain,
    ln1_bias,
    w_in,
    bias_in,
    w_back,
    bias_back,
    ln2_gain,
    ln2_bias,
):
    n = pairing.shape[0] // 2
    inputs = tokens[0]
    vectors = [bias_q, bias_v, bias_out, ln1_gain, ln1_bias, bias_back, ln2_gain, ln2_bias]
    vectors += [bias_in]
    output, grad, left, right, resid, sums, keep, mix, lse, qkv_full = front(
        pairing, lengths, vectors, inputs, cotangent[0], w_qkv, w_out, w_in, w_back, n, 0
    )
    total, token_grad, small_sum = back(
        pairing, lengths, grad, keep, mix, lse, left, right, sums, resid, qkv_full, 1
    )
    (
        output, token_grad, qkv_sum, out_sum, in_sum, back_sum,
        bq, bv, bo, g1, s1, bb, g2, s2, bi,
    ) = finish(total, small_sum, output, token_grad)
    return (
        output[None], token_grad[None], qkv_sum, bq, bv, out_sum, bo, g1, s1, in_sum, bi,
        back_sum, bb, g2, s2,
    )


def solution(mesh):
    return jax.shard_map(
        on_device_spread if mesh.shape["ctx"] == 8 else on_device_any,
        mesh=mesh,
        in_specs=(
            P("fsdp", "ctx", None),
            P("fsdp", "ctx", None),
            P("fsdp"),
            P(),
            P("fsdp", None),
            P("fsdp"),
            P("fsdp"),
            P("fsdp", None),
            P("fsdp"),
            P("fsdp"),
            P("fsdp"),
            P("fsdp", None),
            P("fsdp"),
            P("fsdp", None),
            P("fsdp"),
            P("fsdp"),
            P("fsdp"),
        ),
        out_specs=(
            P("fsdp", "ctx", None),
            P("fsdp", "ctx", None),
            P("fsdp", None),
            P("fsdp"),
            P("fsdp"),
            P("fsdp", None),
            P("fsdp"),
            P("fsdp"),
            P("fsdp"),
            P("fsdp", None),
            P("fsdp"),
            P("fsdp", None),
            P("fsdp"),
            P("fsdp"),
            P("fsdp"),
        ),
        check_vma=False,
    )
```

```python
import functools
import math

import jax
import jax.numpy as jnp
from jax import lax
from jax.experimental import pallas as pl
from jax.experimental.pallas import tpu as pltpu
from jax.sharding import PartitionSpec as P

HEADS = 12
HEAD_DIM = 64
NMEM = 10
BLK = 128


eps = 1e-12
neg_big = -1e30


def layer_norm(value, gain, shift):
    mean = jnp.mean(value, axis=-1, keepdims=True)
    centred = value - mean
    variance = jnp.mean(centred * centred, axis=-1, keepdims=True)
    return centred * lax.rsqrt(variance + eps) * gain + shift


def norm_back(value, gain, grad):
    mean = jnp.mean(value, axis=-1, keepdims=True)
    centred = value - mean
    scale = lax.rsqrt(jnp.mean(centred * centred, axis=-1, keepdims=True) + eps)
    unit = centred * scale
    scaled = grad * gain
    inner = (
        scaled
        - jnp.mean(scaled, axis=-1, keepdims=True)
        - unit * jnp.mean(scaled * unit, axis=-1, keepdims=True)
    )
    return (scale * inner, jnp.sum(grad * unit, axis=0), jnp.sum(grad, axis=0))


def block_width(count):
    return math.gcd(count, 512)


def places(pairing, start, count, half):
    rows = start + jnp.arange(count, dtype=jnp.int32)
    owners = rows // half
    spots = jnp.arange(pairing.shape[0], dtype=jnp.int32)
    picked = jnp.sum(jnp.where(owners[:, None] == spots[None, :], pairing[None, :], 0), axis=1)
    return picked * half + rows % half


def allowed_pairs(query_place, key_place, length):
    before = (key_place[None, :] <= query_place[:, None]) | (key_place[None, :] < NMEM)
    return (key_place[None, :] < length) & before


def heads_of(value):
    return value.reshape(value.shape[0], HEADS, HEAD_DIM)


def forward_fold(query_heads, query_place, pairing, length, half):

    def fold(carry, piece, start):
        keys, values = piece
        count = keys.shape[0]
        width = block_width(count)
        key_place = places(pairing, start, count, half)

        def step(index, state):
            top, total, summed = state
            offset = index * width
            key_heads = heads_of(lax.dynamic_slice_in_dim(keys, offset, width, 0))
            value_heads = heads_of(lax.dynamic_slice_in_dim(values, offset, width, 0))
            mask = allowed_pairs(
                query_place, lax.dynamic_slice_in_dim(key_place, offset, width, 0), length
            )[None]
            scores = (
                jnp.einsum(
                    "qhd,khd->hqk", query_heads, key_heads, preferred_element_type=jnp.float32
                )
                * 0.125
            )
            scores = jnp.where(mask, scores, neg_big)
            new_top = jnp.maximum(top, jnp.max(scores, axis=2))
            shrink = jnp.exp(top - new_top)
            probs = jnp.where(mask, jnp.exp(scores - new_top[:, :, None]), 0.0)
            total = total * shrink + jnp.sum(probs, axis=2)
            update = jnp.einsum(
                "hqk,khd->qhd",
                probs.astype(jnp.bfloat16),
                value_heads,
                preferred_element_type=jnp.float32,
            )
            summed = summed * jnp.transpose(shrink)[:, :, None] + update
            return (new_top, total, summed)

        return lax.fori_loop(0, count // width, step, carry)

    return fold


def query_grad_fold(query_heads, grad_heads, top_sum, delta, query_place, pairing, length, half):

    def fold(carry, piece, start):
        keys, values = piece
        count = keys.shape[0]
        width = block_width(count)
        key_place = places(pairing, start, count, half)

        def step(index, summed):
            offset = index * width
            key_heads = heads_of(lax.dynamic_slice_in_dim(keys, offset, width, 0))
            value_heads = heads_of(lax.dynamic_slice_in_dim(values, offset, width, 0))
            mask = allowed_pairs(
                query_place, lax.dynamic_slice_in_dim(key_place, offset, width, 0), length
            )[None]
            scores = (
                jnp.einsum(
                    "qhd,khd->hqk", query_heads, key_heads, preferred_element_type=jnp.float32
                )
                * 0.125
            )
            probs = jnp.where(mask, jnp.exp(scores - top_sum[:, :, None]), 0.0)
            prob_grad = jnp.einsum(
                "qhd,khd->hqk", grad_heads, value_heads, preferred_element_type=jnp.float32
            )
            score_grad = (probs * (prob_grad - delta[:, :, None])).astype(jnp.bfloat16)
            return (
                summed
                + jnp.einsum(
                    "hqk,khd->qhd", score_grad, key_heads, preferred_element_type=jnp.float32
                )
                * 0.125
            )

        return lax.fori_loop(0, count // width, step, carry)

    return fold


def key_terms(
    key_heads, value_heads, key_place, query_heads, grad_heads, top_sum, delta, query_place, length
):
    scores = (
        jnp.einsum("qhd,khd->hqk", query_heads, key_heads, preferred_element_type=jnp.float32)
        * 0.125
    )
    mask = allowed_pairs(query_place, key_place, length)[None]
    probs = jnp.where(mask, jnp.exp(scores - top_sum[:, :, None]), 0.0)
    prob_grad = jnp.einsum(
        "qhd,khd->hqk", grad_heads, value_heads, preferred_element_type=jnp.float32
    )
    score_grad = (probs * (prob_grad - delta[:, :, None])).astype(jnp.bfloat16)
    value_grad = jnp.einsum(
        "hqk,qhd->khd", probs.astype(jnp.bfloat16), grad_heads, preferred_element_type=jnp.float32
    )
    key_grad = (
        jnp.einsum("hqk,qhd->khd", score_grad, query_heads, preferred_element_type=jnp.float32)
        * 0.125
    )
    return (key_grad, value_grad)


def on_device_any(
    tokens,
    cotangent,
    lengths,
    pairing,
    w_qkv,
    bias_q,
    bias_v,
    w_out,
    bias_out,
    ln1_gain,
    ln1_bias,
    w_in,
    bias_in,
    w_back,
    bias_back,
    ln2_gain,
    ln2_bias,
):
    gathered = (
        lax.all_gather(w_qkv, "fsdp", axis=0, tiled=True),
        lax.all_gather(bias_q, "fsdp", axis=0, tiled=True),
        lax.all_gather(bias_v, "fsdp", axis=0, tiled=True),
        lax.all_gather(w_out, "fsdp", axis=0, tiled=True),
        lax.all_gather(bias_out, "fsdp", axis=0, tiled=True),
        lax.all_gather(ln1_gain, "fsdp", axis=0, tiled=True),
        lax.all_gather(ln1_bias, "fsdp", axis=0, tiled=True),
        lax.all_gather(w_in, "fsdp", axis=0, tiled=True),
        lax.all_gather(bias_in, "fsdp", axis=0, tiled=True),
        lax.all_gather(w_back, "fsdp", axis=0, tiled=True),
        lax.all_gather(bias_back, "fsdp", axis=0, tiled=True),
        lax.all_gather(ln2_gain, "fsdp", axis=0, tiled=True),
        lax.all_gather(ln2_bias, "fsdp", axis=0, tiled=True),
    )
    (
        qkv_all,
        query_bias,
        value_bias,
        out_all,
        out_bias,
        gain_one,
        shift_one,
        in_all,
        in_bias,
        back_all,
        back_bias,
        gain_two,
        shift_two,
    ) = gathered
    rows = tokens.shape[1]
    half = rows // 2
    width = tokens.shape[2]
    length = lengths[0]
    query_place = places(pairing, lax.axis_index("ctx") * rows, rows, half)
    valid = query_place < length
    inputs = tokens[0]
    proj = jnp.dot(inputs, qkv_all, preferred_element_type=jnp.float32)
    queries = (proj[:, :width] + query_bias.astype(jnp.float32)).astype(jnp.bfloat16)
    keys = proj[:, width : 2 * width].astype(jnp.bfloat16)
    values = (proj[:, 2 * width :] + value_bias.astype(jnp.float32)).astype(jnp.bfloat16)
    query_heads = heads_of(queries)
    start_state = (
        jnp.full((HEADS, rows), neg_big, jnp.float32),
        jnp.zeros((HEADS, rows), jnp.float32),
        jnp.zeros((rows, HEADS, HEAD_DIM), jnp.float32),
    )
    fold = forward_fold(query_heads, query_place, pairing, length, half)
    top, total, summed = fold(
        start_state,
        (
            lax.all_gather(keys, "ctx", axis=0, tiled=True),
            lax.all_gather(values, "ctx", axis=0, tiled=True),
        ),
        jnp.int32(0),
    )
    top_sum = top + jnp.log(total)
    attended = (summed / jnp.transpose(total)[:, :, None]).reshape(rows, width)
    attended_low = attended.astype(jnp.bfloat16)
    resid_one = (
        inputs.astype(jnp.float32)
        + jnp.dot(attended_low, out_all, preferred_element_type=jnp.float32)
        + out_bias.astype(jnp.float32)
    )
    hidden = layer_norm(resid_one, gain_one.astype(jnp.float32), shift_one.astype(jnp.float32))
    hidden_low = hidden.astype(jnp.bfloat16)
    upper = jnp.dot(hidden_low, in_all, preferred_element_type=jnp.float32) + in_bias.astype(
        jnp.float32
    )
    active, gelu_back = jax.vjp(lambda value: jax.nn.gelu(value, approximate=False), upper)
    active_low = active.astype(jnp.bfloat16)
    resid_two = (
        hidden
        + jnp.dot(active_low, back_all, preferred_element_type=jnp.float32)
        + back_bias.astype(jnp.float32)
    )
    normed = layer_norm(resid_two, gain_two.astype(jnp.float32), shift_two.astype(jnp.float32))
    output = jnp.where(valid[:, None], normed, 0.0)
    qkv_back, out_back, gain_one_back, in_back, back_back, gain_two_back = (
        qkv_all,
        out_all,
        gain_one,
        in_all,
        back_all,
        gain_two,
    )
    grad_y = jnp.where(valid[:, None], cotangent[0].astype(jnp.float32), 0.0)
    grad_resid_two, gain_two_grad, shift_two_grad = norm_back(
        resid_two, gain_two_back.astype(jnp.float32), grad_y
    )
    grad_mixed = grad_resid_two.astype(jnp.bfloat16)
    back_grad = jnp.einsum("tf,td->fd", active_low, grad_mixed, preferred_element_type=jnp.float32)
    back_bias_grad = jnp.sum(grad_mixed.astype(jnp.float32), axis=0)
    grad_active = jnp.einsum("td,fd->tf", grad_mixed, back_back, preferred_element_type=jnp.float32)
    (grad_upper,) = gelu_back(grad_active)
    grad_upper_low = grad_upper.astype(jnp.bfloat16)
    in_grad = jnp.einsum(
        "td,tf->df", hidden_low, grad_upper_low, preferred_element_type=jnp.float32
    )
    in_bias_grad = jnp.sum(grad_upper_low.astype(jnp.float32), axis=0)
    grad_hidden = grad_resid_two + jnp.einsum(
        "tf,df->td", grad_upper_low, in_back, preferred_element_type=jnp.float32
    )
    grad_resid_one, gain_one_grad, shift_one_grad = norm_back(
        resid_one, gain_one_back.astype(jnp.float32), grad_hidden
    )
    grad_branch = grad_resid_one.astype(jnp.bfloat16)
    out_grad = jnp.einsum(
        "tc,td->cd", attended_low, grad_branch, preferred_element_type=jnp.float32
    )
    out_bias_grad = jnp.sum(grad_branch.astype(jnp.float32), axis=0)
    grad_attended = jnp.einsum(
        "td,cd->tc", grad_branch, out_back, preferred_element_type=jnp.float32
    ).astype(jnp.bfloat16)
    grad_heads = heads_of(grad_attended)
    delta = jnp.transpose(jnp.sum(grad_heads.astype(jnp.float32) * heads_of(attended), axis=2))
    query_fold = query_grad_fold(
        query_heads, grad_heads, top_sum, delta, query_place, pairing, length, half
    )
    empty_heads = jnp.zeros((rows, HEADS, HEAD_DIM), jnp.float32)
    query_grad = query_fold(
        empty_heads,
        (
            lax.all_gather(keys, "ctx", axis=0, tiled=True),
            lax.all_gather(values, "ctx", axis=0, tiled=True),
        ),
        jnp.int32(0),
    )
    stats = jnp.concatenate([jnp.transpose(top_sum), jnp.transpose(delta)], axis=1)
    stats_all = lax.all_gather(stats, "ctx", axis=0, tiled=True)
    key_heads = heads_of(keys)
    value_heads = heads_of(values)
    query_in = lax.all_gather(queries, "ctx", axis=0, tiled=True)
    grad_in = lax.all_gather(grad_attended, "ctx", axis=0, tiled=True)
    count = query_in.shape[0]
    span = block_width(count)
    place_in = places(pairing, jnp.int32(0), count, half)

    def step(index, state):
        offset = index * span
        query_block = heads_of(lax.dynamic_slice_in_dim(query_in, offset, span, 0))
        grad_block = heads_of(lax.dynamic_slice_in_dim(grad_in, offset, span, 0))
        stats_block = lax.dynamic_slice_in_dim(stats_all, offset, span, 0)
        place_block = lax.dynamic_slice_in_dim(place_in, offset, span, 0)
        key_part, value_part = key_terms(
            key_heads,
            value_heads,
            query_place,
            query_block,
            grad_block,
            jnp.transpose(stats_block[:, :HEADS]),
            jnp.transpose(stats_block[:, HEADS:]),
            place_block,
            length,
        )
        return (state[0] + key_part, state[1] + value_part)

    key_sum, value_sum = lax.fori_loop(0, count // span, step, (empty_heads, empty_heads))
    key_grad = key_sum.reshape(rows, width)
    value_grad = value_sum.reshape(rows, width)
    grad_proj = jnp.concatenate(
        [
            query_grad.reshape(rows, width).astype(jnp.bfloat16),
            key_grad.astype(jnp.bfloat16),
            value_grad.astype(jnp.bfloat16),
        ],
        axis=1,
    )
    qkv_grad = jnp.einsum("td,tf->df", inputs, grad_proj, preferred_element_type=jnp.float32)
    query_bias_grad = jnp.sum(grad_proj[:, :width].astype(jnp.float32), axis=0)
    value_bias_grad = jnp.sum(grad_proj[:, 2 * width :].astype(jnp.float32), axis=0)
    token_grad = grad_resid_one + jnp.einsum(
        "tf,df->td", grad_proj, qkv_back, preferred_element_type=jnp.float32
    )
    grads = (
        qkv_grad,
        query_bias_grad,
        value_bias_grad,
        out_grad,
        out_bias_grad,
        gain_one_grad,
        shift_one_grad,
        in_grad,
        in_bias_grad,
        back_grad,
        back_bias_grad,
        gain_two_grad,
        shift_two_grad,
    )
    shards = (
        lax.psum_scatter(
            grads[0].astype(jnp.bfloat16), "fsdp", scatter_dimension=0, tiled=True
        ).astype(jnp.float32),
        lax.psum_scatter(
            grads[1].astype(jnp.bfloat16), "fsdp", scatter_dimension=0, tiled=True
        ).astype(jnp.float32),
        lax.psum_scatter(
            grads[2].astype(jnp.bfloat16), "fsdp", scatter_dimension=0, tiled=True
        ).astype(jnp.float32),
        lax.psum_scatter(
            grads[3].astype(jnp.bfloat16), "fsdp", scatter_dimension=0, tiled=True
        ).astype(jnp.float32),
        lax.psum_scatter(
            grads[4].astype(jnp.bfloat16), "fsdp", scatter_dimension=0, tiled=True
        ).astype(jnp.float32),
        lax.psum_scatter(
            grads[5].astype(jnp.bfloat16), "fsdp", scatter_dimension=0, tiled=True
        ).astype(jnp.float32),
        lax.psum_scatter(
            grads[6].astype(jnp.bfloat16), "fsdp", scatter_dimension=0, tiled=True
        ).astype(jnp.float32),
        lax.psum_scatter(
            grads[7].astype(jnp.bfloat16), "fsdp", scatter_dimension=0, tiled=True
        ).astype(jnp.float32),
        lax.psum_scatter(
            grads[8].astype(jnp.bfloat16), "fsdp", scatter_dimension=0, tiled=True
        ).astype(jnp.float32),
        lax.psum_scatter(
            grads[9].astype(jnp.bfloat16), "fsdp", scatter_dimension=0, tiled=True
        ).astype(jnp.float32),
        lax.psum_scatter(
            grads[10].astype(jnp.bfloat16), "fsdp", scatter_dimension=0, tiled=True
        ).astype(jnp.float32),
        lax.psum_scatter(
            grads[11].astype(jnp.bfloat16), "fsdp", scatter_dimension=0, tiled=True
        ).astype(jnp.float32),
        lax.psum_scatter(
            grads[12].astype(jnp.bfloat16), "fsdp", scatter_dimension=0, tiled=True
        ).astype(jnp.float32),
    )
    totals = (
        lax.psum(shards[0].astype(jnp.bfloat16), "ctx").astype(jnp.float32),
        lax.psum(shards[1].astype(jnp.bfloat16), "ctx").astype(jnp.float32),
        lax.psum(shards[2].astype(jnp.bfloat16), "ctx").astype(jnp.float32),
        lax.psum(shards[3].astype(jnp.bfloat16), "ctx").astype(jnp.float32),
        lax.psum(shards[4].astype(jnp.bfloat16), "ctx").astype(jnp.float32),
        lax.psum(shards[5].astype(jnp.bfloat16), "ctx").astype(jnp.float32),
        lax.psum(shards[6].astype(jnp.bfloat16), "ctx").astype(jnp.float32),
        lax.psum(shards[7].astype(jnp.bfloat16), "ctx").astype(jnp.float32),
        lax.psum(shards[8].astype(jnp.bfloat16), "ctx").astype(jnp.float32),
        lax.psum(shards[9].astype(jnp.bfloat16), "ctx").astype(jnp.float32),
        lax.psum(shards[10].astype(jnp.bfloat16), "ctx").astype(jnp.float32),
        lax.psum(shards[11].astype(jnp.bfloat16), "ctx").astype(jnp.float32),
        lax.psum(shards[12].astype(jnp.bfloat16), "ctx").astype(jnp.float32),
    )
    return (output[None], token_grad[None]) + tuple(totals)


def low_lanes(shape):
    return lax.broadcasted_iota(jnp.int32, shape, 1) < 64


def spot_of(pair_ref, place):
    found = jnp.int32(0)
    for s in range(pair_ref.shape[0]):
        found = jnp.where(pair_ref[s] == place, s, found)
    return found


def attend(c, length, spot, keep_ref, mix_ref, lse_ref, turned_ref):
    left = low_lanes((256, BLK))
    zero = jnp.zeros((), jnp.bfloat16)
    keys = 256 * (c + 1)
    own = keep_ref[0, 2 * c : 2 * c + 2].reshape(256, BLK)
    shared = keep_ref[0, 2 * c + spot]
    query = jnp.concatenate(
        [jnp.where(left, own, zero), jnp.where(left[:BLK], zero, shared)], axis=0
    ) * jnp.bfloat16(0.125)
    key = keep_ref[1, : 2 * c + 2].reshape(keys, BLK)
    value = keep_ref[2, : 2 * c + 2].reshape(keys, BLK)
    scores = mask_scores(dot_nt(key, query), c, spot, length, 0, True)
    top = jnp.max(scores, axis=0, keepdims=True)
    probs = jnp.exp(scores - top)
    total = jnp.sum(probs, axis=0, keepdims=True)
    summed = lax.dot_general(
        value, probs.astype(jnp.bfloat16), (((0,), (0,)), ((), ())),
        preferred_element_type=jnp.float32,
    ) / total
    lse_ref[c] = top + jnp.log(total)
    part = summed[64:, 256:]
    none = jnp.zeros_like(part)
    first = jnp.where(spot == 0, part, none)
    second = jnp.where(spot == 0, none, part)
    mixed = jnp.concatenate([summed[:64, :256], jnp.concatenate([first, second], axis=1)], axis=0)
    mix_ref[c] = mixed
    turned_ref[2 * c : 2 * c + 2] = (
        jnp.transpose(mixed).astype(jnp.bfloat16).reshape(2, BLK, BLK)
    )


def mask_scores(scores, c, spot, length, start, edged):
    keys, width = scores.shape
    row = start + lax.broadcasted_iota(jnp.int32, (keys, width), 0)
    scores = jnp.where(row < length, scores, neg_big)
    if not edged:
        return scores
    edge = 256 * c
    lane = lax.broadcasted_iota(jnp.int32, (256, width), 1)
    query_place = edge + jnp.where(lane < 256, lane, lane - 256 + spot * BLK)
    key_place = edge + lax.broadcasted_iota(jnp.int32, (256, width), 0)
    seen = key_place <= query_place
    if c == 0:
        seen = seen | (key_place < NMEM)
    tail = jnp.where(seen, scores[keys - 256 :], neg_big)
    if keys == 256:
        return tail
    return jnp.concatenate([scores[: keys - 256], tail], axis=0)


def attend_back(
    c, length, spot, keep_ref, g_ref, mix_ref, lse_ref, q_sum, k_sum, v_sum
):
    zero = jnp.zeros((), jnp.bfloat16)
    left = low_lanes((256, BLK))
    left_half = left[:BLK]
    own = keep_ref[0, 2 * c : 2 * c + 2].reshape(256, BLK)
    shared = keep_ref[0, 2 * c + spot]
    query = jnp.concatenate(
        [jnp.where(left, own, zero), jnp.where(left_half, zero, shared)], axis=0
    ) * jnp.bfloat16(0.125)
    g_own = g_ref[2 * c : 2 * c + 2].reshape(256, BLK)
    g_shared = g_ref[2 * c + spot]
    grad = jnp.concatenate(
        [jnp.where(left, g_own, zero), jnp.where(left_half, zero, g_shared)], axis=0
    )
    turned = jnp.transpose(g_own.astype(jnp.float32)) * mix_ref[c]
    delta_own = jnp.sum(turned[:64], axis=0, keepdims=True)
    delta_pair = jnp.sum(turned[64:], axis=0, keepdims=True)
    delta = jnp.concatenate(
        [delta_own, jnp.where(spot == 0, delta_pair[:, :BLK], delta_pair[:, BLK:])], axis=1
    )
    lse = lse_ref[c]
    q_grad = jnp.zeros((384, BLK), jnp.float32)
    last = 2 * c + 2
    step = 8
    for low_block in range(0, last, step):
        high_block = min(low_block + step, last)
        cut = slice(low_block, high_block)
        count = high_block - low_block
        key = keep_ref[1, cut].reshape(count * BLK, BLK)
        value = keep_ref[2, cut].reshape(count * BLK, BLK)
        scores = mask_scores(
            dot_nt(key, query), c, spot, length, low_block * BLK, high_block == last
        )
        probs = jnp.exp(scores - lse)
        score_grad = (probs * (dot_nt(value, grad) - delta)).astype(jnp.bfloat16)
        v_part = dot_nn(probs.astype(jnp.bfloat16), grad)
        k_part = dot_nn(score_grad, query)
        v_sum[cut] += v_part.reshape(count, BLK, BLK)
        k_sum[cut] += k_part.reshape(count, BLK, BLK)
        q_grad = q_grad + lax.dot_general(
            score_grad, key, (((0,), (0,)), ((), ())), preferred_element_type=jnp.float32
        )
    q_grad = q_grad * 0.125
    part = q_grad[256:]
    none = jnp.zeros_like(part)
    first = jnp.where(spot == 0, part, none)
    second = jnp.where(spot == 0, none, part)
    q_sum[2 * c : 2 * c + 2] = jnp.where(
        left, q_grad[:256], jnp.concatenate([first, second], axis=0)
    ).reshape(2, BLK, BLK)


def smem():
    return pl.BlockSpec(memory_space=pltpu.SMEM)


def vmem():
    return pl.BlockSpec(memory_space=pltpu.VMEM)


MESH = pl.DeviceIdType.MESH


def remote(src, dst, sems, at, peer):
    return pltpu.make_async_remote_copy(
        src_ref=src, dst_ref=dst, send_sem=sems.at[(0,) + at], recv_sem=sems.at[(1,) + at],
        device_id=peer, device_id_type=MESH,
    )


def greet(peers):
    barrier = pltpu.get_barrier_semaphore()
    for peer in peers:
        pl.semaphore_signal(barrier, inc=1, device_id=peer, device_id_type=MESH)
    pl.semaphore_wait(barrier, len(peers))


def ring_peers(n):
    me = lax.axis_index("ctx")
    return [{"ctx": lax.rem(me + k, n)} for k in range(1, n)]


def two(block):
    return pl.ds(2 * block, 2)


def one(block):
    return block


def exchange_copies(n, in_ref, out_ref, sems, at=two):
    me = lax.axis_index("ctx")
    copies = []
    for k in range(1, n):
        peer = lax.rem(me + k, n)
        copies.append(
            remote(in_ref.at[at(peer)], out_ref.at[at(me)], sems, (k,), {"ctx": peer})
        )
    return copies


def own_copy(in_ref, out_ref, sem, at=two):
    me = lax.axis_index("ctx")
    return pltpu.make_async_copy(in_ref.at[at(me)], out_ref.at[at(me)], sem)


def beside(first, second, axis):
    return jnp.concatenate([first, second], axis=axis)


def fold(first, second, shared):
    return beside(
        beside(first[:, :HEAD_DIM], second[:, :HEAD_DIM], 1),
        beside(shared[:HEAD_DIM], shared[HEAD_DIM:], 1),
        0,
    )


def fold_pair(value, spot, lead):
    first, second = value[:BLK], value[BLK:]
    return fold(
        first, second, jnp.where(lead == spot, first[:, HEAD_DIM:], second[:, HEAD_DIM:])
    )


def unfold_shared(message):
    return beside(message[BLK:, :HEAD_DIM], message[BLK:, HEAD_DIM:], 0)


def unfold_block(message, later):
    own = jnp.where(later == 0, message[:BLK, :HEAD_DIM], message[:BLK, HEAD_DIM:])
    return beside(own, unfold_shared(message), 1)


def join_folded(messages, lead):
    pieces = []
    for group in range(HEADS // 3):
        pair = [messages(2 * group), messages(2 * group + 1)]
        for message in pair:
            pieces.append(beside(message[:BLK, :HEAD_DIM], message[:BLK, HEAD_DIM:], 0))
        even, odd = [unfold_shared(message) for message in pair]
        pieces.append(
            beside(jnp.where(lead == 0, even, odd), jnp.where(lead == 0, odd, even), 0)
        )
    return jnp.concatenate(pieces, axis=1)


def both(ref, peer):
    value = ref[2 * peer : 2 * peer + 2]
    return value.reshape(-1, value.shape[2])


def join_pairs(pairs):
    pieces = []
    for group in range(HEADS // 3):
        first, second = pairs(2 * group), pairs(2 * group + 1)
        shared = first[:, HEAD_DIM:].astype(jnp.float32) + second[:, HEAD_DIM:].astype(jnp.float32)
        pieces += [first[:, :HEAD_DIM], second[:, :HEAD_DIM], shared.astype(jnp.bfloat16)]
    return jnp.concatenate(pieces, axis=1)


def pair_of(value, peer):
    own = 3 * (peer // 2) + peer % 2
    shared = 3 * (peer // 2) + 2
    cut = lambda head: value[:, head * HEAD_DIM : (head + 1) * HEAD_DIM]
    return jnp.concatenate([cut(own), cut(shared)], axis=1)


def dot_nn(a, b):
    return jnp.dot(a, b, preferred_element_type=jnp.float32)


def dot_nt(a, b):
    return lax.dot_general(a, b, (((1,), (1,)), ((), ())), preferred_element_type=jnp.float32)


def column_sum(value):
    return jnp.sum(value, axis=0, keepdims=True)


def unit_of(value):
    mean = jnp.mean(value, axis=-1, keepdims=True)
    centred = value - mean
    scale = lax.rsqrt(jnp.mean(centred * centred, axis=-1, keepdims=True) + eps)
    return centred * scale, scale


def unit_back(unit, scale, scaled):
    return scale * (
        scaled
        - jnp.mean(scaled, axis=-1, keepdims=True)
        - unit * jnp.mean(scaled * unit, axis=-1, keepdims=True)
    )


(ROW_BQ, ROW_BV, ROW_BO, ROW_G1, ROW_S1, ROW_BB, ROW_G2, ROW_S2, ROW_BI) = range(9)


def gather_copies(src, full, sems, index):
    fsdp = lax.axis_index("fsdp")
    x, core = fsdp // 2, lax.rem(fsdp, 2)
    sibling, across = {"fsdp": 2 * x + 1 - core}, {"fsdp": 2 * (1 - x) + core}
    other = 2 * (1 - x) + core
    return (
        remote(src, full.at[fsdp], sems, (index, 0), across),
        remote(src, full.at[fsdp], sems, (index, 1), sibling),
        remote(full.at[other], full.at[other], sems, (index, 2), sibling),
    )


def chip_peers():
    fsdp = lax.axis_index("fsdp")
    x, core = fsdp // 2, lax.rem(fsdp, 2)
    return [{"fsdp": 2 * x + 1 - core}, {"fsdp": 2 * (1 - x) + core}]


def split_gather(src, full, sems, parts):
    ctx, fsdp = lax.axis_index("ctx"), lax.axis_index("fsdp")
    z, y = ctx // 2, lax.rem(ctx, 2)
    x, core = fsdp // 2, lax.rem(fsdp, 2)
    sibling, across = {"fsdp": 2 * x + 1 - core}, {"fsdp": 2 * (1 - x) + core}
    over_y = {"ctx": 2 * z + 1 - y}
    other = 2 * (1 - x) + core
    count = src.shape[0] // 2
    here = pl.ds(pl.multiple_of(y * count, count), count)
    there = pl.ds(pl.multiple_of((1 - y) * count, count), count)
    cross, side, on, off, whole = [], [], [], [], []
    for p in range(parts):
        width = src.shape[1] // parts
        cols = slice(p * width, (p + 1) * width)
        moved = full.at[other, here, cols]
        late = full.at[other, there, cols]
        cross.append(remote(src.at[here, cols], full.at[fsdp, here, cols], sems, (0, p), across))
        side.append(remote(moved, moved, sems, (1, p), over_y))
        on.append(remote(moved, moved, sems, (2, p), sibling))
        off.append(remote(late, late, sems, (3, p), sibling))
        whole.append(remote(src.at[:, cols], full.at[fsdp, :, cols], sems, (4, p), sibling))
    return cross, side, on, off, whole


def passed(split, p):
    cross, side, on, off, whole = split
    cross[p].wait_recv()
    side[p].start()
    on[p].start()


def handed(split, p):
    cross, side, on, off, whole = split
    side[p].wait_recv()
    off[p].start()


def gathered(split, p):
    cross, side, on, off, whole = split
    for copies in (whole, on, off):
        copies[p].wait_recv()


def front_kernel(
    n, pair_ref, len_ref, *refs
):
    vectors, refs = refs[:9], refs[9:]
    (
        tokens_ref, cot_ref, qkv_src, out_src, in_src, back_src,
        output_ref, grad_ref, left_ref, right_ref, resid_ref, sums_ref,
        keep_ref, mix_ref, lse_ref, qkv_ref,
        small_out, small, rows_ref, token_buf, cot, w_qkv, w_out, w_in, w_back, send_folded, send,
        packed_q, packed_k, packed_v, keep, mix,
        lse, turned, mixed_out, mixed_in, active, slope, output, grad_out, left, right, resid, sums,
        small_sem, qkv_sem, in_split_sem, back_split_sem, gather_sem, send_q, send_k, send_v, in_sem, own_sem, load_sem, ship_sem,
    ) = refs
    send_sem = (send_q, send_k, send_v)
    packed = (packed_q, packed_k, packed_v)
    low, wide = jnp.bfloat16, jnp.float32
    ctx, fsdp = lax.axis_index("ctx"), lax.axis_index("fsdp")
    x, core = fsdp // 2, lax.rem(fsdp, 2)
    spot = lax.rem(ctx, 2)
    lead = lax.rem(pair_ref[2 * ctx], 2)
    width = token_buf.shape[1]
    count = in_src.shape[1] // width
    loads = [
        pltpu.make_async_copy(src, dst, load_sem.at[i])
        for i, (src, dst) in enumerate(
            [
                (tokens_ref, token_buf),
                (cot_ref, cot),
                (qkv_src, w_qkv.at[fsdp]),
                (out_src, w_out.at[fsdp]),
                (in_src, w_in.at[fsdp]),
                (back_src, w_back.at[fsdp]),
            ]
        )
    ]
    cot_load = loads[1]
    for cp in loads[:3]:
        cp.start()
    part = width // 4
    small_out[...] = jnp.zeros_like(small_out)
    for i in range(8):
        small_out[i : i + 1] = vectors[i][...].astype(wide).reshape(1, part)
    inner_bias = vectors[8][...].astype(wide).reshape(1, -1)
    for j in range(4):
        small_out[8 + j : 9 + j] = inner_bias[:, j * part : (j + 1) * part]
    greet(ring_peers(n) + chip_peers())
    smalls = gather_copies(small_out, small, small_sem, 0)
    qkv_split = split_gather(qkv_src, w_qkv, qkv_sem, 3)
    in_split = split_gather(in_src, w_in, in_split_sem, count)
    back_split = split_gather(back_src, w_back, back_split_sem, 2)
    splits = (qkv_split, in_split, back_split)
    for step in (0, 1):
        smalls[step].start()
    for cp in qkv_split[0] + qkv_split[4]:
        cp.start()
    for cp in loads[3:]:
        cp.start()
    shards = gather_copies(out_src, w_out, gather_sem, 0)
    small[fsdp] = small_out[...]
    smalls[0].wait_recv()
    smalls[2].start()
    passed(qkv_split, 0)
    loads[0].wait()
    tokens = token_buf[...]
    left[0] = jnp.transpose(tokens).reshape(4, -1, 2 * BLK)
    smalls[1].wait_recv()
    smalls[2].wait_recv()
    for f in range(4):
        cols = slice(f * part, (f + 1) * part)
        rows_ref[:8, cols] = small[f, :8]
        for j in range(4):
            rows_ref[ROW_BI + f : ROW_BI + f + 1, j * part : (j + 1) * part] = small[
                f, 8 + j : 9 + j
            ]
    rows_ref[12:] = jnp.zeros_like(rows_ref[12:])
    row = lambda i: rows_ref[i : i + 1, :]
    passed(qkv_split, 1)
    handed(qkv_split, 0)
    passed(qkv_split, 2)
    for cp in shards[:2]:
        cp.start()
    for split in (in_split, back_split):
        for cp in split[0] + split[4]:
            cp.start()
    loads[2].wait()
    sends = []
    for p, bias in enumerate((ROW_BQ, None, ROW_BV)):
        if p:
            handed(qkv_split, p)
        gathered(qkv_split, p)
        value = dot_nn(tokens, w_qkv[:, :, p * width : (p + 1) * width].reshape(width, width))
        if bias is not None:
            value = value + row(bias)
        value = value.astype(low)
        for peer in range(n):
            both_heads = pair_of(value, peer)
            if p:
                send[p - 1, 2 * peer : 2 * peer + 2] = both_heads.reshape(2, BLK, BLK)
            else:
                send_folded[peer] = fold_pair(both_heads, peer % 2, lead)
        source, at = (send.at[p - 1], two) if p else (send_folded, one)
        copies = exchange_copies(n, source, packed[p], send_sem[p], at)
        copies.append(own_copy(source, packed[p], own_sem.at[2 + p], at))
        for cp in copies:
            cp.start()
        sends.append(copies)
    shipped = []

    def ship(src, dst):
        cp = pltpu.make_async_copy(src, dst, ship_sem.at[len(shipped)])
        cp.start()
        shipped.append(cp)

    ship(w_qkv, qkv_ref)
    spots = lax.broadcasted_iota(jnp.int32, (2 * BLK, 1), 0)
    place = jnp.where(
        spots < BLK,
        pair_ref[2 * ctx] * BLK + spots,
        pair_ref[2 * ctx + 1] * BLK + spots - BLK,
    )
    valid = place < len_ref[0]
    shards[0].wait_recv()
    shards[2].start()
    for p in range(count):
        passed(in_split, p)
        if p:
            handed(in_split, p - 1)
    passed(back_split, 0)
    handed(in_split, count - 1)
    spots_of = [spot_of(pair_ref, b) for b in range(2 * n)]
    for p in range(3):
        sends[p][-1].wait()
        for cp in sends[p][:-1]:
            cp.wait_recv()
        for b in range(2 * n):
            if p:
                keep[p, b] = packed[p][spots_of[b]]
            else:
                keep[p, b] = unfold_block(
                    packed[p][lax.div(spots_of[b], 2)], lax.rem(spots_of[b], 2)
                )
    passed(back_split, 1)

    ship(keep, keep_ref)
    for c in range(n):
        attend(c, len_ref[0], spot, keep, mix, lse, turned)
    for peer in range(n):
        first, second = turned[pair_ref[2 * peer]], turned[pair_ref[2 * peer + 1]]
        mixed_out[peer] = fold(first, second, first[:, HEAD_DIM:] + second[:, HEAD_DIM:])
    copies = exchange_copies(n, mixed_out, mixed_in, in_sem, one)
    for cp in copies:
        cp.start()
    own_mixed = own_copy(mixed_out, mixed_in, own_sem.at[1], one)
    own_mixed.start()
    ship(mix, mix_ref)
    ship(lse, lse_ref)
    sums[...] = jnp.zeros_like(sums)
    for cp in loads[3:]:
        cp.wait()
    for p in range(2):
        handed(back_split, p)
    shards[1].wait_recv()
    shards[2].wait_recv()
    for p in range(count):
        gathered(in_split, p)
    own_mixed.wait()
    for cp in copies:
        cp.wait_recv()
    attended = join_folded(lambda peer: mixed_in[peer], lead)
    resid_one = (
        tokens.astype(wide)
        + dot_nn(attended, w_out[...].reshape(width, width))
        + row(ROW_BO)
    )
    unit_one, scale_one = unit_of(resid_one)
    hidden = unit_one * row(ROW_G1) + row(ROW_S1)
    hidden_low = hidden.astype(low)
    resid_two = hidden + row(ROW_BB)
    cut = lambda t: pl.ds(pl.multiple_of(t * width, width), width)
    order = [fsdp, 2 * x + 1 - core, 2 * (1 - x) + core, 2 * (1 - x) + 1 - core]
    for step, t in enumerate(order):
        bias = rows_ref[pl.ds(ROW_BI + t, 1), :]
        upper = dot_nn(hidden_low, w_in[:, :, cut(t)].reshape(width, width)) + bias
        share = 0.5 * (1.0 + lax.erf(upper * (0.5**0.5)))
        slope[t] = share + upper * (jnp.exp(-0.5 * upper * upper) * (2 * math.pi) ** -0.5)
        some = (upper * share).astype(low)
        active[t] = some
        if step == 0:
            gathered(back_split, 0)
            gathered(back_split, 1)
        resid_two = resid_two + dot_nn(some, w_back[t])
    unit_two, scale_two = unit_of(resid_two)
    output[...] = jnp.where(valid, unit_two * row(ROW_G2) + row(ROW_S2), 0.0)
    cot_load.wait()
    grad_y = jnp.where(valid, cot[...].astype(wide), 0.0)
    sums[ROW_G2 : ROW_G2 + 1, :] = column_sum(grad_y * unit_two)
    sums[ROW_S2 : ROW_S2 + 1, :] = column_sum(grad_y)
    grad_resid_two = unit_back(unit_two, scale_two, grad_y * row(ROW_G2))
    grad_mixed = grad_resid_two.astype(low)
    right[5] = grad_mixed
    sums[ROW_BB : ROW_BB + 1, :] = column_sum(grad_mixed.astype(wide))
    ship(output, output_ref)
    left[1] = jnp.transpose(attended).reshape(4, -1, 2 * BLK)
    left[2] = jnp.transpose(hidden_low).reshape(4, -1, 2 * BLK)
    for f in range(4):
        turned = jnp.transpose(active[f])
        for r in range(4):
            left[3 + r, f] = turned[r * width // 4 : (r + 1) * width // 4]
    ship(left, left_ref)
    grad_hidden = grad_resid_two
    for t in range(count):
        grad_upper = (dot_nt(grad_mixed, w_back[t]) * slope[t]).astype(low)
        right[1 + t] = grad_upper
        sums[ROW_BI + t : ROW_BI + t + 1, :] = column_sum(grad_upper.astype(wide))
        grad_hidden = grad_hidden + dot_nt(grad_upper, w_in[:, :, cut(t)].reshape(width, width))
    sums[ROW_G1 : ROW_G1 + 1, :] = column_sum(grad_hidden * unit_one)
    sums[ROW_S1 : ROW_S1 + 1, :] = column_sum(grad_hidden)
    grad_resid_one = unit_back(unit_one, scale_one, grad_hidden * row(ROW_G1))
    resid[...] = grad_resid_one
    grad_branch = grad_resid_one.astype(low)
    right[0] = grad_branch
    sums[ROW_BO : ROW_BO + 1, :] = column_sum(grad_branch.astype(wide))
    ship(resid, resid_ref)
    ship(right, right_ref)
    ship(sums, sums_ref)
    grad_attended = dot_nt(grad_branch, w_out[...].reshape(width, width)).astype(low)
    for peer in range(n):
        grad_out[peer] = fold_pair(pair_of(grad_attended, peer), peer % 2, lead)
    ship(grad_out, grad_ref)
    for cps in (smalls, shards, copies) + sum(splits, ()):
        for cp in cps:
            cp.wait_send()
    for cps in sends:
        for cp in cps[:-1]:
            cp.wait_send()
    for cp in shipped:
        cp.wait()


def front(pairing, lengths, vectors, tokens, cotangent, w_qkv, w_out, w_in, w_back, n, name):
    count, width = tokens.shape
    low, wide = jnp.bfloat16, jnp.float32
    dma = pltpu.SemaphoreType.DMA
    shape = jax.ShapeDtypeStruct
    hbm = pl.BlockSpec(memory_space=pltpu.HBM)
    vec = pltpu.VMEM((16, width // 4), wide)
    results = [
        ((count, width), wide),
        ((n, BLK + HEAD_DIM, BLK), low),
        ((7, 4, width // 4, count), low),
        ((6, count, width), low),
        ((count, width), wide),
        ((16, width), wide),
        ((3, 2 * n, BLK, BLK), low),
        ((n, BLK, 2 * BLK), wide),
        ((n, 1, 3 * BLK), wide),
        ((4,) + w_qkv.shape, low),
    ]
    output, grad, left, right, resid, sums, keep, mix, lse, qkv = [pltpu.VMEM(*r) for r in results]
    blocks = pltpu.VMEM((2 * n, BLK, BLK), low)
    return pl.pallas_call(
        functools.partial(front_kernel, n),
        out_shape=tuple(shape(*r) for r in results),
        in_specs=[smem(), smem()] + [vmem()] * 9 + [hbm] * 6,
        out_specs=(hbm,) * 10,
        scratch_shapes=[
            vec,
            pltpu.VMEM((4, 16, width // 4), wide),
            pltpu.VMEM((16, width), wide),
            pltpu.VMEM((count, width), low),
            pltpu.VMEM((count, width), low),
            qkv,
            pltpu.VMEM((4,) + w_out.shape, low),
            pltpu.VMEM((4,) + w_in.shape, low),
            pltpu.VMEM((4,) + w_back.shape, low),
            grad,
            pltpu.VMEM((2, 2 * n, BLK, BLK), low),
            grad,
            blocks,
            blocks,
            keep,
            mix,
            lse,
            blocks,
            grad,
            grad,
            pltpu.VMEM((4, count, width), low),
            pltpu.VMEM((4, count, width), wide),
            output,
            grad,
            left,
            right,
            resid,
            sums,
            dma((2, 1, 3)),
            dma((2, 5, 3)),
            dma((2, 5, 4)),
            dma((2, 5, 2)),
            dma((2, 1, 3)),
            dma((2, n)),
            dma((2, n)),
            dma((2, n)),
            dma((2, n)),
            dma((5,)),
            dma((6,)),
            dma((10,)),
        ],
        compiler_params=pltpu.CompilerParams(
            collective_id=name, has_side_effects=True, vmem_limit_bytes=62 << 20
        ),
        name="front",
    )(pairing, lengths, *vectors, tokens, cotangent, w_qkv, w_out, w_in, w_back)


PARTS = 12


def sum_sources(chunk):
    left = jnp.where(chunk < 4, 3 + chunk, jnp.where(chunk < 8, 2, jnp.where(chunk < 9, 1, 0)))
    right = jnp.where(
        chunk < 4, 8, jnp.where(chunk < 8, chunk, jnp.where(chunk < 9, 3, chunk - 9))
    )
    return left, right


STEPS = 65
PLAN = {
    "pair": {0: 0, 1: 1, 2: 2, 3: 3, 6: 4, 7: 5, 13: 6, 15: 7, 19: 8, 21: 9, 29: 10, 32: 11},
    "x": {3: 0, 4: 1, 5: 2, 7: 3, 12: 4, 13: 5, 14: 6, 18: 7, 23: 8, 30: 9, 36: 10, 41: 11},
    "y": {9: 0, 10: 1, 16: 2, 17: 3, 18: 4, 21: 5, 24: 6, 26: 7, 30: 8, 36: 9, 46: 10, 50: 11},
    "near": {11: 0, 19: 1, 20: 2, 24: 3, 25: 4, 28: 5, 32: 6, 38: 7, 42: 8, 44: 9, 49: 10, 57: 11},
    "far": {22: 0, 25: 1, 26: 2, 31: 3, 33: 4, 39: 5, 41: 6, 44: 7, 47: 8, 52: 9, 55: 10, 60: 11},
    "own": {27: 0, 29: 1, 30: 2, 37: 3, 40: 4, 45: 5, 49: 6, 50: 7, 53: 8, 57: 9, 58: 10, 61: 11},
    "wide": {30: 0, 31: 1, 34: 2, 43: 3, 48: 4, 50: 5, 51: 6, 56: 7, 57: 8, 59: 9, 61: 10, 62: 11},
    "last": {35: 0, 38: 1, 42: 2, 47: 3, 52: 4, 54: 5, 55: 6, 58: 7, 60: 8, 61: 9, 63: 10, 64: 11},
}
ATTEND_AT = (8, 9, 10)
JOIN_AT = (16, 24, 28)
SMALL_AT = (46, 49, 52, 61, 62, 64)
TOKEN_AT = 44


def planned(name, step):
    chunk = jnp.int32(-1)
    for at, which in PLAN[name].items():
        chunk = jnp.where(step == at, which, chunk)
    return chunk


def back_kernel(
    n, pair_ref, len_ref, grad_ref, keep_src, mix_src, lse_src, left_src, right_src,
    sums_src, resid_src, qkv_ref,
    total_out, token_ref, small_out,
    keep_ref, mix_ref, lse_ref, left_ref, sums_ref, resid_ref, total_ref,
    grad_in, g_all, q_sum, k_sum, v_sum, folded_out, folded_in,
    blocks_out, blocks_in, w_qkv, right_all,
    pair_out, pair_in, x_out, x_in, y_out, y_in, y_keep, near_out, near_in, near_keep,
    far_out, far_in, far_keep, s_out, s_in,
    load_sem, ship_sem,
    grad_sem, block_q, block_k, block_v, own_sem, pair_sem, x_sem, y_sem, near_sem, far_sem,
    own_z_sem, wide_sem, last_sem, s_sem,
):
    block_sem = (block_q, block_k, block_v)
    low, wide = jnp.bfloat16, jnp.float32
    ctx = lax.axis_index("ctx")
    fsdp = lax.axis_index("fsdp")
    z, y = ctx // 2, lax.rem(ctx, 2)
    odd, upper = lax.rem(z, 2), z // 2
    x, core = fsdp // 2, lax.rem(fsdp, 2)
    sibling = {"fsdp": 2 * x + 1 - core}
    across = {"fsdp": 2 * (1 - x) + core}
    over_y = {"ctx": 2 * z + 1 - y}
    near = {"ctx": 2 * (2 * upper + 1 - odd) + y}
    far = {"ctx": 2 * (2 * (1 - upper) + odd) + y}
    mine = 2 * odd + upper
    loads = [
        pltpu.make_async_copy(src, dst, load_sem.at[i])
        for i, (src, dst) in enumerate(
            [
                (right_src, right_all.at[3:]),
                (left_src, left_ref),
                (keep_src, keep_ref),
                (mix_src, mix_ref),
                (lse_src, lse_ref),
                (sums_src, sums_ref),
                (resid_src, resid_ref),
            ]
        )
    ]
    for cp in loads:
        cp.start()
    greet(ring_peers(n) + [sibling, across])
    lead = lax.rem(pair_ref[2 * ctx], 2)
    grads = exchange_copies(n, grad_ref, grad_in, grad_sem, one)
    for cp in grads:
        cp.start()
    own_grad = own_copy(grad_ref, grad_in, own_sem.at[0], one)
    own_grad.start()
    load = pltpu.make_async_copy(qkv_ref, w_qkv, own_sem.at[1])
    load.start()
    blocks = [
        exchange_copies(n, folded_out, folded_in, block_sem[0], one)
    ] + [
        exchange_copies(n, blocks_out.at[p], blocks_in.at[p], block_sem[1 + p])
        for p in range(2)
    ]
    own = [own_copy(folded_out, folded_in, own_sem.at[2], one)] + [
        own_copy(blocks_out.at[p], blocks_in.at[p], own_sem.at[3 + p]) for p in range(2)
    ]
    k_sum[...] = jnp.zeros_like(k_sum)
    v_sum[...] = jnp.zeros_like(v_sum)
    chunks = keep_ref.shape[1] // 2

    def attend_some(first, last):
        for c in range(first, last):
            attend_back(
                c, len_ref[0], y, keep_ref, g_all, mix_ref, lse_ref, q_sum, k_sum, v_sum
            )

    def attend_step(t):
        @pl.when(t == ATTEND_AT[0])
        def _():
            own_grad.wait()
            for cp in loads[2:5]:
                cp.wait()
            for cp in grads:
                cp.wait_recv()
            for b in range(2 * chunks):
                found = spot_of(pair_ref, b)
                g_all[b] = unfold_block(grad_in[lax.div(found, 2)], lax.rem(found, 2))
            attend_some(0, chunks // 2)

        @pl.when(t == ATTEND_AT[1])
        def _():
            attend_some(chunks // 2, chunks - 2)

        @pl.when(t == ATTEND_AT[2])
        def _():
            attend_some(chunks - 2, chunks)
            for peer in range(n):
                first, second = q_sum[pair_ref[2 * peer]], q_sum[pair_ref[2 * peer + 1]]
                folded_out[peer] = fold(
                    first, second, first[:, HEAD_DIM:] + second[:, HEAD_DIM:]
                ).astype(low)
            for p, total in enumerate((None, k_sum, v_sum)):
                if p:
                    for s in range(2 * chunks):
                        blocks_out[p - 1, s] = total[pair_ref[s]].astype(low)
                for cp in blocks[p]:
                    cp.start()
                own[p].start()

    def slot(c):
        return lax.rem(c, 4)

    def pair_copy(c):
        return remote(pair_out.at[lax.rem(c, 2)], pair_in.at[c], pair_sem, (c,), sibling)

    def x_copy(c):
        return remote(x_out.at[c], x_in.at[c], x_sem, (c,), across)

    def y_copy(c):
        return remote(y_out.at[slot(c)], y_in.at[c], y_sem, (c,), over_y)

    def near_copy(c):
        return remote(near_out.at[slot(c)], near_in.at[c], near_sem, (c,), near)

    def far_copy(c):
        return remote(far_out.at[slot(c)], far_in.at[c], far_sem, (c,), far)

    def own_z_copy(c):
        piece = total_ref.at[c, y, mine]
        return remote(piece, piece, own_z_sem, (c,), far)

    def wide_copy(c):
        piece = total_ref.at[c, y, two(odd)]
        return remote(piece, piece, wide_sem, (c,), near)

    def last_copy(c):
        piece = total_ref.at[c, y]
        return remote(piece, piece, last_sem, (c,), over_y)

    def reuse(copy, c, slots):
        @pl.when(c >= slots)
        def _():
            copy(c - slots).wait_send()

    def partial(c, shard):
        left, right = sum_sources(c)
        return dot_nn(left_ref[left, shard], right_all[right])

    def stage_pair(c):
        reuse(pair_copy, c, 2)
        for side in range(2):
            pair_out[lax.rem(c, 2), side] = partial(c, 2 * side + 1 - core).astype(low)
        pair_copy(c).start()

    def stage_x(c):
        pair_copy(c).wait_recv()
        x_out[c] = (partial(c, 2 * (1 - x) + core) + pair_in[c, 1 - x].astype(wide)).astype(low)
        x_copy(c).start()

    def stage_y(c):
        mine_sum = partial(c, 2 * x + core) + pair_in[c, x].astype(wide)
        x_copy(c).wait_recv()
        total = mine_sum + x_in[c].astype(wide)
        first, second = total[:, :384], total[:, 384:]
        reuse(y_copy, c, 4)
        y_out[slot(c)] = jnp.where(y == 0, second, first).astype(low)
        y_copy(c).start()
        y_keep[slot(c)] = jnp.where(y == 0, first, second)

    def stage_near(c):
        y_copy(c).wait_recv()
        total = y_keep[slot(c)] + y_in[c].astype(wide)
        first, second = total[:96], total[96:]
        reuse(near_copy, c, 4)
        near_out[slot(c)] = jnp.where(odd == 0, second, first).astype(low)
        near_copy(c).start()
        near_keep[slot(c)] = jnp.where(odd == 0, first, second)

    def stage_far(c):
        near_copy(c).wait_recv()
        total = near_keep[slot(c)] + near_in[c].astype(wide)
        first, second = total[:48], total[48:]
        reuse(far_copy, c, 4)
        far_out[slot(c)] = jnp.where(upper == 0, second, first).astype(low)
        far_copy(c).start()
        far_keep[slot(c)] = jnp.where(upper == 0, first, second)

    def stage_own(c):
        far_copy(c).wait_recv()
        total_ref[c, y, mine] = (far_keep[slot(c)] + far_in[c].astype(wide)).astype(low)
        own_z_copy(c).start()

    def stage_wide(c):
        own_z_copy(c).wait_recv()
        wide_copy(c).start()

    def stage_last(c):
        wide_copy(c).wait_recv()
        last_copy(c).start()

    def small_step(t):
        peers = [sibling, across, over_y, near, far]
        copies = [
            remote(s_out.at[k], s_in.at[k], s_sem, (k,), peer) for k, peer in enumerate(peers)
        ]

        for p in range(3):

            @pl.when(t == JOIN_AT[p])
            def _():
                own[p].wait()
                for cp in blocks[p]:
                    cp.wait_recv()
                if p:
                    right_all[p] = join_pairs(lambda peer: both(blocks_in.at[p - 1], peer))
                else:
                    right_all[p] = join_folded(lambda peer: folded_in[peer], lead)

        @pl.when(t == SMALL_AT[0])
        def _():
            loads[5].wait()
            s_out[0] = sums_ref[...]
            s_out[0, ROW_BQ : ROW_BQ + 1] = column_sum(right_all[0].astype(wide))
            s_out[0, ROW_BV : ROW_BV + 1] = column_sum(right_all[2].astype(wide))
            copies[0].start()

        for k in range(1, 5):

            @pl.when(t == SMALL_AT[k])
            def _():
                copies[k - 1].wait()
                s_out[k] = s_out[k - 1] + s_in[k - 1]
                copies[k].start()

        @pl.when(t == SMALL_AT[5])
        def _():
            copies[4].wait()
            total = s_out[4] + s_in[4]
            quarter = total.shape[1] // 4
            cuts = [slice(f * quarter, (f + 1) * quarter) for f in range(4)]
            pick = lambda choices: sum(
                jnp.where(fsdp == f, choice, 0.0) for f, choice in enumerate(choices)
            )
            small_out[...] = jnp.zeros_like(small_out)
            small_out[:8] = pick([total[:8, cut] for cut in cuts])
            line = pick([total[ROW_BI + f : ROW_BI + f + 1] for f in range(4)])
            for j, cut in enumerate(cuts):
                small_out[8 + j : 9 + j] = line[:, cut]

        @pl.when(t == TOKEN_AT)
        def _():
            load.wait()
            loads[6].wait()
            width = resid_ref.shape[1]
            token_ref[...] = resid_ref[...] + sum(
                dot_nt(
                    right_all[part],
                    w_qkv[:, :, part * width : (part + 1) * width].reshape(width, width),
                )
                for part in range(3)
            )

    stages = [
        ("pair", stage_pair),
        ("x", stage_x),
        ("last", stage_last),
        ("wide", stage_wide),
        ("own", stage_own),
        ("far", stage_far),
        ("near", stage_near),
        ("y", stage_y),
    ]

    def step(t, carry):
        attend_step(t)
        small_step(t)
        for name, stage in stages:
            c = planned(name, t)

            @pl.when(c >= 0)
            def _():
                stage(c)

        return carry

    loads[0].wait()
    loads[1].wait()
    lax.fori_loop(0, STEPS, step, 0)

    def ship(c):
        return pltpu.make_async_copy(total_ref.at[c], total_out.at[c], ship_sem.at[c])

    def drain(c, carry):
        x_copy(c).wait_send()
        own_z_copy(c).wait_send()
        wide_copy(c).wait_send()
        last_copy(c).wait()
        ship(c).start()
        return carry

    lax.fori_loop(0, PARTS, drain, 0)
    for c in range(PARTS - 4, PARTS):
        y_copy(c).wait_send()
        near_copy(c).wait_send()
        far_copy(c).wait_send()
    for c in (PARTS - 2, PARTS - 1):
        pair_copy(c).wait_send()
    for cp in grads + blocks[0] + blocks[1] + blocks[2]:
        cp.wait_send()
    for c in range(PARTS):
        ship(c).wait()


def back(pairing, lengths, grad, keep, mix, lse, left, right, sums, resid, qkv_full, name):
    blocks = keep.shape[1]
    n = blocks // 2
    low, wide = jnp.bfloat16, jnp.float32
    dma = pltpu.SemaphoreType.DMA
    shape = jax.ShapeDtypeStruct
    total = pltpu.VMEM((blocks, BLK, BLK), wide)
    hbm = pl.BlockSpec(memory_space=pltpu.HBM)
    return pl.pallas_call(
        functools.partial(back_kernel, n),
        out_shape=(
            shape((PARTS, 2, 4, 48, 384), low),
            shape(resid.shape, wide),
            shape((16, 192), wide),
        ),
        in_specs=[smem()] * 2 + [hbm] * 9,
        out_specs=(hbm, vmem(), vmem()),
        scratch_shapes=[
            pltpu.VMEM(keep.shape, low),
            pltpu.VMEM(mix.shape, wide),
            pltpu.VMEM(lse.shape, wide),
            pltpu.VMEM(left.shape, low),
            pltpu.VMEM(sums.shape, wide),
            pltpu.VMEM(resid.shape, wide),
            pltpu.VMEM((PARTS, 2, 4, 48, 384), low),
            pltpu.VMEM(grad.shape, low),
            pltpu.VMEM((blocks, BLK, BLK), low),
            total, total, total,
            pltpu.VMEM(grad.shape, low),
            pltpu.VMEM(grad.shape, low),
            pltpu.VMEM((2, blocks, BLK, BLK), low),
            pltpu.VMEM((2, blocks, BLK, BLK), low),
            pltpu.VMEM(qkv_full.shape, low),
            pltpu.VMEM((9,) + right.shape[1:], low),
            pltpu.VMEM((2, 2, 192, 768), low),
            pltpu.VMEM((PARTS, 2, 192, 768), low),
            pltpu.VMEM((PARTS, 192, 768), low),
            pltpu.VMEM((PARTS, 192, 768), low),
            pltpu.VMEM((4, 192, 384), low),
            pltpu.VMEM((PARTS, 192, 384), low),
            pltpu.VMEM((4, 192, 384), wide),
            pltpu.VMEM((4, 96, 384), low),
            pltpu.VMEM((PARTS, 96, 384), low),
            pltpu.VMEM((4, 96, 384), wide),
            pltpu.VMEM((4, 48, 384), low),
            pltpu.VMEM((PARTS, 48, 384), low),
            pltpu.VMEM((4, 48, 384), wide),
            pltpu.VMEM((5,) + sums.shape, wide),
            pltpu.VMEM((5,) + sums.shape, wide),
            dma((7,)),
            dma((PARTS,)),
            dma((2, n)),
            dma((2, n)),
            dma((2, n)),
            dma((2, n)),
            dma((5,)),
        ]
        + [dma((2, PARTS))] * 8
        + [dma((2, 5))],
        compiler_params=pltpu.CompilerParams(
            collective_id=name, has_side_effects=True, vmem_limit_bytes=61 << 20
        ),
        name="back",
    )(pairing, lengths, grad, keep, mix, lse, left, right, sums, resid, qkv_full)


def finish_kernel(
    total_ref, small_ref, output_ref, token_ref,
    output_out, token_out, qkv_out, out_out, in_out, back_out, *refs
):
    lines, (total, small, through, stage, sems) = refs[:9], refs[9:]
    arrive = [
        pltpu.make_async_copy(total_ref.at[c], total.at[c], sems.at[PARTS + 2 + c])
        for c in range(PARTS)
    ] + [
        pltpu.make_async_copy(small_ref, small, sems.at[2 * PARTS + 2]),
        pltpu.make_async_copy(output_ref, through.at[0], sems.at[2 * PARTS + 3]),
        pltpu.make_async_copy(token_ref, through.at[1], sems.at[2 * PARTS + 4]),
    ]
    for cp in arrive:
        cp.start()
    copies = [
        pltpu.make_async_copy(through.at[0], output_out, sems.at[PARTS]),
        pltpu.make_async_copy(through.at[1], token_out, sems.at[PARTS + 1]),
    ]
    targets = [back_out.at[192 * k : 192 * k + 192] for k in range(4)]
    targets += [in_out.at[:, 768 * k : 768 * k + 768] for k in range(4)]
    targets += [out_out]
    targets += [qkv_out.at[:, 768 * k : 768 * k + 768] for k in range(3)]
    for c, target in enumerate(targets):
        arrive[c].wait()
        for half in range(2):
            for spot in range(4):
                stage[c, 48 * spot : 48 * spot + 48, 384 * half : 384 * half + 384] = total[
                    c, half, spot
                ].astype(jnp.float32)
        copies.append(pltpu.make_async_copy(stage.at[c], target, sems.at[c]))
        copies[-1].start()
    for k in range(2):
        arrive[PARTS + 1 + k].wait()
        copies[k].start()
    arrive[PARTS].wait()
    for i in range(8):
        lines[i][...] = small[i]
    for j in range(4):
        lines[8][192 * j : 192 * j + 192] = small[ROW_BI + j]
    for cp in copies:
        cp.wait()


def finish(total, small, output, token):
    shape = jax.ShapeDtypeStruct
    wide = jnp.float32
    hbm = pl.BlockSpec(memory_space=pltpu.HBM)
    return pl.pallas_call(
        finish_kernel,
        out_shape=(
            shape(output.shape, wide),
            shape(token.shape, wide),
            shape((192, 2304), wide),
            shape((192, 768), wide),
            shape((192, 3072), wide),
            shape((768, 768), wide),
        )
        + (shape((192,), wide),) * 8
        + (shape((768,), wide),),
        in_specs=[hbm] * 4,
        out_specs=(hbm,) * 6 + (vmem(),) * 9,
        scratch_shapes=[
            pltpu.VMEM(total.shape, total.dtype),
            pltpu.VMEM(small.shape, wide),
            pltpu.VMEM((2,) + token.shape, wide),
            pltpu.VMEM((PARTS, 192, 768), wide),
            pltpu.SemaphoreType.DMA((2 * PARTS + 5,)),
        ],
        compiler_params=pltpu.CompilerParams(vmem_limit_bytes=62 << 20),
        name="finish",
    )(total, small, output, token)


def on_device_spread(
    tokens,
    cotangent,
    lengths,
    pairing,
    w_qkv,
    bias_q,
    bias_v,
    w_out,
    bias_out,
    ln1_gain,
    ln1_bias,
    w_in,
    bias_in,
    w_back,
    bias_back,
    ln2_gain,
    ln2_bias,
):
    n = pairing.shape[0] // 2
    inputs = tokens[0]
    vectors = [bias_q, bias_v, bias_out, ln1_gain, ln1_bias, bias_back, ln2_gain, ln2_bias]
    vectors += [bias_in]
    output, grad, left, right, resid, sums, keep, mix, lse, qkv_full = front(
        pairing, lengths, vectors, inputs, cotangent[0], w_qkv, w_out, w_in, w_back, n, 0
    )
    total, token_grad, small_sum = back(
        pairing, lengths, grad, keep, mix, lse, left, right, sums, resid, qkv_full, 1
    )
    (
        output, token_grad, qkv_sum, out_sum, in_sum, back_sum,
        bq, bv, bo, g1, s1, bb, g2, s2, bi,
    ) = finish(total, small_sum, output, token_grad)
    return (
        output[None], token_grad[None], qkv_sum, bq, bv, out_sum, bo, g1, s1, in_sum, bi,
        back_sum, bb, g2, s2,
    )


def solution(mesh):
    return jax.shard_map(
        on_device_spread if mesh.shape["ctx"] == 8 else on_device_any,
        mesh=mesh,
        in_specs=(
            P("fsdp", "ctx", None),
            P("fsdp", "ctx", None),
            P("fsdp"),
            P(),
            P("fsdp", None),
            P("fsdp"),
            P("fsdp"),
            P("fsdp", None),
            P("fsdp"),
            P("fsdp"),
            P("fsdp"),
            P("fsdp", None),
            P("fsdp"),
            P("fsdp", None),
            P("fsdp"),
            P("fsdp"),
            P("fsdp"),
        ),
        out_specs=(
            P("fsdp", "ctx", None),
            P("fsdp", "ctx", None),
            P("fsdp", None),
            P("fsdp"),
            P("fsdp"),
            P("fsdp", None),
            P("fsdp"),
            P("fsdp"),
            P("fsdp"),
            P("fsdp", None),
            P("fsdp"),
            P("fsdp", None),
            P("fsdp"),
            P("fsdp"),
            P("fsdp"),
        ),
        check_vma=False,
    )
```

```python
import functools
import math

import jax
import jax.numpy as jnp
from jax import lax
from jax.experimental import pallas as pl
from jax.experimental.pallas import tpu as pltpu
from jax.sharding import PartitionSpec as P

HEADS = 12
HEAD_DIM = 64
NMEM = 10
BLK = 128


eps = 1e-12
neg_big = -1e30


def layer_norm(value, gain, shift):
    mean = jnp.mean(value, axis=-1, keepdims=True)
    centred = value - mean
    variance = jnp.mean(centred * centred, axis=-1, keepdims=True)
    return centred * lax.rsqrt(variance + eps) * gain + shift


def norm_back(value, gain, grad):
    mean = jnp.mean(value, axis=-1, keepdims=True)
    centred = value - mean
    scale = lax.rsqrt(jnp.mean(centred * centred, axis=-1, keepdims=True) + eps)
    unit = centred * scale
    scaled = grad * gain
    inner = (
        scaled
        - jnp.mean(scaled, axis=-1, keepdims=True)
        - unit * jnp.mean(scaled * unit, axis=-1, keepdims=True)
    )
    return (scale * inner, jnp.sum(grad * unit, axis=0), jnp.sum(grad, axis=0))


def block_width(count):
    return math.gcd(count, 512)


def places(pairing, start, count, half):
    rows = start + jnp.arange(count, dtype=jnp.int32)
    owners = rows // half
    spots = jnp.arange(pairing.shape[0], dtype=jnp.int32)
    picked = jnp.sum(jnp.where(owners[:, None] == spots[None, :], pairing[None, :], 0), axis=1)
    return picked * half + rows % half


def allowed_pairs(query_place, key_place, length):
    before = (key_place[None, :] <= query_place[:, None]) | (key_place[None, :] < NMEM)
    return (key_place[None, :] < length) & before


def heads_of(value):
    return value.reshape(value.shape[0], HEADS, HEAD_DIM)


def forward_fold(query_heads, query_place, pairing, length, half):

    def fold(carry, piece, start):
        keys, values = piece
        count = keys.shape[0]
        width = block_width(count)
        key_place = places(pairing, start, count, half)

        def step(index, state):
            top, total, summed = state
            offset = index * width
            key_heads = heads_of(lax.dynamic_slice_in_dim(keys, offset, width, 0))
            value_heads = heads_of(lax.dynamic_slice_in_dim(values, offset, width, 0))
            mask = allowed_pairs(
                query_place, lax.dynamic_slice_in_dim(key_place, offset, width, 0), length
            )[None]
            scores = (
                jnp.einsum(
                    "qhd,khd->hqk", query_heads, key_heads, preferred_element_type=jnp.float32
                )
                * 0.125
            )
            scores = jnp.where(mask, scores, neg_big)
            new_top = jnp.maximum(top, jnp.max(scores, axis=2))
            shrink = jnp.exp(top - new_top)
            probs = jnp.where(mask, jnp.exp(scores - new_top[:, :, None]), 0.0)
            total = total * shrink + jnp.sum(probs, axis=2)
            update = jnp.einsum(
                "hqk,khd->qhd",
                probs.astype(jnp.bfloat16),
                value_heads,
                preferred_element_type=jnp.float32,
            )
            summed = summed * jnp.transpose(shrink)[:, :, None] + update
            return (new_top, total, summed)

        return lax.fori_loop(0, count // width, step, carry)

    return fold


def query_grad_fold(query_heads, grad_heads, top_sum, delta, query_place, pairing, length, half):

    def fold(carry, piece, start):
        keys, values = piece
        count = keys.shape[0]
        width = block_width(count)
        key_place = places(pairing, start, count, half)

        def step(index, summed):
            offset = index * width
            key_heads = heads_of(lax.dynamic_slice_in_dim(keys, offset, width, 0))
            value_heads = heads_of(lax.dynamic_slice_in_dim(values, offset, width, 0))
            mask = allowed_pairs(
                query_place, lax.dynamic_slice_in_dim(key_place, offset, width, 0), length
            )[None]
            scores = (
                jnp.einsum(
                    "qhd,khd->hqk", query_heads, key_heads, preferred_element_type=jnp.float32
                )
                * 0.125
            )
            probs = jnp.where(mask, jnp.exp(scores - top_sum[:, :, None]), 0.0)
            prob_grad = jnp.einsum(
                "qhd,khd->hqk", grad_heads, value_heads, preferred_element_type=jnp.float32
            )
            score_grad = (probs * (prob_grad - delta[:, :, None])).astype(jnp.bfloat16)
            return (
                summed
                + jnp.einsum(
                    "hqk,khd->qhd", score_grad, key_heads, preferred_element_type=jnp.float32
                )
                * 0.125
            )

        return lax.fori_loop(0, count // width, step, carry)

    return fold


def key_terms(
    key_heads, value_heads, key_place, query_heads, grad_heads, top_sum, delta, query_place, length
):
    scores = (
        jnp.einsum("qhd,khd->hqk", query_heads, key_heads, preferred_element_type=jnp.float32)
        * 0.125
    )
    mask = allowed_pairs(query_place, key_place, length)[None]
    probs = jnp.where(mask, jnp.exp(scores - top_sum[:, :, None]), 0.0)
    prob_grad = jnp.einsum(
        "qhd,khd->hqk", grad_heads, value_heads, preferred_element_type=jnp.float32
    )
    score_grad = (probs * (prob_grad - delta[:, :, None])).astype(jnp.bfloat16)
    value_grad = jnp.einsum(
        "hqk,qhd->khd", probs.astype(jnp.bfloat16), grad_heads, preferred_element_type=jnp.float32
    )
    key_grad = (
        jnp.einsum("hqk,qhd->khd", score_grad, query_heads, preferred_element_type=jnp.float32)
        * 0.125
    )
    return (key_grad, value_grad)


def on_device_any(
    tokens,
    cotangent,
    lengths,
    pairing,
    w_qkv,
    bias_q,
    bias_v,
    w_out,
    bias_out,
    ln1_gain,
    ln1_bias,
    w_in,
    bias_in,
    w_back,
    bias_back,
    ln2_gain,
    ln2_bias,
):
    gathered = (
        lax.all_gather(w_qkv, "fsdp", axis=0, tiled=True),
        lax.all_gather(bias_q, "fsdp", axis=0, tiled=True),
        lax.all_gather(bias_v, "fsdp", axis=0, tiled=True),
        lax.all_gather(w_out, "fsdp", axis=0, tiled=True),
        lax.all_gather(bias_out, "fsdp", axis=0, tiled=True),
        lax.all_gather(ln1_gain, "fsdp", axis=0, tiled=True),
        lax.all_gather(ln1_bias, "fsdp", axis=0, tiled=True),
        lax.all_gather(w_in, "fsdp", axis=0, tiled=True),
        lax.all_gather(bias_in, "fsdp", axis=0, tiled=True),
        lax.all_gather(w_back, "fsdp", axis=0, tiled=True),
        lax.all_gather(bias_back, "fsdp", axis=0, tiled=True),
        lax.all_gather(ln2_gain, "fsdp", axis=0, tiled=True),
        lax.all_gather(ln2_bias, "fsdp", axis=0, tiled=True),
    )
    (
        qkv_all,
        query_bias,
        value_bias,
        out_all,
        out_bias,
        gain_one,
        shift_one,
        in_all,
        in_bias,
        back_all,
        back_bias,
        gain_two,
        shift_two,
    ) = gathered
    rows = tokens.shape[1]
    half = rows // 2
    width = tokens.shape[2]
    length = lengths[0]
    query_place = places(pairing, lax.axis_index("ctx") * rows, rows, half)
    valid = query_place < length
    inputs = tokens[0]
    proj = jnp.dot(inputs, qkv_all, preferred_element_type=jnp.float32)
    queries = (proj[:, :width] + query_bias.astype(jnp.float32)).astype(jnp.bfloat16)
    keys = proj[:, width : 2 * width].astype(jnp.bfloat16)
    values = (proj[:, 2 * width :] + value_bias.astype(jnp.float32)).astype(jnp.bfloat16)
    query_heads = heads_of(queries)
    start_state = (
        jnp.full((HEADS, rows), neg_big, jnp.float32),
        jnp.zeros((HEADS, rows), jnp.float32),
        jnp.zeros((rows, HEADS, HEAD_DIM), jnp.float32),
    )
    fold = forward_fold(query_heads, query_place, pairing, length, half)
    top, total, summed = fold(
        start_state,
        (
            lax.all_gather(keys, "ctx", axis=0, tiled=True),
            lax.all_gather(values, "ctx", axis=0, tiled=True),
        ),
        jnp.int32(0),
    )
    top_sum = top + jnp.log(total)
    attended = (summed / jnp.transpose(total)[:, :, None]).reshape(rows, width)
    attended_low = attended.astype(jnp.bfloat16)
    resid_one = (
        inputs.astype(jnp.float32)
        + jnp.dot(attended_low, out_all, preferred_element_type=jnp.float32)
        + out_bias.astype(jnp.float32)
    )
    hidden = layer_norm(resid_one, gain_one.astype(jnp.float32), shift_one.astype(jnp.float32))
    hidden_low = hidden.astype(jnp.bfloat16)
    upper = jnp.dot(hidden_low, in_all, preferred_element_type=jnp.float32) + in_bias.astype(
        jnp.float32
    )
    active, gelu_back = jax.vjp(lambda value: jax.nn.gelu(value, approximate=False), upper)
    active_low = active.astype(jnp.bfloat16)
    resid_two = (
        hidden
        + jnp.dot(active_low, back_all, preferred_element_type=jnp.float32)
        + back_bias.astype(jnp.float32)
    )
    normed = layer_norm(resid_two, gain_two.astype(jnp.float32), shift_two.astype(jnp.float32))
    output = jnp.where(valid[:, None], normed, 0.0)
    qkv_back, out_back, gain_one_back, in_back, back_back, gain_two_back = (
        qkv_all,
        out_all,
        gain_one,
        in_all,
        back_all,
        gain_two,
    )
    grad_y = jnp.where(valid[:, None], cotangent[0].astype(jnp.float32), 0.0)
    grad_resid_two, gain_two_grad, shift_two_grad = norm_back(
        resid_two, gain_two_back.astype(jnp.float32), grad_y
    )
    grad_mixed = grad_resid_two.astype(jnp.bfloat16)
    back_grad = jnp.einsum("tf,td->fd", active_low, grad_mixed, preferred_element_type=jnp.float32)
    back_bias_grad = jnp.sum(grad_mixed.astype(jnp.float32), axis=0)
    grad_active = jnp.einsum("td,fd->tf", grad_mixed, back_back, preferred_element_type=jnp.float32)
    (grad_upper,) = gelu_back(grad_active)
    grad_upper_low = grad_upper.astype(jnp.bfloat16)
    in_grad = jnp.einsum(
        "td,tf->df", hidden_low, grad_upper_low, preferred_element_type=jnp.float32
    )
    in_bias_grad = jnp.sum(grad_upper_low.astype(jnp.float32), axis=0)
    grad_hidden = grad_resid_two + jnp.einsum(
        "tf,df->td", grad_upper_low, in_back, preferred_element_type=jnp.float32
    )
    grad_resid_one, gain_one_grad, shift_one_grad = norm_back(
        resid_one, gain_one_back.astype(jnp.float32), grad_hidden
    )
    grad_branch = grad_resid_one.astype(jnp.bfloat16)
    out_grad = jnp.einsum(
        "tc,td->cd", attended_low, grad_branch, preferred_element_type=jnp.float32
    )
    out_bias_grad = jnp.sum(grad_branch.astype(jnp.float32), axis=0)
    grad_attended = jnp.einsum(
        "td,cd->tc", grad_branch, out_back, preferred_element_type=jnp.float32
    ).astype(jnp.bfloat16)
    grad_heads = heads_of(grad_attended)
    delta = jnp.transpose(jnp.sum(grad_heads.astype(jnp.float32) * heads_of(attended), axis=2))
    query_fold = query_grad_fold(
        query_heads, grad_heads, top_sum, delta, query_place, pairing, length, half
    )
    empty_heads = jnp.zeros((rows, HEADS, HEAD_DIM), jnp.float32)
    query_grad = query_fold(
        empty_heads,
        (
            lax.all_gather(keys, "ctx", axis=0, tiled=True),
            lax.all_gather(values, "ctx", axis=0, tiled=True),
        ),
        jnp.int32(0),
    )
    stats = jnp.concatenate([jnp.transpose(top_sum), jnp.transpose(delta)], axis=1)
    stats_all = lax.all_gather(stats, "ctx", axis=0, tiled=True)
    key_heads = heads_of(keys)
    value_heads = heads_of(values)
    query_in = lax.all_gather(queries, "ctx", axis=0, tiled=True)
    grad_in = lax.all_gather(grad_attended, "ctx", axis=0, tiled=True)
    count = query_in.shape[0]
    span = block_width(count)
    place_in = places(pairing, jnp.int32(0), count, half)

    def step(index, state):
        offset = index * span
        query_block = heads_of(lax.dynamic_slice_in_dim(query_in, offset, span, 0))
        grad_block = heads_of(lax.dynamic_slice_in_dim(grad_in, offset, span, 0))
        stats_block = lax.dynamic_slice_in_dim(stats_all, offset, span, 0)
        place_block = lax.dynamic_slice_in_dim(place_in, offset, span, 0)
        key_part, value_part = key_terms(
            key_heads,
            value_heads,
            query_place,
            query_block,
            grad_block,
            jnp.transpose(stats_block[:, :HEADS]),
            jnp.transpose(stats_block[:, HEADS:]),
            place_block,
            length,
        )
        return (state[0] + key_part, state[1] + value_part)

    key_sum, value_sum = lax.fori_loop(0, count // span, step, (empty_heads, empty_heads))
    key_grad = key_sum.reshape(rows, width)
    value_grad = value_sum.reshape(rows, width)
    grad_proj = jnp.concatenate(
        [
            query_grad.reshape(rows, width).astype(jnp.bfloat16),
            key_grad.astype(jnp.bfloat16),
            value_grad.astype(jnp.bfloat16),
        ],
        axis=1,
    )
    qkv_grad = jnp.einsum("td,tf->df", inputs, grad_proj, preferred_element_type=jnp.float32)
    query_bias_grad = jnp.sum(grad_proj[:, :width].astype(jnp.float32), axis=0)
    value_bias_grad = jnp.sum(grad_proj[:, 2 * width :].astype(jnp.float32), axis=0)
    token_grad = grad_resid_one + jnp.einsum(
        "tf,df->td", grad_proj, qkv_back, preferred_element_type=jnp.float32
    )
    grads = (
        qkv_grad,
        query_bias_grad,
        value_bias_grad,
        out_grad,
        out_bias_grad,
        gain_one_grad,
        shift_one_grad,
        in_grad,
        in_bias_grad,
        back_grad,
        back_bias_grad,
        gain_two_grad,
        shift_two_grad,
    )
    shards = (
        lax.psum_scatter(
            grads[0].astype(jnp.bfloat16), "fsdp", scatter_dimension=0, tiled=True
        ).astype(jnp.float32),
        lax.psum_scatter(
            grads[1].astype(jnp.bfloat16), "fsdp", scatter_dimension=0, tiled=True
        ).astype(jnp.float32),
        lax.psum_scatter(
            grads[2].astype(jnp.bfloat16), "fsdp", scatter_dimension=0, tiled=True
        ).astype(jnp.float32),
        lax.psum_scatter(
            grads[3].astype(jnp.bfloat16), "fsdp", scatter_dimension=0, tiled=True
        ).astype(jnp.float32),
        lax.psum_scatter(
            grads[4].astype(jnp.bfloat16), "fsdp", scatter_dimension=0, tiled=True
        ).astype(jnp.float32),
        lax.psum_scatter(
            grads[5].astype(jnp.bfloat16), "fsdp", scatter_dimension=0, tiled=True
        ).astype(jnp.float32),
        lax.psum_scatter(
            grads[6].astype(jnp.bfloat16), "fsdp", scatter_dimension=0, tiled=True
        ).astype(jnp.float32),
        lax.psum_scatter(
            grads[7].astype(jnp.bfloat16), "fsdp", scatter_dimension=0, tiled=True
        ).astype(jnp.float32),
        lax.psum_scatter(
            grads[8].astype(jnp.bfloat16), "fsdp", scatter_dimension=0, tiled=True
        ).astype(jnp.float32),
        lax.psum_scatter(
            grads[9].astype(jnp.bfloat16), "fsdp", scatter_dimension=0, tiled=True
        ).astype(jnp.float32),
        lax.psum_scatter(
            grads[10].astype(jnp.bfloat16), "fsdp", scatter_dimension=0, tiled=True
        ).astype(jnp.float32),
        lax.psum_scatter(
            grads[11].astype(jnp.bfloat16), "fsdp", scatter_dimension=0, tiled=True
        ).astype(jnp.float32),
        lax.psum_scatter(
            grads[12].astype(jnp.bfloat16), "fsdp", scatter_dimension=0, tiled=True
        ).astype(jnp.float32),
    )
    totals = (
        lax.psum(shards[0].astype(jnp.bfloat16), "ctx").astype(jnp.float32),
        lax.psum(shards[1].astype(jnp.bfloat16), "ctx").astype(jnp.float32),
        lax.psum(shards[2].astype(jnp.bfloat16), "ctx").astype(jnp.float32),
        lax.psum(shards[3].astype(jnp.bfloat16), "ctx").astype(jnp.float32),
        lax.psum(shards[4].astype(jnp.bfloat16), "ctx").astype(jnp.float32),
        lax.psum(shards[5].astype(jnp.bfloat16), "ctx").astype(jnp.float32),
        lax.psum(shards[6].astype(jnp.bfloat16), "ctx").astype(jnp.float32),
        lax.psum(shards[7].astype(jnp.bfloat16), "ctx").astype(jnp.float32),
        lax.psum(shards[8].astype(jnp.bfloat16), "ctx").astype(jnp.float32),
        lax.psum(shards[9].astype(jnp.bfloat16), "ctx").astype(jnp.float32),
        lax.psum(shards[10].astype(jnp.bfloat16), "ctx").astype(jnp.float32),
        lax.psum(shards[11].astype(jnp.bfloat16), "ctx").astype(jnp.float32),
        lax.psum(shards[12].astype(jnp.bfloat16), "ctx").astype(jnp.float32),
    )
    return (output[None], token_grad[None]) + tuple(totals)


def low_lanes(shape):
    return lax.broadcasted_iota(jnp.int32, shape, 1) < 64


def spot_of(pair_ref, place):
    found = jnp.int32(0)
    for s in range(pair_ref.shape[0]):
        found = jnp.where(pair_ref[s] == place, s, found)
    return found


def attend(c, length, spot, keep_ref, mix_ref, lse_ref, turned_ref):
    left = low_lanes((256, BLK))
    zero = jnp.zeros((), jnp.bfloat16)
    keys = 256 * (c + 1)
    own = keep_ref[0, 2 * c : 2 * c + 2].reshape(256, BLK)
    shared = keep_ref[0, 2 * c + spot]
    query = jnp.concatenate(
        [jnp.where(left, own, zero), jnp.where(left[:BLK], zero, shared)], axis=0
    ) * jnp.bfloat16(0.125)
    key = keep_ref[1, : 2 * c + 2].reshape(keys, BLK)
    value = keep_ref[2, : 2 * c + 2].reshape(keys, BLK)
    scores = mask_scores(dot_nt(key, query), c, spot, length, 0, True)
    top = jnp.max(scores, axis=0, keepdims=True)
    probs = jnp.exp(scores - top)
    total = jnp.sum(probs, axis=0, keepdims=True)
    summed = lax.dot_general(
        value, probs.astype(jnp.bfloat16), (((0,), (0,)), ((), ())),
        preferred_element_type=jnp.float32,
    ) / total
    lse_ref[c] = top + jnp.log(total)
    part = summed[64:, 256:]
    none = jnp.zeros_like(part)
    first = jnp.where(spot == 0, part, none)
    second = jnp.where(spot == 0, none, part)
    mixed = jnp.concatenate([summed[:64, :256], jnp.concatenate([first, second], axis=1)], axis=0)
    mix_ref[c] = mixed
    turned_ref[2 * c : 2 * c + 2] = (
        jnp.transpose(mixed).astype(jnp.bfloat16).reshape(2, BLK, BLK)
    )


def mask_scores(scores, c, spot, length, start, edged):
    keys, width = scores.shape
    row = start + lax.broadcasted_iota(jnp.int32, (keys, width), 0)
    scores = jnp.where(row < length, scores, neg_big)
    if not edged:
        return scores
    edge = 256 * c
    lane = lax.broadcasted_iota(jnp.int32, (256, width), 1)
    query_place = edge + jnp.where(lane < 256, lane, lane - 256 + spot * BLK)
    key_place = edge + lax.broadcasted_iota(jnp.int32, (256, width), 0)
    seen = key_place <= query_place
    if c == 0:
        seen = seen | (key_place < NMEM)
    tail = jnp.where(seen, scores[keys - 256 :], neg_big)
    if keys == 256:
        return tail
    return jnp.concatenate([scores[: keys - 256], tail], axis=0)


def attend_back(
    c, length, spot, keep_ref, g_ref, mix_ref, lse_ref, q_sum, k_sum, v_sum
):
    zero = jnp.zeros((), jnp.bfloat16)
    left = low_lanes((256, BLK))
    left_half = left[:BLK]
    own = keep_ref[0, 2 * c : 2 * c + 2].reshape(256, BLK)
    shared = keep_ref[0, 2 * c + spot]
    query = jnp.concatenate(
        [jnp.where(left, own, zero), jnp.where(left_half, zero, shared)], axis=0
    ) * jnp.bfloat16(0.125)
    g_own = g_ref[2 * c : 2 * c + 2].reshape(256, BLK)
    g_shared = g_ref[2 * c + spot]
    grad = jnp.concatenate(
        [jnp.where(left, g_own, zero), jnp.where(left_half, zero, g_shared)], axis=0
    )
    turned = jnp.transpose(g_own.astype(jnp.float32)) * mix_ref[c]
    delta_own = jnp.sum(turned[:64], axis=0, keepdims=True)
    delta_pair = jnp.sum(turned[64:], axis=0, keepdims=True)
    delta = jnp.concatenate(
        [delta_own, jnp.where(spot == 0, delta_pair[:, :BLK], delta_pair[:, BLK:])], axis=1
    )
    lse = lse_ref[c]
    q_grad = jnp.zeros((384, BLK), jnp.float32)
    last = 2 * c + 2
    step = 8
    for low_block in range(0, last, step):
        high_block = min(low_block + step, last)
        cut = slice(low_block, high_block)
        count = high_block - low_block
        key = keep_ref[1, cut].reshape(count * BLK, BLK)
        value = keep_ref[2, cut].reshape(count * BLK, BLK)
        scores = mask_scores(
            dot_nt(key, query), c, spot, length, low_block * BLK, high_block == last
        )
        probs = jnp.exp(scores - lse)
        score_grad = (probs * (dot_nt(value, grad) - delta)).astype(jnp.bfloat16)
        v_part = dot_nn(probs.astype(jnp.bfloat16), grad)
        k_part = dot_nn(score_grad, query)
        v_sum[cut] += v_part.reshape(count, BLK, BLK)
        k_sum[cut] += k_part.reshape(count, BLK, BLK)
        q_grad = q_grad + lax.dot_general(
            score_grad, key, (((0,), (0,)), ((), ())), preferred_element_type=jnp.float32
        )
    q_grad = q_grad * 0.125
    part = q_grad[256:]
    none = jnp.zeros_like(part)
    first = jnp.where(spot == 0, part, none)
    second = jnp.where(spot == 0, none, part)
    q_sum[2 * c : 2 * c + 2] = jnp.where(
        left, q_grad[:256], jnp.concatenate([first, second], axis=0)
    ).reshape(2, BLK, BLK)


def smem():
    return pl.BlockSpec(memory_space=pltpu.SMEM)


def vmem():
    return pl.BlockSpec(memory_space=pltpu.VMEM)


MESH = pl.DeviceIdType.MESH


def remote(src, dst, sems, at, peer):
    return pltpu.make_async_remote_copy(
        src_ref=src, dst_ref=dst, send_sem=sems.at[(0,) + at], recv_sem=sems.at[(1,) + at],
        device_id=peer, device_id_type=MESH,
    )


def greet(peers):
    barrier = pltpu.get_barrier_semaphore()
    for peer in peers:
        pl.semaphore_signal(barrier, inc=1, device_id=peer, device_id_type=MESH)
    pl.semaphore_wait(barrier, len(peers))


def ring_peers(n):
    me = lax.axis_index("ctx")
    return [{"ctx": lax.rem(me + k, n)} for k in range(1, n)]


def two(block):
    return pl.ds(2 * block, 2)


def one(block):
    return block


def exchange_copies(n, in_ref, out_ref, sems, at=two):
    me = lax.axis_index("ctx")
    copies = []
    for k in range(1, n):
        peer = lax.rem(me + k, n)
        copies.append(
            remote(in_ref.at[at(peer)], out_ref.at[at(me)], sems, (k,), {"ctx": peer})
        )
    return copies


def own_copy(in_ref, out_ref, sem, at=two):
    me = lax.axis_index("ctx")
    return pltpu.make_async_copy(in_ref.at[at(me)], out_ref.at[at(me)], sem)


def beside(first, second, axis):
    return jnp.concatenate([first, second], axis=axis)


def fold(first, second, shared):
    return beside(
        beside(first[:, :HEAD_DIM], second[:, :HEAD_DIM], 1),
        beside(shared[:HEAD_DIM], shared[HEAD_DIM:], 1),
        0,
    )


def fold_pair(value, spot, lead):
    first, second = value[:BLK], value[BLK:]
    return fold(
        first, second, jnp.where(lead == spot, first[:, HEAD_DIM:], second[:, HEAD_DIM:])
    )


def unfold_shared(message):
    return beside(message[BLK:, :HEAD_DIM], message[BLK:, HEAD_DIM:], 0)


def unfold_block(message, later):
    own = jnp.where(later == 0, message[:BLK, :HEAD_DIM], message[:BLK, HEAD_DIM:])
    return beside(own, unfold_shared(message), 1)


def join_folded(messages, lead):
    pieces = []
    for group in range(HEADS // 3):
        pair = [messages(2 * group), messages(2 * group + 1)]
        for message in pair:
            pieces.append(beside(message[:BLK, :HEAD_DIM], message[:BLK, HEAD_DIM:], 0))
        even, odd = [unfold_shared(message) for message in pair]
        pieces.append(
            beside(jnp.where(lead == 0, even, odd), jnp.where(lead == 0, odd, even), 0)
        )
    return jnp.concatenate(pieces, axis=1)


def both(ref, peer):
    value = ref[2 * peer : 2 * peer + 2]
    return value.reshape(-1, value.shape[2])


def join_pairs(pairs):
    pieces = []
    for group in range(HEADS // 3):
        first, second = pairs(2 * group), pairs(2 * group + 1)
        shared = first[:, HEAD_DIM:].astype(jnp.float32) + second[:, HEAD_DIM:].astype(jnp.float32)
        pieces += [first[:, :HEAD_DIM], second[:, :HEAD_DIM], shared.astype(jnp.bfloat16)]
    return jnp.concatenate(pieces, axis=1)


def pair_of(value, peer):
    own = 3 * (peer // 2) + peer % 2
    shared = 3 * (peer // 2) + 2
    cut = lambda head: value[:, head * HEAD_DIM : (head + 1) * HEAD_DIM]
    return jnp.concatenate([cut(own), cut(shared)], axis=1)


def dot_nn(a, b):
    return jnp.dot(a, b, preferred_element_type=jnp.float32)


def dot_nt(a, b):
    return lax.dot_general(a, b, (((1,), (1,)), ((), ())), preferred_element_type=jnp.float32)


def column_sum(value):
    return jnp.sum(value, axis=0, keepdims=True)


def unit_of(value):
    mean = jnp.mean(value, axis=-1, keepdims=True)
    centred = value - mean
    scale = lax.rsqrt(jnp.mean(centred * centred, axis=-1, keepdims=True) + eps)
    return centred * scale, scale


def unit_back(unit, scale, scaled):
    return scale * (
        scaled
        - jnp.mean(scaled, axis=-1, keepdims=True)
        - unit * jnp.mean(scaled * unit, axis=-1, keepdims=True)
    )


(ROW_BQ, ROW_BV, ROW_BO, ROW_G1, ROW_S1, ROW_BB, ROW_G2, ROW_S2, ROW_BI) = range(9)


def gather_copies(src, full, sems, index):
    fsdp = lax.axis_index("fsdp")
    x, core = fsdp // 2, lax.rem(fsdp, 2)
    sibling, across = {"fsdp": 2 * x + 1 - core}, {"fsdp": 2 * (1 - x) + core}
    other = 2 * (1 - x) + core
    return (
        remote(src, full.at[fsdp], sems, (index, 0), across),
        remote(src, full.at[fsdp], sems, (index, 1), sibling),
        remote(full.at[other], full.at[other], sems, (index, 2), sibling),
    )


def chip_peers():
    fsdp = lax.axis_index("fsdp")
    x, core = fsdp // 2, lax.rem(fsdp, 2)
    return [{"fsdp": 2 * x + 1 - core}, {"fsdp": 2 * (1 - x) + core}]


def split_gather(src, full, sems, parts):
    ctx, fsdp = lax.axis_index("ctx"), lax.axis_index("fsdp")
    z, y = ctx // 2, lax.rem(ctx, 2)
    x, core = fsdp // 2, lax.rem(fsdp, 2)
    sibling, across = {"fsdp": 2 * x + 1 - core}, {"fsdp": 2 * (1 - x) + core}
    over_y = {"ctx": 2 * z + 1 - y}
    other = 2 * (1 - x) + core
    count = src.shape[0] // 2
    here = pl.ds(pl.multiple_of(y * count, count), count)
    there = pl.ds(pl.multiple_of((1 - y) * count, count), count)
    cross, side, on, off, whole = [], [], [], [], []
    for p in range(parts):
        width = src.shape[1] // parts
        cols = slice(p * width, (p + 1) * width)
        moved = full.at[other, here, cols]
        late = full.at[other, there, cols]
        cross.append(remote(src.at[here, cols], full.at[fsdp, here, cols], sems, (0, p), across))
        side.append(remote(moved, moved, sems, (1, p), over_y))
        on.append(remote(moved, moved, sems, (2, p), sibling))
        off.append(remote(late, late, sems, (3, p), sibling))
        whole.append(remote(src.at[:, cols], full.at[fsdp, :, cols], sems, (4, p), sibling))
    return cross, side, on, off, whole


def passed(split, p):
    cross, side, on, off, whole = split
    cross[p].wait_recv()
    side[p].start()
    on[p].start()


def handed(split, p):
    cross, side, on, off, whole = split
    side[p].wait_recv()
    off[p].start()


def gathered(split, p):
    cross, side, on, off, whole = split
    for copies in (whole, on, off):
        copies[p].wait_recv()


def front_kernel(
    n, pair_ref, len_ref, *refs
):
    vectors, refs = refs[:9], refs[9:]
    (
        tokens_ref, cot_ref, qkv_src, out_src, in_src, back_src,
        output_ref, grad_ref, left_ref, right_ref, resid_ref, sums_ref,
        keep_ref, mix_ref, lse_ref, qkv_ref,
        small_out, small, rows_ref, token_buf, cot, w_qkv, w_out, w_in, w_back, send_folded, send,
        packed_q, packed_k, packed_v, keep, mix,
        lse, turned, mixed_out, mixed_in, active, slope, output, grad_out, left, right, resid, sums,
        small_sem, qkv_sem, in_split_sem, back_split_sem, gather_sem, send_q, send_k, send_v, in_sem, own_sem, load_sem, ship_sem,
    ) = refs
    send_sem = (send_q, send_k, send_v)
    packed = (packed_q, packed_k, packed_v)
    low, wide = jnp.bfloat16, jnp.float32
    ctx, fsdp = lax.axis_index("ctx"), lax.axis_index("fsdp")
    x, core = fsdp // 2, lax.rem(fsdp, 2)
    spot = lax.rem(ctx, 2)
    lead = lax.rem(pair_ref[2 * ctx], 2)
    width = token_buf.shape[1]
    count = in_src.shape[1] // width
    loads = [
        pltpu.make_async_copy(src, dst, load_sem.at[i])
        for i, (src, dst) in enumerate(
            [
                (tokens_ref, token_buf),
                (cot_ref, cot),
                (qkv_src, w_qkv.at[fsdp]),
                (out_src, w_out.at[fsdp]),
                (in_src, w_in.at[fsdp]),
                (back_src, w_back.at[fsdp]),
            ]
        )
    ]
    cot_load = loads[1]
    for cp in loads[:3]:
        cp.start()
    part = width // 4
    small_out[...] = jnp.zeros_like(small_out)
    for i in range(8):
        small_out[i : i + 1] = vectors[i][...].astype(wide).reshape(1, part)
    inner_bias = vectors[8][...].astype(wide).reshape(1, -1)
    for j in range(4):
        small_out[8 + j : 9 + j] = inner_bias[:, j * part : (j + 1) * part]
    greet(ring_peers(n) + chip_peers())
    smalls = gather_copies(small_out, small, small_sem, 0)
    qkv_split = split_gather(qkv_src, w_qkv, qkv_sem, 6)
    in_split = split_gather(in_src, w_in, in_split_sem, count)
    back_split = split_gather(back_src, w_back, back_split_sem, 2)
    splits = (qkv_split, in_split, back_split)
    for step in (0, 1):
        smalls[step].start()
    for cp in qkv_split[0] + qkv_split[4]:
        cp.start()
    for cp in loads[3:]:
        cp.start()
    shards = gather_copies(out_src, w_out, gather_sem, 0)
    small[fsdp] = small_out[...]
    smalls[0].wait_recv()
    smalls[2].start()
    passed(qkv_split, 0)
    passed(qkv_split, 1)
    loads[0].wait()
    tokens = token_buf[...]
    left[0] = jnp.transpose(tokens).reshape(4, -1, 2 * BLK)
    smalls[1].wait_recv()
    smalls[2].wait_recv()
    for f in range(4):
        cols = slice(f * part, (f + 1) * part)
        rows_ref[:8, cols] = small[f, :8]
        for j in range(4):
            rows_ref[ROW_BI + f : ROW_BI + f + 1, j * part : (j + 1) * part] = small[
                f, 8 + j : 9 + j
            ]
    rows_ref[12:] = jnp.zeros_like(rows_ref[12:])
    row = lambda i: rows_ref[i : i + 1, :]
    handed(qkv_split, 0)
    passed(qkv_split, 2)
    handed(qkv_split, 1)
    for p in range(3, 6):
        passed(qkv_split, p)
    for cp in shards[:2]:
        cp.start()
    for split in (in_split, back_split):
        for cp in split[0] + split[4]:
            cp.start()
    loads[2].wait()
    sends = []
    for p, bias in enumerate((ROW_BQ, None, ROW_BV)):
        for q in (2 * p, 2 * p + 1):
            if p:
                handed(qkv_split, q)
            gathered(qkv_split, q)
        value = dot_nn(tokens, w_qkv[:, :, p * width : (p + 1) * width].reshape(width, width))
        if bias is not None:
            value = value + row(bias)
        value = value.astype(low)
        for peer in range(n):
            both_heads = pair_of(value, peer)
            if p:
                send[p - 1, 2 * peer : 2 * peer + 2] = both_heads.reshape(2, BLK, BLK)
            else:
                send_folded[peer] = fold_pair(both_heads, peer % 2, lead)
        source, at = (send.at[p - 1], two) if p else (send_folded, one)
        copies = exchange_copies(n, source, packed[p], send_sem[p], at)
        copies.append(own_copy(source, packed[p], own_sem.at[2 + p], at))
        for cp in copies:
            cp.start()
        sends.append(copies)
    shipped = []

    def ship(src, dst):
        cp = pltpu.make_async_copy(src, dst, ship_sem.at[len(shipped)])
        cp.start()
        shipped.append(cp)

    ship(w_qkv, qkv_ref)
    spots = lax.broadcasted_iota(jnp.int32, (2 * BLK, 1), 0)
    place = jnp.where(
        spots < BLK,
        pair_ref[2 * ctx] * BLK + spots,
        pair_ref[2 * ctx + 1] * BLK + spots - BLK,
    )
    valid = place < len_ref[0]
    shards[0].wait_recv()
    shards[2].start()
    for p in range(count):
        passed(in_split, p)
        if p:
            handed(in_split, p - 1)
    passed(back_split, 0)
    handed(in_split, count - 1)
    spots_of = [spot_of(pair_ref, b) for b in range(2 * n)]
    for p in range(3):
        sends[p][-1].wait()
        for cp in sends[p][:-1]:
            cp.wait_recv()
        for b in range(2 * n):
            if p:
                keep[p, b] = packed[p][spots_of[b]]
            else:
                keep[p, b] = unfold_block(
                    packed[p][lax.div(spots_of[b], 2)], lax.rem(spots_of[b], 2)
                )

    ship(keep, keep_ref)
    for c in range(n):
        attend(c, len_ref[0], spot, keep, mix, lse, turned)
        if c == 0:
            passed(back_split, 1)
    for peer in range(n):
        first, second = turned[pair_ref[2 * peer]], turned[pair_ref[2 * peer + 1]]
        mixed_out[peer] = fold(first, second, first[:, HEAD_DIM:] + second[:, HEAD_DIM:])
    copies = exchange_copies(n, mixed_out, mixed_in, in_sem, one)
    for cp in copies:
        cp.start()
    own_mixed = own_copy(mixed_out, mixed_in, own_sem.at[1], one)
    own_mixed.start()
    ship(mix, mix_ref)
    ship(lse, lse_ref)
    sums[...] = jnp.zeros_like(sums)
    for cp in loads[3:]:
        cp.wait()
    for p in range(2):
        handed(back_split, p)
    shards[1].wait_recv()
    shards[2].wait_recv()
    for p in range(count):
        gathered(in_split, p)
    own_mixed.wait()
    for cp in copies:
        cp.wait_recv()
    attended = join_folded(lambda peer: mixed_in[peer], lead)
    resid_one = (
        tokens.astype(wide)
        + dot_nn(attended, w_out[...].reshape(width, width))
        + row(ROW_BO)
    )
    unit_one, scale_one = unit_of(resid_one)
    hidden = unit_one * row(ROW_G1) + row(ROW_S1)
    hidden_low = hidden.astype(low)
    resid_two = hidden + row(ROW_BB)
    cut = lambda t: pl.ds(pl.multiple_of(t * width, width), width)
    order = [fsdp, 2 * x + 1 - core, 2 * (1 - x) + core, 2 * (1 - x) + 1 - core]
    for step, t in enumerate(order):
        bias = rows_ref[pl.ds(ROW_BI + t, 1), :]
        upper = dot_nn(hidden_low, w_in[:, :, cut(t)].reshape(width, width)) + bias
        share = 0.5 * (1.0 + lax.erf(upper * (0.5**0.5)))
        slope[t] = share + upper * (jnp.exp(-0.5 * upper * upper) * (2 * math.pi) ** -0.5)
        some = (upper * share).astype(low)
        active[t] = some
        if step == 0:
            gathered(back_split, 0)
            gathered(back_split, 1)
        resid_two = resid_two + dot_nn(some, w_back[t])
    unit_two, scale_two = unit_of(resid_two)
    output[...] = jnp.where(valid, unit_two * row(ROW_G2) + row(ROW_S2), 0.0)
    cot_load.wait()
    grad_y = jnp.where(valid, cot[...].astype(wide), 0.0)
    sums[ROW_G2 : ROW_G2 + 1, :] = column_sum(grad_y * unit_two)
    sums[ROW_S2 : ROW_S2 + 1, :] = column_sum(grad_y)
    grad_resid_two = unit_back(unit_two, scale_two, grad_y * row(ROW_G2))
    grad_mixed = grad_resid_two.astype(low)
    right[5] = grad_mixed
    sums[ROW_BB : ROW_BB + 1, :] = column_sum(grad_mixed.astype(wide))
    ship(output, output_ref)
    left[1] = jnp.transpose(attended).reshape(4, -1, 2 * BLK)
    left[2] = jnp.transpose(hidden_low).reshape(4, -1, 2 * BLK)
    for f in range(4):
        turned = jnp.transpose(active[f])
        for r in range(4):
            left[3 + r, f] = turned[r * width // 4 : (r + 1) * width // 4]
    ship(left, left_ref)
    grad_hidden = grad_resid_two
    for t in range(count):
        grad_upper = (dot_nt(grad_mixed, w_back[t]) * slope[t]).astype(low)
        right[1 + t] = grad_upper
        sums[ROW_BI + t : ROW_BI + t + 1, :] = column_sum(grad_upper.astype(wide))
        grad_hidden = grad_hidden + dot_nt(grad_upper, w_in[:, :, cut(t)].reshape(width, width))
    sums[ROW_G1 : ROW_G1 + 1, :] = column_sum(grad_hidden * unit_one)
    sums[ROW_S1 : ROW_S1 + 1, :] = column_sum(grad_hidden)
    grad_resid_one = unit_back(unit_one, scale_one, grad_hidden * row(ROW_G1))
    resid[...] = grad_resid_one
    grad_branch = grad_resid_one.astype(low)
    right[0] = grad_branch
    sums[ROW_BO : ROW_BO + 1, :] = column_sum(grad_branch.astype(wide))
    ship(resid, resid_ref)
    ship(right, right_ref)
    ship(sums, sums_ref)
    grad_attended = dot_nt(grad_branch, w_out[...].reshape(width, width)).astype(low)
    for peer in range(n):
        grad_out[peer] = fold_pair(pair_of(grad_attended, peer), peer % 2, lead)
    ship(grad_out, grad_ref)
    for cps in (smalls, shards, copies) + sum(splits, ()):
        for cp in cps:
            cp.wait_send()
    for cps in sends:
        for cp in cps[:-1]:
            cp.wait_send()
    for cp in shipped:
        cp.wait()


def front(pairing, lengths, vectors, tokens, cotangent, w_qkv, w_out, w_in, w_back, n, name):
    count, width = tokens.shape
    low, wide = jnp.bfloat16, jnp.float32
    dma = pltpu.SemaphoreType.DMA
    shape = jax.ShapeDtypeStruct
    hbm = pl.BlockSpec(memory_space=pltpu.HBM)
    vec = pltpu.VMEM((16, width // 4), wide)
    results = [
        ((count, width), wide),
        ((n, BLK + HEAD_DIM, BLK), low),
        ((7, 4, width // 4, count), low),
        ((6, count, width), low),
        ((count, width), wide),
        ((16, width), wide),
        ((3, 2 * n, BLK, BLK), low),
        ((n, BLK, 2 * BLK), wide),
        ((n, 1, 3 * BLK), wide),
        ((4,) + w_qkv.shape, low),
    ]
    output, grad, left, right, resid, sums, keep, mix, lse, qkv = [pltpu.VMEM(*r) for r in results]
    blocks = pltpu.VMEM((2 * n, BLK, BLK), low)
    return pl.pallas_call(
        functools.partial(front_kernel, n),
        out_shape=tuple(shape(*r) for r in results),
        in_specs=[smem(), smem()] + [vmem()] * 9 + [hbm] * 6,
        out_specs=(hbm,) * 10,
        scratch_shapes=[
            vec,
            pltpu.VMEM((4, 16, width // 4), wide),
            pltpu.VMEM((16, width), wide),
            pltpu.VMEM((count, width), low),
            pltpu.VMEM((count, width), low),
            qkv,
            pltpu.VMEM((4,) + w_out.shape, low),
            pltpu.VMEM((4,) + w_in.shape, low),
            pltpu.VMEM((4,) + w_back.shape, low),
            grad,
            pltpu.VMEM((2, 2 * n, BLK, BLK), low),
            grad,
            blocks,
            blocks,
            keep,
            mix,
            lse,
            blocks,
            grad,
            grad,
            pltpu.VMEM((4, count, width), low),
            pltpu.VMEM((4, count, width), wide),
            output,
            grad,
            left,
            right,
            resid,
            sums,
            dma((2, 1, 3)),
            dma((2, 5, 6)),
            dma((2, 5, 4)),
            dma((2, 5, 2)),
            dma((2, 1, 3)),
            dma((2, n)),
            dma((2, n)),
            dma((2, n)),
            dma((2, n)),
            dma((5,)),
            dma((6,)),
            dma((10,)),
        ],
        compiler_params=pltpu.CompilerParams(
            collective_id=name, has_side_effects=True, vmem_limit_bytes=62 << 20
        ),
        name="front",
    )(pairing, lengths, *vectors, tokens, cotangent, w_qkv, w_out, w_in, w_back)


PARTS = 12


def sum_sources(chunk):
    left = jnp.where(chunk < 4, 3 + chunk, jnp.where(chunk < 8, 2, jnp.where(chunk < 9, 1, 0)))
    right = jnp.where(
        chunk < 4, 8, jnp.where(chunk < 8, chunk, jnp.where(chunk < 9, 3, chunk - 9))
    )
    return left, right


STEPS = 65
PLAN = {
    "pair": {0: 0, 1: 1, 2: 2, 3: 3, 6: 4, 7: 5, 13: 6, 15: 7, 19: 8, 21: 9, 29: 10, 32: 11},
    "x": {3: 0, 4: 1, 5: 2, 7: 3, 12: 4, 13: 5, 14: 6, 18: 7, 23: 8, 30: 9, 36: 10, 41: 11},
    "y": {9: 0, 10: 1, 16: 2, 17: 3, 18: 4, 21: 5, 24: 6, 26: 7, 30: 8, 36: 9, 46: 10, 50: 11},
    "near": {11: 0, 19: 1, 20: 2, 24: 3, 25: 4, 28: 5, 32: 6, 38: 7, 42: 8, 44: 9, 49: 10, 57: 11},
    "far": {22: 0, 25: 1, 26: 2, 31: 3, 33: 4, 39: 5, 41: 6, 44: 7, 47: 8, 52: 9, 55: 10, 60: 11},
    "own": {27: 0, 29: 1, 30: 2, 37: 3, 40: 4, 45: 5, 49: 6, 50: 7, 53: 8, 57: 9, 58: 10, 61: 11},
    "wide": {30: 0, 31: 1, 34: 2, 43: 3, 48: 4, 50: 5, 51: 6, 56: 7, 57: 8, 59: 9, 61: 10, 62: 11},
    "last": {35: 0, 38: 1, 42: 2, 47: 3, 52: 4, 54: 5, 55: 6, 58: 7, 60: 8, 61: 9, 63: 10, 64: 11},
}
ATTEND_AT = (8, 9, 10)
JOIN_AT = (16, 24, 28)
SMALL_AT = (46, 49, 52, 61, 62, 64)
TOKEN_AT = 44


def planned(name, step):
    chunk = jnp.int32(-1)
    for at, which in PLAN[name].items():
        chunk = jnp.where(step == at, which, chunk)
    return chunk


def back_kernel(
    n, pair_ref, len_ref, grad_ref, keep_src, mix_src, lse_src, left_src, right_src,
    sums_src, resid_src, qkv_ref,
    total_out, token_out, small_dst,
    token_ref, small_out, keep_ref, mix_ref, lse_ref, left_ref, sums_ref, resid_ref, total_ref,
    grad_in, g_all, q_sum, k_sum, v_sum, folded_out, folded_in,
    blocks_out, blocks_in, w_qkv, right_all,
    pair_out, pair_in, x_out, x_in, y_out, y_in, y_keep, near_out, near_in, near_keep,
    far_out, far_in, far_keep, s_out, s_in,
    load_sem, ship_sem,
    grad_sem, block_q, block_k, block_v, own_sem, pair_sem, x_sem, y_sem, near_sem, far_sem,
    own_z_sem, wide_sem, last_sem, s_sem,
):
    block_sem = (block_q, block_k, block_v)
    low, wide = jnp.bfloat16, jnp.float32
    ctx = lax.axis_index("ctx")
    fsdp = lax.axis_index("fsdp")
    z, y = ctx // 2, lax.rem(ctx, 2)
    odd, upper = lax.rem(z, 2), z // 2
    x, core = fsdp // 2, lax.rem(fsdp, 2)
    sibling = {"fsdp": 2 * x + 1 - core}
    across = {"fsdp": 2 * (1 - x) + core}
    over_y = {"ctx": 2 * z + 1 - y}
    near = {"ctx": 2 * (2 * upper + 1 - odd) + y}
    far = {"ctx": 2 * (2 * (1 - upper) + odd) + y}
    mine = 2 * odd + upper
    loads = [
        pltpu.make_async_copy(src, dst, load_sem.at[i])
        for i, (src, dst) in enumerate(
            [
                (right_src, right_all.at[3:]),
                (left_src, left_ref),
                (keep_src, keep_ref),
                (mix_src, mix_ref),
                (lse_src, lse_ref),
                (sums_src, sums_ref),
                (resid_src, resid_ref),
            ]
        )
    ]
    for cp in loads:
        cp.start()
    greet(ring_peers(n) + [sibling, across])
    lead = lax.rem(pair_ref[2 * ctx], 2)
    grads = exchange_copies(n, grad_ref, grad_in, grad_sem, one)
    for cp in grads:
        cp.start()
    own_grad = own_copy(grad_ref, grad_in, own_sem.at[0], one)
    own_grad.start()
    load = pltpu.make_async_copy(qkv_ref, w_qkv, own_sem.at[1])
    load.start()
    blocks = [
        exchange_copies(n, folded_out, folded_in, block_sem[0], one)
    ] + [
        exchange_copies(n, blocks_out.at[p], blocks_in.at[p], block_sem[1 + p])
        for p in range(2)
    ]
    own = [own_copy(folded_out, folded_in, own_sem.at[2], one)] + [
        own_copy(blocks_out.at[p], blocks_in.at[p], own_sem.at[3 + p]) for p in range(2)
    ]
    k_sum[...] = jnp.zeros_like(k_sum)
    v_sum[...] = jnp.zeros_like(v_sum)
    chunks = keep_ref.shape[1] // 2

    def attend_some(first, last):
        for c in range(first, last):
            attend_back(
                c, len_ref[0], y, keep_ref, g_all, mix_ref, lse_ref, q_sum, k_sum, v_sum
            )

    def attend_step(t):
        @pl.when(t == ATTEND_AT[0])
        def _():
            own_grad.wait()
            for cp in loads[2:5]:
                cp.wait()
            for cp in grads:
                cp.wait_recv()
            for b in range(2 * chunks):
                found = spot_of(pair_ref, b)
                g_all[b] = unfold_block(grad_in[lax.div(found, 2)], lax.rem(found, 2))
            attend_some(0, chunks // 2)

        @pl.when(t == ATTEND_AT[1])
        def _():
            attend_some(chunks // 2, chunks - 2)

        @pl.when(t == ATTEND_AT[2])
        def _():
            attend_some(chunks - 2, chunks)
            for peer in range(n):
                first, second = q_sum[pair_ref[2 * peer]], q_sum[pair_ref[2 * peer + 1]]
                folded_out[peer] = fold(
                    first, second, first[:, HEAD_DIM:] + second[:, HEAD_DIM:]
                ).astype(low)
            for p, total in enumerate((None, k_sum, v_sum)):
                if p:
                    for s in range(2 * chunks):
                        blocks_out[p - 1, s] = total[pair_ref[s]].astype(low)
                for cp in blocks[p]:
                    cp.start()
                own[p].start()

    def slot(c):
        return lax.rem(c, 4)

    def pair_copy(c):
        return remote(pair_out.at[lax.rem(c, 2)], pair_in.at[c], pair_sem, (c,), sibling)

    def x_copy(c):
        return remote(x_out.at[c], x_in.at[c], x_sem, (c,), across)

    def y_copy(c):
        return remote(y_out.at[slot(c)], y_in.at[c], y_sem, (c,), over_y)

    def near_copy(c):
        return remote(near_out.at[slot(c)], near_in.at[c], near_sem, (c,), near)

    def far_copy(c):
        return remote(far_out.at[slot(c)], far_in.at[c], far_sem, (c,), far)

    def own_z_copy(c):
        piece = total_ref.at[c, y, mine]
        return remote(piece, piece, own_z_sem, (c,), far)

    def wide_copy(c):
        piece = total_ref.at[c, y, two(odd)]
        return remote(piece, piece, wide_sem, (c,), near)

    def last_copy(c):
        piece = total_ref.at[c, y]
        return remote(piece, piece, last_sem, (c,), over_y)

    def reuse(copy, c, slots):
        @pl.when(c >= slots)
        def _():
            copy(c - slots).wait_send()

    def partial(c, shard):
        left, right = sum_sources(c)
        return dot_nn(left_ref[left, shard], right_all[right])

    def stage_pair(c):
        reuse(pair_copy, c, 2)
        for side in range(2):
            pair_out[lax.rem(c, 2), side] = partial(c, 2 * side + 1 - core).astype(low)
        pair_copy(c).start()

    def stage_x(c):
        pair_copy(c).wait_recv()
        x_out[c] = (partial(c, 2 * (1 - x) + core) + pair_in[c, 1 - x].astype(wide)).astype(low)
        x_copy(c).start()

    def stage_y(c):
        mine_sum = partial(c, 2 * x + core) + pair_in[c, x].astype(wide)
        x_copy(c).wait_recv()
        total = mine_sum + x_in[c].astype(wide)
        first, second = total[:, :384], total[:, 384:]
        reuse(y_copy, c, 4)
        y_out[slot(c)] = jnp.where(y == 0, second, first).astype(low)
        y_copy(c).start()
        y_keep[slot(c)] = jnp.where(y == 0, first, second)

    def stage_near(c):
        y_copy(c).wait_recv()
        total = y_keep[slot(c)] + y_in[c].astype(wide)
        first, second = total[:96], total[96:]
        reuse(near_copy, c, 4)
        near_out[slot(c)] = jnp.where(odd == 0, second, first).astype(low)
        near_copy(c).start()
        near_keep[slot(c)] = jnp.where(odd == 0, first, second)

    def stage_far(c):
        near_copy(c).wait_recv()
        total = near_keep[slot(c)] + near_in[c].astype(wide)
        first, second = total[:48], total[48:]
        reuse(far_copy, c, 4)
        far_out[slot(c)] = jnp.where(upper == 0, second, first).astype(low)
        far_copy(c).start()
        far_keep[slot(c)] = jnp.where(upper == 0, first, second)

    def stage_own(c):
        far_copy(c).wait_recv()
        total_ref[c, y, mine] = (far_keep[slot(c)] + far_in[c].astype(wide)).astype(low)
        own_z_copy(c).start()

    def stage_wide(c):
        own_z_copy(c).wait_recv()
        wide_copy(c).start()

    def stage_last(c):
        wide_copy(c).wait_recv()
        last_copy(c).start()

    token_ship = pltpu.make_async_copy(token_ref, token_out, ship_sem.at[PARTS])
    small_ship = pltpu.make_async_copy(small_out, small_dst, ship_sem.at[PARTS + 1])

    def small_step(t):
        peers = [sibling, across, over_y, near, far]
        copies = [
            remote(s_out.at[k], s_in.at[k], s_sem, (k,), peer) for k, peer in enumerate(peers)
        ]

        for p in range(3):

            @pl.when(t == JOIN_AT[p])
            def _():
                own[p].wait()
                for cp in blocks[p]:
                    cp.wait_recv()
                if p:
                    right_all[p] = join_pairs(lambda peer: both(blocks_in.at[p - 1], peer))
                else:
                    right_all[p] = join_folded(lambda peer: folded_in[peer], lead)

        @pl.when(t == SMALL_AT[0])
        def _():
            loads[5].wait()
            s_out[0] = sums_ref[...]
            s_out[0, ROW_BQ : ROW_BQ + 1] = column_sum(right_all[0].astype(wide))
            s_out[0, ROW_BV : ROW_BV + 1] = column_sum(right_all[2].astype(wide))
            copies[0].start()

        for k in range(1, 5):

            @pl.when(t == SMALL_AT[k])
            def _():
                copies[k - 1].wait()
                s_out[k] = s_out[k - 1] + s_in[k - 1]
                copies[k].start()

        @pl.when(t == SMALL_AT[5])
        def _():
            copies[4].wait()
            total = s_out[4] + s_in[4]
            quarter = total.shape[1] // 4
            cuts = [slice(f * quarter, (f + 1) * quarter) for f in range(4)]
            pick = lambda choices: sum(
                jnp.where(fsdp == f, choice, 0.0) for f, choice in enumerate(choices)
            )
            small_out[...] = jnp.zeros_like(small_out)
            small_out[:8] = pick([total[:8, cut] for cut in cuts])
            line = pick([total[ROW_BI + f : ROW_BI + f + 1] for f in range(4)])
            for j, cut in enumerate(cuts):
                small_out[8 + j : 9 + j] = line[:, cut]
            small_ship.start()

        @pl.when(t == TOKEN_AT)
        def _():
            load.wait()
            loads[6].wait()
            width = resid_ref.shape[1]
            token_ref[...] = resid_ref[...] + sum(
                dot_nt(
                    right_all[part],
                    w_qkv[:, :, part * width : (part + 1) * width].reshape(width, width),
                )
                for part in range(3)
            )
            token_ship.start()

    stages = [
        ("pair", stage_pair),
        ("x", stage_x),
        ("last", stage_last),
        ("wide", stage_wide),
        ("own", stage_own),
        ("far", stage_far),
        ("near", stage_near),
        ("y", stage_y),
    ]

    def step(t, carry):
        attend_step(t)
        small_step(t)
        for name, stage in stages:
            c = planned(name, t)

            @pl.when(c >= 0)
            def _():
                stage(c)

        return carry

    loads[0].wait()
    loads[1].wait()
    lax.fori_loop(0, STEPS, step, 0)

    def ship(c):
        return pltpu.make_async_copy(total_ref.at[c], total_out.at[c], ship_sem.at[c])

    def drain(c, carry):
        x_copy(c).wait_send()
        own_z_copy(c).wait_send()
        wide_copy(c).wait_send()
        last_copy(c).wait()
        ship(c).start()
        return carry

    lax.fori_loop(0, PARTS, drain, 0)
    for c in range(PARTS - 4, PARTS):
        y_copy(c).wait_send()
        near_copy(c).wait_send()
        far_copy(c).wait_send()
    for c in (PARTS - 2, PARTS - 1):
        pair_copy(c).wait_send()
    for cp in grads + blocks[0] + blocks[1] + blocks[2]:
        cp.wait_send()
    for c in range(PARTS):
        ship(c).wait()
    token_ship.wait()
    small_ship.wait()


def back(pairing, lengths, grad, keep, mix, lse, left, right, sums, resid, qkv_full, name):
    blocks = keep.shape[1]
    n = blocks // 2
    low, wide = jnp.bfloat16, jnp.float32
    dma = pltpu.SemaphoreType.DMA
    shape = jax.ShapeDtypeStruct
    total = pltpu.VMEM((blocks, BLK, BLK), wide)
    hbm = pl.BlockSpec(memory_space=pltpu.HBM)
    return pl.pallas_call(
        functools.partial(back_kernel, n),
        out_shape=(
            shape((PARTS, 2, 4, 48, 384), low),
            shape(resid.shape, wide),
            shape((16, 192), wide),
        ),
        in_specs=[smem()] * 2 + [hbm] * 9,
        out_specs=(hbm,) * 3,
        scratch_shapes=[
            pltpu.VMEM(resid.shape, wide),
            pltpu.VMEM((16, 192), wide),
            pltpu.VMEM(keep.shape, low),
            pltpu.VMEM(mix.shape, wide),
            pltpu.VMEM(lse.shape, wide),
            pltpu.VMEM(left.shape, low),
            pltpu.VMEM(sums.shape, wide),
            pltpu.VMEM(resid.shape, wide),
            pltpu.VMEM((PARTS, 2, 4, 48, 384), low),
            pltpu.VMEM(grad.shape, low),
            pltpu.VMEM((blocks, BLK, BLK), low),
            total, total, total,
            pltpu.VMEM(grad.shape, low),
            pltpu.VMEM(grad.shape, low),
            pltpu.VMEM((2, blocks, BLK, BLK), low),
            pltpu.VMEM((2, blocks, BLK, BLK), low),
            pltpu.VMEM(qkv_full.shape, low),
            pltpu.VMEM((9,) + right.shape[1:], low),
            pltpu.VMEM((2, 2, 192, 768), low),
            pltpu.VMEM((PARTS, 2, 192, 768), low),
            pltpu.VMEM((PARTS, 192, 768), low),
            pltpu.VMEM((PARTS, 192, 768), low),
            pltpu.VMEM((4, 192, 384), low),
            pltpu.VMEM((PARTS, 192, 384), low),
            pltpu.VMEM((4, 192, 384), wide),
            pltpu.VMEM((4, 96, 384), low),
            pltpu.VMEM((PARTS, 96, 384), low),
            pltpu.VMEM((4, 96, 384), wide),
            pltpu.VMEM((4, 48, 384), low),
            pltpu.VMEM((PARTS, 48, 384), low),
            pltpu.VMEM((4, 48, 384), wide),
            pltpu.VMEM((5,) + sums.shape, wide),
            pltpu.VMEM((5,) + sums.shape, wide),
            dma((7,)),
            dma((PARTS + 2,)),
            dma((2, n)),
            dma((2, n)),
            dma((2, n)),
            dma((2, n)),
            dma((5,)),
        ]
        + [dma((2, PARTS))] * 8
        + [dma((2, 5))],
        compiler_params=pltpu.CompilerParams(
            collective_id=name, has_side_effects=True, vmem_limit_bytes=61 << 20
        ),
        name="back",
    )(pairing, lengths, grad, keep, mix, lse, left, right, sums, resid, qkv_full)


def finish_kernel(
    total_ref, small_ref, output_ref, token_ref,
    output_out, token_out, qkv_out, out_out, in_out, back_out, *refs
):
    lines, (total, small, through, stage, sems) = refs[:9], refs[9:]
    arrive = [
        pltpu.make_async_copy(total_ref.at[c], total.at[c], sems.at[PARTS + 2 + c])
        for c in range(PARTS)
    ] + [
        pltpu.make_async_copy(small_ref, small, sems.at[2 * PARTS + 2]),
        pltpu.make_async_copy(output_ref, through.at[0], sems.at[2 * PARTS + 3]),
        pltpu.make_async_copy(token_ref, through.at[1], sems.at[2 * PARTS + 4]),
    ]
    for cp in arrive:
        cp.start()
    copies = [
        pltpu.make_async_copy(through.at[0], output_out, sems.at[PARTS]),
        pltpu.make_async_copy(through.at[1], token_out, sems.at[PARTS + 1]),
    ]
    targets = [back_out.at[192 * k : 192 * k + 192] for k in range(4)]
    targets += [in_out.at[:, 768 * k : 768 * k + 768] for k in range(4)]
    targets += [out_out]
    targets += [qkv_out.at[:, 768 * k : 768 * k + 768] for k in range(3)]
    for c, target in enumerate(targets):
        arrive[c].wait()
        for half in range(2):
            for spot in range(4):
                stage[c, 48 * spot : 48 * spot + 48, 384 * half : 384 * half + 384] = total[
                    c, half, spot
                ].astype(jnp.float32)
        copies.append(pltpu.make_async_copy(stage.at[c], target, sems.at[c]))
        copies[-1].start()
    for k in range(2):
        arrive[PARTS + 1 + k].wait()
        copies[k].start()
    arrive[PARTS].wait()
    for i in range(8):
        lines[i][...] = small[i]
    for j in range(4):
        lines[8][192 * j : 192 * j + 192] = small[ROW_BI + j]
    for cp in copies:
        cp.wait()


def finish(total, small, output, token):
    shape = jax.ShapeDtypeStruct
    wide = jnp.float32
    hbm = pl.BlockSpec(memory_space=pltpu.HBM)
    return pl.pallas_call(
        finish_kernel,
        out_shape=(
            shape(output.shape, wide),
            shape(token.shape, wide),
            shape((192, 2304), wide),
            shape((192, 768), wide),
            shape((192, 3072), wide),
            shape((768, 768), wide),
        )
        + (shape((192,), wide),) * 8
        + (shape((768,), wide),),
        in_specs=[hbm] * 4,
        out_specs=(hbm,) * 6 + (vmem(),) * 9,
        scratch_shapes=[
            pltpu.VMEM(total.shape, total.dtype),
            pltpu.VMEM(small.shape, wide),
            pltpu.VMEM((2,) + token.shape, wide),
            pltpu.VMEM((PARTS, 192, 768), wide),
            pltpu.SemaphoreType.DMA((2 * PARTS + 5,)),
        ],
        compiler_params=pltpu.CompilerParams(vmem_limit_bytes=62 << 20),
        name="finish",
    )(total, small, output, token)


def on_device_spread(
    tokens,
    cotangent,
    lengths,
    pairing,
    w_qkv,
    bias_q,
    bias_v,
    w_out,
    bias_out,
    ln1_gain,
    ln1_bias,
    w_in,
    bias_in,
    w_back,
    bias_back,
    ln2_gain,
    ln2_bias,
):
    n = pairing.shape[0] // 2
    inputs = tokens[0]
    vectors = [bias_q, bias_v, bias_out, ln1_gain, ln1_bias, bias_back, ln2_gain, ln2_bias]
    vectors += [bias_in]
    output, grad, left, right, resid, sums, keep, mix, lse, qkv_full = front(
        pairing, lengths, vectors, inputs, cotangent[0], w_qkv, w_out, w_in, w_back, n, 0
    )
    total, token_grad, small_sum = back(
        pairing, lengths, grad, keep, mix, lse, left, right, sums, resid, qkv_full, 1
    )
    (
        output, token_grad, qkv_sum, out_sum, in_sum, back_sum,
        bq, bv, bo, g1, s1, bb, g2, s2, bi,
    ) = finish(total, small_sum, output, token_grad)
    return (
        output[None], token_grad[None], qkv_sum, bq, bv, out_sum, bo, g1, s1, in_sum, bi,
        back_sum, bb, g2, s2,
    )


def solution(mesh):
    return jax.shard_map(
        on_device_spread if mesh.shape["ctx"] == 8 else on_device_any,
        mesh=mesh,
        in_specs=(
            P("fsdp", "ctx", None),
            P("fsdp", "ctx", None),
            P("fsdp"),
            P(),
            P("fsdp", None),
            P("fsdp"),
            P("fsdp"),
            P("fsdp", None),
            P("fsdp"),
            P("fsdp"),
            P("fsdp"),
            P("fsdp", None),
            P("fsdp"),
            P("fsdp", None),
            P("fsdp"),
            P("fsdp"),
            P("fsdp"),
        ),
        out_specs=(
            P("fsdp", "ctx", None),
            P("fsdp", "ctx", None),
            P("fsdp", None),
            P("fsdp"),
            P("fsdp"),
            P("fsdp", None),
            P("fsdp"),
            P("fsdp"),
            P("fsdp"),
            P("fsdp", None),
            P("fsdp"),
            P("fsdp", None),
            P("fsdp"),
            P("fsdp"),
            P("fsdp"),
        ),
        check_vma=False,
    )
```

```python
import functools
import math

import jax
import jax.numpy as jnp
from jax import lax
from jax.experimental import pallas as pl
from jax.experimental.pallas import tpu as pltpu
from jax.sharding import PartitionSpec as P

HEADS = 12
HEAD_DIM = 64
NMEM = 10
BLK = 128


eps = 1e-12
neg_big = -1e30


def layer_norm(value, gain, shift):
    mean = jnp.mean(value, axis=-1, keepdims=True)
    centred = value - mean
    variance = jnp.mean(centred * centred, axis=-1, keepdims=True)
    return centred * lax.rsqrt(variance + eps) * gain + shift


def norm_back(value, gain, grad):
    mean = jnp.mean(value, axis=-1, keepdims=True)
    centred = value - mean
    scale = lax.rsqrt(jnp.mean(centred * centred, axis=-1, keepdims=True) + eps)
    unit = centred * scale
    scaled = grad * gain
    inner = (
        scaled
        - jnp.mean(scaled, axis=-1, keepdims=True)
        - unit * jnp.mean(scaled * unit, axis=-1, keepdims=True)
    )
    return (scale * inner, jnp.sum(grad * unit, axis=0), jnp.sum(grad, axis=0))


def block_width(count):
    return math.gcd(count, 512)


def places(pairing, start, count, half):
    rows = start + jnp.arange(count, dtype=jnp.int32)
    owners = rows // half
    spots = jnp.arange(pairing.shape[0], dtype=jnp.int32)
    picked = jnp.sum(jnp.where(owners[:, None] == spots[None, :], pairing[None, :], 0), axis=1)
    return picked * half + rows % half


def allowed_pairs(query_place, key_place, length):
    before = (key_place[None, :] <= query_place[:, None]) | (key_place[None, :] < NMEM)
    return (key_place[None, :] < length) & before


def heads_of(value):
    return value.reshape(value.shape[0], HEADS, HEAD_DIM)


def forward_fold(query_heads, query_place, pairing, length, half):

    def fold(carry, piece, start):
        keys, values = piece
        count = keys.shape[0]
        width = block_width(count)
        key_place = places(pairing, start, count, half)

        def step(index, state):
            top, total, summed = state
            offset = index * width
            key_heads = heads_of(lax.dynamic_slice_in_dim(keys, offset, width, 0))
            value_heads = heads_of(lax.dynamic_slice_in_dim(values, offset, width, 0))
            mask = allowed_pairs(
                query_place, lax.dynamic_slice_in_dim(key_place, offset, width, 0), length
            )[None]
            scores = (
                jnp.einsum(
                    "qhd,khd->hqk", query_heads, key_heads, preferred_element_type=jnp.float32
                )
                * 0.125
            )
            scores = jnp.where(mask, scores, neg_big)
            new_top = jnp.maximum(top, jnp.max(scores, axis=2))
            shrink = jnp.exp(top - new_top)
            probs = jnp.where(mask, jnp.exp(scores - new_top[:, :, None]), 0.0)
            total = total * shrink + jnp.sum(probs, axis=2)
            update = jnp.einsum(
                "hqk,khd->qhd",
                probs.astype(jnp.bfloat16),
                value_heads,
                preferred_element_type=jnp.float32,
            )
            summed = summed * jnp.transpose(shrink)[:, :, None] + update
            return (new_top, total, summed)

        return lax.fori_loop(0, count // width, step, carry)

    return fold


def query_grad_fold(query_heads, grad_heads, top_sum, delta, query_place, pairing, length, half):

    def fold(carry, piece, start):
        keys, values = piece
        count = keys.shape[0]
        width = block_width(count)
        key_place = places(pairing, start, count, half)

        def step(index, summed):
            offset = index * width
            key_heads = heads_of(lax.dynamic_slice_in_dim(keys, offset, width, 0))
            value_heads = heads_of(lax.dynamic_slice_in_dim(values, offset, width, 0))
            mask = allowed_pairs(
                query_place, lax.dynamic_slice_in_dim(key_place, offset, width, 0), length
            )[None]
            scores = (
                jnp.einsum(
                    "qhd,khd->hqk", query_heads, key_heads, preferred_element_type=jnp.float32
                )
                * 0.125
            )
            probs = jnp.where(mask, jnp.exp(scores - top_sum[:, :, None]), 0.0)
            prob_grad = jnp.einsum(
                "qhd,khd->hqk", grad_heads, value_heads, preferred_element_type=jnp.float32
            )
            score_grad = (probs * (prob_grad - delta[:, :, None])).astype(jnp.bfloat16)
            return (
                summed
                + jnp.einsum(
                    "hqk,khd->qhd", score_grad, key_heads, preferred_element_type=jnp.float32
                )
                * 0.125
            )

        return lax.fori_loop(0, count // width, step, carry)

    return fold


def key_terms(
    key_heads, value_heads, key_place, query_heads, grad_heads, top_sum, delta, query_place, length
):
    scores = (
        jnp.einsum("qhd,khd->hqk", query_heads, key_heads, preferred_element_type=jnp.float32)
        * 0.125
    )
    mask = allowed_pairs(query_place, key_place, length)[None]
    probs = jnp.where(mask, jnp.exp(scores - top_sum[:, :, None]), 0.0)
    prob_grad = jnp.einsum(
        "qhd,khd->hqk", grad_heads, value_heads, preferred_element_type=jnp.float32
    )
    score_grad = (probs * (prob_grad - delta[:, :, None])).astype(jnp.bfloat16)
    value_grad = jnp.einsum(
        "hqk,qhd->khd", probs.astype(jnp.bfloat16), grad_heads, preferred_element_type=jnp.float32
    )
    key_grad = (
        jnp.einsum("hqk,qhd->khd", score_grad, query_heads, preferred_element_type=jnp.float32)
        * 0.125
    )
    return (key_grad, value_grad)


def on_device_any(
    tokens,
    cotangent,
    lengths,
    pairing,
    w_qkv,
    bias_q,
    bias_v,
    w_out,
    bias_out,
    ln1_gain,
    ln1_bias,
    w_in,
    bias_in,
    w_back,
    bias_back,
    ln2_gain,
    ln2_bias,
):
    gathered = (
        lax.all_gather(w_qkv, "fsdp", axis=0, tiled=True),
        lax.all_gather(bias_q, "fsdp", axis=0, tiled=True),
        lax.all_gather(bias_v, "fsdp", axis=0, tiled=True),
        lax.all_gather(w_out, "fsdp", axis=0, tiled=True),
        lax.all_gather(bias_out, "fsdp", axis=0, tiled=True),
        lax.all_gather(ln1_gain, "fsdp", axis=0, tiled=True),
        lax.all_gather(ln1_bias, "fsdp", axis=0, tiled=True),
        lax.all_gather(w_in, "fsdp", axis=0, tiled=True),
        lax.all_gather(bias_in, "fsdp", axis=0, tiled=True),
        lax.all_gather(w_back, "fsdp", axis=0, tiled=True),
        lax.all_gather(bias_back, "fsdp", axis=0, tiled=True),
        lax.all_gather(ln2_gain, "fsdp", axis=0, tiled=True),
        lax.all_gather(ln2_bias, "fsdp", axis=0, tiled=True),
    )
    (
        qkv_all,
        query_bias,
        value_bias,
        out_all,
        out_bias,
        gain_one,
        shift_one,
        in_all,
        in_bias,
        back_all,
        back_bias,
        gain_two,
        shift_two,
    ) = gathered
    rows = tokens.shape[1]
    half = rows // 2
    width = tokens.shape[2]
    length = lengths[0]
    query_place = places(pairing, lax.axis_index("ctx") * rows, rows, half)
    valid = query_place < length
    inputs = tokens[0]
    proj = jnp.dot(inputs, qkv_all, preferred_element_type=jnp.float32)
    queries = (proj[:, :width] + query_bias.astype(jnp.float32)).astype(jnp.bfloat16)
    keys = proj[:, width : 2 * width].astype(jnp.bfloat16)
    values = (proj[:, 2 * width :] + value_bias.astype(jnp.float32)).astype(jnp.bfloat16)
    query_heads = heads_of(queries)
    start_state = (
        jnp.full((HEADS, rows), neg_big, jnp.float32),
        jnp.zeros((HEADS, rows), jnp.float32),
        jnp.zeros((rows, HEADS, HEAD_DIM), jnp.float32),
    )
    fold = forward_fold(query_heads, query_place, pairing, length, half)
    top, total, summed = fold(
        start_state,
        (
            lax.all_gather(keys, "ctx", axis=0, tiled=True),
            lax.all_gather(values, "ctx", axis=0, tiled=True),
        ),
        jnp.int32(0),
    )
    top_sum = top + jnp.log(total)
    attended = (summed / jnp.transpose(total)[:, :, None]).reshape(rows, width)
    attended_low = attended.astype(jnp.bfloat16)
    resid_one = (
        inputs.astype(jnp.float32)
        + jnp.dot(attended_low, out_all, preferred_element_type=jnp.float32)
        + out_bias.astype(jnp.float32)
    )
    hidden = layer_norm(resid_one, gain_one.astype(jnp.float32), shift_one.astype(jnp.float32))
    hidden_low = hidden.astype(jnp.bfloat16)
    upper = jnp.dot(hidden_low, in_all, preferred_element_type=jnp.float32) + in_bias.astype(
        jnp.float32
    )
    active, gelu_back = jax.vjp(lambda value: jax.nn.gelu(value, approximate=False), upper)
    active_low = active.astype(jnp.bfloat16)
    resid_two = (
        hidden
        + jnp.dot(active_low, back_all, preferred_element_type=jnp.float32)
        + back_bias.astype(jnp.float32)
    )
    normed = layer_norm(resid_two, gain_two.astype(jnp.float32), shift_two.astype(jnp.float32))
    output = jnp.where(valid[:, None], normed, 0.0)
    qkv_back, out_back, gain_one_back, in_back, back_back, gain_two_back = (
        qkv_all,
        out_all,
        gain_one,
        in_all,
        back_all,
        gain_two,
    )
    grad_y = jnp.where(valid[:, None], cotangent[0].astype(jnp.float32), 0.0)
    grad_resid_two, gain_two_grad, shift_two_grad = norm_back(
        resid_two, gain_two_back.astype(jnp.float32), grad_y
    )
    grad_mixed = grad_resid_two.astype(jnp.bfloat16)
    back_grad = jnp.einsum("tf,td->fd", active_low, grad_mixed, preferred_element_type=jnp.float32)
    back_bias_grad = jnp.sum(grad_mixed.astype(jnp.float32), axis=0)
    grad_active = jnp.einsum("td,fd->tf", grad_mixed, back_back, preferred_element_type=jnp.float32)
    (grad_upper,) = gelu_back(grad_active)
    grad_upper_low = grad_upper.astype(jnp.bfloat16)
    in_grad = jnp.einsum(
        "td,tf->df", hidden_low, grad_upper_low, preferred_element_type=jnp.float32
    )
    in_bias_grad = jnp.sum(grad_upper_low.astype(jnp.float32), axis=0)
    grad_hidden = grad_resid_two + jnp.einsum(
        "tf,df->td", grad_upper_low, in_back, preferred_element_type=jnp.float32
    )
    grad_resid_one, gain_one_grad, shift_one_grad = norm_back(
        resid_one, gain_one_back.astype(jnp.float32), grad_hidden
    )
    grad_branch = grad_resid_one.astype(jnp.bfloat16)
    out_grad = jnp.einsum(
        "tc,td->cd", attended_low, grad_branch, preferred_element_type=jnp.float32
    )
    out_bias_grad = jnp.sum(grad_branch.astype(jnp.float32), axis=0)
    grad_attended = jnp.einsum(
        "td,cd->tc", grad_branch, out_back, preferred_element_type=jnp.float32
    ).astype(jnp.bfloat16)
    grad_heads = heads_of(grad_attended)
    delta = jnp.transpose(jnp.sum(grad_heads.astype(jnp.float32) * heads_of(attended), axis=2))
    query_fold = query_grad_fold(
        query_heads, grad_heads, top_sum, delta, query_place, pairing, length, half
    )
    empty_heads = jnp.zeros((rows, HEADS, HEAD_DIM), jnp.float32)
    query_grad = query_fold(
        empty_heads,
        (
            lax.all_gather(keys, "ctx", axis=0, tiled=True),
            lax.all_gather(values, "ctx", axis=0, tiled=True),
        ),
        jnp.int32(0),
    )
    stats = jnp.concatenate([jnp.transpose(top_sum), jnp.transpose(delta)], axis=1)
    stats_all = lax.all_gather(stats, "ctx", axis=0, tiled=True)
    key_heads = heads_of(keys)
    value_heads = heads_of(values)
    query_in = lax.all_gather(queries, "ctx", axis=0, tiled=True)
    grad_in = lax.all_gather(grad_attended, "ctx", axis=0, tiled=True)
    count = query_in.shape[0]
    span = block_width(count)
    place_in = places(pairing, jnp.int32(0), count, half)

    def step(index, state):
        offset = index * span
        query_block = heads_of(lax.dynamic_slice_in_dim(query_in, offset, span, 0))
        grad_block = heads_of(lax.dynamic_slice_in_dim(grad_in, offset, span, 0))
        stats_block = lax.dynamic_slice_in_dim(stats_all, offset, span, 0)
        place_block = lax.dynamic_slice_in_dim(place_in, offset, span, 0)
        key_part, value_part = key_terms(
            key_heads,
            value_heads,
            query_place,
            query_block,
            grad_block,
            jnp.transpose(stats_block[:, :HEADS]),
            jnp.transpose(stats_block[:, HEADS:]),
            place_block,
            length,
        )
        return (state[0] + key_part, state[1] + value_part)

    key_sum, value_sum = lax.fori_loop(0, count // span, step, (empty_heads, empty_heads))
    key_grad = key_sum.reshape(rows, width)
    value_grad = value_sum.reshape(rows, width)
    grad_proj = jnp.concatenate(
        [
            query_grad.reshape(rows, width).astype(jnp.bfloat16),
            key_grad.astype(jnp.bfloat16),
            value_grad.astype(jnp.bfloat16),
        ],
        axis=1,
    )
    qkv_grad = jnp.einsum("td,tf->df", inputs, grad_proj, preferred_element_type=jnp.float32)
    query_bias_grad = jnp.sum(grad_proj[:, :width].astype(jnp.float32), axis=0)
    value_bias_grad = jnp.sum(grad_proj[:, 2 * width :].astype(jnp.float32), axis=0)
    token_grad = grad_resid_one + jnp.einsum(
        "tf,df->td", grad_proj, qkv_back, preferred_element_type=jnp.float32
    )
    grads = (
        qkv_grad,
        query_bias_grad,
        value_bias_grad,
        out_grad,
        out_bias_grad,
        gain_one_grad,
        shift_one_grad,
        in_grad,
        in_bias_grad,
        back_grad,
        back_bias_grad,
        gain_two_grad,
        shift_two_grad,
    )
    shards = (
        lax.psum_scatter(
            grads[0].astype(jnp.bfloat16), "fsdp", scatter_dimension=0, tiled=True
        ).astype(jnp.float32),
        lax.psum_scatter(
            grads[1].astype(jnp.bfloat16), "fsdp", scatter_dimension=0, tiled=True
        ).astype(jnp.float32),
        lax.psum_scatter(
            grads[2].astype(jnp.bfloat16), "fsdp", scatter_dimension=0, tiled=True
        ).astype(jnp.float32),
        lax.psum_scatter(
            grads[3].astype(jnp.bfloat16), "fsdp", scatter_dimension=0, tiled=True
        ).astype(jnp.float32),
        lax.psum_scatter(
            grads[4].astype(jnp.bfloat16), "fsdp", scatter_dimension=0, tiled=True
        ).astype(jnp.float32),
        lax.psum_scatter(
            grads[5].astype(jnp.bfloat16), "fsdp", scatter_dimension=0, tiled=True
        ).astype(jnp.float32),
        lax.psum_scatter(
            grads[6].astype(jnp.bfloat16), "fsdp", scatter_dimension=0, tiled=True
        ).astype(jnp.float32),
        lax.psum_scatter(
            grads[7].astype(jnp.bfloat16), "fsdp", scatter_dimension=0, tiled=True
        ).astype(jnp.float32),
        lax.psum_scatter(
            grads[8].astype(jnp.bfloat16), "fsdp", scatter_dimension=0, tiled=True
        ).astype(jnp.float32),
        lax.psum_scatter(
            grads[9].astype(jnp.bfloat16), "fsdp", scatter_dimension=0, tiled=True
        ).astype(jnp.float32),
        lax.psum_scatter(
            grads[10].astype(jnp.bfloat16), "fsdp", scatter_dimension=0, tiled=True
        ).astype(jnp.float32),
        lax.psum_scatter(
            grads[11].astype(jnp.bfloat16), "fsdp", scatter_dimension=0, tiled=True
        ).astype(jnp.float32),
        lax.psum_scatter(
            grads[12].astype(jnp.bfloat16), "fsdp", scatter_dimension=0, tiled=True
        ).astype(jnp.float32),
    )
    totals = (
        lax.psum(shards[0].astype(jnp.bfloat16), "ctx").astype(jnp.float32),
        lax.psum(shards[1].astype(jnp.bfloat16), "ctx").astype(jnp.float32),
        lax.psum(shards[2].astype(jnp.bfloat16), "ctx").astype(jnp.float32),
        lax.psum(shards[3].astype(jnp.bfloat16), "ctx").astype(jnp.float32),
        lax.psum(shards[4].astype(jnp.bfloat16), "ctx").astype(jnp.float32),
        lax.psum(shards[5].astype(jnp.bfloat16), "ctx").astype(jnp.float32),
        lax.psum(shards[6].astype(jnp.bfloat16), "ctx").astype(jnp.float32),
        lax.psum(shards[7].astype(jnp.bfloat16), "ctx").astype(jnp.float32),
        lax.psum(shards[8].astype(jnp.bfloat16), "ctx").astype(jnp.float32),
        lax.psum(shards[9].astype(jnp.bfloat16), "ctx").astype(jnp.float32),
        lax.psum(shards[10].astype(jnp.bfloat16), "ctx").astype(jnp.float32),
        lax.psum(shards[11].astype(jnp.bfloat16), "ctx").astype(jnp.float32),
        lax.psum(shards[12].astype(jnp.bfloat16), "ctx").astype(jnp.float32),
    )
    return (output[None], token_grad[None]) + tuple(totals)


def low_lanes(shape):
    return lax.broadcasted_iota(jnp.int32, shape, 1) < 64


def spot_of(pair_ref, place):
    found = jnp.int32(0)
    for s in range(pair_ref.shape[0]):
        found = jnp.where(pair_ref[s] == place, s, found)
    return found


def attend(c, length, spot, keep_ref, mix_ref, lse_ref, turned_ref):
    left = low_lanes((256, BLK))
    zero = jnp.zeros((), jnp.bfloat16)
    keys = 256 * (c + 1)
    own = keep_ref[0, 2 * c : 2 * c + 2].reshape(256, BLK)
    shared = keep_ref[0, 2 * c + spot]
    query = jnp.concatenate(
        [jnp.where(left, own, zero), jnp.where(left[:BLK], zero, shared)], axis=0
    ) * jnp.bfloat16(0.125)
    key = keep_ref[1, : 2 * c + 2].reshape(keys, BLK)
    value = keep_ref[2, : 2 * c + 2].reshape(keys, BLK)
    scores = mask_scores(dot_nt(key, query), c, spot, length, 0, True)
    top = jnp.max(scores, axis=0, keepdims=True)
    probs = jnp.exp(scores - top)
    total = jnp.sum(probs, axis=0, keepdims=True)
    summed = lax.dot_general(
        value, probs.astype(jnp.bfloat16), (((0,), (0,)), ((), ())),
        preferred_element_type=jnp.float32,
    ) / total
    lse_ref[c] = top + jnp.log(total)
    part = summed[64:, 256:]
    none = jnp.zeros_like(part)
    first = jnp.where(spot == 0, part, none)
    second = jnp.where(spot == 0, none, part)
    mixed = jnp.concatenate([summed[:64, :256], jnp.concatenate([first, second], axis=1)], axis=0)
    mix_ref[c] = mixed
    turned_ref[2 * c : 2 * c + 2] = (
        jnp.transpose(mixed).astype(jnp.bfloat16).reshape(2, BLK, BLK)
    )


def mask_scores(scores, c, spot, length, start, edged):
    keys, width = scores.shape
    row = start + lax.broadcasted_iota(jnp.int32, (keys, width), 0)
    scores = jnp.where(row < length, scores, neg_big)
    if not edged:
        return scores
    edge = 256 * c
    lane = lax.broadcasted_iota(jnp.int32, (256, width), 1)
    query_place = edge + jnp.where(lane < 256, lane, lane - 256 + spot * BLK)
    key_place = edge + lax.broadcasted_iota(jnp.int32, (256, width), 0)
    seen = key_place <= query_place
    if c == 0:
        seen = seen | (key_place < NMEM)
    tail = jnp.where(seen, scores[keys - 256 :], neg_big)
    if keys == 256:
        return tail
    return jnp.concatenate([scores[: keys - 256], tail], axis=0)


def attend_back(
    c, length, spot, keep_ref, g_ref, mix_ref, lse_ref, q_sum, k_sum, v_sum
):
    zero = jnp.zeros((), jnp.bfloat16)
    left = low_lanes((256, BLK))
    left_half = left[:BLK]
    own = keep_ref[0, 2 * c : 2 * c + 2].reshape(256, BLK)
    shared = keep_ref[0, 2 * c + spot]
    query = jnp.concatenate(
        [jnp.where(left, own, zero), jnp.where(left_half, zero, shared)], axis=0
    ) * jnp.bfloat16(0.125)
    g_own = g_ref[2 * c : 2 * c + 2].reshape(256, BLK)
    g_shared = g_ref[2 * c + spot]
    grad = jnp.concatenate(
        [jnp.where(left, g_own, zero), jnp.where(left_half, zero, g_shared)], axis=0
    )
    turned = jnp.transpose(g_own.astype(jnp.float32)) * mix_ref[c]
    delta_own = jnp.sum(turned[:64], axis=0, keepdims=True)
    delta_pair = jnp.sum(turned[64:], axis=0, keepdims=True)
    delta = jnp.concatenate(
        [delta_own, jnp.where(spot == 0, delta_pair[:, :BLK], delta_pair[:, BLK:])], axis=1
    )
    lse = lse_ref[c]
    q_grad = jnp.zeros((384, BLK), jnp.float32)
    last = 2 * c + 2
    step = 8
    for low_block in range(0, last, step):
        high_block = min(low_block + step, last)
        cut = slice(low_block, high_block)
        count = high_block - low_block
        key = keep_ref[1, cut].reshape(count * BLK, BLK)
        value = keep_ref[2, cut].reshape(count * BLK, BLK)
        scores = mask_scores(
            dot_nt(key, query), c, spot, length, low_block * BLK, high_block == last
        )
        probs = jnp.exp(scores - lse)
        score_grad = (probs * (dot_nt(value, grad) - delta)).astype(jnp.bfloat16)
        v_part = dot_nn(probs.astype(jnp.bfloat16), grad)
        k_part = dot_nn(score_grad, query)
        v_sum[cut] += v_part.reshape(count, BLK, BLK)
        k_sum[cut] += k_part.reshape(count, BLK, BLK)
        q_grad = q_grad + lax.dot_general(
            score_grad, key, (((0,), (0,)), ((), ())), preferred_element_type=jnp.float32
        )
    q_grad = q_grad * 0.125
    part = q_grad[256:]
    none = jnp.zeros_like(part)
    first = jnp.where(spot == 0, part, none)
    second = jnp.where(spot == 0, none, part)
    q_sum[2 * c : 2 * c + 2] = jnp.where(
        left, q_grad[:256], jnp.concatenate([first, second], axis=0)
    ).reshape(2, BLK, BLK)


def smem():
    return pl.BlockSpec(memory_space=pltpu.SMEM)


def vmem():
    return pl.BlockSpec(memory_space=pltpu.VMEM)


MESH = pl.DeviceIdType.MESH


def remote(src, dst, sems, at, peer):
    return pltpu.make_async_remote_copy(
        src_ref=src, dst_ref=dst, send_sem=sems.at[(0,) + at], recv_sem=sems.at[(1,) + at],
        device_id=peer, device_id_type=MESH,
    )


def hail(peers):
    barrier = pltpu.get_barrier_semaphore()
    for peer in peers:
        pl.semaphore_signal(barrier, inc=1, device_id=peer, device_id_type=MESH)


def greet(peers):
    hail(peers)
    pl.semaphore_wait(pltpu.get_barrier_semaphore(), len(peers))


def ring_peers(n):
    me = lax.axis_index("ctx")
    return [{"ctx": lax.rem(me + k, n)} for k in range(1, n)]


def two(block):
    return pl.ds(2 * block, 2)


def one(block):
    return block


def exchange_copies(n, in_ref, out_ref, sems, at=two):
    me = lax.axis_index("ctx")
    copies = []
    for k in range(1, n):
        peer = lax.rem(me + k, n)
        copies.append(
            remote(in_ref.at[at(peer)], out_ref.at[at(me)], sems, (k,), {"ctx": peer})
        )
    return copies


def own_copy(in_ref, out_ref, sem, at=two):
    me = lax.axis_index("ctx")
    return pltpu.make_async_copy(in_ref.at[at(me)], out_ref.at[at(me)], sem)


def beside(first, second, axis):
    return jnp.concatenate([first, second], axis=axis)


def fold(first, second, shared):
    return beside(
        beside(first[:, :HEAD_DIM], second[:, :HEAD_DIM], 1),
        beside(shared[:HEAD_DIM], shared[HEAD_DIM:], 1),
        0,
    )


def fold_pair(value, spot, lead):
    first, second = value[:BLK], value[BLK:]
    return fold(
        first, second, jnp.where(lead == spot, first[:, HEAD_DIM:], second[:, HEAD_DIM:])
    )


def unfold_shared(message):
    return beside(message[BLK:, :HEAD_DIM], message[BLK:, HEAD_DIM:], 0)


def unfold_block(message, later):
    own = jnp.where(later == 0, message[:BLK, :HEAD_DIM], message[:BLK, HEAD_DIM:])
    return beside(own, unfold_shared(message), 1)


def join_folded(messages, lead):
    pieces = []
    for group in range(HEADS // 3):
        pair = [messages(2 * group), messages(2 * group + 1)]
        for message in pair:
            pieces.append(beside(message[:BLK, :HEAD_DIM], message[:BLK, HEAD_DIM:], 0))
        even, odd = [unfold_shared(message) for message in pair]
        pieces.append(
            beside(jnp.where(lead == 0, even, odd), jnp.where(lead == 0, odd, even), 0)
        )
    return jnp.concatenate(pieces, axis=1)


def both(ref, peer):
    value = ref[2 * peer : 2 * peer + 2]
    return value.reshape(-1, value.shape[2])


def join_pairs(pairs):
    pieces = []
    for group in range(HEADS // 3):
        first, second = pairs(2 * group), pairs(2 * group + 1)
        shared = first[:, HEAD_DIM:].astype(jnp.float32) + second[:, HEAD_DIM:].astype(jnp.float32)
        pieces += [first[:, :HEAD_DIM], second[:, :HEAD_DIM], shared.astype(jnp.bfloat16)]
    return jnp.concatenate(pieces, axis=1)


def pair_of(value, peer):
    own = 3 * (peer // 2) + peer % 2
    shared = 3 * (peer // 2) + 2
    cut = lambda head: value[:, head * HEAD_DIM : (head + 1) * HEAD_DIM]
    return jnp.concatenate([cut(own), cut(shared)], axis=1)


def dot_nn(a, b):
    return jnp.dot(a, b, preferred_element_type=jnp.float32)


def dot_nt(a, b):
    return lax.dot_general(a, b, (((1,), (1,)), ((), ())), preferred_element_type=jnp.float32)


def column_sum(value):
    return jnp.sum(value, axis=0, keepdims=True)


def unit_of(value):
    mean = jnp.mean(value, axis=-1, keepdims=True)
    centred = value - mean
    scale = lax.rsqrt(jnp.mean(centred * centred, axis=-1, keepdims=True) + eps)
    return centred * scale, scale


def unit_back(unit, scale, scaled):
    return scale * (
        scaled
        - jnp.mean(scaled, axis=-1, keepdims=True)
        - unit * jnp.mean(scaled * unit, axis=-1, keepdims=True)
    )


(ROW_BQ, ROW_BV, ROW_BO, ROW_G1, ROW_S1, ROW_BB, ROW_G2, ROW_S2, ROW_BI) = range(9)


def gather_copies(src, full, sems, index):
    fsdp = lax.axis_index("fsdp")
    x, core = fsdp // 2, lax.rem(fsdp, 2)
    sibling, across = {"fsdp": 2 * x + 1 - core}, {"fsdp": 2 * (1 - x) + core}
    other = 2 * (1 - x) + core
    return (
        remote(src, full.at[fsdp], sems, (index, 0), across),
        remote(src, full.at[fsdp], sems, (index, 1), sibling),
        remote(full.at[other], full.at[other], sems, (index, 2), sibling),
    )


def chip_peers():
    fsdp = lax.axis_index("fsdp")
    x, core = fsdp // 2, lax.rem(fsdp, 2)
    return [{"fsdp": 2 * x + 1 - core}, {"fsdp": 2 * (1 - x) + core}]


def split_gather(src, full, sems, parts):
    ctx, fsdp = lax.axis_index("ctx"), lax.axis_index("fsdp")
    z, y = ctx // 2, lax.rem(ctx, 2)
    x, core = fsdp // 2, lax.rem(fsdp, 2)
    sibling, across = {"fsdp": 2 * x + 1 - core}, {"fsdp": 2 * (1 - x) + core}
    over_y = {"ctx": 2 * z + 1 - y}
    other = 2 * (1 - x) + core
    count = src.shape[0] // 2
    here = pl.ds(pl.multiple_of(y * count, count), count)
    there = pl.ds(pl.multiple_of((1 - y) * count, count), count)
    cross, side, on, off, whole = [], [], [], [], []
    for p in range(parts):
        width = src.shape[1] // parts
        cols = slice(p * width, (p + 1) * width)
        moved = full.at[other, here, cols]
        late = full.at[other, there, cols]
        cross.append(remote(src.at[here, cols], full.at[fsdp, here, cols], sems, (0, p), across))
        side.append(remote(moved, moved, sems, (1, p), over_y))
        on.append(remote(moved, moved, sems, (2, p), sibling))
        off.append(remote(late, late, sems, (3, p), sibling))
        whole.append(remote(src.at[:, cols], full.at[fsdp, :, cols], sems, (4, p), sibling))
    return cross, side, on, off, whole


def passed(split, p):
    cross, side, on, off, whole = split
    cross[p].wait_recv()
    side[p].start()
    on[p].start()


def handed(split, p):
    cross, side, on, off, whole = split
    side[p].wait_recv()
    off[p].start()


def gathered(split, p):
    cross, side, on, off, whole = split
    for copies in (whole, on, off):
        copies[p].wait_recv()


def front_kernel(
    n, pair_ref, len_ref, *refs
):
    vectors, refs = refs[:9], refs[9:]
    (
        tokens_ref, cot_ref, qkv_src, out_src, in_src, back_src,
        output_ref, grad_ref, left_ref, right_ref, resid_ref, sums_ref,
        keep_ref, mix_ref, lse_ref, qkv_ref,
        small_out, small, rows_ref, token_buf, cot, w_qkv, w_out, w_in, w_back, send_folded, send,
        packed_q, packed_k, packed_v, keep, mix,
        lse, turned, mixed_out, mixed_in, active, slope, output, grad_out, left, right, resid, sums,
        small_sem, qkv_sem, in_split_sem, back_split_sem, gather_sem, send_q, send_k, send_v, in_sem, own_sem, load_sem, ship_sem,
    ) = refs
    send_sem = (send_q, send_k, send_v)
    packed = (packed_q, packed_k, packed_v)
    low, wide = jnp.bfloat16, jnp.float32
    ctx, fsdp = lax.axis_index("ctx"), lax.axis_index("fsdp")
    x, core = fsdp // 2, lax.rem(fsdp, 2)
    spot = lax.rem(ctx, 2)
    lead = lax.rem(pair_ref[2 * ctx], 2)
    width = token_buf.shape[1]
    count = in_src.shape[1] // width
    loads = [
        pltpu.make_async_copy(src, dst, load_sem.at[i])
        for i, (src, dst) in enumerate(
            [
                (tokens_ref, token_buf),
                (cot_ref, cot),
                (qkv_src, w_qkv.at[fsdp]),
                (out_src, w_out.at[fsdp]),
                (in_src, w_in.at[fsdp]),
                (back_src, w_back.at[fsdp]),
            ]
        )
    ]
    cot_load = loads[1]
    peers = ring_peers(n) + chip_peers()
    hail(peers)
    for cp in loads[:3]:
        cp.start()
    part = width // 4
    small_out[...] = jnp.zeros_like(small_out)
    for i in range(8):
        small_out[i : i + 1] = vectors[i][...].astype(wide).reshape(1, part)
    inner_bias = vectors[8][...].astype(wide).reshape(1, -1)
    for j in range(4):
        small_out[8 + j : 9 + j] = inner_bias[:, j * part : (j + 1) * part]
    pl.semaphore_wait(pltpu.get_barrier_semaphore(), len(peers))
    smalls = gather_copies(small_out, small, small_sem, 0)
    qkv_split = split_gather(qkv_src, w_qkv, qkv_sem, 6)
    in_split = split_gather(in_src, w_in, in_split_sem, count)
    back_split = split_gather(back_src, w_back, back_split_sem, 2)
    splits = (qkv_split, in_split, back_split)
    qkv_split[0][0].start()
    for step in (0, 1):
        smalls[step].start()
    for cp in qkv_split[0][1:] + qkv_split[4]:
        cp.start()
    for cp in loads[3:]:
        cp.start()
    shards = gather_copies(out_src, w_out, gather_sem, 0)
    small[fsdp] = small_out[...]
    smalls[0].wait_recv()
    smalls[2].start()
    passed(qkv_split, 0)
    passed(qkv_split, 1)
    loads[0].wait()
    tokens = token_buf[...]
    left[0] = jnp.transpose(tokens).reshape(4, -1, 2 * BLK)
    smalls[1].wait_recv()
    smalls[2].wait_recv()
    for f in range(4):
        cols = slice(f * part, (f + 1) * part)
        rows_ref[:8, cols] = small[f, :8]
        for j in range(4):
            rows_ref[ROW_BI + f : ROW_BI + f + 1, j * part : (j + 1) * part] = small[
                f, 8 + j : 9 + j
            ]
    rows_ref[12:] = jnp.zeros_like(rows_ref[12:])
    row = lambda i: rows_ref[i : i + 1, :]
    handed(qkv_split, 0)
    passed(qkv_split, 2)
    handed(qkv_split, 1)
    for p in range(3, 6):
        passed(qkv_split, p)
    for cp in shards[:2]:
        cp.start()
    for split in (in_split, back_split):
        for cp in split[0] + split[4]:
            cp.start()
    loads[2].wait()
    sends = []
    for p, bias in enumerate((ROW_BQ, None, ROW_BV)):
        for q in (2 * p, 2 * p + 1):
            if p:
                handed(qkv_split, q)
            gathered(qkv_split, q)
        value = dot_nn(tokens, w_qkv[:, :, p * width : (p + 1) * width].reshape(width, width))
        if bias is not None:
            value = value + row(bias)
        value = value.astype(low)
        for peer in range(n):
            both_heads = pair_of(value, peer)
            if p:
                send[p - 1, 2 * peer : 2 * peer + 2] = both_heads.reshape(2, BLK, BLK)
            else:
                send_folded[peer] = fold_pair(both_heads, peer % 2, lead)
        source, at = (send.at[p - 1], two) if p else (send_folded, one)
        copies = exchange_copies(n, source, packed[p], send_sem[p], at)
        copies.append(own_copy(source, packed[p], own_sem.at[2 + p], at))
        for cp in copies:
            cp.start()
        sends.append(copies)
    shipped = []

    def ship(src, dst):
        cp = pltpu.make_async_copy(src, dst, ship_sem.at[len(shipped)])
        cp.start()
        shipped.append(cp)

    ship(w_qkv, qkv_ref)
    spots = lax.broadcasted_iota(jnp.int32, (2 * BLK, 1), 0)
    place = jnp.where(
        spots < BLK,
        pair_ref[2 * ctx] * BLK + spots,
        pair_ref[2 * ctx + 1] * BLK + spots - BLK,
    )
    valid = place < len_ref[0]
    shards[0].wait_recv()
    shards[2].start()
    for p in range(count):
        passed(in_split, p)
        if p:
            handed(in_split, p - 1)
    passed(back_split, 0)
    handed(in_split, count - 1)
    spots_of = [spot_of(pair_ref, b) for b in range(2 * n)]
    for p in range(3):
        sends[p][-1].wait()
        for cp in sends[p][:-1]:
            cp.wait_recv()
        for b in range(2 * n):
            if p:
                keep[p, b] = packed[p][spots_of[b]]
            else:
                keep[p, b] = unfold_block(
                    packed[p][lax.div(spots_of[b], 2)], lax.rem(spots_of[b], 2)
                )

    ship(keep, keep_ref)
    for c in range(n):
        attend(c, len_ref[0], spot, keep, mix, lse, turned)
        if c == 0:
            passed(back_split, 1)
    for peer in range(n):
        first, second = turned[pair_ref[2 * peer]], turned[pair_ref[2 * peer + 1]]
        mixed_out[peer] = fold(first, second, first[:, HEAD_DIM:] + second[:, HEAD_DIM:])
    copies = exchange_copies(n, mixed_out, mixed_in, in_sem, one)
    for cp in copies:
        cp.start()
    own_mixed = own_copy(mixed_out, mixed_in, own_sem.at[1], one)
    own_mixed.start()
    ship(mix, mix_ref)
    ship(lse, lse_ref)
    sums[...] = jnp.zeros_like(sums)
    for cp in loads[3:]:
        cp.wait()
    for p in range(2):
        handed(back_split, p)
    shards[1].wait_recv()
    shards[2].wait_recv()
    for p in range(count):
        gathered(in_split, p)
    own_mixed.wait()
    for cp in copies:
        cp.wait_recv()
    attended = join_folded(lambda peer: mixed_in[peer], lead)
    resid_one = (
        tokens.astype(wide)
        + dot_nn(attended, w_out[...].reshape(width, width))
        + row(ROW_BO)
    )
    unit_one, scale_one = unit_of(resid_one)
    hidden = unit_one * row(ROW_G1) + row(ROW_S1)
    hidden_low = hidden.astype(low)
    resid_two = hidden + row(ROW_BB)
    cut = lambda t: pl.ds(pl.multiple_of(t * width, width), width)
    order = [fsdp, 2 * x + 1 - core, 2 * (1 - x) + core, 2 * (1 - x) + 1 - core]
    for step, t in enumerate(order):
        bias = rows_ref[pl.ds(ROW_BI + t, 1), :]
        upper = dot_nn(hidden_low, w_in[:, :, cut(t)].reshape(width, width)) + bias
        share = 0.5 * (1.0 + lax.erf(upper * (0.5**0.5)))
        slope[t] = share + upper * (jnp.exp(-0.5 * upper * upper) * (2 * math.pi) ** -0.5)
        some = (upper * share).astype(low)
        active[t] = some
        if step == 0:
            gathered(back_split, 0)
            gathered(back_split, 1)
        resid_two = resid_two + dot_nn(some, w_back[t])
    unit_two, scale_two = unit_of(resid_two)
    output[...] = jnp.where(valid, unit_two * row(ROW_G2) + row(ROW_S2), 0.0)
    cot_load.wait()
    grad_y = jnp.where(valid, cot[...].astype(wide), 0.0)
    sums[ROW_G2 : ROW_G2 + 1, :] = column_sum(grad_y * unit_two)
    sums[ROW_S2 : ROW_S2 + 1, :] = column_sum(grad_y)
    grad_resid_two = unit_back(unit_two, scale_two, grad_y * row(ROW_G2))
    grad_mixed = grad_resid_two.astype(low)
    right[5] = grad_mixed
    sums[ROW_BB : ROW_BB + 1, :] = column_sum(grad_mixed.astype(wide))
    ship(output, output_ref)
    left[1] = jnp.transpose(attended).reshape(4, -1, 2 * BLK)
    left[2] = jnp.transpose(hidden_low).reshape(4, -1, 2 * BLK)
    for f in range(4):
        turned = jnp.transpose(active[f])
        for r in range(4):
            left[3 + r, f] = turned[r * width // 4 : (r + 1) * width // 4]
    ship(left, left_ref)
    grad_hidden = grad_resid_two
    for t in range(count):
        grad_upper = (dot_nt(grad_mixed, w_back[t]) * slope[t]).astype(low)
        right[1 + t] = grad_upper
        sums[ROW_BI + t : ROW_BI + t + 1, :] = column_sum(grad_upper.astype(wide))
        grad_hidden = grad_hidden + dot_nt(grad_upper, w_in[:, :, cut(t)].reshape(width, width))
    sums[ROW_G1 : ROW_G1 + 1, :] = column_sum(grad_hidden * unit_one)
    sums[ROW_S1 : ROW_S1 + 1, :] = column_sum(grad_hidden)
    grad_resid_one = unit_back(unit_one, scale_one, grad_hidden * row(ROW_G1))
    resid[...] = grad_resid_one
    grad_branch = grad_resid_one.astype(low)
    right[0] = grad_branch
    sums[ROW_BO : ROW_BO + 1, :] = column_sum(grad_branch.astype(wide))
    ship(resid, resid_ref)
    ship(right, right_ref)
    ship(sums, sums_ref)
    grad_attended = dot_nt(grad_branch, w_out[...].reshape(width, width)).astype(low)
    for peer in range(n):
        grad_out[peer] = fold_pair(pair_of(grad_attended, peer), peer % 2, lead)
    ship(grad_out, grad_ref)
    for cps in (smalls, shards, copies) + sum(splits, ()):
        for cp in cps:
            cp.wait_send()
    for cps in sends:
        for cp in cps[:-1]:
            cp.wait_send()
    for cp in shipped:
        cp.wait()


def front(pairing, lengths, vectors, tokens, cotangent, w_qkv, w_out, w_in, w_back, n, name):
    count, width = tokens.shape
    low, wide = jnp.bfloat16, jnp.float32
    dma = pltpu.SemaphoreType.DMA
    shape = jax.ShapeDtypeStruct
    hbm = pl.BlockSpec(memory_space=pltpu.HBM)
    vec = pltpu.VMEM((16, width // 4), wide)
    results = [
        ((count, width), wide),
        ((n, BLK + HEAD_DIM, BLK), low),
        ((7, 4, width // 4, count), low),
        ((6, count, width), low),
        ((count, width), wide),
        ((16, width), wide),
        ((3, 2 * n, BLK, BLK), low),
        ((n, BLK, 2 * BLK), wide),
        ((n, 1, 3 * BLK), wide),
        ((4,) + w_qkv.shape, low),
    ]
    output, grad, left, right, resid, sums, keep, mix, lse, qkv = [pltpu.VMEM(*r) for r in results]
    blocks = pltpu.VMEM((2 * n, BLK, BLK), low)
    return pl.pallas_call(
        functools.partial(front_kernel, n),
        out_shape=tuple(shape(*r) for r in results),
        in_specs=[smem(), smem()] + [vmem()] * 9 + [hbm] * 6,
        out_specs=(hbm,) * 10,
        scratch_shapes=[
            vec,
            pltpu.VMEM((4, 16, width // 4), wide),
            pltpu.VMEM((16, width), wide),
            pltpu.VMEM((count, width), low),
            pltpu.VMEM((count, width), low),
            qkv,
            pltpu.VMEM((4,) + w_out.shape, low),
            pltpu.VMEM((4,) + w_in.shape, low),
            pltpu.VMEM((4,) + w_back.shape, low),
            grad,
            pltpu.VMEM((2, 2 * n, BLK, BLK), low),
            grad,
            blocks,
            blocks,
            keep,
            mix,
            lse,
            blocks,
            grad,
            grad,
            pltpu.VMEM((4, count, width), low),
            pltpu.VMEM((4, count, width), wide),
            output,
            grad,
            left,
            right,
            resid,
            sums,
            dma((2, 1, 3)),
            dma((2, 5, 6)),
            dma((2, 5, 4)),
            dma((2, 5, 2)),
            dma((2, 1, 3)),
            dma((2, n)),
            dma((2, n)),
            dma((2, n)),
            dma((2, n)),
            dma((5,)),
            dma((6,)),
            dma((10,)),
        ],
        compiler_params=pltpu.CompilerParams(
            collective_id=name, has_side_effects=True, vmem_limit_bytes=62 << 20
        ),
        name="front",
    )(pairing, lengths, *vectors, tokens, cotangent, w_qkv, w_out, w_in, w_back)


PARTS = 12


def sum_sources(chunk):
    left = jnp.where(chunk < 4, 3 + chunk, jnp.where(chunk < 8, 2, jnp.where(chunk < 9, 1, 0)))
    right = jnp.where(
        chunk < 4, 8, jnp.where(chunk < 8, chunk, jnp.where(chunk < 9, 3, chunk - 9))
    )
    return left, right


STEPS = 65
PLAN = {
    "pair": {0: 0, 1: 1, 2: 2, 3: 3, 6: 4, 7: 5, 13: 6, 15: 7, 19: 8, 21: 9, 29: 10, 32: 11},
    "x": {3: 0, 4: 1, 5: 2, 7: 3, 12: 4, 13: 5, 14: 6, 18: 7, 23: 8, 30: 9, 36: 10, 41: 11},
    "y": {9: 0, 10: 1, 16: 2, 17: 3, 18: 4, 21: 5, 24: 6, 26: 7, 30: 8, 36: 9, 46: 10, 50: 11},
    "near": {11: 0, 19: 1, 20: 2, 24: 3, 25: 4, 28: 5, 32: 6, 38: 7, 42: 8, 44: 9, 49: 10, 57: 11},
    "far": {22: 0, 25: 1, 26: 2, 31: 3, 33: 4, 39: 5, 41: 6, 44: 7, 47: 8, 52: 9, 55: 10, 60: 11},
    "own": {27: 0, 29: 1, 30: 2, 37: 3, 40: 4, 45: 5, 49: 6, 50: 7, 53: 8, 57: 9, 58: 10, 61: 11},
    "wide": {30: 0, 31: 1, 34: 2, 43: 3, 48: 4, 50: 5, 51: 6, 56: 7, 57: 8, 59: 9, 61: 10, 62: 11},
    "last": {35: 0, 38: 1, 42: 2, 47: 3, 52: 4, 54: 5, 55: 6, 58: 7, 60: 8, 61: 9, 63: 10, 64: 11},
}
ATTEND_AT = (8, 9, 10)
JOIN_AT = (16, 24, 28)
SMALL_AT = (46, 49, 52, 61, 62, 64)
TOKEN_AT = 44


def planned(name, step):
    chunk = jnp.int32(-1)
    for at, which in PLAN[name].items():
        chunk = jnp.where(step == at, which, chunk)
    return chunk


def back_kernel(
    n, pair_ref, len_ref, grad_ref, keep_src, mix_src, lse_src, left_src, right_src,
    sums_src, resid_src, qkv_ref,
    total_out, token_out, small_dst,
    token_ref, small_out, keep_ref, mix_ref, lse_ref, left_ref, sums_ref, resid_ref, total_ref,
    grad_in, g_all, q_sum, k_sum, v_sum, folded_out, folded_in,
    blocks_out, blocks_in, w_qkv, right_all,
    pair_out, pair_in, x_out, x_in, y_out, y_in, y_keep, near_out, near_in, near_keep,
    far_out, far_in, far_keep, s_out, s_in,
    load_sem, ship_sem,
    grad_sem, block_q, block_k, block_v, own_sem, pair_sem, x_sem, y_sem, near_sem, far_sem,
    own_z_sem, wide_sem, last_sem, s_sem,
):
    block_sem = (block_q, block_k, block_v)
    low, wide = jnp.bfloat16, jnp.float32
    ctx = lax.axis_index("ctx")
    fsdp = lax.axis_index("fsdp")
    z, y = ctx // 2, lax.rem(ctx, 2)
    odd, upper = lax.rem(z, 2), z // 2
    x, core = fsdp // 2, lax.rem(fsdp, 2)
    sibling = {"fsdp": 2 * x + 1 - core}
    across = {"fsdp": 2 * (1 - x) + core}
    over_y = {"ctx": 2 * z + 1 - y}
    near = {"ctx": 2 * (2 * upper + 1 - odd) + y}
    far = {"ctx": 2 * (2 * (1 - upper) + odd) + y}
    mine = 2 * odd + upper
    loads = [
        pltpu.make_async_copy(src, dst, load_sem.at[i])
        for i, (src, dst) in enumerate(
            [
                (right_src, right_all.at[3:]),
                (left_src, left_ref),
                (keep_src, keep_ref),
                (mix_src, mix_ref),
                (lse_src, lse_ref),
                (sums_src, sums_ref),
                (resid_src, resid_ref),
            ]
        )
    ]
    for cp in loads:
        cp.start()
    greet(ring_peers(n) + [sibling, across])
    lead = lax.rem(pair_ref[2 * ctx], 2)
    grads = exchange_copies(n, grad_ref, grad_in, grad_sem, one)
    for cp in grads:
        cp.start()
    own_grad = own_copy(grad_ref, grad_in, own_sem.at[0], one)
    own_grad.start()
    load = pltpu.make_async_copy(qkv_ref, w_qkv, own_sem.at[1])
    load.start()
    blocks = [
        exchange_copies(n, folded_out, folded_in, block_sem[0], one)
    ] + [
        exchange_copies(n, blocks_out.at[p], blocks_in.at[p], block_sem[1 + p])
        for p in range(2)
    ]
    own = [own_copy(folded_out, folded_in, own_sem.at[2], one)] + [
        own_copy(blocks_out.at[p], blocks_in.at[p], own_sem.at[3 + p]) for p in range(2)
    ]
    k_sum[...] = jnp.zeros_like(k_sum)
    v_sum[...] = jnp.zeros_like(v_sum)
    chunks = keep_ref.shape[1] // 2

    def attend_some(first, last):
        for c in range(first, last):
            attend_back(
                c, len_ref[0], y, keep_ref, g_all, mix_ref, lse_ref, q_sum, k_sum, v_sum
            )

    def attend_step(t):
        @pl.when(t == ATTEND_AT[0])
        def _():
            own_grad.wait()
            for cp in loads[2:5]:
                cp.wait()
            for cp in grads:
                cp.wait_recv()
            for b in range(2 * chunks):
                found = spot_of(pair_ref, b)
                g_all[b] = unfold_block(grad_in[lax.div(found, 2)], lax.rem(found, 2))
            attend_some(0, chunks // 2)

        @pl.when(t == ATTEND_AT[1])
        def _():
            attend_some(chunks // 2, chunks - 2)

        @pl.when(t == ATTEND_AT[2])
        def _():
            attend_some(chunks - 2, chunks)
            for peer in range(n):
                first, second = q_sum[pair_ref[2 * peer]], q_sum[pair_ref[2 * peer + 1]]
                folded_out[peer] = fold(
                    first, second, first[:, HEAD_DIM:] + second[:, HEAD_DIM:]
                ).astype(low)
            for p, total in enumerate((None, k_sum, v_sum)):
                if p:
                    for s in range(2 * chunks):
                        blocks_out[p - 1, s] = total[pair_ref[s]].astype(low)
                for cp in blocks[p]:
                    cp.start()
                own[p].start()

    def slot(c):
        return lax.rem(c, 4)

    def pair_copy(c):
        return remote(pair_out.at[lax.rem(c, 2)], pair_in.at[c], pair_sem, (c,), sibling)

    def x_copy(c):
        return remote(x_out.at[c], x_in.at[c], x_sem, (c,), across)

    def y_copy(c):
        return remote(y_out.at[slot(c)], y_in.at[c], y_sem, (c,), over_y)

    def near_copy(c):
        return remote(near_out.at[slot(c)], near_in.at[c], near_sem, (c,), near)

    def far_copy(c):
        return remote(far_out.at[slot(c)], far_in.at[c], far_sem, (c,), far)

    def own_z_copy(c):
        piece = total_ref.at[c, y, mine]
        return remote(piece, piece, own_z_sem, (c,), far)

    def wide_copy(c):
        piece = total_ref.at[c, y, two(odd)]
        return remote(piece, piece, wide_sem, (c,), near)

    def last_copy(c):
        piece = total_ref.at[c, y]
        return remote(piece, piece, last_sem, (c,), over_y)

    def reuse(copy, c, slots):
        @pl.when(c >= slots)
        def _():
            copy(c - slots).wait_send()

    def partial(c, shard):
        left, right = sum_sources(c)
        return dot_nn(left_ref[left, shard], right_all[right])

    def stage_pair(c):
        reuse(pair_copy, c, 2)
        for side in range(2):
            pair_out[lax.rem(c, 2), side] = partial(c, 2 * side + 1 - core).astype(low)
        pair_copy(c).start()

    def stage_x(c):
        pair_copy(c).wait_recv()
        x_out[c] = (partial(c, 2 * (1 - x) + core) + pair_in[c, 1 - x].astype(wide)).astype(low)
        x_copy(c).start()

    def stage_y(c):
        mine_sum = partial(c, 2 * x + core) + pair_in[c, x].astype(wide)
        x_copy(c).wait_recv()
        total = mine_sum + x_in[c].astype(wide)
        first, second = total[:, :384], total[:, 384:]
        reuse(y_copy, c, 4)
        y_out[slot(c)] = jnp.where(y == 0, second, first).astype(low)
        y_copy(c).start()
        y_keep[slot(c)] = jnp.where(y == 0, first, second)

    def stage_near(c):
        y_copy(c).wait_recv()
        total = y_keep[slot(c)] + y_in[c].astype(wide)
        first, second = total[:96], total[96:]
        reuse(near_copy, c, 4)
        near_out[slot(c)] = jnp.where(odd == 0, second, first).astype(low)
        near_copy(c).start()
        near_keep[slot(c)] = jnp.where(odd == 0, first, second)

    def stage_far(c):
        near_copy(c).wait_recv()
        total = near_keep[slot(c)] + near_in[c].astype(wide)
        first, second = total[:48], total[48:]
        reuse(far_copy, c, 4)
        far_out[slot(c)] = jnp.where(upper == 0, second, first).astype(low)
        far_copy(c).start()
        far_keep[slot(c)] = jnp.where(upper == 0, first, second)

    def stage_own(c):
        far_copy(c).wait_recv()
        total_ref[c, y, mine] = (far_keep[slot(c)] + far_in[c].astype(wide)).astype(low)
        own_z_copy(c).start()

    def stage_wide(c):
        own_z_copy(c).wait_recv()
        wide_copy(c).start()

    def stage_last(c):
        wide_copy(c).wait_recv()
        last_copy(c).start()

    token_ship = pltpu.make_async_copy(token_ref, token_out, ship_sem.at[PARTS])
    small_ship = pltpu.make_async_copy(small_out, small_dst, ship_sem.at[PARTS + 1])

    def small_step(t):
        peers = [sibling, across, over_y, near, far]
        copies = [
            remote(s_out.at[k], s_in.at[k], s_sem, (k,), peer) for k, peer in enumerate(peers)
        ]

        for p in range(3):

            @pl.when(t == JOIN_AT[p])
            def _():
                own[p].wait()
                for cp in blocks[p]:
                    cp.wait_recv()
                if p:
                    right_all[p] = join_pairs(lambda peer: both(blocks_in.at[p - 1], peer))
                else:
                    right_all[p] = join_folded(lambda peer: folded_in[peer], lead)

        @pl.when(t == SMALL_AT[0])
        def _():
            loads[5].wait()
            s_out[0] = sums_ref[...]
            s_out[0, ROW_BQ : ROW_BQ + 1] = column_sum(right_all[0].astype(wide))
            s_out[0, ROW_BV : ROW_BV + 1] = column_sum(right_all[2].astype(wide))
            copies[0].start()

        for k in range(1, 5):

            @pl.when(t == SMALL_AT[k])
            def _():
                copies[k - 1].wait()
                s_out[k] = s_out[k - 1] + s_in[k - 1]
                copies[k].start()

        @pl.when(t == SMALL_AT[5])
        def _():
            copies[4].wait()
            total = s_out[4] + s_in[4]
            quarter = total.shape[1] // 4
            cuts = [slice(f * quarter, (f + 1) * quarter) for f in range(4)]
            pick = lambda choices: sum(
                jnp.where(fsdp == f, choice, 0.0) for f, choice in enumerate(choices)
            )
            small_out[...] = jnp.zeros_like(small_out)
            small_out[:8] = pick([total[:8, cut] for cut in cuts])
            line = pick([total[ROW_BI + f : ROW_BI + f + 1] for f in range(4)])
            for j, cut in enumerate(cuts):
                small_out[8 + j : 9 + j] = line[:, cut]
            small_ship.start()

        @pl.when(t == TOKEN_AT)
        def _():
            load.wait()
            loads[6].wait()
            width = resid_ref.shape[1]
            token_ref[...] = resid_ref[...] + sum(
                dot_nt(
                    right_all[part],
                    w_qkv[:, :, part * width : (part + 1) * width].reshape(width, width),
                )
                for part in range(3)
            )
            token_ship.start()

    stages = [
        ("pair", stage_pair),
        ("x", stage_x),
        ("last", stage_last),
        ("wide", stage_wide),
        ("own", stage_own),
        ("far", stage_far),
        ("near", stage_near),
        ("y", stage_y),
    ]

    def step(t, carry):
        attend_step(t)
        small_step(t)
        for name, stage in stages:
            c = planned(name, t)

            @pl.when(c >= 0)
            def _():
                stage(c)

        return carry

    loads[0].wait()
    loads[1].wait()
    lax.fori_loop(0, STEPS, step, 0)

    def ship(c):
        return pltpu.make_async_copy(total_ref.at[c], total_out.at[c], ship_sem.at[c])

    def drain(c, carry):
        x_copy(c).wait_send()
        own_z_copy(c).wait_send()
        wide_copy(c).wait_send()
        last_copy(c).wait()
        ship(c).start()
        return carry

    lax.fori_loop(0, PARTS, drain, 0)
    for c in range(PARTS - 4, PARTS):
        y_copy(c).wait_send()
        near_copy(c).wait_send()
        far_copy(c).wait_send()
    for c in (PARTS - 2, PARTS - 1):
        pair_copy(c).wait_send()
    for cp in grads + blocks[0] + blocks[1] + blocks[2]:
        cp.wait_send()
    for c in range(PARTS):
        ship(c).wait()
    token_ship.wait()
    small_ship.wait()


def back(pairing, lengths, grad, keep, mix, lse, left, right, sums, resid, qkv_full, name):
    blocks = keep.shape[1]
    n = blocks // 2
    low, wide = jnp.bfloat16, jnp.float32
    dma = pltpu.SemaphoreType.DMA
    shape = jax.ShapeDtypeStruct
    total = pltpu.VMEM((blocks, BLK, BLK), wide)
    hbm = pl.BlockSpec(memory_space=pltpu.HBM)
    return pl.pallas_call(
        functools.partial(back_kernel, n),
        out_shape=(
            shape((PARTS, 2, 4, 48, 384), low),
            shape(resid.shape, wide),
            shape((16, 192), wide),
        ),
        in_specs=[smem()] * 2 + [hbm] * 9,
        out_specs=(hbm,) * 3,
        scratch_shapes=[
            pltpu.VMEM(resid.shape, wide),
            pltpu.VMEM((16, 192), wide),
            pltpu.VMEM(keep.shape, low),
            pltpu.VMEM(mix.shape, wide),
            pltpu.VMEM(lse.shape, wide),
            pltpu.VMEM(left.shape, low),
            pltpu.VMEM(sums.shape, wide),
            pltpu.VMEM(resid.shape, wide),
            pltpu.VMEM((PARTS, 2, 4, 48, 384), low),
            pltpu.VMEM(grad.shape, low),
            pltpu.VMEM((blocks, BLK, BLK), low),
            total, total, total,
            pltpu.VMEM(grad.shape, low),
            pltpu.VMEM(grad.shape, low),
            pltpu.VMEM((2, blocks, BLK, BLK), low),
            pltpu.VMEM((2, blocks, BLK, BLK), low),
            pltpu.VMEM(qkv_full.shape, low),
            pltpu.VMEM((9,) + right.shape[1:], low),
            pltpu.VMEM((2, 2, 192, 768), low),
            pltpu.VMEM((PARTS, 2, 192, 768), low),
            pltpu.VMEM((PARTS, 192, 768), low),
            pltpu.VMEM((PARTS, 192, 768), low),
            pltpu.VMEM((4, 192, 384), low),
            pltpu.VMEM((PARTS, 192, 384), low),
            pltpu.VMEM((4, 192, 384), wide),
            pltpu.VMEM((4, 96, 384), low),
            pltpu.VMEM((PARTS, 96, 384), low),
            pltpu.VMEM((4, 96, 384), wide),
            pltpu.VMEM((4, 48, 384), low),
            pltpu.VMEM((PARTS, 48, 384), low),
            pltpu.VMEM((4, 48, 384), wide),
            pltpu.VMEM((5,) + sums.shape, wide),
            pltpu.VMEM((5,) + sums.shape, wide),
            dma((7,)),
            dma((PARTS + 2,)),
            dma((2, n)),
            dma((2, n)),
            dma((2, n)),
            dma((2, n)),
            dma((5,)),
        ]
        + [dma((2, PARTS))] * 8
        + [dma((2, 5))],
        compiler_params=pltpu.CompilerParams(
            collective_id=name, has_side_effects=True, vmem_limit_bytes=61 << 20
        ),
        name="back",
    )(pairing, lengths, grad, keep, mix, lse, left, right, sums, resid, qkv_full)


def finish_kernel(
    total_ref, small_ref, output_ref, token_ref,
    output_out, token_out, qkv_out, out_out, in_out, back_out, *refs
):
    lines, (total, small, through, stage, sems) = refs[:9], refs[9:]
    arrive = [
        pltpu.make_async_copy(total_ref.at[c], total.at[c], sems.at[PARTS + 2 + c])
        for c in range(PARTS)
    ] + [
        pltpu.make_async_copy(small_ref, small, sems.at[2 * PARTS + 2]),
        pltpu.make_async_copy(output_ref, through.at[0], sems.at[2 * PARTS + 3]),
        pltpu.make_async_copy(token_ref, through.at[1], sems.at[2 * PARTS + 4]),
    ]
    for cp in arrive:
        cp.start()
    copies = [
        pltpu.make_async_copy(through.at[0], output_out, sems.at[PARTS]),
        pltpu.make_async_copy(through.at[1], token_out, sems.at[PARTS + 1]),
    ]
    targets = [back_out.at[192 * k : 192 * k + 192] for k in range(4)]
    targets += [in_out.at[:, 768 * k : 768 * k + 768] for k in range(4)]
    targets += [out_out]
    targets += [qkv_out.at[:, 768 * k : 768 * k + 768] for k in range(3)]
    for c, target in enumerate(targets):
        arrive[c].wait()
        for half in range(2):
            for spot in range(4):
                stage[c, 48 * spot : 48 * spot + 48, 384 * half : 384 * half + 384] = total[
                    c, half, spot
                ].astype(jnp.float32)
        copies.append(pltpu.make_async_copy(stage.at[c], target, sems.at[c]))
        copies[-1].start()
    for k in range(2):
        arrive[PARTS + 1 + k].wait()
        copies[k].start()
    arrive[PARTS].wait()
    for i in range(8):
        lines[i][...] = small[i]
    for j in range(4):
        lines[8][192 * j : 192 * j + 192] = small[ROW_BI + j]
    for cp in copies:
        cp.wait()


def finish(total, small, output, token):
    shape = jax.ShapeDtypeStruct
    wide = jnp.float32
    hbm = pl.BlockSpec(memory_space=pltpu.HBM)
    return pl.pallas_call(
        finish_kernel,
        out_shape=(
            shape(output.shape, wide),
            shape(token.shape, wide),
            shape((192, 2304), wide),
            shape((192, 768), wide),
            shape((192, 3072), wide),
            shape((768, 768), wide),
        )
        + (shape((192,), wide),) * 8
        + (shape((768,), wide),),
        in_specs=[hbm] * 4,
        out_specs=(hbm,) * 6 + (vmem(),) * 9,
        scratch_shapes=[
            pltpu.VMEM(total.shape, total.dtype),
            pltpu.VMEM(small.shape, wide),
            pltpu.VMEM((2,) + token.shape, wide),
            pltpu.VMEM((PARTS, 192, 768), wide),
            pltpu.SemaphoreType.DMA((2 * PARTS + 5,)),
        ],
        compiler_params=pltpu.CompilerParams(vmem_limit_bytes=62 << 20),
        name="finish",
    )(total, small, output, token)


def on_device_spread(
    tokens,
    cotangent,
    lengths,
    pairing,
    w_qkv,
    bias_q,
    bias_v,
    w_out,
    bias_out,
    ln1_gain,
    ln1_bias,
    w_in,
    bias_in,
    w_back,
    bias_back,
    ln2_gain,
    ln2_bias,
):
    n = pairing.shape[0] // 2
    inputs = tokens[0]
    vectors = [bias_q, bias_v, bias_out, ln1_gain, ln1_bias, bias_back, ln2_gain, ln2_bias]
    vectors += [bias_in]
    output, grad, left, right, resid, sums, keep, mix, lse, qkv_full = front(
        pairing, lengths, vectors, inputs, cotangent[0], w_qkv, w_out, w_in, w_back, n, 0
    )
    total, token_grad, small_sum = back(
        pairing, lengths, grad, keep, mix, lse, left, right, sums, resid, qkv_full, 1
    )
    (
        output, token_grad, qkv_sum, out_sum, in_sum, back_sum,
        bq, bv, bo, g1, s1, bb, g2, s2, bi,
    ) = finish(total, small_sum, output, token_grad)
    return (
        output[None], token_grad[None], qkv_sum, bq, bv, out_sum, bo, g1, s1, in_sum, bi,
        back_sum, bb, g2, s2,
    )


def solution(mesh):
    return jax.shard_map(
        on_device_spread if mesh.shape["ctx"] == 8 else on_device_any,
        mesh=mesh,
        in_specs=(
            P("fsdp", "ctx", None),
            P("fsdp", "ctx", None),
            P("fsdp"),
            P(),
            P("fsdp", None),
            P("fsdp"),
            P("fsdp"),
            P("fsdp", None),
            P("fsdp"),
            P("fsdp"),
            P("fsdp"),
            P("fsdp", None),
            P("fsdp"),
            P("fsdp", None),
            P("fsdp"),
            P("fsdp"),
            P("fsdp"),
        ),
        out_specs=(
            P("fsdp", "ctx", None),
            P("fsdp", "ctx", None),
            P("fsdp", None),
            P("fsdp"),
            P("fsdp"),
            P("fsdp", None),
            P("fsdp"),
            P("fsdp"),
            P("fsdp"),
            P("fsdp", None),
            P("fsdp"),
            P("fsdp", None),
            P("fsdp"),
            P("fsdp"),
            P("fsdp"),
        ),
        check_vma=False,
    )
```
